32 devices in a mesh: blk: 16 (over z, y, core), head: 2 (over x).
Axes of the slice: x: 2, y: 2, z: 4, core: 2. Of those that a mesh axis runs over, the one named last changes fastest.
Arguments:
- tokens: bfloat16 [4096, 2048], P(('blk', 'head')), may hold values from -6 to 6
- attn_gain: bfloat16 [2048], P('blk'), may hold values from 0.25 to 1.75
- w_query: bfloat16 [2048, 2048], P('blk', 'head'), may hold values from -0.125 to 0.125
- w_key: bfloat16 [2048, 1024], P('blk', 'head'), may hold values from -0.125 to 0.125
- w_value: bfloat16 [2048, 1024], P('blk', 'head'), may hold values from -0.125 to 0.125
- w_out: bfloat16 [2048, 2048], P(('head', 'blk')), may hold values from -3.5 to 3.5
- mlp_gain: bfloat16 [2048], P('blk'), may hold values from 0.25 to 1.75
- w_gate: bfloat16 [2048, 8192], P('blk', 'head'), may hold values from -0.125 to 0.125
- w_up: bfloat16 [2048, 8192], P('blk', 'head'), may hold values from -0.125 to 0.125
- w_down: bfloat16 [8192, 2048], P(('head', 'blk')), may hold values from -0.0625 to 0.0625
- block_ids: int32 [4096], P('blk'), may hold values from 0 to 31, never falling along the last dimension, each value on 1 to 256 neighbouring positions
- positions: int32 [4096], P('blk'), may hold values from 0 to 6142, as said below
- cotangent: bfloat16 [4096, 2048], P(('blk', 'head')), may hold values from -6 to 6
Outputs:
- output: bfloat16 [4096, 2048], P(('blk', 'head'))
- tokens_grad: bfloat16 [4096, 2048], P(('blk', 'head'))
- attn_gain_grad: float32 [2048], P('blk')
- w_query_grad: float32 [2048, 2048], P('blk', 'head')
- w_key_grad: float32 [2048, 1024], P('blk', 'head')
- w_value_grad: float32 [2048, 1024], P('blk', 'head')
- w_out_grad: float32 [2048, 2048], P(('head', 'blk'))
- mlp_gain_grad: float32 [2048], P('blk')
- w_gate_grad: float32 [2048, 8192], P('blk', 'head')
- w_up_grad: float32 [2048, 8192], P('blk', 'head')
- w_down_grad: float32 [8192, 2048], P(('head', 'blk'))
The draws below stay inside these ranges and needn't reach their ends.
Inputs may be any that keep to these rules, and one draw needn't show every extreme that they name: `block_ids`: block numbers never fall along the sequence; each block holds 1 to 256 tokens and some block exactly 256. `positions`: the first token has position 0 and each following one a position 1 or 2 higher; the last token has position 6142.
All inputs are finite; a program needn't handle non-finite values.
Results may differ from the reference program's by a relative error of at most 0.018.
Values may be sent and summed in bfloat16 or wider, within the bound.
A program may use at most 256 MiB of HBM per device.

```python
import math
import jax
import jax.numpy as jnp
import numpy as np
from jax import lax

D = 2048
HQ = 8
KV = 4
HD = 256
FF = 8192
BLOCK = 256
SEQ = 4096
BLOCKS = 32


def draw_positions(key, part):
    key = jax.random.fold_in(key, 7)
    order = jax.random.permutation(key, SEQ - 1)
    strides = 1 + (order < (SEQ - 1) // 2).astype(jnp.int32)
    return jnp.concatenate([jnp.zeros((1,), jnp.int32), jnp.cumsum(strides).astype(jnp.int32)]).astype(jnp.int32)


def raised(values, key, source, target, blocks, factor):
    owner, partner = [(jnp.arange(values.shape[axis_at]) // (values.shape[axis_at] // blocks)).reshape([-1 if axis == axis_at else 1 for axis in range(values.ndim)]) for axis_at in (source, target)]
    chosen = jax.random.permutation(key, blocks)[partner]
    strong = (owner == chosen) | (owner == (partner + blocks // 2) % blocks)
    return jnp.where(strong, factor * values, values)


def shard_levels(rng, extent, cuts, smallest, top_value):
    gain = 1.0
    for position, blocks in cuts:
        steps = jax.random.uniform(jax.random.fold_in(jax.random.fold_in(rng, 6), position), (blocks,), jnp.float32, smallest / len(cuts), top_value / len(cuts))
        gain = gain * jnp.repeat(jnp.exp(steps), extent[position] // blocks).reshape((-1,) + (1,) * (len(extent) - 1 - position))
    return gain


def split_up(count, total, most, slope):
    portions = [(1 << 20) // math.isqrt(grade ** slope) + 1 for grade in range(2, count + 1)]
    spare, counts = total - most - (count - 1), [1] * (count - 1)
    while spare > 0:
        candidates = [i for i in range(count - 1) if counts[i] < most]
        whole, budget = sum([portions[i] for i in candidates]), spare
        for i in candidates:
            addition = min(most - counts[i], max(1, budget * portions[i] // whole), spare)
            counts[i] = counts[i] + addition
            spare = spare - addition
    return np.array([most] + counts)


def uneven(key, amount, total, limit, lean):
    if amount == 2:
        one = jax.random.randint(key, (), max(1, total - limit), min(limit, total - 1) + 1)
        return jnp.stack([one, total - one])
    sizes = jnp.asarray(split_up(amount, total, limit, lean), jnp.int32)
    twos = (amount - 1) // 2
    source_of, taker = sizes[1:1 + 2 * twos:2], sizes[2:2 + 2 * twos:2]
    margin = jnp.minimum(source_of - 1, limit - taker)
    shifted = jax.random.randint(jax.random.fold_in(key, 1), (twos,), 0, 1 << 20) % (margin + 1)
    sizes = sizes.at[1:1 + 2 * twos:2].set(source_of - shifted).at[2:2 + 2 * twos:2].set(taker + shifted)
    return sizes[jax.random.permutation(jax.random.fold_in(key, 2), amount)]


def bell_draw(key, shape, spread, limit, split=(), kind=jnp.bfloat16):
    drawn = spread * jax.random.normal(key, shape, jnp.float32)
    if split:
        drawn = drawn * shard_levels(key, shape, split, -0.22, 0.18)
    return jnp.clip(drawn, -limit, limit).astype(kind)


def bell_draw_with(rng, shape, scale, limit, shards, heavy, held_as=jnp.bfloat16):
    values = scale * jax.random.normal(rng, shape, jnp.float32)
    if shards:
        values = values * shard_levels(rng, shape, shards, -0.22, 0.18)
    return jnp.clip(raised(values, jax.random.fold_in(rng, 3), *heavy), -limit, limit).astype(held_as)


def setup_inputs(seed: int = 0) -> dict:
    streams_of = jax.random.split(jax.random.key(seed), 14)
    tokens = bell_draw_with(streams_of[0], (SEQ, D), 1.0, 6.0, ((0, 32),), (0, 1, 32, 2.75))
    attn_gain = jnp.clip(1.0 + 0.15 * jax.random.normal(streams_of[1], (D,), jnp.float32), 0.25, 1.75).astype(jnp.bfloat16)
    w_query = bell_draw(streams_of[2], (D, HQ * HD), D ** -0.5, 0.125, ((0, 16), (1, 2)))
    w_key = bell_draw(streams_of[3], (D, KV * HD), D ** -0.5, 0.125, ((0, 16), (1, 2)))
    w_value = bell_draw(streams_of[4], (D, KV * HD), D ** -0.5, 0.125, ((0, 16), (1, 2)))
    w_out = bell_draw(streams_of[5], (HQ * HD, D), (max(1, 12288 // SEQ)) ** -0.5, 3.5, ((0, 32),))
    mlp_gain = jnp.clip(1.0 + 0.15 * jax.random.normal(streams_of[6], (D,), jnp.float32), 0.25, 1.75).astype(jnp.bfloat16)
    w_gate = bell_draw(streams_of[7], (D, FF), D ** -0.5, 0.125, ((0, 16), (1, 2)))
    w_up = bell_draw(streams_of[8], (D, FF), D ** -0.5, 0.125, ((0, 16), (1, 2)))
    w_down = bell_draw(streams_of[9], (FF, D), FF ** -0.5, 0.0625, ((0, 32),))
    block_ids = jnp.searchsorted(jnp.cumsum(uneven(streams_of[10], BLOCKS, SEQ, BLOCK, 2)), jnp.arange(SEQ), side="right").astype(jnp.int32)
    positions = draw_positions(jax.random.fold_in(streams_of[13], 71), 0)
    cotangent = bell_draw_with(streams_of[12], (SEQ, D), 1.0, 6.0, ((0, 32),), (0, 1, 32, 2.75))
    return {"tokens": tokens, "attn_gain": attn_gain, "w_query": w_query, "w_key": w_key, "w_value": w_value, "w_out": w_out, "mlp_gain": mlp_gain, "w_gate": w_gate, "w_up": w_up, "w_down": w_down, "block_ids": block_ids, "positions": positions, "cotangent": cotangent}


@jax.custom_vjp
def low(v):
    return lax.optimization_barrier(v.astype(jnp.bfloat16)).astype(jnp.float32)

@jax.custom_vjp
def low_back(v):
    return v

def low_keep(v):
    return (low(v), None)

def low_pass(kept, grad):
    return (grad,)

def back_keep(v):
    return (v, None)

def back_low(kept, grad):
    return (low(grad),)
low.defvjp(low_keep, low_pass)
low_back.defvjp(back_keep, back_low)
eps_norm = 1e-06
rope_base = 1000042.0

def matmul_high(left, right):
    return jnp.dot(left, right, precision=lax.Precision.HIGHEST, preferred_element_type=jnp.float32)

def rms_scale(rows):
    return lax.rsqrt(lax.optimization_barrier(jnp.mean(rows * rows, axis=-1, keepdims=True)) + eps_norm)

def rope_tables(positions):
    inv_freqs = rope_base ** (-2.0 * jnp.arange(HD // 2, dtype=jnp.float32) / HD)
    angles = positions.astype(jnp.float32)[:, None] * inv_freqs[None, :]
    return (jnp.cos(angles)[:, None, :], jnp.sin(angles)[:, None, :])

def rotate(heads, cos_table, sine_table):
    half_size = heads.shape[-1] // 2
    lower_half = heads[..., :half_size]
    upper_half = heads[..., half_size:]
    return jnp.concatenate([lower_half * cos_table - upper_half * sine_table, upper_half * cos_table + lower_half * sine_table], axis=-1)

def reference(tokens, attn_gain, w_query, w_key, w_value, w_out, mlp_gain, w_gate, w_up, w_down, block_ids, positions, cotangent):
    cos_table, sine_table = rope_tables(positions)
    group_size = HQ // KV
    rows_block = min(512, SEQ)
    block_count = SEQ // rows_block
    score_scale = HD ** (-0.5)
    query_ids = block_ids.reshape(block_count, rows_block)

    def forward(params, inputs):
        gain_attn, query_w, key_w, value_w, out_w, gain_mlp, gate_w, up_w, down_w = params
        normed = low(inputs * rms_scale(inputs) * gain_attn)
        queries = low(rotate(low_back(matmul_high(normed, query_w)).reshape(SEQ, HQ, HD), cos_table, sine_table))
        keys = low(rotate(low_back(matmul_high(normed, key_w)).reshape(SEQ, KV, HD), cos_table, sine_table))
        values = low_back(low(matmul_high(normed, value_w))).reshape(SEQ, KV, HD)

        def attend(query_piece):
            query_rows, row_ids = query_piece
            grouped = query_rows.reshape(rows_block, KV, group_size, HD)
            scores = jnp.einsum('qkgd,ckd->kgqc', grouped, keys, precision=lax.Precision.HIGHEST) * score_scale
            scores = low_back(scores)
            visible = block_ids[None, :] <= row_ids[:, None]
            scores = jnp.where(visible[None, None], scores, -1e+30)
            row_max = lax.optimization_barrier(jnp.max(scores, axis=-1, keepdims=True))
            weights = jnp.exp(scores - row_max)
            probabilities = low(weights / lax.optimization_barrier(jnp.sum(weights, axis=-1, keepdims=True)))
            mixed_rows = jnp.einsum('kgqc,ckd->qkgd', probabilities, values, precision=lax.Precision.HIGHEST)
            return mixed_rows.reshape(rows_block, HQ * HD)
        heads_out = lax.map(jax.checkpoint(attend), (queries.reshape(block_count, rows_block, HQ, HD), query_ids))
        attended = low_back(low(heads_out.reshape(SEQ, HQ * HD)))
        hidden = inputs + low_back(matmul_high(attended, out_w))
        normed_mlp = low(hidden * rms_scale(hidden) * gain_mlp)
        gate_pre = low_back(matmul_high(normed_mlp, gate_w))
        up_pre = low_back(matmul_high(normed_mlp, up_w))
        active = low(jax.nn.silu(gate_pre) * up_pre)
        return hidden + matmul_high(active, down_w)
    params = (attn_gain.astype(jnp.float32), w_query.astype(jnp.float32), w_key.astype(jnp.float32), w_value.astype(jnp.float32), w_out.astype(jnp.float32), mlp_gain.astype(jnp.float32), w_gate.astype(jnp.float32), w_up.astype(jnp.float32), w_down.astype(jnp.float32))
    output, pullback = jax.vjp(forward, params, tokens.astype(jnp.float32))
    param_grads, input_grad = pullback(cotangent.astype(jnp.float32))
    return (output.astype(jnp.bfloat16), input_grad.astype(jnp.bfloat16), param_grads[0], param_grads[1], param_grads[2], param_grads[3], param_grads[4], param_grads[5], param_grads[6], param_grads[7], param_grads[8])
```

```python
import jax
import jax.numpy as jnp
from jax import lax
from jax.experimental import pallas as pl
from jax.experimental.pallas import tpu as pltpu
from jax.sharding import PartitionSpec as P

HD = 256


eps_norm = 1e-06
rope_base = 1000042.0


def rms_scale(rows):
    return lax.rsqrt(jnp.mean(rows * rows, axis=-1, keepdims=True) + eps_norm)


def rope_tables(positions):
    inv_freqs = rope_base ** (-2.0 * jnp.arange(HD // 2, dtype=jnp.float32) / HD)
    angles = positions.astype(jnp.float32)[:, None] * inv_freqs[None, :]
    return (jnp.cos(angles)[:, None, :], jnp.sin(angles)[:, None, :])


def rotate(heads, cos_table, sine_table):
    half_size = heads.shape[-1] // 2
    lower_half = heads[..., :half_size]
    upper_half = heads[..., half_size:]
    return jnp.concatenate(
        [
            lower_half * cos_table - upper_half * sine_table,
            upper_half * cos_table + lower_half * sine_table,
        ],
        axis=-1,
    )


def product(left, right):
    return jnp.dot(left, right, preferred_element_type=jnp.float32)


def times_transposed(left, right):
    return lax.dot_general(
        left, right, (((1,), (1,)), ((), ())), preferred_element_type=jnp.float32
    )


def transposed_times(left, right):
    return lax.dot_general(
        left, right, (((0,), (0,)), ((), ())), preferred_element_type=jnp.float32
    )


def norm_backward(grad_normed, inputs, inv_scale, gain_rows):
    unit_rows = inputs * inv_scale
    grad_unit = grad_normed * gain_rows
    gain_term = jnp.sum(grad_normed * unit_rows, axis=0)
    grad_inputs = inv_scale * (
        grad_unit - unit_rows * jnp.mean(grad_unit * unit_rows, axis=-1, keepdims=True)
    )
    return (grad_inputs, gain_term)


def body(
    tokens,
    attn_gain,
    w_query,
    w_key,
    w_value,
    w_out,
    mlp_gain,
    w_gate,
    w_up,
    w_down,
    block_ids,
    positions,
    cotangent,
):
    rows_own = tokens.shape[0]
    head_rank = lax.axis_index("head")
    tokens_all, cot_all = (
        lax.all_gather(tokens, "head", axis=0, tiled=True),
        lax.all_gather(cotangent, "head", axis=0, tiled=True),
    )
    rows_all = tokens_all.shape[0]
    gain_attn, query_w, key_w, value_w, out_w = (
        lax.all_gather(attn_gain, "blk", axis=0, tiled=True),
        lax.all_gather(w_query, "blk", axis=0, tiled=True),
        lax.all_gather(w_key, "blk", axis=0, tiled=True),
        lax.all_gather(w_value, "blk", axis=0, tiled=True),
        lax.all_gather(w_out, "blk", axis=0, tiled=True),
    )
    gain_mlp, gate_w, up_w, down_w = (
        lax.all_gather(mlp_gain, "blk", axis=0, tiled=True),
        lax.all_gather(w_gate, "blk", axis=0, tiled=True),
        lax.all_gather(w_up, "blk", axis=0, tiled=True),
        lax.all_gather(w_down, "blk", axis=0, tiled=True),
    )
    key_ids = lax.all_gather(block_ids, "blk", axis=0, tiled=True)
    heads_local = query_w.shape[1] // HD
    kv_local = key_w.shape[1] // HD
    kv_width = kv_local * HD
    group_size = heads_local // kv_local
    cos_table, sine_table = rope_tables(positions)
    score_scale = HD ** (-0.5)
    seq_len = key_ids.shape[0]
    key_block = min(2048, seq_len)
    block_total = seq_len // key_block
    block_steps = jnp.arange(block_total)
    top_query = jnp.max(block_ids)
    inputs = tokens_all.astype(jnp.float32)
    inv_attn = rms_scale(inputs)
    normed = (inputs * inv_attn * gain_attn.astype(jnp.float32)).astype(jnp.bfloat16)
    queries = rotate(
        product(normed, query_w).reshape(rows_all, heads_local, HD), cos_table, sine_table
    ).astype(jnp.bfloat16)
    keys_own = rotate(product(normed, key_w).reshape(rows_all, kv_local, HD), cos_table, sine_table)
    keys_own = keys_own.astype(jnp.bfloat16).reshape(rows_all, kv_width)
    values_own = product(normed, value_w).astype(jnp.bfloat16)
    keys_all, values_all = (
        lax.all_gather(keys_own, "blk", axis=0, tiled=True),
        lax.all_gather(values_own, "blk", axis=0, tiled=True),
    )
    grouped = queries.reshape(rows_all, kv_local, group_size, HD)

    def slice_keys(key_start, count):
        key_rows = lax.dynamic_slice_in_dim(keys_all, key_start, count, 0).reshape(
            count, kv_local, HD
        )
        value_rows = lax.dynamic_slice_in_dim(values_all, key_start, count, 0).reshape(
            count, kv_local, HD
        )
        block_keys = lax.dynamic_slice_in_dim(key_ids, key_start, count, 0)
        return (key_rows, value_rows, block_keys)

    def scores_for(key_rows, block_keys):
        scores = (
            jnp.einsum("qkgd,ckd->kgqc", grouped, key_rows, preferred_element_type=jnp.float32)
            * score_scale
        )
        visible = (block_keys[None, :] <= block_ids[:, None])[None, None]
        return (scores, visible)

    def max_sum(state_pair, step_index):
        key_start = step_index * key_block

        def max_live(pair):
            run_max, run_sum = pair
            key_rows, value_rows, block_keys = slice_keys(key_start, key_block)
            scores, visible = scores_for(key_rows, block_keys)
            scores = jnp.where(visible, scores, -1e30)
            new_max = jnp.maximum(run_max, jnp.max(scores, axis=-1))
            kept_terms = jnp.where(visible, jnp.exp(scores - new_max[..., None]), 0.0)
            return (new_max, run_sum * jnp.exp(run_max - new_max) + jnp.sum(kept_terms, axis=-1))

        def max_skipped(pair):
            return pair

        return (lax.cond(key_ids[key_start] <= top_query, max_live, max_skipped, state_pair), None)

    start_max = jnp.full((kv_local, group_size, rows_all), -1e30, jnp.float32)
    start_sum = jnp.zeros((kv_local, group_size, rows_all), jnp.float32)
    (run_max, run_sum), unused_max = lax.scan(max_sum, (start_max, start_sum), block_steps)
    log_total = run_max + jnp.log(run_sum)

    def weighted(accum_rows, step_index):
        key_start = step_index * key_block

        def weighted_live(accum):
            key_rows, value_rows, block_keys = slice_keys(key_start, key_block)
            scores, visible = scores_for(key_rows, block_keys)
            probabilities = jnp.where(visible, jnp.exp(scores - log_total[..., None]), 0.0).astype(
                jnp.bfloat16
            )
            return accum + jnp.einsum(
                "kgqc,ckd->qkgd", probabilities, value_rows, preferred_element_type=jnp.float32
            )

        def weighted_skipped(accum):
            return accum

        return (
            lax.cond(key_ids[key_start] <= top_query, weighted_live, weighted_skipped, accum_rows),
            None,
        )

    attended, unused_rows = lax.scan(
        weighted, jnp.zeros((rows_all, kv_local, group_size, HD), jnp.float32), block_steps
    )
    attended_low = attended.reshape(rows_all, heads_local * HD).astype(jnp.bfloat16)
    branch_sum = lax.psum(product(attended_low, out_w).astype(jnp.bfloat16), "head").astype(
        jnp.float32
    )
    hidden = inputs + branch_sum
    inv_mlp = rms_scale(hidden)
    normed_mlp = (hidden * inv_mlp * gain_mlp.astype(jnp.float32)).astype(jnp.bfloat16)
    gate_pre = product(normed_mlp, gate_w)
    up_pre = product(normed_mlp, up_w)
    sigmoid_gate = jax.nn.sigmoid(gate_pre)
    active = (gate_pre * sigmoid_gate * up_pre).astype(jnp.bfloat16)
    mlp_own = lax.psum_scatter(
        product(active, down_w).astype(jnp.bfloat16), "head", scatter_dimension=0, tiled=True
    ).astype(jnp.float32)
    hidden_own = lax.dynamic_slice_in_dim(hidden, head_rank * rows_own, rows_own, 0)
    output = (hidden_own + mlp_own).astype(jnp.bfloat16)
    gain_attn, query_w, key_w, value_w, out_w = (
        lax.all_gather(attn_gain, "blk", axis=0, tiled=True),
        lax.all_gather(w_query, "blk", axis=0, tiled=True),
        lax.all_gather(w_key, "blk", axis=0, tiled=True),
        lax.all_gather(w_value, "blk", axis=0, tiled=True),
        lax.all_gather(w_out, "blk", axis=0, tiled=True),
    )
    gain_mlp, gate_w, up_w, down_w = (
        lax.all_gather(mlp_gain, "blk", axis=0, tiled=True),
        lax.all_gather(w_gate, "blk", axis=0, tiled=True),
        lax.all_gather(w_up, "blk", axis=0, tiled=True),
        lax.all_gather(w_down, "blk", axis=0, tiled=True),
    )
    grad_active = times_transposed(cot_all, down_w)
    grad_gate = (
        grad_active * up_pre * sigmoid_gate * (1.0 + gate_pre * (1.0 - sigmoid_gate))
    ).astype(jnp.bfloat16)
    grad_up = (grad_active * gate_pre * sigmoid_gate).astype(jnp.bfloat16)
    grad_gate_w = transposed_times(normed_mlp, grad_gate)
    grad_up_w = transposed_times(normed_mlp, grad_up)
    grad_down_w = transposed_times(active, cot_all)
    grad_normed_part = times_transposed(grad_gate, gate_w) + times_transposed(grad_up, up_w)
    grad_normed_mlp = lax.psum(grad_normed_part.astype(jnp.bfloat16), "head").astype(jnp.float32)
    grad_hidden_norm, gain_mlp_term = norm_backward(
        grad_normed_mlp, hidden, inv_mlp, gain_mlp.astype(jnp.float32)
    )
    grad_hidden = cot_all.astype(jnp.float32) + grad_hidden_norm
    mlp_results = (
        lax.psum_scatter(gain_mlp_term, "blk", scatter_dimension=0, tiled=True),
        lax.psum_scatter(grad_gate_w, "blk", scatter_dimension=0, tiled=True),
        lax.psum_scatter(grad_up_w, "blk", scatter_dimension=0, tiled=True),
        lax.psum_scatter(grad_down_w, "blk", scatter_dimension=0, tiled=True),
    )
    grad_branch = grad_hidden.astype(jnp.bfloat16)
    grad_out_w = transposed_times(attended_low, grad_branch)
    grad_attended = times_transposed(grad_branch, out_w).astype(jnp.bfloat16)
    grad_grouped = grad_attended.reshape(rows_all, kv_local, group_size, HD)
    delta_rows = jnp.transpose(
        jnp.sum(grad_grouped.astype(jnp.float32) * attended, axis=-1), (1, 2, 0)
    )

    def pair_backward(key_rows, value_rows, block_keys):
        count = key_rows.shape[0]
        scores, visible = scores_for(key_rows, block_keys)
        probabilities = jnp.where(visible, jnp.exp(scores - log_total[..., None]), 0.0)
        grad_probs = jnp.einsum(
            "qkgd,ckd->kgqc", grad_grouped, value_rows, preferred_element_type=jnp.float32
        )
        grad_scores = (probabilities * (grad_probs - delta_rows[..., None])).astype(jnp.bfloat16)
        query_terms = jnp.einsum(
            "kgqc,ckd->qkgd", grad_scores, key_rows, preferred_element_type=jnp.float32
        )
        key_terms = (
            jnp.einsum("kgqc,qkgd->ckd", grad_scores, grouped, preferred_element_type=jnp.float32)
            * score_scale
        )
        value_terms = jnp.einsum(
            "kgqc,qkgd->ckd",
            probabilities.astype(jnp.bfloat16),
            grad_grouped,
            preferred_element_type=jnp.float32,
        )
        return (
            query_terms,
            key_terms.reshape(count, kv_width),
            value_terms.reshape(count, kv_width),
        )

    query_zeros = jnp.zeros((rows_all, kv_local, group_size, HD), jnp.float32)

    def backward_block(accum_rows, step_index):
        key_start = step_index * key_block

        def backward_live(unused_arg):
            key_rows, value_rows, block_keys = slice_keys(key_start, key_block)
            return pair_backward(key_rows, value_rows, block_keys)

        def backward_skipped(unused_arg):
            empty_terms = jnp.zeros((key_block, kv_width), jnp.float32)
            return (query_zeros, empty_terms, empty_terms)

        query_terms, key_terms, value_terms = lax.cond(
            key_ids[key_start] <= top_query, backward_live, backward_skipped, 0
        )
        return (accum_rows + query_terms, (key_terms, value_terms))

    grad_query_rot, (key_terms, value_terms) = lax.scan(backward_block, query_zeros, block_steps)
    key_terms = key_terms.reshape(seq_len, kv_width)
    value_terms = value_terms.reshape(seq_len, kv_width)
    key_grad_own, value_grad_own = (
        lax.psum_scatter(key_terms, "blk", scatter_dimension=0, tiled=True),
        lax.psum_scatter(value_terms, "blk", scatter_dimension=0, tiled=True),
    )
    grad_query_rot = grad_query_rot * score_scale
    grad_key = rotate(key_grad_own.reshape(rows_all, kv_local, HD), cos_table, -sine_table)
    grad_key = grad_key.reshape(rows_all, kv_width).astype(jnp.bfloat16)
    grad_value = value_grad_own.astype(jnp.bfloat16)
    grad_query = rotate(grad_query_rot.reshape(rows_all, heads_local, HD), cos_table, -sine_table)
    grad_query = grad_query.reshape(rows_all, heads_local * HD).astype(jnp.bfloat16)
    grad_query_w = transposed_times(normed, grad_query)
    grad_key_w = transposed_times(normed, grad_key)
    grad_value_w = transposed_times(normed, grad_value)
    grad_normed_part = (
        times_transposed(grad_query, query_w)
        + times_transposed(grad_key, key_w)
        + times_transposed(grad_value, value_w)
    )
    grad_normed = lax.psum(grad_normed_part.astype(jnp.bfloat16), "head").astype(jnp.float32)
    grad_inputs_norm, gain_attn_term = norm_backward(
        grad_normed, inputs, inv_attn, gain_attn.astype(jnp.float32)
    )
    grad_inputs = grad_hidden + grad_inputs_norm
    grad_own = lax.dynamic_slice_in_dim(grad_inputs, head_rank * rows_own, rows_own, 0).astype(
        jnp.bfloat16
    )
    attn_results = (
        lax.psum_scatter(gain_attn_term, "blk", scatter_dimension=0, tiled=True),
        lax.psum_scatter(grad_query_w, "blk", scatter_dimension=0, tiled=True),
        lax.psum_scatter(grad_key_w, "blk", scatter_dimension=0, tiled=True),
        lax.psum_scatter(grad_value_w, "blk", scatter_dimension=0, tiled=True),
        lax.psum_scatter(grad_out_w, "blk", scatter_dimension=0, tiled=True),
    )
    return (
        output,
        grad_own,
        attn_results[0],
        attn_results[1],
        attn_results[2],
        attn_results[3],
        attn_results[4],
        mlp_results[0],
        mlp_results[1],
        mlp_results[2],
        mlp_results[3],
    )


MESH = pl.DeviceIdType.MESH
LINE = 4
VMEM_BYTES = 60 * 2**20


def place():
    blk, head = lax.axis_index("blk"), lax.axis_index("head")
    return blk // 4, (blk // 2) % 2, blk % 2, head


def device(z, y, c, h):
    return (z * 4 + y * 2 + c, h)


def remote(src, dst, send_sem, recv_sem, target):
    return pltpu.make_async_remote_copy(
        src_ref=src,
        dst_ref=dst,
        send_sem=send_sem,
        recv_sem=recv_sem,
        device_id=target,
        device_id_type=MESH,
    )


def greet(target):
    pl.semaphore_signal(
        pltpu.get_barrier_semaphore(), inc=1, device_id=target, device_id_type=MESH
    )


def greet_all(blk_total, head_total):
    blk, head = lax.axis_index("blk"), lax.axis_index("head")
    for other in range(blk_total):
        for half in range(head_total):

            @pl.when(jnp.logical_or(blk != other, head != half))
            def _():
                greet((jnp.int32(other), jnp.int32(half)))

    pl.semaphore_wait(pltpu.get_barrier_semaphore(), blk_total * head_total - 1)


def greet_plane():
    z, y, c, h = place()

    @pl.when(z > 0)
    def _():
        greet(device(z - 1, y, c, h))

    @pl.when(z < LINE - 1)
    def _():
        greet(device(z + 1, y, c, h))

    greet(device(z, 1 - y, c, h))
    pl.semaphore_wait(
        pltpu.get_barrier_semaphore(),
        1 + (z + LINE - 1) // LINE + (LINE - 1 - z + LINE - 1) // LINE,
    )


class Gather:
    CUTS = ((0, 64), (64, 48), (112, 16), (112, 16))
    SEMS = [(3, 4)] * 4 + [(4, 2)] * 2 + [(2,)]

    @staticmethod
    def scratch():
        return [pltpu.SemaphoreType.DMA(shape) for shape in Gather.SEMS] + [
            pltpu.SemaphoreType.DMA
        ]

    def __init__(self, src, out, sems):
        self.src, self.out = src, out
        (self.up_s, self.up_r, self.dn_s, self.dn_r, self.y_s, self.y_r, self.b_sr, self.own_sem) = sems
        self.z, self.y, self.c, self.h = place()

    def piece(self, line, elem):
        y = 1 - self.y if elem == 3 else self.y
        start, size = self.CUTS[elem]
        return self.out.at[line * 2 + y, pl.ds(start, size)]

    def first(self, elem):
        if elem == 3:
            return self.piece(self.z, 3)
        start, size = self.CUTS[elem]
        return self.src.at[pl.ds(start, size)]

    def up(self, step, elem):
        src = self.first(elem) if step == 0 else self.piece(self.z - step, elem)
        return remote(
            src, self.piece(self.z - step, elem), self.up_s.at[step, elem], self.up_r.at[step, elem],
            device(self.z + 1, self.y, self.c, self.h),
        )

    def down(self, step, elem):
        src = self.first(elem) if step == 0 else self.piece(self.z + step, elem)
        return remote(
            src, self.piece(self.z + step, elem), self.dn_s.at[step, elem], self.dn_r.at[step, elem],
            device(self.z - 1, self.y, self.c, self.h),
        )

    def up_in(self, step, elem):
        ref = self.piece(self.z - 1 - step, elem)
        return remote(ref, ref, self.up_s.at[step, elem], self.up_r.at[step, elem], device(self.z, self.y, self.c, self.h))

    def down_in(self, step, elem):
        ref = self.piece(self.z + 1 + step, elem)
        return remote(ref, ref, self.dn_s.at[step, elem], self.dn_r.at[step, elem], device(self.z, self.y, self.c, self.h))

    def across(self, line, elem, own=False):
        src = self.first(elem) if own else self.piece(line, elem)
        return remote(
            src, self.piece(line, elem), self.y_s.at[line, elem], self.y_r.at[line, elem],
            device(self.z, 1 - self.y, self.c, self.h),
        )

    def across_in(self, line, elem):
        start, size = self.CUTS[elem]
        ref = self.out.at[line * 2 + 1 - self.y, pl.ds(start, size)]
        return remote(ref, ref, self.y_s.at[line, elem], self.y_r.at[line, elem], device(self.z, self.y, self.c, self.h))

    def across_b(self):
        return remote(
            self.first(2), self.piece(self.z, 2), self.b_sr.at[0], self.b_sr.at[1],
            device(self.z, 1 - self.y, self.c, self.h),
        )

    def across_b_in(self):
        ref = self.piece(self.z, 3)
        return remote(ref, ref, self.b_sr.at[0], self.b_sr.at[1], device(self.z, self.y, self.c, self.h))

    def own_copy(self):
        return pltpu.make_async_copy(self.src, self.out.at[self.z * 2 + self.y], self.own_sem)

    def start(self):
        self.own_copy().start()
        self.across_b().start()
        for elem in (0, 1, 2):

            @pl.when(self.z < LINE - 1)
            def _():
                self.up(0, elem).start()

            @pl.when(self.z > 0)
            def _():
                self.down(0, elem).start()

            if elem < 2:
                self.across(self.z, elem, own=True).start()

    def relay_b(self):
        self.across_b_in().wait_recv()

        @pl.when(self.z < LINE - 1)
        def _():
            self.up(0, 3).start()

        @pl.when(self.z > 0)
        def _():
            self.down(0, 3).start()

    def relay(self, step, elem):
        @pl.when(self.z - 1 - step >= 0)
        def _():
            self.up_in(step, elem).wait_recv()
            if step < LINE - 2:

                @pl.when(self.z < LINE - 1)
                def _():
                    self.up(step + 1, elem).start()

            if elem < 2:
                self.across(self.z - 1 - step, elem).start()

        @pl.when(self.z + 1 + step <= LINE - 1)
        def _():
            self.down_in(step, elem).wait_recv()
            if step < LINE - 2:

                @pl.when(self.z > 0)
                def _():
                    self.down(step + 1, elem).start()

            if elem < 2:
                self.across(self.z + 1 + step, elem).start()

    def relays(self):
        self.relay_b()
        for step in range(LINE - 1):
            for elem in (0, 1, 2, 3):
                self.relay(step, elem)

    def finish(self):
        for line in range(LINE):
            for elem in (0, 1):
                self.across_in(line, elem).wait_recv()
        for line in range(LINE):
            for elem in (0, 1):
                self.across(line, elem).wait_send()
        self.across_b().wait_send()
        for step in range(LINE - 1):
            for elem in range(4):

                @pl.when(jnp.logical_and(self.z < LINE - 1, self.z - step >= 0))
                def _():
                    self.up(step, elem).wait_send()

                @pl.when(jnp.logical_and(self.z > 0, self.z + step <= LINE - 1))
                def _():
                    self.down(step, elem).wait_send()

        self.own_copy().wait()


def gather_kernel(src, out, *sems):
    greet_plane()
    gather = Gather(src, out, sems)
    gather.start()
    gather.relays()
    gather.finish()


ANY = pl.BlockSpec(memory_space=pl.ANY)
INSIDE = pl.BlockSpec(memory_space=pltpu.VMEM)


def kernel_params(collective_id):
    return pltpu.CompilerParams(
        collective_id=collective_id, has_side_effects=True, vmem_limit_bytes=VMEM_BYTES
    )


def gather_plane(rows):
    return pl.pallas_call(
        gather_kernel,
        out_shape=jax.ShapeDtypeStruct((2 * LINE,) + rows.shape, rows.dtype),
        in_specs=[ANY],
        out_specs=ANY,
        scratch_shapes=Gather.scratch(),
        compiler_params=kernel_params(1),
        name="gather_plane",
    )(rows)


class Reduce:
    CUTS = ((0, 64), (64, 64))

    @staticmethod
    def scratch(width):
        inbox = pltpu.VMEM((LINE, 128, width), jnp.bfloat16)
        return [inbox] * 3 + [pltpu.SemaphoreType.DMA((LINE, 2))] * 6

    def __init__(self, parts, refs):
        self.parts = parts
        self.y_in, self.up_in, self.dn_in = refs[:3]
        self.y_s, self.y_r, self.up_s, self.up_r, self.dn_s, self.dn_r = refs[3:]
        self.z, self.y, self.c, self.h = place()
        z = self.z
        self.order = (3 - 3 * (z // 2), (2 + 3 * z) % 5, 1 + z % 2, z)

    def rows(self, cut):
        return pl.ds(*self.CUTS[cut])

    def across(self, line, cut):
        return remote(
            self.parts.at[line * 2 + 1 - self.y, self.rows(cut)], self.y_in.at[line, self.rows(cut)],
            self.y_s.at[line, cut], self.y_r.at[line, cut], device(self.z, 1 - self.y, self.c, self.h),
        )

    def up(self, line, cut):
        return remote(
            self.parts.at[line * 2 + self.y, self.rows(cut)], self.up_in.at[line, self.rows(cut)],
            self.up_s.at[line, cut], self.up_r.at[line, cut], device(self.z + 1, self.y, self.c, self.h),
        )

    def down(self, line, cut):
        return remote(
            self.parts.at[line * 2 + self.y, self.rows(cut)], self.dn_in.at[line, self.rows(cut)],
            self.dn_s.at[line, cut], self.dn_r.at[line, cut], device(self.z - 1, self.y, self.c, self.h),
        )

    def start(self, place_at):
        for cut in range(2):
            self.across(self.order[place_at], cut).start()

    def own(self, line, cut):
        return self.parts.at[line * 2 + self.y, self.rows(cut)]

    def relay(self, place_at):
        line = self.order[place_at]
        for cut in range(2):
            rows = self.rows(cut)
            self.across(line, cut).wait_recv()
            target = self.parts.at[line * 2 + self.y]

            @pl.when(line > self.z)
            def _():
                @pl.when(self.z > 0)
                def _():
                    self.up(line, cut).wait_recv()
                    total = (
                        target[rows].astype(jnp.float32)
                        + self.y_in[line, rows].astype(jnp.float32)
                        + self.up_in[line, rows].astype(jnp.float32)
                    )
                    target[rows] = total.astype(jnp.bfloat16)

                @pl.when(self.z == 0)
                def _():
                    total = target[rows].astype(jnp.float32) + self.y_in[line, rows].astype(jnp.float32)
                    target[rows] = total.astype(jnp.bfloat16)

                self.up(line, cut).start()

            @pl.when(line < self.z)
            def _():
                @pl.when(self.z < LINE - 1)
                def _():
                    self.down(line, cut).wait_recv()
                    total = (
                        target[rows].astype(jnp.float32)
                        + self.y_in[line, rows].astype(jnp.float32)
                        + self.dn_in[line, rows].astype(jnp.float32)
                    )
                    target[rows] = total.astype(jnp.bfloat16)

                @pl.when(self.z == LINE - 1)
                def _():
                    total = target[rows].astype(jnp.float32) + self.y_in[line, rows].astype(jnp.float32)
                    target[rows] = total.astype(jnp.bfloat16)

                self.down(line, cut).start()

    def total(self, out):
        line = self.z
        for cut in range(2):
            rows = self.rows(cut)
            self.across(line, cut).wait_recv()
            out[rows] = self.parts[line * 2 + self.y, rows].astype(jnp.float32) + self.y_in[line, rows].astype(jnp.float32)
        for cut in range(2):
            rows = self.rows(cut)

            @pl.when(self.z > 0)
            def _():
                self.up(line, cut).wait_recv()
                out[rows] += self.up_in[line, rows].astype(jnp.float32)

            @pl.when(self.z < LINE - 1)
            def _():
                self.down(line, cut).wait_recv()
                out[rows] += self.dn_in[line, rows].astype(jnp.float32)

    def finish(self):
        for line in range(LINE):
            for cut in range(2):
                self.across(line, cut).wait_send()

                @pl.when(self.z < line)
                def _():
                    self.up(line, cut).wait_send()

                @pl.when(self.z > line)
                def _():
                    self.down(line, cut).wait_send()


def reduce_kernel(parts_in, out, parts, in_sem, *refs):
    load = pltpu.make_async_copy(parts_in, parts, in_sem)
    load.start()
    greet_plane()
    reduce = Reduce(parts, refs)
    load.wait()
    for place_at in range(4):
        reduce.start(place_at)
    for place_at in range(3):
        reduce.relay(place_at)
    reduce.total(out)
    reduce.finish()


def reduce_plane(parts):
    shape = parts.shape
    return pl.pallas_call(
        reduce_kernel,
        out_shape=jax.ShapeDtypeStruct(shape[1:], jnp.float32),
        in_specs=[ANY],
        out_specs=INSIDE,
        scratch_shapes=[pltpu.VMEM(shape, jnp.bfloat16), pltpu.SemaphoreType.DMA] + Reduce.scratch(shape[2]),
        compiler_params=kernel_params(2),
        name="reduce_plane",
    )(parts)


def dma(*shape):
    return pltpu.SemaphoreType.DMA(shape) if shape else pltpu.SemaphoreType.DMA


def local(src, dst, sem):
    return pltpu.make_async_copy(src, dst, sem)


class AttnSpread:
    @staticmethod
    def scratch():
        return [dma(3, 4, 2), dma(3, 8), dma(3), dma(2), dma(2), dma(2), dma(1), dma(2)]

    def __init__(self, weights, outs, sems):
        self.weights, (self.qkv, self.out_w) = weights, outs
        (self.s, self.r, self.own, self.sib, self.o_s, self.o_r, self.o_own, self.o_sib) = sems
        self.z, self.y, self.c, self.h = place()

    def source(self, kind, line):
        start = line * HD if kind == 0 else (line // 2) * HD
        return self.weights[kind].at[:, pl.ds(start, HD)]

    def slot(self, kind, chip):
        return self.qkv.at[chip, self.c, :, pl.ds(kind * HD, HD)]

    def is_self(self, line, half):
        return (self.z == line) & (self.y == self.h) & (self.h == half)

    def push(self, kind, line, half):
        chip = self.z * 2 + self.y
        return remote(
            self.source(kind, line), self.slot(kind, chip), self.s.at[kind, line, half], self.r.at[kind, chip],
            device(line, self.h, self.c, half),
        )

    def keep(self, kind, line):
        return local(self.source(kind, line), self.slot(kind, self.z * 2 + self.y), self.own.at[kind])

    def pull(self, kind, chip):
        ref = self.slot(kind, chip)
        return remote(ref, ref, self.s.at[kind, 0, 0], self.r.at[kind, chip], device(self.z, self.y, self.c, self.h))

    def from_self(self, chip):
        return (self.z * 2 + self.y == chip) & (self.h == self.y)

    def share(self):
        ref = self.qkv.at[:, self.c]
        return remote(ref, ref, self.sib.at[0], self.sib.at[1], device(self.z, self.y, 1 - self.c, self.h))

    def share_in(self):
        ref = self.qkv.at[:, 1 - self.c]
        return remote(ref, ref, self.sib.at[0], self.sib.at[1], device(self.z, self.y, self.c, self.h))

    def out_push(self, half):
        return remote(
            self.weights[3], self.out_w.at[self.y, self.c], self.o_s.at[half], self.o_r.at[self.y],
            device(self.z, self.h, self.c, half),
        )

    def out_keep(self):
        return local(self.weights[3], self.out_w.at[self.y, self.c], self.o_own.at[0])

    def out_pull(self, pair):
        ref = self.out_w.at[pair, self.c]
        return remote(ref, ref, self.o_s.at[0], self.o_r.at[pair], device(self.z, self.y, self.c, self.h))

    def out_share(self):
        ref = self.out_w.at[:, self.c]
        return remote(ref, ref, self.o_sib.at[0], self.o_sib.at[1], device(self.z, self.y, 1 - self.c, self.h))

    def out_share_in(self):
        ref = self.out_w.at[:, 1 - self.c]
        return remote(ref, ref, self.o_sib.at[0], self.o_sib.at[1], device(self.z, self.y, self.c, self.h))

    def each_push(self, act_remote, act_local):
        for line in range(LINE):
            for half in range(2):
                mine = self.is_self(line, half)

                @pl.when(jnp.logical_not(mine))
                def _():
                    for kind in range(3):
                        act_remote(self.push(kind, line, half))

                @pl.when(mine)
                def _():
                    for kind in range(3):
                        act_local(self.keep(kind, line))

    def each_out_push(self, act_remote, act_local):
        for half in range(2):
            mine = (self.y == self.h) & (self.h == half)

            @pl.when(jnp.logical_not(mine))
            def _():
                act_remote(self.out_push(half))

            @pl.when(mine)
            def _():
                act_local(self.out_keep())

    def start(self):
        self.each_push(lambda copy: copy.start(), lambda copy: copy.start())
        self.each_out_push(lambda copy: copy.start(), lambda copy: copy.start())

    def relay(self):
        self.each_push(lambda copy: None, lambda copy: copy.wait())
        for chip in range(8):

            @pl.when(jnp.logical_not(self.from_self(chip)))
            def _():
                for kind in range(3):
                    self.pull(kind, chip).wait_recv()

        self.share().start()
        self.each_out_push(lambda copy: None, lambda copy: copy.wait())
        for pair in range(2):

            @pl.when(jnp.logical_not((self.y == pair) & (self.h == self.y)))
            def _():
                self.out_pull(pair).wait_recv()

        self.out_share().start()

    def finish(self):
        self.share_in().wait_recv()
        self.out_share_in().wait_recv()
        self.share().wait_send()
        self.out_share().wait_send()
        self.each_push(lambda copy: copy.wait_send(), lambda copy: None)
        self.each_out_push(lambda copy: copy.wait_send(), lambda copy: None)


class MlpSpread:
    @staticmethod
    def scratch():
        return [dma(2, 8), dma(2, 8), dma(2, 8), dma(2, 8), dma(2), dma(2, 2), dma(1), dma(2), dma(2)]

    def __init__(self, weights, outs, sems):
        self.weights, self.outs = weights, outs
        (self.s, self.r, self.x_s, self.x_r, self.own, self.sib, self.d_own, self.d_x, self.d_sib) = sems
        self.z, self.y, self.c, self.h = place()
        self.chip = self.z * 2 + self.y
        self.part = weights[0].shape[1] // 8

    def columns(self, index):
        return pl.ds(pl.multiple_of(index * self.part, self.part), self.part)

    def slot(self, kind, chip):
        return self.outs[kind].at[chip, self.c, :, self.columns(self.h)]

    def other(self, step):
        return (self.chip + step) % 8

    def source_of(self, step):
        return (self.chip + 8 - step) % 8

    def push(self, kind, step):
        chip = self.other(step)
        return remote(
            self.weights[kind].at[:, self.columns(chip)], self.slot(kind, self.chip), self.s.at[kind, step],
            self.r.at[kind, step], device(chip // 2, chip % 2, self.c, self.h),
        )

    def pull(self, kind, step):
        ref = self.slot(kind, self.source_of(step))
        return remote(ref, ref, self.s.at[kind, step], self.r.at[kind, step], device(self.z, self.y, self.c, self.h))

    def keep(self, kind):
        return local(self.weights[kind].at[:, self.columns(self.chip)], self.slot(kind, self.chip), self.own.at[kind])

    def over(self, kind, step):
        ref = self.slot(kind, self.source_of(step))
        return remote(
            ref, ref, self.x_s.at[kind, step], self.x_r.at[kind, step], device(self.z, self.y, self.c, 1 - self.h)
        )

    def over_in(self, kind, step):
        ref = self.outs[kind].at[self.source_of(step), self.c, :, self.columns(1 - self.h)]
        return remote(
            ref, ref, self.x_s.at[kind, step], self.x_r.at[kind, step], device(self.z, self.y, self.c, self.h)
        )

    def share(self, kind):
        ref = self.outs[kind].at[:, self.c]
        return remote(
            ref, ref, self.sib.at[kind, 0], self.sib.at[kind, 1], device(self.z, self.y, 1 - self.c, self.h)
        )

    def share_in(self, kind):
        ref = self.outs[kind].at[:, 1 - self.c]
        return remote(ref, ref, self.sib.at[kind, 0], self.sib.at[kind, 1], device(self.z, self.y, self.c, self.h))

    def down_keep(self):
        return local(self.weights[2], self.outs[2].at[self.h, self.c], self.d_own.at[0])

    def down_over(self):
        return remote(
            self.weights[2], self.outs[2].at[self.h, self.c], self.d_x.at[0], self.d_x.at[1],
            device(self.z, self.y, self.c, 1 - self.h),
        )

    def down_over_in(self):
        ref = self.outs[2].at[1 - self.h, self.c]
        return remote(ref, ref, self.d_x.at[0], self.d_x.at[1], device(self.z, self.y, self.c, self.h))

    def down_share(self):
        ref = self.outs[2].at[:, self.c]
        return remote(ref, ref, self.d_sib.at[0], self.d_sib.at[1], device(self.z, self.y, 1 - self.c, self.h))

    def down_share_in(self):
        ref = self.outs[2].at[:, 1 - self.c]
        return remote(ref, ref, self.d_sib.at[0], self.d_sib.at[1], device(self.z, self.y, self.c, self.h))

    def start(self, kinds=(0, 1)):
        for kind in kinds:
            self.keep(kind).start()
            for step in range(1, 8):
                self.push(kind, step).start()

    def start_down(self):
        self.down_keep().start()
        self.down_over().start()

    def relay(self, kind):
        self.keep(kind).wait()
        self.over(kind, 0).start()
        for step in range(1, 8):
            self.pull(kind, step).wait_recv()
            self.over(kind, step).start()

    def relay_share(self, kind):
        for step in range(8):
            self.over_in(kind, step).wait_recv()
        self.share(kind).start()

    def relay_down(self):
        self.down_keep().wait()
        self.down_over_in().wait_recv()
        self.down_share().start()

    def finish(self):
        for kind in range(2):
            self.share_in(kind).wait_recv()
            self.share(kind).wait_send()
            for step in range(8):
                self.over(kind, step).wait_send()
                if step:
                    self.push(kind, step).wait_send()
        self.down_share_in().wait_recv()
        self.down_share().wait_send()
        self.down_over().wait_send()


class NoteSpread:
    @staticmethod
    def scratch():
        return [dma(16), dma(16), dma(1)]

    def __init__(self, note, out, sems):
        self.note, self.out = note, out
        self.s, self.r, self.own = sems
        self.blk, self.h = lax.axis_index("blk"), lax.axis_index("head")

    def push(self, step):
        other = (self.blk + step) % 16
        return remote(self.note, self.out.at[self.blk], self.s.at[step], self.r.at[step], (other, self.h))

    def pull(self, step):
        ref = self.out.at[(self.blk + 16 - step) % 16]
        return remote(ref, ref, self.s.at[step], self.r.at[step], (self.blk, self.h))

    def keep(self):
        return local(self.note, self.out.at[self.blk], self.own.at[0])

    def start(self):
        self.keep().start()
        for step in range(1, 16):
            self.push(step).start()

    def finish(self):
        self.keep().wait()
        for step in range(1, 16):
            self.pull(step).wait_recv()
            self.push(step).wait_send()


def split_refs(refs, counts):
    groups, at = [], 0
    for count in counts:
        groups.append(refs[at : at + count])
        at += count
    return groups


def spread_kernel(tokens, cot, note, wq, wk, wv, wo, wg, wu, wd, tok_out, cot_out, note_out, qkv, out_w, gate, up, down, *sems):
    tok_sems, cot_sems, note_sems, attn_sems, mlp_sems = split_refs(sems, (8, 8, 3, 8, 9))
    greet_all(16, 2)
    tok = Gather(tokens, tok_out, tok_sems)
    notes = NoteSpread(note, note_out, note_sems)
    attn = AttnSpread((wq, wk, wv, wo), (qkv, out_w), attn_sems)
    mlp = MlpSpread((wg, wu, wd), (gate, up, down), mlp_sems)
    tok.start()
    notes.start()
    attn.start()
    mlp.start_down()
    tok.relays()
    attn.relay()
    mlp.start()
    cots = Gather(cot, cot_out, cot_sems)
    cots.start()
    mlp.relay(0)
    cots.relays()
    mlp.relay(1)
    mlp.relay_share(0)
    mlp.relay_share(1)
    mlp.relay_down()
    tok.finish()
    cots.finish()
    notes.finish()
    attn.finish()
    mlp.finish()


def spread(tokens, cot, note, wq, wk, wv, wo, wg, wu, wd):
    def shape(*dims):
        return jax.ShapeDtypeStruct(dims, jnp.bfloat16)

    rows, width = tokens.shape
    depth = wq.shape[0]
    part = wg.shape[1] // 8
    return pl.pallas_call(
        spread_kernel,
        out_shape=(
            shape(8, rows, width),
            shape(8, rows, width),
            jax.ShapeDtypeStruct((16,) + note.shape, jnp.float32),
            shape(8, 2, depth, 3 * HD),
            shape(2, 2, wo.shape[0], width),
            shape(8, 2, depth, 2 * part),
            shape(8, 2, depth, 2 * part),
            shape(2, 2, wd.shape[0], width),
        ),
        in_specs=[ANY] * 10,
        out_specs=(ANY,) * 8,
        scratch_shapes=Gather.scratch() + Gather.scratch() + NoteSpread.scratch() + AttnSpread.scratch() + MlpSpread.scratch(),
        compiler_params=kernel_params(3),
        name="spread",
    )(tokens, cot, note, wq, wk, wv, wo, wg, wu, wd)


def greet_square(z, y, c, h):
    greet(device(z, y, 1 - c, h))
    greet(device(z, y, c, 1 - h))
    pl.semaphore_wait(pltpu.get_barrier_semaphore(), 2)


def keys_kernel(kv, out, own, x_s, x_r, c_s, c_r):
    z, y, c, h = place()
    greet_square(z, y, c, h)

    def keep(cut):
        rows = pl.ds(cut * 2, 2)
        return local(kv.at[rows], out.at[rows, c, h], own.at[cut])

    def over(cut, half):
        rows = pl.ds(cut * 2, 2)
        return remote(kv.at[rows], out.at[rows, c, half], x_s.at[cut], x_r.at[cut], device(z, y, c, 1 - h))

    def share(cut, core):
        ref = out.at[pl.ds(cut * 2, 2), core]
        return remote(ref, ref, c_s.at[cut], c_r.at[cut], device(z, y, 1 - c, h))

    for cut in range(4):
        over(cut, h).start()
        keep(cut).start()
    for cut in range(4):
        keep(cut).wait()
        over(cut, 1 - h).wait_recv()
        share(cut, c).start()
    for cut in range(4):
        share(cut, 1 - c).wait_recv()
        share(cut, c).wait_send()
        over(cut, h).wait_send()


def gather_keys(kv):
    eight, rows, width = kv.shape
    return pl.pallas_call(
        keys_kernel,
        out_shape=jax.ShapeDtypeStruct((eight, 2, 2, rows, width), kv.dtype),
        in_specs=[ANY],
        out_specs=ANY,
        scratch_shapes=[dma(4)] * 5,
        compiler_params=kernel_params(4),
        name="gather_keys",
    )(kv)


def add_into(target, *others):
    total = target[...].astype(jnp.float32)
    for other in others:
        total += other[...].astype(jnp.float32)
    target[...] = total.astype(target.dtype)


def key_grads_kernel(parts_in, out, parts, sib_in, x_in, z_in, load_sem, c_s, c_r, x_s, x_r, z_s, z_r):
    z, y, c, h = place()
    pair = z + 1 - 2 * (z % 2)
    load = local(parts_in, parts, load_sem)
    load.start()
    greet(device(z, y, 1 - c, h))
    greet(device(z, y, c, 1 - h))
    greet(device(pair, y, c, h))
    pl.semaphore_wait(pltpu.get_barrier_semaphore(), 3)
    load.wait()

    def share(cut):
        rows = pl.ds(cut * 2, 2)
        return remote(
            parts.at[rows, 1 - c], sib_in.at[rows], c_s.at[cut], c_r.at[cut], device(z, y, 1 - c, h)
        )

    def over(cut):
        rows = pl.ds(cut * 2, 2)
        return remote(
            parts.at[rows, c, 1 - h], x_in.at[rows], x_s.at[cut], x_r.at[cut], device(z, y, c, 1 - h)
        )

    def across(cut, column):
        rows = pl.ds(cut * 2, 2)
        columns = pl.ds(pl.multiple_of(column * HD, HD), HD)
        return remote(
            parts.at[rows, c, h, :, columns], z_in.at[rows], z_s.at[cut], z_r.at[cut], device(pair, y, c, h)
        )

    for cut in range(4):
        share(cut).start()
    for cut in range(4):
        rows = pl.ds(cut * 2, 2)
        share(cut).wait_recv()
        add_into(parts.at[rows, c, 1 - h], sib_in.at[rows, 1 - h])
        over(cut).start()
    for cut in range(4):
        rows = pl.ds(cut * 2, 2)
        over(cut).wait_recv()
        add_into(parts.at[rows, c, h], sib_in.at[rows, h], x_in.at[rows])
        across(cut, 1 - z % 2).start()
    for cut in range(4):
        rows = pl.ds(cut * 2, 2)
        columns = pl.ds(pl.multiple_of((z % 2) * HD, HD), HD)
        across(cut, 0).wait_recv()
        out[rows] = parts[rows, c, h, :, columns].astype(jnp.float32) + z_in[rows].astype(jnp.float32)
    for cut in range(4):
        share(cut).wait_send()
        over(cut).wait_send()
        across(cut, 0).wait_send()


def reduce_keys(parts):
    eight, cores, halves, rows, width = parts.shape

    def room(*dims):
        return pltpu.VMEM(dims, jnp.bfloat16)

    return pl.pallas_call(
        key_grads_kernel,
        out_shape=jax.ShapeDtypeStruct((eight, rows, HD), jnp.float32),
        in_specs=[ANY],
        out_specs=INSIDE,
        scratch_shapes=[
            room(*parts.shape), room(eight, 2, rows, width), room(eight, rows, width), room(eight, rows, HD), dma(),
        ] + [dma(4)] * 6,
        compiler_params=kernel_params(5),
        name="reduce_keys",
    )(parts)


def weight_grads_kernel(
    gate_in, up_in, down_in, query_in, side_in, out_in, gains_in,
    gate_out, up_out, down_out, query_out, key_out, value_out, out_out, gains_out,
    gate, up, down, query, side, outw,
    gate_sib, up_sib, down_sib, query_sib, side_sib, outw_sib,
    gate_x, up_x, down_x, query_x, side_x, outw_x,
    gains_box,
    load_sems, sib_s, sib_r, x_s, x_r, a2a_s, a2a_r, small_s, small_r, y_sr, gain_s, gain_r, keep_sems,
):
    z, y, c, h = place()
    chip = z * 2 + y
    blk = lax.axis_index("blk")
    me = device(z, y, c, h)
    loads = [
        local(src, dst, load_sems.at[i])
        for i, (src, dst) in enumerate(
            ((gate_in, gate), (up_in, up), (down_in, down), (query_in, query), (side_in, side), (out_in, outw))
        )
    ]
    for load in loads:
        load.start()
    greet_all(16, 2)

    def gain_push(step):
        other = (blk + (step // 2)) % 16
        half = (h + step % 2) % 2
        return remote(
            gains_in.at[other], gains_box.at[step], gain_s.at[step], gain_r.at[step], (other, half)
        )

    for step in range(1, 32):
        gain_push(step).start()
    keep_gain = local(gains_in.at[blk], gains_box.at[0], keep_sems.at[0])
    keep_gain.start()

    stores = ((gate, gate_sib), (up, up_sib), (down, down_sib), (query, query_sib), (side, side_sib), (outw, outw_sib))

    def share(i):
        store, box = stores[i]
        return remote(store.at[:, 1 - c], box, sib_s.at[i], sib_r.at[i], device(z, y, 1 - c, h))

    order = (0, 1, 2, 3, 4, 5)
    for i in order:
        loads[i].wait()
        share(i).start()

    half_width = gate.shape[3] // 2

    def columns(index):
        return pl.ds(pl.multiple_of(index * half_width, half_width), half_width)

    def over(i):
        if i < 2:
            store, box = ((gate, gate_x), (up, up_x))[i]
            src = store.at[:, c, :, columns(1 - h)]
        elif i == 2:
            src, box = down.at[1 - h, c], down_x
        else:
            store, box = {3: (query, query_x), 4: (side, side_x), 5: (outw, outw_x)}[i]
            src = store.at[:, c]
        return remote(src, box, x_s.at[i], x_r.at[i], device(z, y, c, 1 - h))

    outs = (gate_out, up_out)

    def scatter(i, step):
        store = (gate, up)[i]
        target = (chip + step) % 8
        return remote(
            store.at[target, c, :, columns(h)], outs[i].at[:, columns(chip)], a2a_s.at[i, step], a2a_r.at[i, step],
            device(target // 2, target % 2, c, h),
        )

    def scatter_in(i, step):
        source = (chip + 8 - step) % 8
        ref = outs[i].at[:, columns(source)]
        return remote(ref, ref, a2a_s.at[i, step], a2a_r.at[i, step], me)

    def scatter_keep(i):
        store = (gate, up)[i]
        return local(store.at[chip, c, :, columns(h)], outs[i].at[:, columns(chip)], keep_sems.at[1 + i])

    for i in (0, 1):
        store, box = stores[i]
        share(i).wait_recv()

        @pl.loop(0, 8)
        def _(p):
            add_into(store.at[p, c], box.at[p])

        over(i).start()
    share(2).wait_recv()
    for half in range(2):
        add_into(down.at[half, c], down_sib.at[half])
    over(2).start()
    for i in (3, 4, 5):
        store, box = stores[i]
        share(i).wait_recv()
        for p in range(box.shape[0]):
            add_into(store.at[p, c], box.at[p])

        @pl.when(h != y)
        def _():
            over(i).start()

    def small_out(kind, target):
        if kind == 0:
            return query_out.at[:, pl.ds(pl.multiple_of(z * HD, HD), HD)]
        return (key_out, value_out)[kind - 1].at[:, pl.ds(pl.multiple_of((z // 2) * HD, HD), HD)]

    def small(kind, step):
        store = query if kind == 0 else side
        target = (chip + step) % 8
        return remote(
            store.at[target, c], small_out(kind, target), small_s.at[kind, step], small_r.at[kind, z, step],
            device(target // 2, target % 2, c, h),
        )

    def small_keep(kind):
        store = query if kind == 0 else side
        return local(store.at[chip, c], small_out(kind, chip), keep_sems.at[3 + kind])

    def out_move():
        return remote(outw.at[1 - y, c], out_out, y_sr.at[0], y_sr.at[1], device(z, 1 - y, c, h))

    def out_keep():
        return local(outw.at[y, c], out_out, keep_sems.at[6])

    for i, box in ((0, gate_x), (1, up_x)):
        store = (gate, up)[i]
        over(i).wait_recv()

        @pl.loop(0, 8)
        def _(p):
            add_into(store.at[p, c, :, columns(h)], box.at[p])

        scatter_keep(i).start()
        for step in range(1, 8):
            scatter(i, step).start()

    @pl.when(h == y)
    def _():
        for i in (3, 4, 5):
            store, box = {3: (query, query_x), 4: (side, side_x), 5: (outw, outw_x)}[i]
            over(i).wait_recv()
            for p in range(box.shape[0]):
                add_into(store.at[p, c], box.at[p])
        small_keep(0).start()
        for step in range(1, 8):
            small(0, step).start()

        @pl.when(z % 2 == 0)
        def _():
            small_keep(1).start()
            for step in range(1, 8):
                small(1, step).start()

        @pl.when(z % 2 == 1)
        def _():
            small_keep(2).start()
            for step in range(1, 8):
                small(2, step).start()

        out_move().start()
        out_keep().start()

    over(2).wait_recv()
    down_out[...] = (
        down[h, c].astype(jnp.float32) + down_x[...].astype(jnp.float32)
    )

    keep_gain.wait()
    for step in range(1, 32):
        gain_push(step).wait_recv()
    total = gains_box[0]
    for step in range(1, 32):
        total += gains_box[step]
    gains_out[...] = total

    for i in (0, 1):
        for step in range(1, 8):
            scatter_in(i, step).wait_recv()
        scatter_keep(i).wait()

    def small_in(kind, line, step):
        if kind == 0:
            ref = query_out.at[:, pl.ds(line * HD, HD)]
        else:
            ref = (key_out, value_out)[kind - 1].at[:, pl.ds((line // 2) * HD, HD)]
        return remote(ref, ref, small_s.at[kind, step], small_r.at[kind, line, step], me)

    for kind in range(3):
        for line in range(LINE):
            if kind and line % 2 != kind - 1:
                continue
            source = line * 2 + h
            step = (chip + 8 - source) % 8

            @pl.when(step != 0)
            def _():
                small_in(kind, line, step).wait_recv()

            @pl.when(step == 0)
            def _():
                small_keep(kind).wait()

    @pl.when(h != y)
    def _():
        remote(out_out, out_out, y_sr.at[0], y_sr.at[1], me).wait_recv()
        for i in (3, 4, 5):
            over(i).wait_send()

    @pl.when(h == y)
    def _():
        out_keep().wait()
        out_move().wait_send()
        for step in range(1, 8):
            small(0, step).wait_send()

        @pl.when(z % 2 == 0)
        def _():
            for step in range(1, 8):
                small(1, step).wait_send()

        @pl.when(z % 2 == 1)
        def _():
            for step in range(1, 8):
                small(2, step).wait_send()

    for i in range(6):
        share(i).wait_send()
    for i in range(3):
        over(i).wait_send()
    for i in (0, 1):
        for step in range(1, 8):
            scatter(i, step).wait_send()
    for step in range(1, 32):
        gain_push(step).wait_send()


def reduce_weights(gate, up, down, query, side, outw, gains):
    parts = (gate, up, down, query, side, outw)

    def room(*dims):
        return pltpu.VMEM(dims, jnp.bfloat16)

    def shape(*dims, dtype=jnp.bfloat16):
        return jax.ShapeDtypeStruct(dims, dtype)

    depth, wide = gate.shape[2], gate.shape[3]
    sib = [room(part.shape[0], *part.shape[2:]) for part in parts]
    over = [
        room(8, depth, wide // 2), room(8, depth, wide // 2), room(*down.shape[2:]),
        room(8, depth, HD), room(8, depth, HD), room(2, *outw.shape[2:]),
    ]
    return pl.pallas_call(
        weight_grads_kernel,
        out_shape=(
            shape(depth, 4 * wide), shape(depth, 4 * wide), shape(*down.shape[2:], dtype=jnp.float32),
            shape(depth, 4 * HD), shape(depth, 2 * HD), shape(depth, 2 * HD), shape(*outw.shape[2:]),
            shape(*gains.shape[1:], dtype=jnp.float32),
        ),
        in_specs=[ANY] * 7,
        out_specs=(ANY, ANY, INSIDE, ANY, ANY, ANY, ANY, INSIDE),
        scratch_shapes=[room(*part.shape) for part in parts] + sib + over + [
            pltpu.VMEM((32,) + gains.shape[1:], jnp.float32),
            dma(6), dma(6), dma(6), dma(6), dma(6), dma(2, 8), dma(2, 8), dma(3, 8), dma(3, 4, 8), dma(2),
            dma(32), dma(32), dma(8),
        ],
        compiler_params=kernel_params(6),
        name="reduce_weights",
    )(gate, up, down, query, side, outw, gains)


def fast_body(
    tokens,
    attn_gain,
    w_query,
    w_key,
    w_value,
    w_out,
    mlp_gain,
    w_gate,
    w_up,
    w_down,
    block_ids,
    positions,
    cotangent,
):
    z, y, core, half = place()
    rows, width = tokens.shape
    token_rows = 8 * rows
    f32, bf16 = jnp.float32, jnp.bfloat16

    def own_half(values):
        return lax.dynamic_index_in_dim(values, half, 0, False)

    note = jnp.concatenate(
        [
            positions.astype(f32).reshape(2, rows),
            block_ids.astype(f32).reshape(2, rows),
            attn_gain.astype(f32)[None],
            mlp_gain.astype(f32)[None],
            jnp.zeros((2, rows), f32),
        ]
    )
    tokens_all, cot_all, notes, qkv_w, out_w, gate_w, up_w, down_w = spread(
        tokens, cotangent, note, w_query, w_key, w_value, w_out, w_gate, w_up, w_down
    )
    tokens_all = tokens_all.reshape(token_rows, width)
    cot_all = cot_all.reshape(token_rows, width)
    qkv_w = qkv_w.reshape(width, 3 * HD)
    out_w = out_w.reshape(HD, width)
    hidden_part = gate_w.shape[3]
    gate_w = gate_w.reshape(width, hidden_part)
    up_w = up_w.reshape(width, hidden_part)
    down_w = down_w.reshape(hidden_part, width)
    gain_attn = notes[:, 4].reshape(1, width)
    gain_mlp = notes[:, 5].reshape(1, width)
    mine = lax.dynamic_index_in_dim(notes.reshape(8, 2, 8, rows), core, 1, False)
    positions_mine = lax.dynamic_index_in_dim(mine[:, 0:2], half, 1, False).reshape(token_rows)
    ids_mine = lax.dynamic_index_in_dim(mine[:, 2:4], half, 1, False).reshape(token_rows)
    key_ids = notes[:, 2:4].reshape(32 * rows)

    inputs_all = tokens_all.astype(f32)
    normed = (inputs_all * rms_scale(inputs_all) * gain_attn).astype(bf16)
    cos_table, sine_table = rope_tables(positions_mine)
    cos_table, sine_table = cos_table[:, 0], sine_table[:, 0]
    projected = product(normed, qkv_w)
    query = rotate(projected[:, :HD], cos_table, sine_table).astype(bf16)
    key = rotate(projected[:, HD : 2 * HD], cos_table, sine_table).astype(bf16)
    value = projected[:, 2 * HD :].astype(bf16)
    keys_values = gather_keys(jnp.concatenate([key, value], axis=1).reshape(8, rows, 2 * HD))
    keys_values = keys_values.reshape(32 * rows, 2 * HD)
    keys, values = keys_values[:, :HD], keys_values[:, HD:]
    score_scale = HD ** (-0.5)
    visible = key_ids[None, :] <= ids_mine[:, None]
    scores = jnp.where(visible, times_transposed(query, keys) * score_scale, -1e30)
    row_max = jnp.max(scores, axis=-1, keepdims=True)
    weights = jnp.exp(scores - row_max)
    log_total = row_max + jnp.log(jnp.sum(weights, axis=-1, keepdims=True))
    probabilities = jnp.exp(scores - log_total)
    attended = product(probabilities.astype(bf16), values)
    attended_low = attended.astype(bf16)
    branch = reduce_plane(product(attended_low, out_w).astype(bf16).reshape(8, rows, width))

    inputs = tokens.astype(f32)
    inv_attn = rms_scale(inputs)
    hidden = inputs + branch
    inv_mlp = rms_scale(hidden)
    normed_mlp = gather_plane((hidden * inv_mlp * gain_mlp).astype(bf16)).reshape(token_rows, width)
    gate_pre = product(normed_mlp, gate_w)
    up_pre = product(normed_mlp, up_w)
    sigmoid_gate = jax.nn.sigmoid(gate_pre)
    active = (gate_pre * sigmoid_gate * up_pre).astype(bf16)
    mlp_own = reduce_plane(product(active, down_w).astype(bf16).reshape(8, rows, width))
    output = (hidden + mlp_own).astype(bf16)
    grad_active = times_transposed(cot_all, down_w)
    grad_gate = (
        grad_active * up_pre * sigmoid_gate * (1.0 + gate_pre * (1.0 - sigmoid_gate))
    ).astype(bf16)
    grad_up = (grad_active * gate_pre * sigmoid_gate).astype(bf16)
    grad_normed_part = times_transposed(grad_gate, gate_w) + times_transposed(grad_up, up_w)
    grad_normed_mlp = reduce_plane(grad_normed_part.astype(bf16).reshape(8, rows, width))
    grad_gate_w = transposed_times(normed_mlp, grad_gate)
    grad_up_w = transposed_times(normed_mlp, grad_up)
    grad_down_w = transposed_times(active, cot_all)
    grad_hidden_norm, gain_mlp_term = norm_backward(grad_normed_mlp, hidden, inv_mlp, gain_mlp)
    grad_hidden = cotangent.astype(f32) + grad_hidden_norm

    grad_branch = gather_plane(grad_hidden.astype(bf16)).reshape(token_rows, width)
    grad_out_w = transposed_times(attended_low, grad_branch)
    grad_attended = times_transposed(grad_branch, out_w).astype(bf16)
    delta = jnp.sum(grad_attended.astype(f32) * attended, axis=-1, keepdims=True)
    grad_probs = times_transposed(grad_attended, values)
    grad_scores = (probabilities * (grad_probs - delta)).astype(bf16)
    grad_query_rot = product(grad_scores, keys) * score_scale
    grad_key_rot = transposed_times(grad_scores, query) * score_scale
    grad_value_part = transposed_times(probabilities.astype(bf16), grad_attended)
    side = reduce_keys(
        jnp.concatenate([grad_key_rot, grad_value_part], axis=1)
        .astype(bf16)
        .reshape(8, 2, 2, rows, 2 * HD)
    ).reshape(token_rows, HD)
    is_key = z % 2 == 0
    side_grad = jnp.where(is_key, rotate(side, cos_table, -sine_table), side).astype(bf16)
    grad_query = rotate(grad_query_rot, cos_table, -sine_table).astype(bf16)
    side_w = jnp.where(is_key, qkv_w[:, HD : 2 * HD], qkv_w[:, 2 * HD :])
    grad_normed_part = times_transposed(grad_query, qkv_w[:, :HD]) + times_transposed(
        side_grad, side_w
    )
    grad_normed = reduce_plane(grad_normed_part.astype(bf16).reshape(8, rows, width))
    grad_query_w = transposed_times(normed, grad_query)
    grad_side_w = transposed_times(normed, side_grad)
    grad_inputs_norm, gain_attn_term = norm_backward(grad_normed, inputs, inv_attn, gain_attn)
    tokens_grad = (grad_hidden + grad_inputs_norm).astype(bf16)

    gains = jnp.concatenate(
        [
            gain_attn_term.reshape(16, 1, rows),
            gain_mlp_term.reshape(16, 1, rows),
            jnp.zeros((16, 6, rows), f32),
        ],
        axis=1,
    )
    depth = w_query.shape[0]
    gate_grad, up_grad, down_grad, query_grad, key_grad, value_grad, out_grad, gain_grads = reduce_weights(
        grad_gate_w.astype(bf16).reshape(8, 2, depth, hidden_part),
        grad_up_w.astype(bf16).reshape(8, 2, depth, hidden_part),
        grad_down_w.astype(bf16).reshape(2, 2, w_down.shape[0], width),
        grad_query_w.astype(bf16).reshape(8, 2, depth, HD),
        grad_side_w.astype(bf16).reshape(8, 2, depth, HD),
        grad_out_w.astype(bf16).reshape(2, 2, w_out.shape[0], width),
        gains,
    )
    return (
        output,
        tokens_grad,
        gain_grads[0],
        query_grad.astype(f32),
        key_grad.astype(f32),
        value_grad.astype(f32),
        out_grad.astype(f32),
        gain_grads[1],
        gate_grad.astype(f32),
        up_grad.astype(f32),
        down_grad,
    )


def solution(mesh):
    placed = (
        P(("blk", "head"), None),
        P("blk"),
        P("blk", "head"),
        P("blk", "head"),
        P("blk", "head"),
        P(("head", "blk"), None),
        P("blk"),
        P("blk", "head"),
        P("blk", "head"),
        P(("head", "blk"), None),
        P("blk"),
        P("blk"),
        P(("blk", "head"), None),
    )
    fits = mesh.shape["blk"] == 16 and mesh.shape["head"] == 2
    return jax.shard_map(
        fast_body if fits else body,
        mesh=mesh,
        in_specs=placed,
        out_specs=(
            P(("blk", "head"), None),
            P(("blk", "head"), None),
            P("blk"),
            P("blk", "head"),
            P("blk", "head"),
            P("blk", "head"),
            P(("head", "blk"), None),
            P("blk"),
            P("blk", "head"),
            P("blk", "head"),
            P(("head", "blk"), None),
        ),
        check_vma=False,
    )
```

```python
import jax
import jax.numpy as jnp
from jax import lax
from jax.experimental import pallas as pl
from jax.experimental.pallas import tpu as pltpu
from jax.sharding import PartitionSpec as P

HD = 256


eps_norm = 1e-06
rope_base = 1000042.0


def rms_scale(rows):
    return lax.rsqrt(jnp.mean(rows * rows, axis=-1, keepdims=True) + eps_norm)


def rope_tables(positions):
    inv_freqs = rope_base ** (-2.0 * jnp.arange(HD // 2, dtype=jnp.float32) / HD)
    angles = positions.astype(jnp.float32)[:, None] * inv_freqs[None, :]
    return (jnp.cos(angles)[:, None, :], jnp.sin(angles)[:, None, :])


def rotate(heads, cos_table, sine_table):
    half_size = heads.shape[-1] // 2
    lower_half = heads[..., :half_size]
    upper_half = heads[..., half_size:]
    return jnp.concatenate(
        [
            lower_half * cos_table - upper_half * sine_table,
            upper_half * cos_table + lower_half * sine_table,
        ],
        axis=-1,
    )


def product(left, right):
    return jnp.dot(left, right, preferred_element_type=jnp.float32)


def times_transposed(left, right):
    return lax.dot_general(
        left, right, (((1,), (1,)), ((), ())), preferred_element_type=jnp.float32
    )


def transposed_times(left, right):
    return lax.dot_general(
        left, right, (((0,), (0,)), ((), ())), preferred_element_type=jnp.float32
    )


def norm_backward(grad_normed, inputs, inv_scale, gain_rows):
    unit_rows = inputs * inv_scale
    grad_unit = grad_normed * gain_rows
    gain_term = jnp.sum(grad_normed * unit_rows, axis=0)
    grad_inputs = inv_scale * (
        grad_unit - unit_rows * jnp.mean(grad_unit * unit_rows, axis=-1, keepdims=True)
    )
    return (grad_inputs, gain_term)


def body(
    tokens,
    attn_gain,
    w_query,
    w_key,
    w_value,
    w_out,
    mlp_gain,
    w_gate,
    w_up,
    w_down,
    block_ids,
    positions,
    cotangent,
):
    rows_own = tokens.shape[0]
    head_rank = lax.axis_index("head")
    tokens_all, cot_all = (
        lax.all_gather(tokens, "head", axis=0, tiled=True),
        lax.all_gather(cotangent, "head", axis=0, tiled=True),
    )
    rows_all = tokens_all.shape[0]
    gain_attn, query_w, key_w, value_w, out_w = (
        lax.all_gather(attn_gain, "blk", axis=0, tiled=True),
        lax.all_gather(w_query, "blk", axis=0, tiled=True),
        lax.all_gather(w_key, "blk", axis=0, tiled=True),
        lax.all_gather(w_value, "blk", axis=0, tiled=True),
        lax.all_gather(w_out, "blk", axis=0, tiled=True),
    )
    gain_mlp, gate_w, up_w, down_w = (
        lax.all_gather(mlp_gain, "blk", axis=0, tiled=True),
        lax.all_gather(w_gate, "blk", axis=0, tiled=True),
        lax.all_gather(w_up, "blk", axis=0, tiled=True),
        lax.all_gather(w_down, "blk", axis=0, tiled=True),
    )
    key_ids = lax.all_gather(block_ids, "blk", axis=0, tiled=True)
    heads_local = query_w.shape[1] // HD
    kv_local = key_w.shape[1] // HD
    kv_width = kv_local * HD
    group_size = heads_local // kv_local
    cos_table, sine_table = rope_tables(positions)
    score_scale = HD ** (-0.5)
    seq_len = key_ids.shape[0]
    key_block = min(2048, seq_len)
    block_total = seq_len // key_block
    block_steps = jnp.arange(block_total)
    top_query = jnp.max(block_ids)
    inputs = tokens_all.astype(jnp.float32)
    inv_attn = rms_scale(inputs)
    normed = (inputs * inv_attn * gain_attn.astype(jnp.float32)).astype(jnp.bfloat16)
    queries = rotate(
        product(normed, query_w).reshape(rows_all, heads_local, HD), cos_table, sine_table
    ).astype(jnp.bfloat16)
    keys_own = rotate(product(normed, key_w).reshape(rows_all, kv_local, HD), cos_table, sine_table)
    keys_own = keys_own.astype(jnp.bfloat16).reshape(rows_all, kv_width)
    values_own = product(normed, value_w).astype(jnp.bfloat16)
    keys_all, values_all = (
        lax.all_gather(keys_own, "blk", axis=0, tiled=True),
        lax.all_gather(values_own, "blk", axis=0, tiled=True),
    )
    grouped = queries.reshape(rows_all, kv_local, group_size, HD)

    def slice_keys(key_start, count):
        key_rows = lax.dynamic_slice_in_dim(keys_all, key_start, count, 0).reshape(
            count, kv_local, HD
        )
        value_rows = lax.dynamic_slice_in_dim(values_all, key_start, count, 0).reshape(
            count, kv_local, HD
        )
        block_keys = lax.dynamic_slice_in_dim(key_ids, key_start, count, 0)
        return (key_rows, value_rows, block_keys)

    def scores_for(key_rows, block_keys):
        scores = (
            jnp.einsum("qkgd,ckd->kgqc", grouped, key_rows, preferred_element_type=jnp.float32)
            * score_scale
        )
        visible = (block_keys[None, :] <= block_ids[:, None])[None, None]
        return (scores, visible)

    def max_sum(state_pair, step_index):
        key_start = step_index * key_block

        def max_live(pair):
            run_max, run_sum = pair
            key_rows, value_rows, block_keys = slice_keys(key_start, key_block)
            scores, visible = scores_for(key_rows, block_keys)
            scores = jnp.where(visible, scores, -1e30)
            new_max = jnp.maximum(run_max, jnp.max(scores, axis=-1))
            kept_terms = jnp.where(visible, jnp.exp(scores - new_max[..., None]), 0.0)
            return (new_max, run_sum * jnp.exp(run_max - new_max) + jnp.sum(kept_terms, axis=-1))

        def max_skipped(pair):
            return pair

        return (lax.cond(key_ids[key_start] <= top_query, max_live, max_skipped, state_pair), None)

    start_max = jnp.full((kv_local, group_size, rows_all), -1e30, jnp.float32)
    start_sum = jnp.zeros((kv_local, group_size, rows_all), jnp.float32)
    (run_max, run_sum), unused_max = lax.scan(max_sum, (start_max, start_sum), block_steps)
    log_total = run_max + jnp.log(run_sum)

    def weighted(accum_rows, step_index):
        key_start = step_index * key_block

        def weighted_live(accum):
            key_rows, value_rows, block_keys = slice_keys(key_start, key_block)
            scores, visible = scores_for(key_rows, block_keys)
            probabilities = jnp.where(visible, jnp.exp(scores - log_total[..., None]), 0.0).astype(
                jnp.bfloat16
            )
            return accum + jnp.einsum(
                "kgqc,ckd->qkgd", probabilities, value_rows, preferred_element_type=jnp.float32
            )

        def weighted_skipped(accum):
            return accum

        return (
            lax.cond(key_ids[key_start] <= top_query, weighted_live, weighted_skipped, accum_rows),
            None,
        )

    attended, unused_rows = lax.scan(
        weighted, jnp.zeros((rows_all, kv_local, group_size, HD), jnp.float32), block_steps
    )
    attended_low = attended.reshape(rows_all, heads_local * HD).astype(jnp.bfloat16)
    branch_sum = lax.psum(product(attended_low, out_w).astype(jnp.bfloat16), "head").astype(
        jnp.float32
    )
    hidden = inputs + branch_sum
    inv_mlp = rms_scale(hidden)
    normed_mlp = (hidden * inv_mlp * gain_mlp.astype(jnp.float32)).astype(jnp.bfloat16)
    gate_pre = product(normed_mlp, gate_w)
    up_pre = product(normed_mlp, up_w)
    sigmoid_gate = jax.nn.sigmoid(gate_pre)
    active = (gate_pre * sigmoid_gate * up_pre).astype(jnp.bfloat16)
    mlp_own = lax.psum_scatter(
        product(active, down_w).astype(jnp.bfloat16), "head", scatter_dimension=0, tiled=True
    ).astype(jnp.float32)
    hidden_own = lax.dynamic_slice_in_dim(hidden, head_rank * rows_own, rows_own, 0)
    output = (hidden_own + mlp_own).astype(jnp.bfloat16)
    gain_attn, query_w, key_w, value_w, out_w = (
        lax.all_gather(attn_gain, "blk", axis=0, tiled=True),
        lax.all_gather(w_query, "blk", axis=0, tiled=True),
        lax.all_gather(w_key, "blk", axis=0, tiled=True),
        lax.all_gather(w_value, "blk", axis=0, tiled=True),
        lax.all_gather(w_out, "blk", axis=0, tiled=True),
    )
    gain_mlp, gate_w, up_w, down_w = (
        lax.all_gather(mlp_gain, "blk", axis=0, tiled=True),
        lax.all_gather(w_gate, "blk", axis=0, tiled=True),
        lax.all_gather(w_up, "blk", axis=0, tiled=True),
        lax.all_gather(w_down, "blk", axis=0, tiled=True),
    )
    grad_active = times_transposed(cot_all, down_w)
    grad_gate = (
        grad_active * up_pre * sigmoid_gate * (1.0 + gate_pre * (1.0 - sigmoid_gate))
    ).astype(jnp.bfloat16)
    grad_up = (grad_active * gate_pre * sigmoid_gate).astype(jnp.bfloat16)
    grad_gate_w = transposed_times(normed_mlp, grad_gate)
    grad_up_w = transposed_times(normed_mlp, grad_up)
    grad_down_w = transposed_times(active, cot_all)
    grad_normed_part = times_transposed(grad_gate, gate_w) + times_transposed(grad_up, up_w)
    grad_normed_mlp = lax.psum(grad_normed_part.astype(jnp.bfloat16), "head").astype(jnp.float32)
    grad_hidden_norm, gain_mlp_term = norm_backward(
        grad_normed_mlp, hidden, inv_mlp, gain_mlp.astype(jnp.float32)
    )
    grad_hidden = cot_all.astype(jnp.float32) + grad_hidden_norm
    mlp_results = (
        lax.psum_scatter(gain_mlp_term, "blk", scatter_dimension=0, tiled=True),
        lax.psum_scatter(grad_gate_w, "blk", scatter_dimension=0, tiled=True),
        lax.psum_scatter(grad_up_w, "blk", scatter_dimension=0, tiled=True),
        lax.psum_scatter(grad_down_w, "blk", scatter_dimension=0, tiled=True),
    )
    grad_branch = grad_hidden.astype(jnp.bfloat16)
    grad_out_w = transposed_times(attended_low, grad_branch)
    grad_attended = times_transposed(grad_branch, out_w).astype(jnp.bfloat16)
    grad_grouped = grad_attended.reshape(rows_all, kv_local, group_size, HD)
    delta_rows = jnp.transpose(
        jnp.sum(grad_grouped.astype(jnp.float32) * attended, axis=-1), (1, 2, 0)
    )

    def pair_backward(key_rows, value_rows, block_keys):
        count = key_rows.shape[0]
        scores, visible = scores_for(key_rows, block_keys)
        probabilities = jnp.where(visible, jnp.exp(scores - log_total[..., None]), 0.0)
        grad_probs = jnp.einsum(
            "qkgd,ckd->kgqc", grad_grouped, value_rows, preferred_element_type=jnp.float32
        )
        grad_scores = (probabilities * (grad_probs - delta_rows[..., None])).astype(jnp.bfloat16)
        query_terms = jnp.einsum(
            "kgqc,ckd->qkgd", grad_scores, key_rows, preferred_element_type=jnp.float32
        )
        key_terms = (
            jnp.einsum("kgqc,qkgd->ckd", grad_scores, grouped, preferred_element_type=jnp.float32)
            * score_scale
        )
        value_terms = jnp.einsum(
            "kgqc,qkgd->ckd",
            probabilities.astype(jnp.bfloat16),
            grad_grouped,
            preferred_element_type=jnp.float32,
        )
        return (
            query_terms,
            key_terms.reshape(count, kv_width),
            value_terms.reshape(count, kv_width),
        )

    query_zeros = jnp.zeros((rows_all, kv_local, group_size, HD), jnp.float32)

    def backward_block(accum_rows, step_index):
        key_start = step_index * key_block

        def backward_live(unused_arg):
            key_rows, value_rows, block_keys = slice_keys(key_start, key_block)
            return pair_backward(key_rows, value_rows, block_keys)

        def backward_skipped(unused_arg):
            empty_terms = jnp.zeros((key_block, kv_width), jnp.float32)
            return (query_zeros, empty_terms, empty_terms)

        query_terms, key_terms, value_terms = lax.cond(
            key_ids[key_start] <= top_query, backward_live, backward_skipped, 0
        )
        return (accum_rows + query_terms, (key_terms, value_terms))

    grad_query_rot, (key_terms, value_terms) = lax.scan(backward_block, query_zeros, block_steps)
    key_terms = key_terms.reshape(seq_len, kv_width)
    value_terms = value_terms.reshape(seq_len, kv_width)
    key_grad_own, value_grad_own = (
        lax.psum_scatter(key_terms, "blk", scatter_dimension=0, tiled=True),
        lax.psum_scatter(value_terms, "blk", scatter_dimension=0, tiled=True),
    )
    grad_query_rot = grad_query_rot * score_scale
    grad_key = rotate(key_grad_own.reshape(rows_all, kv_local, HD), cos_table, -sine_table)
    grad_key = grad_key.reshape(rows_all, kv_width).astype(jnp.bfloat16)
    grad_value = value_grad_own.astype(jnp.bfloat16)
    grad_query = rotate(grad_query_rot.reshape(rows_all, heads_local, HD), cos_table, -sine_table)
    grad_query = grad_query.reshape(rows_all, heads_local * HD).astype(jnp.bfloat16)
    grad_query_w = transposed_times(normed, grad_query)
    grad_key_w = transposed_times(normed, grad_key)
    grad_value_w = transposed_times(normed, grad_value)
    grad_normed_part = (
        times_transposed(grad_query, query_w)
        + times_transposed(grad_key, key_w)
        + times_transposed(grad_value, value_w)
    )
    grad_normed = lax.psum(grad_normed_part.astype(jnp.bfloat16), "head").astype(jnp.float32)
    grad_inputs_norm, gain_attn_term = norm_backward(
        grad_normed, inputs, inv_attn, gain_attn.astype(jnp.float32)
    )
    grad_inputs = grad_hidden + grad_inputs_norm
    grad_own = lax.dynamic_slice_in_dim(grad_inputs, head_rank * rows_own, rows_own, 0).astype(
        jnp.bfloat16
    )
    attn_results = (
        lax.psum_scatter(gain_attn_term, "blk", scatter_dimension=0, tiled=True),
        lax.psum_scatter(grad_query_w, "blk", scatter_dimension=0, tiled=True),
        lax.psum_scatter(grad_key_w, "blk", scatter_dimension=0, tiled=True),
        lax.psum_scatter(grad_value_w, "blk", scatter_dimension=0, tiled=True),
        lax.psum_scatter(grad_out_w, "blk", scatter_dimension=0, tiled=True),
    )
    return (
        output,
        grad_own,
        attn_results[0],
        attn_results[1],
        attn_results[2],
        attn_results[3],
        attn_results[4],
        mlp_results[0],
        mlp_results[1],
        mlp_results[2],
        mlp_results[3],
    )


MESH = pl.DeviceIdType.MESH
LINE = 4
VMEM_BYTES = 60 * 2**20


def place():
    blk, head = lax.axis_index("blk"), lax.axis_index("head")
    return blk // 4, (blk // 2) % 2, blk % 2, head


def device(z, y, c, h):
    return (z * 4 + y * 2 + c, h)


def remote(src, dst, send_sem, recv_sem, target):
    return pltpu.make_async_remote_copy(
        src_ref=src,
        dst_ref=dst,
        send_sem=send_sem,
        recv_sem=recv_sem,
        device_id=target,
        device_id_type=MESH,
    )


def greet(target):
    pl.semaphore_signal(
        pltpu.get_barrier_semaphore(), inc=1, device_id=target, device_id_type=MESH
    )


def greet_all(blk_total, head_total):
    blk, head = lax.axis_index("blk"), lax.axis_index("head")
    for other in range(blk_total):
        for half in range(head_total):

            @pl.when(jnp.logical_or(blk != other, head != half))
            def _():
                greet((jnp.int32(other), jnp.int32(half)))

    pl.semaphore_wait(pltpu.get_barrier_semaphore(), blk_total * head_total - 1)


def greet_plane(more=0):
    z, y, c, h = place()

    @pl.when(z > 0)
    def _():
        greet(device(z - 1, y, c, h))

    @pl.when(z < LINE - 1)
    def _():
        greet(device(z + 1, y, c, h))

    greet(device(z, 1 - y, c, h))
    pl.semaphore_wait(
        pltpu.get_barrier_semaphore(),
        1 + more + (z + LINE - 1) // LINE + (LINE - 1 - z + LINE - 1) // LINE,
    )


class Gather:
    CUTS = ((0, 64), (64, 48), (112, 16), (112, 16))
    SEMS = [(3, 4)] * 4 + [(4, 2)] * 2 + [(2,)]

    @staticmethod
    def scratch():
        return [pltpu.SemaphoreType.DMA(shape) for shape in Gather.SEMS] + [
            pltpu.SemaphoreType.DMA
        ]

    def __init__(self, src, out, sems):
        self.src, self.out = src, out
        (self.up_s, self.up_r, self.dn_s, self.dn_r, self.y_s, self.y_r, self.b_sr, self.own_sem) = sems
        self.z, self.y, self.c, self.h = place()

    def piece(self, line, elem):
        y = 1 - self.y if elem == 3 else self.y
        start, size = self.CUTS[elem]
        return self.out.at[line * 2 + y, pl.ds(start, size)]

    def first(self, elem):
        if elem == 3:
            return self.piece(self.z, 3)
        start, size = self.CUTS[elem]
        return self.src.at[pl.ds(start, size)]

    def up(self, step, elem):
        src = self.first(elem) if step == 0 else self.piece(self.z - step, elem)
        return remote(
            src, self.piece(self.z - step, elem), self.up_s.at[step, elem], self.up_r.at[step, elem],
            device(self.z + 1, self.y, self.c, self.h),
        )

    def down(self, step, elem):
        src = self.first(elem) if step == 0 else self.piece(self.z + step, elem)
        return remote(
            src, self.piece(self.z + step, elem), self.dn_s.at[step, elem], self.dn_r.at[step, elem],
            device(self.z - 1, self.y, self.c, self.h),
        )

    def up_in(self, step, elem):
        ref = self.piece(self.z - 1 - step, elem)
        return remote(ref, ref, self.up_s.at[step, elem], self.up_r.at[step, elem], device(self.z, self.y, self.c, self.h))

    def down_in(self, step, elem):
        ref = self.piece(self.z + 1 + step, elem)
        return remote(ref, ref, self.dn_s.at[step, elem], self.dn_r.at[step, elem], device(self.z, self.y, self.c, self.h))

    def across(self, line, elem, own=False):
        src = self.first(elem) if own else self.piece(line, elem)
        return remote(
            src, self.piece(line, elem), self.y_s.at[line, elem], self.y_r.at[line, elem],
            device(self.z, 1 - self.y, self.c, self.h),
        )

    def across_in(self, line, elem):
        start, size = self.CUTS[elem]
        ref = self.out.at[line * 2 + 1 - self.y, pl.ds(start, size)]
        return remote(ref, ref, self.y_s.at[line, elem], self.y_r.at[line, elem], device(self.z, self.y, self.c, self.h))

    def across_b(self):
        return remote(
            self.first(2), self.piece(self.z, 2), self.b_sr.at[0], self.b_sr.at[1],
            device(self.z, 1 - self.y, self.c, self.h),
        )

    def across_b_in(self):
        ref = self.piece(self.z, 3)
        return remote(ref, ref, self.b_sr.at[0], self.b_sr.at[1], device(self.z, self.y, self.c, self.h))

    def own_copy(self):
        return pltpu.make_async_copy(self.src, self.out.at[self.z * 2 + self.y], self.own_sem)

    def start(self):
        self.own_copy().start()
        self.across_b().start()
        for elem in (0, 1, 2):

            @pl.when(self.z < LINE - 1)
            def _():
                self.up(0, elem).start()

            @pl.when(self.z > 0)
            def _():
                self.down(0, elem).start()

            if elem < 2:
                self.across(self.z, elem, own=True).start()

    def relay_b(self):
        self.across_b_in().wait_recv()

        @pl.when(self.z < LINE - 1)
        def _():
            self.up(0, 3).start()

        @pl.when(self.z > 0)
        def _():
            self.down(0, 3).start()

    def relay(self, step, elem):
        @pl.when(self.z - 1 - step >= 0)
        def _():
            self.up_in(step, elem).wait_recv()
            if step < LINE - 2:

                @pl.when(self.z < LINE - 1)
                def _():
                    self.up(step + 1, elem).start()

            if elem < 2:
                self.across(self.z - 1 - step, elem).start()

        @pl.when(self.z + 1 + step <= LINE - 1)
        def _():
            self.down_in(step, elem).wait_recv()
            if step < LINE - 2:

                @pl.when(self.z > 0)
                def _():
                    self.down(step + 1, elem).start()

            if elem < 2:
                self.across(self.z + 1 + step, elem).start()

    def relays(self):
        self.relay_b()
        for step in range(LINE - 1):
            for elem in (0, 1, 2, 3):
                self.relay(step, elem)

    def finish(self):
        for line in range(LINE):
            for elem in (0, 1):
                self.across_in(line, elem).wait_recv()
        for line in range(LINE):
            for elem in (0, 1):
                self.across(line, elem).wait_send()
        self.across_b().wait_send()
        for step in range(LINE - 1):
            for elem in range(4):

                @pl.when(jnp.logical_and(self.z < LINE - 1, self.z - step >= 0))
                def _():
                    self.up(step, elem).wait_send()

                @pl.when(jnp.logical_and(self.z > 0, self.z + step <= LINE - 1))
                def _():
                    self.down(step, elem).wait_send()

        self.own_copy().wait()


def gather_kernel(src, out, *sems):
    greet_plane()
    gather = Gather(src, out, sems)
    gather.start()
    gather.relays()
    gather.finish()


ANY = pl.BlockSpec(memory_space=pl.ANY)
INSIDE = pl.BlockSpec(memory_space=pltpu.VMEM)


def kernel_params(collective_id):
    return pltpu.CompilerParams(
        collective_id=collective_id, has_side_effects=True, vmem_limit_bytes=VMEM_BYTES
    )


def gather_plane(rows):
    return pl.pallas_call(
        gather_kernel,
        out_shape=jax.ShapeDtypeStruct((2 * LINE,) + rows.shape, rows.dtype),
        in_specs=[INSIDE],
        out_specs=ANY,
        scratch_shapes=Gather.scratch(),
        compiler_params=kernel_params(1),
        name="gather_plane",
    )(rows)


class Reduce:
    CUTS = ((0, 64), (64, 64))

    @staticmethod
    def scratch(width):
        inbox = pltpu.VMEM((LINE, 128, width), jnp.bfloat16)
        return [inbox] * 3 + [pltpu.SemaphoreType.DMA((LINE, 2))] * 6

    def __init__(self, parts, refs):
        self.parts = parts
        self.y_in, self.up_in, self.dn_in = refs[:3]
        self.y_s, self.y_r, self.up_s, self.up_r, self.dn_s, self.dn_r = refs[3:]
        self.z, self.y, self.c, self.h = place()
        z = self.z
        self.order = (3 - 3 * (z // 2), (2 + 3 * z) % 5, 1 + z % 2, z)

    def rows(self, cut):
        return pl.ds(*self.CUTS[cut])

    def across(self, line, cut):
        return remote(
            self.parts.at[line * 2 + 1 - self.y, self.rows(cut)], self.y_in.at[line, self.rows(cut)],
            self.y_s.at[line, cut], self.y_r.at[line, cut], device(self.z, 1 - self.y, self.c, self.h),
        )

    def up(self, line, cut):
        return remote(
            self.parts.at[line * 2 + self.y, self.rows(cut)], self.up_in.at[line, self.rows(cut)],
            self.up_s.at[line, cut], self.up_r.at[line, cut], device(self.z + 1, self.y, self.c, self.h),
        )

    def down(self, line, cut):
        return remote(
            self.parts.at[line * 2 + self.y, self.rows(cut)], self.dn_in.at[line, self.rows(cut)],
            self.dn_s.at[line, cut], self.dn_r.at[line, cut], device(self.z - 1, self.y, self.c, self.h),
        )

    def start(self, place_at):
        for cut in range(2):
            self.across(self.order[place_at], cut).start()

    def own(self, line, cut):
        return self.parts.at[line * 2 + self.y, self.rows(cut)]

    def relay(self, place_at):
        line = self.order[place_at]
        for cut in range(2):
            rows = self.rows(cut)
            self.across(line, cut).wait_recv()
            target = self.parts.at[line * 2 + self.y]

            @pl.when(line > self.z)
            def _():
                @pl.when(self.z > 0)
                def _():
                    self.up(line, cut).wait_recv()
                    total = (
                        target[rows].astype(jnp.float32)
                        + self.y_in[line, rows].astype(jnp.float32)
                        + self.up_in[line, rows].astype(jnp.float32)
                    )
                    target[rows] = total.astype(jnp.bfloat16)

                @pl.when(self.z == 0)
                def _():
                    total = target[rows].astype(jnp.float32) + self.y_in[line, rows].astype(jnp.float32)
                    target[rows] = total.astype(jnp.bfloat16)

                self.up(line, cut).start()

            @pl.when(line < self.z)
            def _():
                @pl.when(self.z < LINE - 1)
                def _():
                    self.down(line, cut).wait_recv()
                    total = (
                        target[rows].astype(jnp.float32)
                        + self.y_in[line, rows].astype(jnp.float32)
                        + self.dn_in[line, rows].astype(jnp.float32)
                    )
                    target[rows] = total.astype(jnp.bfloat16)

                @pl.when(self.z == LINE - 1)
                def _():
                    total = target[rows].astype(jnp.float32) + self.y_in[line, rows].astype(jnp.float32)
                    target[rows] = total.astype(jnp.bfloat16)

                self.down(line, cut).start()

    def total(self, out):
        line = self.z
        for cut in range(2):
            rows = self.rows(cut)
            self.across(line, cut).wait_recv()
            out[rows] = self.parts[line * 2 + self.y, rows].astype(jnp.float32) + self.y_in[line, rows].astype(jnp.float32)
        for cut in range(2):
            rows = self.rows(cut)

            @pl.when(self.z > 0)
            def _():
                self.up(line, cut).wait_recv()
                out[rows] += self.up_in[line, rows].astype(jnp.float32)

            @pl.when(self.z < LINE - 1)
            def _():
                self.down(line, cut).wait_recv()
                out[rows] += self.dn_in[line, rows].astype(jnp.float32)

    def finish(self):
        for line in range(LINE):
            for cut in range(2):
                self.across(line, cut).wait_send()

                @pl.when(self.z < line)
                def _():
                    self.up(line, cut).wait_send()

                @pl.when(self.z > line)
                def _():
                    self.down(line, cut).wait_send()


def reduce_kernel(parts_in, out, parts, in_sem, *refs):
    load = pltpu.make_async_copy(parts_in, parts, in_sem)
    load.start()
    greet_plane()
    reduce = Reduce(parts, refs)
    load.wait()
    for place_at in range(4):
        reduce.start(place_at)
    for place_at in range(3):
        reduce.relay(place_at)
    reduce.total(out)
    reduce.finish()


def reduce_plane(parts):
    shape = parts.shape
    return pl.pallas_call(
        reduce_kernel,
        out_shape=jax.ShapeDtypeStruct(shape[1:], jnp.float32),
        in_specs=[ANY],
        out_specs=INSIDE,
        scratch_shapes=[pltpu.VMEM(shape, jnp.bfloat16), pltpu.SemaphoreType.DMA] + Reduce.scratch(shape[2]),
        compiler_params=kernel_params(2),
        name="reduce_plane",
    )(parts)


def dma(*shape):
    return pltpu.SemaphoreType.DMA(shape) if shape else pltpu.SemaphoreType.DMA


def local(src, dst, sem):
    return pltpu.make_async_copy(src, dst, sem)


class AttnSpread:
    @staticmethod
    def scratch():
        return [dma(3, 4), dma(3, 4), dma(3, 8), dma(3), dma(4), dma(4), dma(4), dma(4), dma(4), dma(4)]

    def __init__(self, weights, outs, sems):
        self.weights, (self.qkv, self.out_w) = weights, outs
        (self.s, self.f_s, self.r, self.own, self.x_s, self.x_r, self.c_s, self.c_r, self.o_s, self.o_r) = sems
        self.z, self.y, self.c, self.h = place()
        self.chip = self.z * 2 + self.y
        self.me = device(self.z, self.y, self.c, self.h)
        self.owner = self.h == self.y

    def source(self, kind, line):
        start = line * HD if kind == 0 else (line // 2) * HD
        return self.weights[kind].at[:, pl.ds(pl.multiple_of(start, HD), HD)]

    def slot(self, kind, chip):
        return self.qkv.at[chip, self.c, :, pl.ds(kind * HD, HD)]

    def push(self, kind, step):
        line = (self.z + step) % LINE
        return remote(
            self.source(kind, line), self.slot(kind, self.chip), self.s.at[kind, step], self.r.at[kind, self.chip],
            device(line, self.h, self.c, self.h),
        )

    def push_far(self, kind, step):
        line = (self.z + step) % LINE
        return remote(
            self.source(kind, line), self.slot(kind, self.chip), self.f_s.at[kind, step], self.r.at[kind, self.chip],
            device(line, self.h, self.c, 1 - self.h),
        )

    def keep(self, kind):
        return local(self.source(kind, self.z), self.slot(kind, self.chip), self.own.at[kind])

    def pull(self, kind, chip):
        ref = self.slot(kind, chip)
        return remote(ref, ref, self.s.at[kind, 0], self.r.at[kind, chip], self.me)

    def near(self, step):
        return ((self.z + LINE - step) % LINE) * 2 + self.y

    def far(self, step):
        return ((self.z + LINE - step) % LINE) * 2 + 1 - self.y

    def over(self, step):
        ref = self.qkv.at[self.near(step), self.c]
        return remote(ref, ref, self.x_s.at[step], self.x_r.at[step], device(self.z, self.y, self.c, 1 - self.h))

    def share(self, line, core):
        ref = self.qkv.at[pl.ds(line * 2, 2), core]
        return remote(ref, ref, self.c_s.at[line], self.c_r.at[line], device(self.z, self.y, 1 - self.c, self.h))

    def out_push(self):
        return remote(
            self.weights[3], self.out_w.at[self.y, self.c], self.o_s.at[0], self.o_r.at[0],
            device(self.z, 1 - self.y, self.c, self.h),
        )

    def out_keep(self):
        return local(self.weights[3], self.out_w.at[self.y, self.c], self.o_s.at[1])

    def out_pull(self):
        ref = self.out_w.at[1 - self.y, self.c]
        return remote(ref, ref, self.o_s.at[0], self.o_r.at[0], self.me)

    def out_over(self):
        ref = self.out_w.at[:, self.c]
        return remote(ref, ref, self.o_s.at[2], self.o_r.at[2], device(self.z, self.y, self.c, 1 - self.h))

    def out_share(self, core):
        ref = self.out_w.at[:, core]
        return remote(ref, ref, self.o_s.at[3], self.o_r.at[3], device(self.z, self.y, 1 - self.c, self.h))

    def start(self):
        for kind in range(3):

            @pl.when(self.owner)
            def _():
                self.keep(kind).start()

            @pl.when(jnp.logical_not(self.owner))
            def _():
                self.push(kind, 0).start()
                self.push_far(kind, 0).start()

        for step in range(1, LINE):
            for kind in range(3):
                self.push(kind, step).start()

            @pl.when(jnp.logical_not(self.owner))
            def _():
                for kind in range(3):
                    self.push_far(kind, step).start()

        @pl.when(self.owner)
        def _():
            self.out_keep().start()

        @pl.when(jnp.logical_not(self.owner))
        def _():
            self.out_push().start()

    def relay(self):
        @pl.when(self.owner)
        def _():
            for step in range(LINE):
                for kind in range(3):
                    if step:
                        self.pull(kind, self.near(step)).wait_recv()
                    else:
                        self.keep(kind).wait()
                self.over(step).start()
            self.out_keep().wait()
            self.out_pull().wait_recv()
            self.out_over().start()

    def relay_share(self):
        for step in range(LINE):

            @pl.when(jnp.logical_not(self.owner))
            def _():
                self.over(step).wait_recv()

            for kind in range(3):
                self.pull(kind, self.far(step)).wait_recv()
            self.share((self.z + LINE - step) % LINE, self.c).start()

        @pl.when(jnp.logical_not(self.owner))
        def _():
            self.out_over().wait_recv()

        self.out_share(self.c).start()

    def finish(self):
        for line in range(LINE):
            self.share(line, 1 - self.c).wait_recv()
            self.share(line, self.c).wait_send()
        self.out_share(1 - self.c).wait_recv()
        self.out_share(self.c).wait_send()
        for kind in range(3):
            for step in range(1, LINE):
                self.push(kind, step).wait_send()

        @pl.when(self.owner)
        def _():
            for step in range(LINE):
                self.over(step).wait_send()
            self.out_over().wait_send()

        @pl.when(jnp.logical_not(self.owner))
        def _():
            for kind in range(3):
                self.push(kind, 0).wait_send()
                for step in range(LINE):
                    self.push_far(kind, step).wait_send()
            self.out_push().wait_send()


class MlpSpread:
    @staticmethod
    def scratch():
        return [dma(2, 8), dma(2, 8), dma(2)]

    def __init__(self, weights, outs, sems):
        self.weights, self.outs = weights, outs
        self.s, self.r, self.own = sems
        self.z, self.y, self.c, self.h = place()
        self.chip = self.z * 2 + self.y
        self.part = weights[0].shape[1] // 8

    def columns(self, index):
        return pl.ds(pl.multiple_of(index * self.part, self.part), self.part)

    def push(self, kind, step):
        chip = (self.chip + step) % 8
        return remote(
            self.weights[kind].at[:, self.columns(chip)], self.outs[kind].at[self.chip], self.s.at[kind, step],
            self.r.at[kind, step], device(chip // 2, chip % 2, self.c, self.h),
        )

    def pull(self, kind, step):
        ref = self.outs[kind].at[(self.chip + 8 - step) % 8]
        return remote(ref, ref, self.s.at[kind, step], self.r.at[kind, step], device(self.z, self.y, self.c, self.h))

    def keep(self, kind):
        return local(self.weights[kind].at[:, self.columns(self.chip)], self.outs[kind].at[self.chip], self.own.at[kind])

    def start(self):
        for kind in range(2):
            self.keep(kind).start()
            for step in range(1, 8):
                self.push(kind, step).start()

    def finish(self):
        for kind in range(2):
            self.keep(kind).wait()
            for step in range(1, 8):
                self.pull(kind, step).wait_recv()
                self.push(kind, step).wait_send()


class MlpShare:
    @staticmethod
    def scratch():
        return [dma(2), dma(2, 2), dma(2, 2), dma(2, 2), dma(2, 2)]

    def __init__(self, quarters, outs, sems):
        self.quarters, self.outs = quarters, outs
        self.own, self.x_s, self.x_r, self.c_s, self.c_r = sems
        self.z, self.y, self.c, self.h = place()
        self.part = quarters[0].shape[2]

    def slot(self, kind, cut, half):
        columns = pl.ds(pl.multiple_of(half * self.part, self.part), self.part)
        return self.outs[kind].at[pl.ds(cut * 4, 4), self.c, :, columns]

    def keep(self, kind):
        columns = pl.ds(pl.multiple_of(self.h * self.part, self.part), self.part)
        return local(self.quarters[kind], self.outs[kind].at[:, self.c, :, columns], self.own.at[kind])

    def over(self, kind, cut, half):
        return remote(
            self.quarters[kind].at[pl.ds(cut * 4, 4)], self.slot(kind, cut, half), self.x_s.at[kind, cut],
            self.x_r.at[kind, cut], device(self.z, self.y, self.c, 1 - self.h),
        )

    def share(self, kind, cut, core):
        ref = self.outs[kind].at[pl.ds(cut * 4, 4), core]
        return remote(
            ref, ref, self.c_s.at[kind, cut], self.c_r.at[kind, cut], device(self.z, self.y, 1 - self.c, self.h)
        )

    def start(self):
        for kind in range(2):
            for cut in range(2):
                self.over(kind, cut, self.h).start()
            self.keep(kind).start()

    def relay(self):
        for kind in range(2):
            self.keep(kind).wait()
            for cut in range(2):
                self.over(kind, cut, 1 - self.h).wait_recv()
                self.share(kind, cut, self.c).start()

    def finish(self):
        for kind in range(2):
            for cut in range(2):
                self.share(kind, cut, 1 - self.c).wait_recv()
                self.share(kind, cut, self.c).wait_send()
                self.over(kind, cut, self.h).wait_send()


class DownSpread:
    @staticmethod
    def scratch():
        return [dma(1), dma(2), dma(2)]

    def __init__(self, weight, out, sems):
        self.weight, self.out = weight, out
        self.d_own, self.d_x, self.d_sib = sems
        self.z, self.y, self.c, self.h = place()

    def keep(self):
        return local(self.weight, self.out.at[self.h, self.c], self.d_own.at[0])

    def over(self):
        return remote(
            self.weight, self.out.at[self.h, self.c], self.d_x.at[0], self.d_x.at[1],
            device(self.z, self.y, self.c, 1 - self.h),
        )

    def over_in(self):
        ref = self.out.at[1 - self.h, self.c]
        return remote(ref, ref, self.d_x.at[0], self.d_x.at[1], device(self.z, self.y, self.c, self.h))

    def share(self):
        ref = self.out.at[:, self.c]
        return remote(ref, ref, self.d_sib.at[0], self.d_sib.at[1], device(self.z, self.y, 1 - self.c, self.h))

    def share_in(self):
        ref = self.out.at[:, 1 - self.c]
        return remote(ref, ref, self.d_sib.at[0], self.d_sib.at[1], device(self.z, self.y, self.c, self.h))

    def start(self):
        self.keep().start()
        self.over().start()

    def relay(self):
        self.keep().wait()
        self.over_in().wait_recv()
        self.share().start()

    def finish(self):
        self.share_in().wait_recv()
        self.share().wait_send()
        self.over().wait_send()


class NoteSpread:
    @staticmethod
    def scratch():
        return [dma(16), dma(16), dma(1)]

    def __init__(self, note, out, sems):
        self.note, self.out = note, out
        self.s, self.r, self.own = sems
        self.blk, self.h = lax.axis_index("blk"), lax.axis_index("head")

    def push(self, step):
        other = (self.blk + step) % 16
        return remote(self.note, self.out.at[self.blk], self.s.at[step], self.r.at[step], (other, self.h))

    def pull(self, step):
        ref = self.out.at[(self.blk + 16 - step) % 16]
        return remote(ref, ref, self.s.at[step], self.r.at[step], (self.blk, self.h))

    def keep(self):
        return local(self.note, self.out.at[self.blk], self.own.at[0])

    def start(self):
        self.keep().start()
        for step in range(1, 16):
            self.push(step).start()

    def finish(self):
        self.keep().wait()
        for step in range(1, 16):
            self.pull(step).wait_recv()
            self.push(step).wait_send()


def split_refs(refs, counts):
    groups, at = [], 0
    for count in counts:
        groups.append(refs[at : at + count])
        at += count
    return groups


def spread_kernel(tokens, note, wq, wk, wv, wo, tok_out, note_out, qkv, out_w, *sems):
    tok_sems, note_sems, attn_sems = split_refs(sems, (8, 3, 10))
    greet_all(16, 2)
    tok = Gather(tokens, tok_out, tok_sems)
    notes = NoteSpread(note, note_out, note_sems)
    attn = AttnSpread((wq, wk, wv, wo), (qkv, out_w), attn_sems)
    attn.start()
    tok.start()
    notes.start()
    tok.relay_b()
    for elem in (2, 0, 1, 3):
        tok.relay(0, elem)
    attn.relay()
    for elem in (2, 0, 1, 3):
        tok.relay(1, elem)
    attn.relay_share()
    for elem in (2, 0, 1, 3):
        tok.relay(2, elem)
    notes.finish()
    attn.finish()
    tok.finish()


def spread(tokens, note, wq, wk, wv, wo):
    def shape(*dims):
        return jax.ShapeDtypeStruct(dims, jnp.bfloat16)

    rows, width = tokens.shape
    depth = wq.shape[0]
    return pl.pallas_call(
        spread_kernel,
        out_shape=(
            shape(8, rows, width),
            jax.ShapeDtypeStruct((16,) + note.shape, jnp.float32),
            shape(8, 2, depth, 3 * HD),
            shape(2, 2, wo.shape[0], width),
        ),
        in_specs=[INSIDE] * 6,
        out_specs=(ANY,) * 4,
        scratch_shapes=Gather.scratch() + NoteSpread.scratch() + AttnSpread.scratch(),
        compiler_params=kernel_params(3),
        name="spread",
    )(tokens, note, wq, wk, wv, wo)


def reduce_share_kernel(parts_in, gate_in, up_in, out, gate, up, parts, in_sem, *refs):
    reduce_refs, share_sems = split_refs(refs, (9, 5))
    load = pltpu.make_async_copy(parts_in, parts, in_sem)
    load.start()
    z, y, c, h = place()
    greet(device(z, y, 1 - c, h))
    greet(device(z, y, c, 1 - h))
    greet_plane(2)
    reduce = Reduce(parts, reduce_refs)
    share = MlpShare((gate_in, up_in), (gate, up), share_sems)
    share.start()
    load.wait()
    for place_at in range(4):
        reduce.start(place_at)
    for place_at in range(3):
        reduce.relay(place_at)
    reduce.total(out)
    reduce.finish()
    share.relay()
    share.finish()


def reduce_share(parts, gate, up):
    shape = parts.shape
    eight, depth, part = gate.shape
    full = jax.ShapeDtypeStruct((eight, 2, depth, 2 * part), gate.dtype)
    return pl.pallas_call(
        reduce_share_kernel,
        out_shape=(jax.ShapeDtypeStruct(shape[1:], jnp.float32), full, full),
        in_specs=[ANY, INSIDE, INSIDE],
        out_specs=(INSIDE, ANY, ANY),
        scratch_shapes=[pltpu.VMEM(shape, jnp.bfloat16), dma()] + Reduce.scratch(shape[2]) + MlpShare.scratch(),
        compiler_params=kernel_params(7),
        name="reduce_share",
    )(parts, gate, up)


def gather_share_kernel(src, wd, out, down, *sems):
    gather_sems, down_sems = split_refs(sems, (8, 3))
    z, y, c, h = place()
    greet(device(z, y, 1 - c, h))
    greet(device(z, y, c, 1 - h))
    greet_plane(2)
    gather = Gather(src, out, gather_sems)
    downs = DownSpread(wd, down, down_sems)
    gather.start()
    downs.start()
    gather.relays()
    downs.relay()
    gather.finish()
    downs.finish()


def gather_share(rows, wd):
    return pl.pallas_call(
        gather_share_kernel,
        out_shape=(
            jax.ShapeDtypeStruct((2 * LINE,) + rows.shape, rows.dtype),
            jax.ShapeDtypeStruct((2, 2) + wd.shape, wd.dtype),
        ),
        in_specs=[INSIDE] * 2,
        out_specs=(ANY,) * 2,
        scratch_shapes=Gather.scratch() + DownSpread.scratch(),
        compiler_params=kernel_params(8),
        name="gather_share",
    )(rows, wd)


def attend_kernel(
    query, kv, query_ids, key_ids, cot, wg, wu,
    kv_out, attended_out, attended_low_out, log_out, cot_out, gate, up,
    keys, scores, total, own, x_s, x_r, c_s, c_r, out_sem, *sems,
):
    z, y, c, h = place()
    cot_sems, mlp_sems = split_refs(sems, (8, 3))
    greet_all(16, 2)
    rows, width = key_ids.shape[2], query.shape[1]
    pair = query.shape[0] // LINE
    cots = Gather(cot, cot_out, cot_sems)
    mlp = MlpSpread((wg, wu), (gate, up), mlp_sems)

    def keep(cut):
        part = pl.ds(cut * 2, 2)
        return local(kv.at[part], keys.at[part, c, h], own.at[cut])

    def over(cut, half):
        part = pl.ds(cut * 2, 2)
        return remote(kv.at[part], keys.at[part, c, half], x_s.at[cut], x_r.at[cut], device(z, y, c, 1 - h))

    def share(cut, core):
        ref = keys.at[pl.ds(cut * 2, 2), core]
        return remote(ref, ref, c_s.at[cut], c_r.at[cut], device(z, y, 1 - c, h))

    for cut in range(LINE):
        over(cut, h).start()
        keep(cut).start()
    mlp.start()
    cots.start()

    def pass_on(cut):
        keep(cut).wait()
        over(cut, 1 - h).wait_recv()
        share(cut, c).start()

    def attend(place_at):
        part = pl.ds(place_at * pair, pair)
        count = min(2 * place_at + 3, 8)
        ids = query_ids[part]

        def maxima(block, best):
            key = keys[block, :, :, :, :width].reshape(rows, width)
            part_scores = times_transposed(query[part], key)
            part_scores = jnp.where(key_ids[block] <= ids, part_scores, -1e30)
            scores[block] = part_scores
            for lane in range(rows // 128):
                best = jnp.maximum(best, part_scores[:, lane * 128 : lane * 128 + 128])
            return best

        best = lax.fori_loop(0, count, maxima, jnp.full((pair, 128), -1e30, jnp.float32))
        row_max = jnp.max(best, axis=1, keepdims=True)
        total[...] = jnp.zeros_like(total)

        def mix(block, sums):
            weights = jnp.exp(scores[block] - row_max)
            value = keys[block, :, :, :, width:].reshape(rows, width)
            total[...] += product(weights.astype(jnp.bfloat16), value)
            for lane in range(rows // 128):
                sums = sums + weights[:, lane * 128 : lane * 128 + 128]
            return sums

        sums = lax.fori_loop(0, count, mix, jnp.zeros((pair, 128), jnp.float32))
        row_sum = jnp.sum(sums, axis=1, keepdims=True)
        mixed = total[...] / row_sum
        attended_out[part] = mixed
        attended_low_out[part] = mixed.astype(jnp.bfloat16)
        log_out[part] = row_max + jnp.log(row_sum)

    pass_on(0)
    pass_on(1)
    share(0, 1 - c).wait_recv()
    share(1, 1 - c).wait_recv()
    attend(0)
    cots.relay_b()
    for elem in (2, 0, 1, 3):
        cots.relay(0, elem)
    pass_on(2)
    share(2, 1 - c).wait_recv()
    attend(1)
    pass_on(3)
    share(3, 1 - c).wait_recv()
    store = local(keys, kv_out, out_sem)
    store.start()
    attend(2)
    for elem in (2, 0, 1, 3):
        cots.relay(1, elem)
    attend(3)
    for elem in (2, 0, 1, 3):
        cots.relay(2, elem)
    cots.finish()
    mlp.finish()
    for cut in range(LINE):
        share(cut, c).wait_send()
        over(cut, h).wait_send()
    store.wait()


def attend_keys(query, kv, query_ids, key_ids, cot, wg, wu):
    eight, rows, width = kv.shape
    depth, part = wg.shape[0], wg.shape[1] // 8
    tokens = query.shape[0]

    def shape(*dims, dtype=jnp.bfloat16):
        return jax.ShapeDtypeStruct(dims, dtype)

    return pl.pallas_call(
        attend_kernel,
        out_shape=(
            shape(eight, 2, 2, rows, width),
            shape(tokens, HD, dtype=jnp.float32),
            shape(tokens, HD),
            shape(tokens, 1, dtype=jnp.float32),
            shape(8, *cot.shape),
            shape(8, depth, part),
            shape(8, depth, part),
        ),
        in_specs=[INSIDE] * 7,
        out_specs=(ANY, INSIDE, INSIDE, INSIDE, ANY, ANY, ANY),
        scratch_shapes=[
            pltpu.VMEM((eight, 2, 2, rows, width), jnp.bfloat16),
            pltpu.VMEM((eight, tokens // LINE, 4 * rows), jnp.float32),
            pltpu.VMEM((tokens // LINE, HD), jnp.float32),
        ] + [dma(4)] * 5 + [dma()] + Gather.scratch() + MlpSpread.scratch(),
        compiler_params=kernel_params(4),
        name="attend_keys",
    )(query, kv, query_ids, key_ids, cot, wg, wu)


def add_into(target, *others):
    total = target[...].astype(jnp.float32)
    for other in others:
        total += other[...].astype(jnp.float32)
    target[...] = total.astype(target.dtype)


class QuarterReduce:
    @staticmethod
    def scratch(depth, wide):
        store = pltpu.VMEM((8, 2, depth, wide), jnp.bfloat16)
        sib = pltpu.VMEM((8, depth, wide), jnp.bfloat16)
        over = pltpu.VMEM((8, depth, wide // 2), jnp.bfloat16)
        return [store, store, sib, sib, over, over] + [dma(2)] + [dma(2, 2)] * 4

    def __init__(self, sources, outs, refs):
        self.sources, self.outs = sources, outs
        self.store, self.sib, self.box = refs[0:2], refs[2:4], refs[4:6]
        self.load_s, self.c_s, self.c_r, self.x_s, self.x_r = refs[6:]
        self.z, self.y, self.c, self.h = place()
        self.part = self.box[0].shape[2]

    def columns(self, half):
        return pl.ds(pl.multiple_of(half * self.part, self.part), self.part)

    def load(self, kind):
        return local(self.sources[kind], self.store[kind], self.load_s.at[kind])

    def share(self, kind, cut):
        chips = pl.ds(cut * 4, 4)
        return remote(
            self.store[kind].at[chips, 1 - self.c], self.sib[kind].at[chips], self.c_s.at[kind, cut],
            self.c_r.at[kind, cut], device(self.z, self.y, 1 - self.c, self.h),
        )

    def over(self, kind, cut):
        chips = pl.ds(cut * 4, 4)
        return remote(
            self.store[kind].at[chips, self.c, :, self.columns(1 - self.h)], self.box[kind].at[chips],
            self.x_s.at[kind, cut], self.x_r.at[kind, cut], device(self.z, self.y, self.c, 1 - self.h),
        )

    def start_loads(self):
        for kind in range(2):
            self.load(kind).start()

    def start(self, kind):
        self.load(kind).wait()
        for cut in range(2):
            self.share(kind, cut).start()

    def relay(self, kind):
        columns = self.columns(1 - self.h)
        for cut in range(2):
            self.share(kind, cut).wait_recv()

            @pl.loop(cut * 4, cut * 4 + 4)
            def _(chip):
                add_into(self.store[kind].at[chip, self.c, :, columns], self.sib[kind].at[chip, :, columns])

            self.over(kind, cut).start()

    def finish(self, kind):
        columns = self.columns(self.h)
        for cut in range(2):
            self.over(kind, cut).wait_recv()

            @pl.loop(cut * 4, cut * 4 + 4)
            def _(chip):
                total = self.store[kind][chip, self.c, :, columns].astype(jnp.float32)
                total += self.sib[kind][chip, :, columns].astype(jnp.float32)
                total += self.box[kind][chip].astype(jnp.float32)
                self.outs[kind][chip] = total.astype(jnp.bfloat16)

        for cut in range(2):
            self.share(kind, cut).wait_send()
            self.over(kind, cut).wait_send()


class QuarterScatter:
    @staticmethod
    def scratch():
        return [dma(2, 8), dma(2, 8), dma(2)]

    def __init__(self, quarters, outs, sems):
        self.quarters, self.outs = quarters, outs
        self.s, self.r, self.own = sems
        self.z, self.y, self.c, self.h = place()
        self.chip = self.z * 2 + self.y
        self.part = quarters[0].shape[2]

    def columns(self, chip):
        return pl.ds(pl.multiple_of(chip * self.part, self.part), self.part)

    def push(self, kind, step):
        target = (self.chip + step) % 8
        return remote(
            self.quarters[kind].at[target], self.outs[kind].at[:, self.columns(self.chip)], self.s.at[kind, step],
            self.r.at[kind, step], device(target // 2, target % 2, self.c, self.h),
        )

    def pull(self, kind, step):
        ref = self.outs[kind].at[:, self.columns((self.chip + 8 - step) % 8)]
        return remote(ref, ref, self.s.at[kind, step], self.r.at[kind, step], device(self.z, self.y, self.c, self.h))

    def keep(self, kind):
        return local(self.quarters[kind].at[self.chip], self.outs[kind].at[:, self.columns(self.chip)], self.own.at[kind])

    def start(self):
        for kind in range(2):
            self.keep(kind).start()
            for step in range(1, 8):
                self.push(kind, step).start()

    def finish(self):
        for kind in range(2):
            self.keep(kind).wait()
            for step in range(1, 8):
                self.pull(kind, step).wait_recv()
                self.push(kind, step).wait_send()


class DownReduce:
    @staticmethod
    def scratch(rows, width):
        return [
            pltpu.VMEM((2, 2, rows, width), jnp.bfloat16),
            pltpu.VMEM((2, rows, width), jnp.bfloat16),
            pltpu.VMEM((rows, width), jnp.bfloat16),
            dma(1), dma(2), dma(2),
        ]

    def __init__(self, source, out, refs):
        self.source, self.out = source, out
        self.store, self.sib, self.box, self.load_s, self.c_sr, self.x_sr = refs
        self.z, self.y, self.c, self.h = place()

    def load(self):
        return local(self.source, self.store, self.load_s.at[0])

    def share(self):
        return remote(
            self.store.at[:, 1 - self.c], self.sib, self.c_sr.at[0], self.c_sr.at[1],
            device(self.z, self.y, 1 - self.c, self.h),
        )

    def over(self):
        return remote(
            self.store.at[1 - self.h, self.c], self.box, self.x_sr.at[0], self.x_sr.at[1],
            device(self.z, self.y, self.c, 1 - self.h),
        )

    def start(self):
        self.load().wait()
        self.share().start()

    def relay(self):
        self.share().wait_recv()
        add_into(self.store.at[1 - self.h, self.c], self.sib.at[1 - self.h])
        self.over().start()

    def finish(self):
        self.over().wait_recv()
        total = self.store[self.h, self.c].astype(jnp.float32) + self.sib[self.h].astype(jnp.float32)
        self.out[...] = total + self.box[...].astype(jnp.float32)
        self.share().wait_send()
        self.over().wait_send()


def reduce_grads_kernel(parts_in, gate_in, up_in, out, gate, up, parts, in_sem, *refs):
    reduce_refs, grad_refs = split_refs(refs, (9, 11))
    load = pltpu.make_async_copy(parts_in, parts, in_sem)
    load.start()
    z, y, c, h = place()
    grads = QuarterReduce((gate_in, up_in), (gate, up), grad_refs)
    grads.start_loads()
    greet(device(z, y, 1 - c, h))
    greet(device(z, y, c, 1 - h))
    greet_plane(2)
    reduce = Reduce(parts, reduce_refs)
    load.wait()
    for place_at in range(4):
        reduce.start(place_at)
    grads.start(0)
    grads.start(1)
    grads.relay(0)
    reduce.relay(0)
    grads.relay(1)
    reduce.relay(1)
    reduce.relay(2)
    reduce.total(out)
    grads.finish(0)
    grads.finish(1)
    reduce.finish()


def reduce_grads(parts, gate, up):
    shape = parts.shape
    depth, wide = gate.shape[2:]
    quarter = jax.ShapeDtypeStruct((8, depth, wide // 2), gate.dtype)
    return pl.pallas_call(
        reduce_grads_kernel,
        out_shape=(jax.ShapeDtypeStruct(shape[1:], jnp.float32), quarter, quarter),
        in_specs=[ANY] * 3,
        out_specs=(INSIDE,) * 3,
        scratch_shapes=[pltpu.VMEM(shape, jnp.bfloat16), dma()]
        + Reduce.scratch(shape[2])
        + QuarterReduce.scratch(depth, wide),
        compiler_params=kernel_params(9),
        name="reduce_grads",
    )(parts, gate, up)


def gather_grads_kernel(src, down_in, out, down, *refs):
    gather_sems, down_refs = split_refs(refs, (8, 6))
    z, y, c, h = place()
    downs = DownReduce(down_in, down, down_refs)
    downs.load().start()
    greet(device(z, y, 1 - c, h))
    greet(device(z, y, c, 1 - h))
    greet_plane(2)
    gather = Gather(src, out, gather_sems)
    gather.start()
    downs.start()
    gather.relay_b()
    downs.relay()
    for step in range(LINE - 1):
        for elem in (2, 0, 1, 3):
            gather.relay(step, elem)
    downs.finish()
    gather.finish()


def gather_grads(rows, down):
    return pl.pallas_call(
        gather_grads_kernel,
        out_shape=(
            jax.ShapeDtypeStruct((2 * LINE,) + rows.shape, rows.dtype),
            jax.ShapeDtypeStruct(down.shape[2:], jnp.float32),
        ),
        in_specs=[INSIDE, ANY],
        out_specs=(ANY, INSIDE),
        scratch_shapes=Gather.scratch() + DownReduce.scratch(*down.shape[2:]),
        compiler_params=kernel_params(10),
        name="gather_grads",
    )(rows, down)


def attend_back_kernel(
    query, grad_out, keys_in, keys_turned, log_row, delta_row, query_row, key_column, gate_in, up_in,
    side_out, grad_query, gate, up,
    keys, turned, parts, grad_key, grad_value, sib_in, x_in, z_in,
    load_s, c_s, c_r, x_s, x_r, z_s, z_r, *sems,
):
    z, y, c, h = place()
    mate = z + 1 - 2 * (z % 2)
    loads = [local(keys_in, keys, load_s.at[0]), local(keys_turned, turned, load_s.at[1])]
    for load in loads:
        load.start()
    greet_all(16, 2)
    scatter = QuarterScatter((gate_in, up_in), (gate, up), sems)
    scatter.start()
    rows, width = key_column.shape[1], query.shape[1]
    pair = query.shape[0] // LINE

    def share(block):
        return remote(
            parts.at[block, 1 - c], sib_in.at[block], c_s.at[block], c_r.at[block], device(z, y, 1 - c, h)
        )

    def over(block):
        return remote(
            parts.at[block, c, 1 - h], x_in.at[block], x_s.at[block], x_r.at[block], device(z, y, c, 1 - h)
        )

    def columns(kind):
        return pl.ds(pl.multiple_of(kind * width, width), width)

    def across(block):
        return remote(
            parts.at[block, c, h, :, columns(1 - z % 2)], z_in.at[block], z_s.at[block], z_r.at[block],
            device(mate, y, c, h),
        )

    def stage_two(block):
        share(block).wait_recv()
        add_into(parts.at[block, c, 1 - h], sib_in.at[block, 1 - h])
        over(block).start()

    def stage_three(block):
        over(block).wait_recv()
        add_into(parts.at[block, c, h], sib_in.at[block, h], x_in.at[block])
        across(block).start()

    def stage_four(block):
        across(block).wait_recv()
        side_out[block] = parts[block, c, h, :, columns(z % 2)].astype(jnp.float32) + z_in[block].astype(jnp.float32)

    for load in loads:
        load.wait()
    grad_query[...] = jnp.zeros_like(grad_query)
    for block in range(8):
        key = keys[block, :, :, :, :width].reshape(rows, width)
        value = keys[block, :, :, :, width:].reshape(rows, width)
        grad_key[...] = jnp.zeros_like(grad_key)
        grad_value[...] = jnp.zeros_like(grad_value)

        @pl.loop(max(0, (block - 1) // 2), LINE)
        def _(place_at):
            part = pl.ds(pl.multiple_of(place_at * pair, pair), pair)
            part_scores = times_transposed(key, query[part])
            visible = key_column[block] <= query_row[place_at]
            weights = jnp.where(visible, jnp.exp(part_scores - log_row[place_at]), 0.0)
            grad_weights = times_transposed(value, grad_out[part])
            grad_scores = (weights * (grad_weights - delta_row[place_at])).astype(jnp.bfloat16)
            grad_key[...] += product(grad_scores, query[part])
            grad_value[...] += product(weights.astype(jnp.bfloat16), grad_out[part])
            grad_query[place_at] += product(turned[block], grad_scores)

        parts[block, :, :, :, :width] = grad_key[...].astype(jnp.bfloat16).reshape(2, 2, rows // 4, width)
        parts[block, :, :, :, width:] = grad_value[...].astype(jnp.bfloat16).reshape(2, 2, rows // 4, width)
        share(block).start()
        if block >= 1:
            stage_two(block - 1)
        if block >= 4:
            stage_three(block - 4)
    stage_two(7)
    for block in range(4, 8):
        stage_three(block)
        stage_four(block - 4)
    for block in range(4, 8):
        stage_four(block)
    for block in range(8):
        share(block).wait_send()
        over(block).wait_send()
        across(block).wait_send()
    scatter.finish()


def attend_back(query, grad_out, keys, keys_turned, log_row, delta_row, query_row, key_column, gate, up):
    eight, _, _, rows, width = keys.shape
    tokens = query.shape[0]
    depth, part = gate.shape[1:]

    def room(*dims, dtype=jnp.bfloat16):
        return pltpu.VMEM(dims, dtype)

    def shape(*dims, dtype=jnp.bfloat16):
        return jax.ShapeDtypeStruct(dims, dtype)

    return pl.pallas_call(
        attend_back_kernel,
        out_shape=(
            shape(eight, rows, HD, dtype=jnp.float32),
            shape(LINE, HD, tokens // LINE, dtype=jnp.float32),
            shape(depth, 8 * part),
            shape(depth, 8 * part),
        ),
        in_specs=[INSIDE, INSIDE, ANY, ANY, INSIDE, INSIDE, INSIDE, INSIDE, INSIDE, INSIDE],
        out_specs=(INSIDE, INSIDE, ANY, ANY),
        scratch_shapes=[
            room(*keys.shape), room(*keys_turned.shape), room(*keys.shape),
            room(4 * rows, HD, dtype=jnp.float32), room(4 * rows, HD, dtype=jnp.float32),
            room(eight, 2, rows, width), room(eight, rows, width), room(eight, rows, HD),
            dma(2),
        ] + [dma(8)] * 6 + QuarterScatter.scratch(),
        compiler_params=kernel_params(11),
        name="attend_back",
    )(query, grad_out, keys, keys_turned, log_row, delta_row, query_row, key_column, gate, up)


class HeadGrads:
    @staticmethod
    def scratch(depth, out_rows, width):
        def room(*dims):
            return pltpu.VMEM(dims, jnp.bfloat16)

        return [
            room(8, 2, depth, HD), room(8, 2, depth, HD), room(2, 2, out_rows, width),
            room(8, depth, HD), room(8, depth, HD), room(2, out_rows, width),
            room(8, depth, HD), room(8, depth, HD), room(2, out_rows, width),
            dma(3), dma(3), dma(3), dma(3), dma(3), dma(3, 8), dma(3, 4, 8), dma(2), dma(4),
        ]

    def __init__(self, sources, outs, refs):
        self.sources, self.outs = sources, outs
        self.store, self.sib, self.box = refs[0:3], refs[3:6], refs[6:9]
        (self.load_s, self.c_s, self.c_r, self.x_s, self.x_r, self.s, self.r, self.y_sr, self.own) = refs[9:]
        self.z, self.y, self.c, self.h = place()
        self.chip = self.z * 2 + self.y
        self.me = device(self.z, self.y, self.c, self.h)
        self.owner = self.h == self.y

    def load(self, i):
        return local(self.sources[i], self.store[i], self.load_s.at[i])

    def share(self, i):
        return remote(
            self.store[i].at[:, 1 - self.c], self.sib[i], self.c_s.at[i], self.c_r.at[i],
            device(self.z, self.y, 1 - self.c, self.h),
        )

    def over(self, i):
        return remote(
            self.store[i].at[:, self.c], self.box[i], self.x_s.at[i], self.x_r.at[i],
            device(self.z, self.y, self.c, 1 - self.h),
        )

    def target(self, kind, line):
        start = line * HD if kind == 0 else (line // 2) * HD
        return self.outs[kind].at[:, pl.ds(pl.multiple_of(start, HD), HD)]

    def push(self, kind, step):
        chip = (self.chip + step) % 8
        return remote(
            self.store[min(kind, 1)].at[chip, self.c], self.target(kind, self.z), self.s.at[kind, step],
            self.r.at[kind, self.z, step], device(chip // 2, chip % 2, self.c, self.h),
        )

    def keep(self, kind):
        return local(self.store[min(kind, 1)].at[self.chip, self.c], self.target(kind, self.z), self.own.at[kind])

    def pull(self, kind, line, step):
        ref = self.target(kind, line)
        return remote(ref, ref, self.s.at[kind, step], self.r.at[kind, line, step], self.me)

    def out_move(self):
        return remote(
            self.store[2].at[1 - self.y, self.c], self.outs[3], self.y_sr.at[0], self.y_sr.at[1],
            device(self.z, 1 - self.y, self.c, self.h),
        )

    def out_keep(self):
        return local(self.store[2].at[self.y, self.c], self.outs[3], self.own.at[3])

    def start_loads(self):
        for i in range(3):
            self.load(i).start()

    def start(self):
        for i in (2, 0, 1):
            self.load(i).wait()
            self.share(i).start()

    def relay(self):
        for i in (2, 0, 1):
            self.share(i).wait_recv()

            @pl.loop(0, self.sib[i].shape[0])
            def _(at):
                add_into(self.store[i].at[at, self.c], self.sib[i].at[at])

            @pl.when(jnp.logical_not(self.owner))
            def _():
                self.over(i).start()

    def scatter(self):
        @pl.when(self.owner)
        def _():
            for i in (2, 0, 1):
                self.over(i).wait_recv()

                @pl.loop(0, self.sib[i].shape[0])
                def _(at):
                    add_into(self.store[i].at[at, self.c], self.box[i].at[at])

                if i == 2:
                    self.out_move().start()
                    self.out_keep().start()
                elif i == 0:
                    self.keep(0).start()
                    for step in range(1, 8):
                        self.push(0, step).start()
                else:
                    for kind in (1, 2):

                        @pl.when(self.z % 2 == kind - 1)
                        def _():
                            self.keep(kind).start()
                            for step in range(1, 8):
                                self.push(kind, step).start()

    def finish(self):
        for kind in range(3):
            for line in range(LINE):
                if kind and line % 2 != kind - 1:
                    continue
                step = (self.chip + 8 - (line * 2 + self.h)) % 8

                @pl.when(step != 0)
                def _():
                    self.pull(kind, line, step).wait_recv()

                @pl.when(step == 0)
                def _():
                    self.keep(kind).wait()

        @pl.when(jnp.logical_not(self.owner))
        def _():
            remote(self.outs[3], self.outs[3], self.y_sr.at[0], self.y_sr.at[1], self.me).wait_recv()
            for i in range(3):
                self.over(i).wait_send()

        @pl.when(self.owner)
        def _():
            self.out_keep().wait()
            self.out_move().wait_send()
            for step in range(1, 8):
                self.push(0, step).wait_send()
            for kind in (1, 2):

                @pl.when(self.z % 2 == kind - 1)
                def _():
                    for step in range(1, 8):
                        self.push(kind, step).wait_send()

        for i in range(3):
            self.share(i).wait_send()


def reduce_heads_kernel(
    parts_in, query_in, side_in, out_in, out, query, key, value, outw, parts, in_sem, *refs
):
    reduce_refs, head_refs = split_refs(refs, (9, 18))
    load = pltpu.make_async_copy(parts_in, parts, in_sem)
    load.start()
    heads = HeadGrads((query_in, side_in, out_in), (query, key, value, outw), head_refs)
    heads.start_loads()
    greet_all(16, 2)
    reduce = Reduce(parts, reduce_refs)
    load.wait()
    for place_at in range(4):
        reduce.start(place_at)
    heads.start()
    heads.relay()
    reduce.relay(0)
    reduce.relay(1)
    heads.scatter()
    reduce.relay(2)
    reduce.total(out)
    heads.finish()
    reduce.finish()


def reduce_heads(parts, query, side, outw):
    shape = parts.shape
    depth = query.shape[2]
    out_rows, width = outw.shape[2:]

    def room(*dims):
        return jax.ShapeDtypeStruct(dims, jnp.bfloat16)

    return pl.pallas_call(
        reduce_heads_kernel,
        out_shape=(
            jax.ShapeDtypeStruct(shape[1:], jnp.float32),
            room(depth, 4 * HD), room(depth, 2 * HD), room(depth, 2 * HD), room(out_rows, width),
        ),
        in_specs=[ANY] * 4,
        out_specs=(INSIDE, ANY, ANY, ANY, ANY),
        scratch_shapes=[pltpu.VMEM(shape, jnp.bfloat16), dma()]
        + Reduce.scratch(shape[2])
        + HeadGrads.scratch(depth, out_rows, width),
        compiler_params=kernel_params(6),
        name="reduce_heads",
    )(parts, query, side, outw)


def gains_kernel(gains, out, box, own, send_sems, recv_sems):
    blk, h = lax.axis_index("blk"), lax.axis_index("head")
    greet_all(16, 2)

    def push(step):
        other = (blk + step // 2) % 16
        return remote(
            gains.at[other], box.at[step], send_sems.at[step], recv_sems.at[step], (other, (h + step % 2) % 2)
        )

    keep = local(gains.at[blk], box.at[0], own.at[0])
    keep.start()
    for step in range(1, 32):
        push(step).start()
    keep.wait()
    total = box[0]
    for step in range(1, 32):
        push(step).wait_recv()
        total += box[step]
    out[...] = total
    for step in range(1, 32):
        push(step).wait_send()


def reduce_gains(gains):
    return pl.pallas_call(
        gains_kernel,
        out_shape=jax.ShapeDtypeStruct(gains.shape[1:], gains.dtype),
        in_specs=[INSIDE],
        out_specs=INSIDE,
        scratch_shapes=[pltpu.VMEM((32,) + gains.shape[1:], gains.dtype), dma(1), dma(32), dma(32)],
        compiler_params=kernel_params(12),
        name="reduce_gains",
    )(gains)


def fast_body(
    tokens,
    attn_gain,
    w_query,
    w_key,
    w_value,
    w_out,
    mlp_gain,
    w_gate,
    w_up,
    w_down,
    block_ids,
    positions,
    cotangent,
):
    z, y, core, half = place()
    rows, width = tokens.shape
    token_rows = 8 * rows
    f32, bf16 = jnp.float32, jnp.bfloat16

    def own_half(values):
        return lax.dynamic_index_in_dim(values, half, 0, False)

    note = jnp.concatenate(
        [
            positions.astype(f32).reshape(2, rows),
            block_ids.astype(f32).reshape(2, rows),
            attn_gain.astype(f32)[None],
            mlp_gain.astype(f32)[None],
            jnp.zeros((2, rows), f32),
        ]
    )
    tokens_all, notes, qkv_w, out_w = spread(tokens, note, w_query, w_key, w_value, w_out)
    tokens_all = tokens_all.reshape(token_rows, width)
    qkv_w = qkv_w.reshape(width, 3 * HD)
    out_w = out_w.reshape(HD, width)
    gain_attn = notes[:, 4].reshape(1, width)
    gain_mlp = notes[:, 5].reshape(1, width)
    mine = lax.dynamic_index_in_dim(notes.reshape(8, 2, 8, rows), core, 1, False)
    positions_mine = lax.dynamic_index_in_dim(mine[:, 0:2], half, 1, False).reshape(token_rows)
    ids_mine = lax.dynamic_index_in_dim(mine[:, 2:4], half, 1, False).reshape(token_rows)
    key_ids = notes[:, 2:4].reshape(32 * rows)

    score_scale = HD ** (-0.5)
    inputs_all = tokens_all.astype(f32)
    normed = (inputs_all * rms_scale(inputs_all) * gain_attn).astype(bf16)
    cos_table, sine_table = rope_tables(positions_mine)
    cos_table, sine_table = cos_table[:, 0], sine_table[:, 0]
    projected = product(normed, qkv_w)
    query = rotate(projected[:, :HD], cos_table, sine_table).astype(bf16)
    key = rotate(projected[:, HD : 2 * HD], cos_table, sine_table).astype(bf16)
    value = projected[:, 2 * HD :].astype(bf16)
    scaled_query = (query.astype(f32) * score_scale).astype(bf16)
    keys_values, attended, attended_low, log_total, cot_all, gate_w, up_w = attend_keys(
        scaled_query,
        jnp.concatenate([key, value], axis=1).reshape(8, rows, 2 * HD),
        ids_mine[:, None],
        key_ids.reshape(8, 1, 4 * rows),
        cotangent,
        w_gate,
        w_up,
    )
    cot_all = cot_all.reshape(token_rows, width)
    branch, gate_w, up_w = reduce_share(
        product(attended_low, out_w).astype(bf16).reshape(8, rows, width), gate_w, up_w
    )
    hidden_part = gate_w.shape[3]
    gate_w = gate_w.reshape(width, hidden_part)
    up_w = up_w.reshape(width, hidden_part)

    inputs = tokens.astype(f32)
    inv_attn = rms_scale(inputs)
    hidden = inputs + branch
    inv_mlp = rms_scale(hidden)
    normed_mlp, down_w = gather_share((hidden * inv_mlp * gain_mlp).astype(bf16), w_down)
    normed_mlp = normed_mlp.reshape(token_rows, width)
    down_w = down_w.reshape(hidden_part, width)
    gate_pre = product(normed_mlp, gate_w)
    up_pre = product(normed_mlp, up_w)
    sigmoid_gate = jax.nn.sigmoid(gate_pre)
    active = (gate_pre * sigmoid_gate * up_pre).astype(bf16)
    mlp_own = reduce_plane(product(active, down_w).astype(bf16).reshape(8, rows, width))
    output = (hidden + mlp_own).astype(bf16)
    grad_active = times_transposed(cot_all, down_w)
    grad_gate = (
        grad_active * up_pre * sigmoid_gate * (1.0 + gate_pre * (1.0 - sigmoid_gate))
    ).astype(bf16)
    grad_up = (grad_active * gate_pre * sigmoid_gate).astype(bf16)
    grad_normed_part = times_transposed(grad_gate, gate_w) + times_transposed(grad_up, up_w)
    depth = w_query.shape[0]
    grad_normed_mlp, gate_quarter, up_quarter = reduce_grads(
        grad_normed_part.astype(bf16).reshape(8, rows, width),
        transposed_times(normed_mlp, grad_gate).astype(bf16).reshape(8, 2, depth, hidden_part),
        transposed_times(normed_mlp, grad_up).astype(bf16).reshape(8, 2, depth, hidden_part),
    )
    grad_down_w = transposed_times(active, cot_all).astype(bf16)
    grad_hidden_norm, gain_mlp_term = norm_backward(grad_normed_mlp, hidden, inv_mlp, gain_mlp)
    grad_hidden = cotangent.astype(f32) + grad_hidden_norm

    grad_branch, down_grad = gather_grads(
        grad_hidden.astype(bf16), grad_down_w.reshape(2, 2, w_down.shape[0], width)
    )
    grad_branch = grad_branch.reshape(token_rows, width)
    grad_out_w = transposed_times(attended_low, grad_branch)
    grad_attended = times_transposed(grad_branch, out_w).astype(bf16)
    delta = jnp.sum(grad_attended.astype(f32) * attended, axis=-1)
    keys_turned = jnp.swapaxes(keys_values[..., :HD].reshape(8, 4 * rows, HD), 1, 2)
    side, grad_query_rot, gate_grad, up_grad = attend_back(
        scaled_query,
        grad_attended,
        keys_values,
        keys_turned,
        log_total.reshape(LINE, 1, token_rows // LINE),
        delta.reshape(LINE, 1, token_rows // LINE),
        ids_mine.reshape(LINE, 1, token_rows // LINE),
        key_ids.reshape(8, 4 * rows, 1),
        gate_quarter,
        up_quarter,
    )
    side = side.reshape(token_rows, HD)
    grad_query_rot = jnp.swapaxes(grad_query_rot, 1, 2).reshape(token_rows, HD) * score_scale
    is_key = z % 2 == 0
    side_grad = jnp.where(is_key, rotate(side, cos_table, -sine_table), side).astype(bf16)
    grad_query = rotate(grad_query_rot, cos_table, -sine_table).astype(bf16)
    side_w = jnp.where(is_key, qkv_w[:, HD : 2 * HD], qkv_w[:, 2 * HD :])
    grad_normed_part = times_transposed(grad_query, qkv_w[:, :HD]) + times_transposed(
        side_grad, side_w
    )
    grad_normed, query_grad, key_grad, value_grad, out_grad = reduce_heads(
        grad_normed_part.astype(bf16).reshape(8, rows, width),
        transposed_times(normed, grad_query).astype(bf16).reshape(8, 2, depth, HD),
        transposed_times(normed, side_grad).astype(bf16).reshape(8, 2, depth, HD),
        grad_out_w.astype(bf16).reshape(2, 2, w_out.shape[0], width),
    )
    grad_inputs_norm, gain_attn_term = norm_backward(grad_normed, inputs, inv_attn, gain_attn)
    tokens_grad = (grad_hidden + grad_inputs_norm).astype(bf16)

    gains = jnp.concatenate(
        [
            gain_attn_term.reshape(16, 1, rows),
            gain_mlp_term.reshape(16, 1, rows),
            jnp.zeros((16, 6, rows), f32),
        ],
        axis=1,
    )
    gain_grads = reduce_gains(gains)
    return (
        output,
        tokens_grad,
        gain_grads[0],
        query_grad.astype(f32),
        key_grad.astype(f32),
        value_grad.astype(f32),
        out_grad.astype(f32),
        gain_grads[1],
        gate_grad.astype(f32),
        up_grad.astype(f32),
        down_grad,
    )


def solution(mesh):
    placed = (
        P(("blk", "head"), None),
        P("blk"),
        P("blk", "head"),
        P("blk", "head"),
        P("blk", "head"),
        P(("head", "blk"), None),
        P("blk"),
        P("blk", "head"),
        P("blk", "head"),
        P(("head", "blk"), None),
        P("blk"),
        P("blk"),
        P(("blk", "head"), None),
    )
    fits = mesh.shape["blk"] == 16 and mesh.shape["head"] == 2
    return jax.shard_map(
        fast_body if fits else body,
        mesh=mesh,
        in_specs=placed,
        out_specs=(
            P(("blk", "head"), None),
            P(("blk", "head"), None),
            P("blk"),
            P("blk", "head"),
            P("blk", "head"),
            P("blk", "head"),
            P(("head", "blk"), None),
            P("blk"),
            P("blk", "head"),
            P("blk", "head"),
            P(("head", "blk"), None),
        ),
        check_vma=False,
    )
```

```python
import jax
import jax.numpy as jnp
from jax import lax
from jax.experimental import pallas as pl
from jax.experimental.pallas import tpu as pltpu
from jax.sharding import PartitionSpec as P

HD = 256


eps_norm = 1e-06
rope_base = 1000042.0


def rms_scale(rows):
    return lax.rsqrt(jnp.mean(rows * rows, axis=-1, keepdims=True) + eps_norm)


def rope_tables(positions):
    inv_freqs = rope_base ** (-2.0 * jnp.arange(HD // 2, dtype=jnp.float32) / HD)
    angles = positions.astype(jnp.float32)[:, None] * inv_freqs[None, :]
    return (jnp.cos(angles)[:, None, :], jnp.sin(angles)[:, None, :])


def rotate(heads, cos_table, sine_table):
    half_size = heads.shape[-1] // 2
    lower_half = heads[..., :half_size]
    upper_half = heads[..., half_size:]
    return jnp.concatenate(
        [
            lower_half * cos_table - upper_half * sine_table,
            upper_half * cos_table + lower_half * sine_table,
        ],
        axis=-1,
    )


def product(left, right):
    return jnp.dot(left, right, preferred_element_type=jnp.float32)


def times_transposed(left, right):
    return lax.dot_general(
        left, right, (((1,), (1,)), ((), ())), preferred_element_type=jnp.float32
    )


def transposed_times(left, right):
    return lax.dot_general(
        left, right, (((0,), (0,)), ((), ())), preferred_element_type=jnp.float32
    )


def norm_backward(grad_normed, inputs, inv_scale, gain_rows):
    unit_rows = inputs * inv_scale
    grad_unit = grad_normed * gain_rows
    gain_term = jnp.sum(grad_normed * unit_rows, axis=0)
    grad_inputs = inv_scale * (
        grad_unit - unit_rows * jnp.mean(grad_unit * unit_rows, axis=-1, keepdims=True)
    )
    return (grad_inputs, gain_term)


def body(
    tokens,
    attn_gain,
    w_query,
    w_key,
    w_value,
    w_out,
    mlp_gain,
    w_gate,
    w_up,
    w_down,
    block_ids,
    positions,
    cotangent,
):
    rows_own = tokens.shape[0]
    head_rank = lax.axis_index("head")
    tokens_all, cot_all = (
        lax.all_gather(tokens, "head", axis=0, tiled=True),
        lax.all_gather(cotangent, "head", axis=0, tiled=True),
    )
    rows_all = tokens_all.shape[0]
    gain_attn, query_w, key_w, value_w, out_w = (
        lax.all_gather(attn_gain, "blk", axis=0, tiled=True),
        lax.all_gather(w_query, "blk", axis=0, tiled=True),
        lax.all_gather(w_key, "blk", axis=0, tiled=True),
        lax.all_gather(w_value, "blk", axis=0, tiled=True),
        lax.all_gather(w_out, "blk", axis=0, tiled=True),
    )
    gain_mlp, gate_w, up_w, down_w = (
        lax.all_gather(mlp_gain, "blk", axis=0, tiled=True),
        lax.all_gather(w_gate, "blk", axis=0, tiled=True),
        lax.all_gather(w_up, "blk", axis=0, tiled=True),
        lax.all_gather(w_down, "blk", axis=0, tiled=True),
    )
    key_ids = lax.all_gather(block_ids, "blk", axis=0, tiled=True)
    heads_local = query_w.shape[1] // HD
    kv_local = key_w.shape[1] // HD
    kv_width = kv_local * HD
    group_size = heads_local // kv_local
    cos_table, sine_table = rope_tables(positions)
    score_scale = HD ** (-0.5)
    seq_len = key_ids.shape[0]
    key_block = min(2048, seq_len)
    block_total = seq_len // key_block
    block_steps = jnp.arange(block_total)
    top_query = jnp.max(block_ids)
    inputs = tokens_all.astype(jnp.float32)
    inv_attn = rms_scale(inputs)
    normed = (inputs * inv_attn * gain_attn.astype(jnp.float32)).astype(jnp.bfloat16)
    queries = rotate(
        product(normed, query_w).reshape(rows_all, heads_local, HD), cos_table, sine_table
    ).astype(jnp.bfloat16)
    keys_own = rotate(product(normed, key_w).reshape(rows_all, kv_local, HD), cos_table, sine_table)
    keys_own = keys_own.astype(jnp.bfloat16).reshape(rows_all, kv_width)
    values_own = product(normed, value_w).astype(jnp.bfloat16)
    keys_all, values_all = (
        lax.all_gather(keys_own, "blk", axis=0, tiled=True),
        lax.all_gather(values_own, "blk", axis=0, tiled=True),
    )
    grouped = queries.reshape(rows_all, kv_local, group_size, HD)

    def slice_keys(key_start, count):
        key_rows = lax.dynamic_slice_in_dim(keys_all, key_start, count, 0).reshape(
            count, kv_local, HD
        )
        value_rows = lax.dynamic_slice_in_dim(values_all, key_start, count, 0).reshape(
            count, kv_local, HD
        )
        block_keys = lax.dynamic_slice_in_dim(key_ids, key_start, count, 0)
        return (key_rows, value_rows, block_keys)

    def scores_for(key_rows, block_keys):
        scores = (
            jnp.einsum("qkgd,ckd->kgqc", grouped, key_rows, preferred_element_type=jnp.float32)
            * score_scale
        )
        visible = (block_keys[None, :] <= block_ids[:, None])[None, None]
        return (scores, visible)

    def max_sum(state_pair, step_index):
        key_start = step_index * key_block

        def max_live(pair):
            run_max, run_sum = pair
            key_rows, value_rows, block_keys = slice_keys(key_start, key_block)
            scores, visible = scores_for(key_rows, block_keys)
            scores = jnp.where(visible, scores, -1e30)
            new_max = jnp.maximum(run_max, jnp.max(scores, axis=-1))
            kept_terms = jnp.where(visible, jnp.exp(scores - new_max[..., None]), 0.0)
            return (new_max, run_sum * jnp.exp(run_max - new_max) + jnp.sum(kept_terms, axis=-1))

        def max_skipped(pair):
            return pair

        return (lax.cond(key_ids[key_start] <= top_query, max_live, max_skipped, state_pair), None)

    start_max = jnp.full((kv_local, group_size, rows_all), -1e30, jnp.float32)
    start_sum = jnp.zeros((kv_local, group_size, rows_all), jnp.float32)
    (run_max, run_sum), unused_max = lax.scan(max_sum, (start_max, start_sum), block_steps)
    log_total = run_max + jnp.log(run_sum)

    def weighted(accum_rows, step_index):
        key_start = step_index * key_block

        def weighted_live(accum):
            key_rows, value_rows, block_keys = slice_keys(key_start, key_block)
            scores, visible = scores_for(key_rows, block_keys)
            probabilities = jnp.where(visible, jnp.exp(scores - log_total[..., None]), 0.0).astype(
                jnp.bfloat16
            )
            return accum + jnp.einsum(
                "kgqc,ckd->qkgd", probabilities, value_rows, preferred_element_type=jnp.float32
            )

        def weighted_skipped(accum):
            return accum

        return (
            lax.cond(key_ids[key_start] <= top_query, weighted_live, weighted_skipped, accum_rows),
            None,
        )

    attended, unused_rows = lax.scan(
        weighted, jnp.zeros((rows_all, kv_local, group_size, HD), jnp.float32), block_steps
    )
    attended_low = attended.reshape(rows_all, heads_local * HD).astype(jnp.bfloat16)
    branch_sum = lax.psum(product(attended_low, out_w).astype(jnp.bfloat16), "head").astype(
        jnp.float32
    )
    hidden = inputs + branch_sum
    inv_mlp = rms_scale(hidden)
    normed_mlp = (hidden * inv_mlp * gain_mlp.astype(jnp.float32)).astype(jnp.bfloat16)
    gate_pre = product(normed_mlp, gate_w)
    up_pre = product(normed_mlp, up_w)
    sigmoid_gate = jax.nn.sigmoid(gate_pre)
    active = (gate_pre * sigmoid_gate * up_pre).astype(jnp.bfloat16)
    mlp_own = lax.psum_scatter(
        product(active, down_w).astype(jnp.bfloat16), "head", scatter_dimension=0, tiled=True
    ).astype(jnp.float32)
    hidden_own = lax.dynamic_slice_in_dim(hidden, head_rank * rows_own, rows_own, 0)
    output = (hidden_own + mlp_own).astype(jnp.bfloat16)
    gain_attn, query_w, key_w, value_w, out_w = (
        lax.all_gather(attn_gain, "blk", axis=0, tiled=True),
        lax.all_gather(w_query, "blk", axis=0, tiled=True),
        lax.all_gather(w_key, "blk", axis=0, tiled=True),
        lax.all_gather(w_value, "blk", axis=0, tiled=True),
        lax.all_gather(w_out, "blk", axis=0, tiled=True),
    )
    gain_mlp, gate_w, up_w, down_w = (
        lax.all_gather(mlp_gain, "blk", axis=0, tiled=True),
        lax.all_gather(w_gate, "blk", axis=0, tiled=True),
        lax.all_gather(w_up, "blk", axis=0, tiled=True),
        lax.all_gather(w_down, "blk", axis=0, tiled=True),
    )
    grad_active = times_transposed(cot_all, down_w)
    grad_gate = (
        grad_active * up_pre * sigmoid_gate * (1.0 + gate_pre * (1.0 - sigmoid_gate))
    ).astype(jnp.bfloat16)
    grad_up = (grad_active * gate_pre * sigmoid_gate).astype(jnp.bfloat16)
    grad_gate_w = transposed_times(normed_mlp, grad_gate)
    grad_up_w = transposed_times(normed_mlp, grad_up)
    grad_down_w = transposed_times(active, cot_all)
    grad_normed_part = times_transposed(grad_gate, gate_w) + times_transposed(grad_up, up_w)
    grad_normed_mlp = lax.psum(grad_normed_part.astype(jnp.bfloat16), "head").astype(jnp.float32)
    grad_hidden_norm, gain_mlp_term = norm_backward(
        grad_normed_mlp, hidden, inv_mlp, gain_mlp.astype(jnp.float32)
    )
    grad_hidden = cot_all.astype(jnp.float32) + grad_hidden_norm
    mlp_results = (
        lax.psum_scatter(gain_mlp_term, "blk", scatter_dimension=0, tiled=True),
        lax.psum_scatter(grad_gate_w, "blk", scatter_dimension=0, tiled=True),
        lax.psum_scatter(grad_up_w, "blk", scatter_dimension=0, tiled=True),
        lax.psum_scatter(grad_down_w, "blk", scatter_dimension=0, tiled=True),
    )
    grad_branch = grad_hidden.astype(jnp.bfloat16)
    grad_out_w = transposed_times(attended_low, grad_branch)
    grad_attended = times_transposed(grad_branch, out_w).astype(jnp.bfloat16)
    grad_grouped = grad_attended.reshape(rows_all, kv_local, group_size, HD)
    delta_rows = jnp.transpose(
        jnp.sum(grad_grouped.astype(jnp.float32) * attended, axis=-1), (1, 2, 0)
    )

    def pair_backward(key_rows, value_rows, block_keys):
        count = key_rows.shape[0]
        scores, visible = scores_for(key_rows, block_keys)
        probabilities = jnp.where(visible, jnp.exp(scores - log_total[..., None]), 0.0)
        grad_probs = jnp.einsum(
            "qkgd,ckd->kgqc", grad_grouped, value_rows, preferred_element_type=jnp.float32
        )
        grad_scores = (probabilities * (grad_probs - delta_rows[..., None])).astype(jnp.bfloat16)
        query_terms = jnp.einsum(
            "kgqc,ckd->qkgd", grad_scores, key_rows, preferred_element_type=jnp.float32
        )
        key_terms = (
            jnp.einsum("kgqc,qkgd->ckd", grad_scores, grouped, preferred_element_type=jnp.float32)
            * score_scale
        )
        value_terms = jnp.einsum(
            "kgqc,qkgd->ckd",
            probabilities.astype(jnp.bfloat16),
            grad_grouped,
            preferred_element_type=jnp.float32,
        )
        return (
            query_terms,
            key_terms.reshape(count, kv_width),
            value_terms.reshape(count, kv_width),
        )

    query_zeros = jnp.zeros((rows_all, kv_local, group_size, HD), jnp.float32)

    def backward_block(accum_rows, step_index):
        key_start = step_index * key_block

        def backward_live(unused_arg):
            key_rows, value_rows, block_keys = slice_keys(key_start, key_block)
            return pair_backward(key_rows, value_rows, block_keys)

        def backward_skipped(unused_arg):
            empty_terms = jnp.zeros((key_block, kv_width), jnp.float32)
            return (query_zeros, empty_terms, empty_terms)

        query_terms, key_terms, value_terms = lax.cond(
            key_ids[key_start] <= top_query, backward_live, backward_skipped, 0
        )
        return (accum_rows + query_terms, (key_terms, value_terms))

    grad_query_rot, (key_terms, value_terms) = lax.scan(backward_block, query_zeros, block_steps)
    key_terms = key_terms.reshape(seq_len, kv_width)
    value_terms = value_terms.reshape(seq_len, kv_width)
    key_grad_own, value_grad_own = (
        lax.psum_scatter(key_terms, "blk", scatter_dimension=0, tiled=True),
        lax.psum_scatter(value_terms, "blk", scatter_dimension=0, tiled=True),
    )
    grad_query_rot = grad_query_rot * score_scale
    grad_key = rotate(key_grad_own.reshape(rows_all, kv_local, HD), cos_table, -sine_table)
    grad_key = grad_key.reshape(rows_all, kv_width).astype(jnp.bfloat16)
    grad_value = value_grad_own.astype(jnp.bfloat16)
    grad_query = rotate(grad_query_rot.reshape(rows_all, heads_local, HD), cos_table, -sine_table)
    grad_query = grad_query.reshape(rows_all, heads_local * HD).astype(jnp.bfloat16)
    grad_query_w = transposed_times(normed, grad_query)
    grad_key_w = transposed_times(normed, grad_key)
    grad_value_w = transposed_times(normed, grad_value)
    grad_normed_part = (
        times_transposed(grad_query, query_w)
        + times_transposed(grad_key, key_w)
        + times_transposed(grad_value, value_w)
    )
    grad_normed = lax.psum(grad_normed_part.astype(jnp.bfloat16), "head").astype(jnp.float32)
    grad_inputs_norm, gain_attn_term = norm_backward(
        grad_normed, inputs, inv_attn, gain_attn.astype(jnp.float32)
    )
    grad_inputs = grad_hidden + grad_inputs_norm
    grad_own = lax.dynamic_slice_in_dim(grad_inputs, head_rank * rows_own, rows_own, 0).astype(
        jnp.bfloat16
    )
    attn_results = (
        lax.psum_scatter(gain_attn_term, "blk", scatter_dimension=0, tiled=True),
        lax.psum_scatter(grad_query_w, "blk", scatter_dimension=0, tiled=True),
        lax.psum_scatter(grad_key_w, "blk", scatter_dimension=0, tiled=True),
        lax.psum_scatter(grad_value_w, "blk", scatter_dimension=0, tiled=True),
        lax.psum_scatter(grad_out_w, "blk", scatter_dimension=0, tiled=True),
    )
    return (
        output,
        grad_own,
        attn_results[0],
        attn_results[1],
        attn_results[2],
        attn_results[3],
        attn_results[4],
        mlp_results[0],
        mlp_results[1],
        mlp_results[2],
        mlp_results[3],
    )


MESH = pl.DeviceIdType.MESH
LINE = 4
VMEM_BYTES = 60 * 2**20


def place():
    blk, head = lax.axis_index("blk"), lax.axis_index("head")
    return blk // 4, (blk // 2) % 2, blk % 2, head


def device(z, y, c, h):
    return (z * 4 + y * 2 + c, h)


def remote(src, dst, send_sem, recv_sem, target):
    return pltpu.make_async_remote_copy(
        src_ref=src,
        dst_ref=dst,
        send_sem=send_sem,
        recv_sem=recv_sem,
        device_id=target,
        device_id_type=MESH,
    )


def greet(target):
    pl.semaphore_signal(
        pltpu.get_barrier_semaphore(), inc=1, device_id=target, device_id_type=MESH
    )


def greet_all(blk_total, head_total):
    blk, head = lax.axis_index("blk"), lax.axis_index("head")
    for other in range(blk_total):
        for half in range(head_total):

            @pl.when(jnp.logical_or(blk != other, head != half))
            def _():
                greet((jnp.int32(other), jnp.int32(half)))

    pl.semaphore_wait(pltpu.get_barrier_semaphore(), blk_total * head_total - 1)


def greet_plane(more=0):
    z, y, c, h = place()

    @pl.when(z > 0)
    def _():
        greet(device(z - 1, y, c, h))

    @pl.when(z < LINE - 1)
    def _():
        greet(device(z + 1, y, c, h))

    greet(device(z, 1 - y, c, h))
    pl.semaphore_wait(
        pltpu.get_barrier_semaphore(),
        1 + more + (z + LINE - 1) // LINE + (LINE - 1 - z + LINE - 1) // LINE,
    )


class Gather:
    CUTS = ((0, 64), (64, 48), (112, 16), (112, 16))
    SEMS = [(3, 4)] * 4 + [(4, 2)] * 2 + [(2,)]

    @staticmethod
    def scratch():
        return [pltpu.SemaphoreType.DMA(shape) for shape in Gather.SEMS] + [
            pltpu.SemaphoreType.DMA
        ]

    def __init__(self, src, out, sems):
        self.src, self.out = src, out
        (self.up_s, self.up_r, self.dn_s, self.dn_r, self.y_s, self.y_r, self.b_sr, self.own_sem) = sems
        self.z, self.y, self.c, self.h = place()

    def piece(self, line, elem):
        y = 1 - self.y if elem == 3 else self.y
        start, size = self.CUTS[elem]
        return self.out.at[line * 2 + y, pl.ds(start, size)]

    def first(self, elem):
        if elem == 3:
            return self.piece(self.z, 3)
        start, size = self.CUTS[elem]
        return self.src.at[pl.ds(start, size)]

    def up(self, step, elem):
        src = self.first(elem) if step == 0 else self.piece(self.z - step, elem)
        return remote(
            src, self.piece(self.z - step, elem), self.up_s.at[step, elem], self.up_r.at[step, elem],
            device(self.z + 1, self.y, self.c, self.h),
        )

    def down(self, step, elem):
        src = self.first(elem) if step == 0 else self.piece(self.z + step, elem)
        return remote(
            src, self.piece(self.z + step, elem), self.dn_s.at[step, elem], self.dn_r.at[step, elem],
            device(self.z - 1, self.y, self.c, self.h),
        )

    def up_in(self, step, elem):
        ref = self.piece(self.z - 1 - step, elem)
        return remote(ref, ref, self.up_s.at[step, elem], self.up_r.at[step, elem], device(self.z, self.y, self.c, self.h))

    def down_in(self, step, elem):
        ref = self.piece(self.z + 1 + step, elem)
        return remote(ref, ref, self.dn_s.at[step, elem], self.dn_r.at[step, elem], device(self.z, self.y, self.c, self.h))

    def across(self, line, elem, own=False):
        src = self.first(elem) if own else self.piece(line, elem)
        return remote(
            src, self.piece(line, elem), self.y_s.at[line, elem], self.y_r.at[line, elem],
            device(self.z, 1 - self.y, self.c, self.h),
        )

    def across_in(self, line, elem):
        start, size = self.CUTS[elem]
        ref = self.out.at[line * 2 + 1 - self.y, pl.ds(start, size)]
        return remote(ref, ref, self.y_s.at[line, elem], self.y_r.at[line, elem], device(self.z, self.y, self.c, self.h))

    def across_b(self):
        return remote(
            self.first(2), self.piece(self.z, 2), self.b_sr.at[0], self.b_sr.at[1],
            device(self.z, 1 - self.y, self.c, self.h),
        )

    def across_b_in(self):
        ref = self.piece(self.z, 3)
        return remote(ref, ref, self.b_sr.at[0], self.b_sr.at[1], device(self.z, self.y, self.c, self.h))

    def own_copy(self):
        return pltpu.make_async_copy(self.src, self.out.at[self.z * 2 + self.y], self.own_sem)

    def start(self):
        self.own_copy().start()
        self.across_b().start()
        for elem in (0, 1, 2):

            @pl.when(self.z < LINE - 1)
            def _():
                self.up(0, elem).start()

            @pl.when(self.z > 0)
            def _():
                self.down(0, elem).start()

            if elem < 2:
                self.across(self.z, elem, own=True).start()

    def relay_b(self):
        self.across_b_in().wait_recv()

        @pl.when(self.z < LINE - 1)
        def _():
            self.up(0, 3).start()

        @pl.when(self.z > 0)
        def _():
            self.down(0, 3).start()

    def relay(self, step, elem):
        @pl.when(self.z - 1 - step >= 0)
        def _():
            self.up_in(step, elem).wait_recv()
            if step < LINE - 2:

                @pl.when(self.z < LINE - 1)
                def _():
                    self.up(step + 1, elem).start()

            if elem < 2:
                self.across(self.z - 1 - step, elem).start()

        @pl.when(self.z + 1 + step <= LINE - 1)
        def _():
            self.down_in(step, elem).wait_recv()
            if step < LINE - 2:

                @pl.when(self.z > 0)
                def _():
                    self.down(step + 1, elem).start()

            if elem < 2:
                self.across(self.z + 1 + step, elem).start()

    def relays(self):
        self.relay_b()
        for step in range(LINE - 1):
            for elem in (0, 1, 2, 3):
                self.relay(step, elem)

    def finish(self):
        for line in range(LINE):
            for elem in (0, 1):
                self.across_in(line, elem).wait_recv()
        for line in range(LINE):
            for elem in (0, 1):
                self.across(line, elem).wait_send()
        self.finish_sends()
        self.own_copy().wait()

    def finish_sends(self):
        self.across_b().wait_send()
        for step in range(LINE - 1):
            for elem in range(4):

                @pl.when(jnp.logical_and(self.z < LINE - 1, self.z - step >= 0))
                def _():
                    self.up(step, elem).wait_send()

                @pl.when(jnp.logical_and(self.z > 0, self.z + step <= LINE - 1))
                def _():
                    self.down(step, elem).wait_send()


def gather_kernel(src, out, *sems):
    greet_plane()
    gather = Gather(src, out, sems)
    gather.start()
    gather.relays()
    gather.finish()


ANY = pl.BlockSpec(memory_space=pl.ANY)
INSIDE = pl.BlockSpec(memory_space=pltpu.VMEM)


def kernel_params(collective_id):
    return pltpu.CompilerParams(
        collective_id=collective_id, has_side_effects=True, vmem_limit_bytes=VMEM_BYTES
    )


def gather_plane(rows):
    return pl.pallas_call(
        gather_kernel,
        out_shape=jax.ShapeDtypeStruct((2 * LINE,) + rows.shape, rows.dtype),
        in_specs=[INSIDE],
        out_specs=ANY,
        scratch_shapes=Gather.scratch(),
        compiler_params=kernel_params(1),
        name="gather_plane",
    )(rows)


class Reduce:
    CUTS = ((0, 64), (64, 64))

    @staticmethod
    def scratch(width):
        inbox = pltpu.VMEM((LINE, 128, width), jnp.bfloat16)
        return [inbox] * 3 + [pltpu.SemaphoreType.DMA((LINE, 2))] * 6

    def __init__(self, parts, refs):
        self.parts = parts
        self.y_in, self.up_in, self.dn_in = refs[:3]
        self.y_s, self.y_r, self.up_s, self.up_r, self.dn_s, self.dn_r = refs[3:]
        self.z, self.y, self.c, self.h = place()
        z = self.z
        self.order = (3 - 3 * (z // 2), (2 + 3 * z) % 5, 1 + z % 2, z)

    def rows(self, cut):
        return pl.ds(*self.CUTS[cut])

    def across(self, line, cut):
        return remote(
            self.parts.at[line * 2 + 1 - self.y, self.rows(cut)], self.y_in.at[line, self.rows(cut)],
            self.y_s.at[line, cut], self.y_r.at[line, cut], device(self.z, 1 - self.y, self.c, self.h),
        )

    def up(self, line, cut):
        return remote(
            self.parts.at[line * 2 + self.y, self.rows(cut)], self.up_in.at[line, self.rows(cut)],
            self.up_s.at[line, cut], self.up_r.at[line, cut], device(self.z + 1, self.y, self.c, self.h),
        )

    def down(self, line, cut):
        return remote(
            self.parts.at[line * 2 + self.y, self.rows(cut)], self.dn_in.at[line, self.rows(cut)],
            self.dn_s.at[line, cut], self.dn_r.at[line, cut], device(self.z - 1, self.y, self.c, self.h),
        )

    def start(self, place_at):
        for cut in range(2):
            self.across(self.order[place_at], cut).start()

    def own(self, line, cut):
        return self.parts.at[line * 2 + self.y, self.rows(cut)]

    def relay(self, place_at):
        line = self.order[place_at]
        for cut in range(2):
            rows = self.rows(cut)
            self.across(line, cut).wait_recv()
            target = self.parts.at[line * 2 + self.y]

            @pl.when(line > self.z)
            def _():
                @pl.when(self.z > 0)
                def _():
                    self.up(line, cut).wait_recv()
                    total = (
                        target[rows].astype(jnp.float32)
                        + self.y_in[line, rows].astype(jnp.float32)
                        + self.up_in[line, rows].astype(jnp.float32)
                    )
                    target[rows] = total.astype(jnp.bfloat16)

                @pl.when(self.z == 0)
                def _():
                    total = target[rows].astype(jnp.float32) + self.y_in[line, rows].astype(jnp.float32)
                    target[rows] = total.astype(jnp.bfloat16)

                self.up(line, cut).start()

            @pl.when(line < self.z)
            def _():
                @pl.when(self.z < LINE - 1)
                def _():
                    self.down(line, cut).wait_recv()
                    total = (
                        target[rows].astype(jnp.float32)
                        + self.y_in[line, rows].astype(jnp.float32)
                        + self.dn_in[line, rows].astype(jnp.float32)
                    )
                    target[rows] = total.astype(jnp.bfloat16)

                @pl.when(self.z == LINE - 1)
                def _():
                    total = target[rows].astype(jnp.float32) + self.y_in[line, rows].astype(jnp.float32)
                    target[rows] = total.astype(jnp.bfloat16)

                self.down(line, cut).start()

    def total(self, out):
        line = self.z
        for cut in range(2):
            rows = self.rows(cut)
            self.across(line, cut).wait_recv()
            out[rows] = self.parts[line * 2 + self.y, rows].astype(jnp.float32) + self.y_in[line, rows].astype(jnp.float32)
        for cut in range(2):
            rows = self.rows(cut)

            @pl.when(self.z > 0)
            def _():
                self.up(line, cut).wait_recv()
                out[rows] += self.up_in[line, rows].astype(jnp.float32)

            @pl.when(self.z < LINE - 1)
            def _():
                self.down(line, cut).wait_recv()
                out[rows] += self.dn_in[line, rows].astype(jnp.float32)

    def finish(self):
        for line in range(LINE):
            for cut in range(2):
                self.across(line, cut).wait_send()

                @pl.when(self.z < line)
                def _():
                    self.up(line, cut).wait_send()

                @pl.when(self.z > line)
                def _():
                    self.down(line, cut).wait_send()


def reduce_kernel(parts_in, out, parts, in_sem, *refs):
    load = pltpu.make_async_copy(parts_in, parts, in_sem)
    load.start()
    greet_plane()
    reduce = Reduce(parts, refs)
    load.wait()
    for place_at in range(4):
        reduce.start(place_at)
    for place_at in range(3):
        reduce.relay(place_at)
    reduce.total(out)
    reduce.finish()


def reduce_plane(parts):
    shape = parts.shape
    return pl.pallas_call(
        reduce_kernel,
        out_shape=jax.ShapeDtypeStruct(shape[1:], jnp.float32),
        in_specs=[ANY],
        out_specs=INSIDE,
        scratch_shapes=[pltpu.VMEM(shape, jnp.bfloat16), pltpu.SemaphoreType.DMA] + Reduce.scratch(shape[2]),
        compiler_params=kernel_params(2),
        name="reduce_plane",
    )(parts)


def dma(*shape):
    return pltpu.SemaphoreType.DMA(shape) if shape else pltpu.SemaphoreType.DMA


def local(src, dst, sem):
    return pltpu.make_async_copy(src, dst, sem)


class AttnSpread:
    @staticmethod
    def scratch():
        return [dma(3, 4), dma(3, 4), dma(3, 8), dma(3), dma(4), dma(4), dma(4), dma(4), dma(4), dma(4)]

    def __init__(self, weights, outs, sems):
        self.weights, (self.qkv, self.out_w) = weights, outs
        (self.s, self.f_s, self.r, self.own, self.x_s, self.x_r, self.c_s, self.c_r, self.o_s, self.o_r) = sems
        self.z, self.y, self.c, self.h = place()
        self.chip = self.z * 2 + self.y
        self.me = device(self.z, self.y, self.c, self.h)
        self.owner = self.h == self.y

    def source(self, kind, line):
        start = line * HD if kind == 0 else (line // 2) * HD
        return self.weights[kind].at[:, pl.ds(pl.multiple_of(start, HD), HD)]

    def slot(self, kind, chip):
        return self.qkv.at[chip, self.c, :, pl.ds(kind * HD, HD)]

    def push(self, kind, step):
        line = (self.z + step) % LINE
        return remote(
            self.source(kind, line), self.slot(kind, self.chip), self.s.at[kind, step], self.r.at[kind, self.chip],
            device(line, self.h, self.c, self.h),
        )

    def push_far(self, kind, step):
        line = (self.z + step) % LINE
        return remote(
            self.source(kind, line), self.slot(kind, self.chip), self.f_s.at[kind, step], self.r.at[kind, self.chip],
            device(line, self.h, self.c, 1 - self.h),
        )

    def keep(self, kind):
        return local(self.source(kind, self.z), self.slot(kind, self.chip), self.own.at[kind])

    def pull(self, kind, chip):
        ref = self.slot(kind, chip)
        return remote(ref, ref, self.s.at[kind, 0], self.r.at[kind, chip], self.me)

    def near(self, step):
        return ((self.z + LINE - step) % LINE) * 2 + self.y

    def far(self, step):
        return ((self.z + LINE - step) % LINE) * 2 + 1 - self.y

    def over(self, step):
        ref = self.qkv.at[self.near(step), self.c]
        return remote(ref, ref, self.x_s.at[step], self.x_r.at[step], device(self.z, self.y, self.c, 1 - self.h))

    def share(self, line, core):
        ref = self.qkv.at[pl.ds(line * 2, 2), core]
        return remote(ref, ref, self.c_s.at[line], self.c_r.at[line], device(self.z, self.y, 1 - self.c, self.h))

    def out_push(self):
        return remote(
            self.weights[3], self.out_w.at[self.y, self.c], self.o_s.at[0], self.o_r.at[0],
            device(self.z, 1 - self.y, self.c, self.h),
        )

    def out_keep(self):
        return local(self.weights[3], self.out_w.at[self.y, self.c], self.o_s.at[1])

    def out_pull(self):
        ref = self.out_w.at[1 - self.y, self.c]
        return remote(ref, ref, self.o_s.at[0], self.o_r.at[0], self.me)

    def out_over(self):
        ref = self.out_w.at[:, self.c]
        return remote(ref, ref, self.o_s.at[2], self.o_r.at[2], device(self.z, self.y, self.c, 1 - self.h))

    def out_share(self, core):
        ref = self.out_w.at[:, core]
        return remote(ref, ref, self.o_s.at[3], self.o_r.at[3], device(self.z, self.y, 1 - self.c, self.h))

    def start(self):
        for kind in range(3):

            @pl.when(self.owner)
            def _():
                self.keep(kind).start()

            @pl.when(jnp.logical_not(self.owner))
            def _():
                self.push(kind, 0).start()
                self.push_far(kind, 0).start()

        for step in range(1, LINE):
            for kind in range(3):
                self.push(kind, step).start()

            @pl.when(jnp.logical_not(self.owner))
            def _():
                for kind in range(3):
                    self.push_far(kind, step).start()

        @pl.when(self.owner)
        def _():
            self.out_keep().start()

        @pl.when(jnp.logical_not(self.owner))
        def _():
            self.out_push().start()

    def relay(self, step):
        @pl.when(self.owner)
        def _():
            for kind in range(3):
                if step:
                    self.pull(kind, self.near(step)).wait_recv()
                else:
                    self.keep(kind).wait()
            self.over(step).start()

    def relay_out(self):
        @pl.when(self.owner)
        def _():
            self.out_keep().wait()
            self.out_pull().wait_recv()
            self.out_over().start()

    def relay_share(self, step):
        @pl.when(jnp.logical_not(self.owner))
        def _():
            self.over(step).wait_recv()

        for kind in range(3):
            self.pull(kind, self.far(step)).wait_recv()
        self.share((self.z + LINE - step) % LINE, self.c).start()

    def relay_out_share(self):
        @pl.when(jnp.logical_not(self.owner))
        def _():
            self.out_over().wait_recv()

        self.out_share(self.c).start()

    def finish(self):
        for line in range(LINE):
            self.share(line, 1 - self.c).wait_recv()
            self.share(line, self.c).wait_send()
        self.out_share(1 - self.c).wait_recv()
        self.out_share(self.c).wait_send()
        for kind in range(3):
            for step in range(1, LINE):
                self.push(kind, step).wait_send()

        @pl.when(self.owner)
        def _():
            for step in range(LINE):
                self.over(step).wait_send()
            self.out_over().wait_send()

        @pl.when(jnp.logical_not(self.owner))
        def _():
            for kind in range(3):
                self.push(kind, 0).wait_send()
                for step in range(LINE):
                    self.push_far(kind, step).wait_send()
            self.out_push().wait_send()


class MlpSpread:
    @staticmethod
    def scratch():
        return [dma(2, 8), dma(2, 8), dma(2)]

    def __init__(self, weights, outs, sems):
        self.weights, self.outs = weights, outs
        self.s, self.r, self.own = sems
        self.z, self.y, self.c, self.h = place()
        self.chip = self.z * 2 + self.y
        self.part = weights[0].shape[1] // 8

    def columns(self, index):
        return pl.ds(pl.multiple_of(index * self.part, self.part), self.part)

    def push(self, kind, step):
        chip = (self.chip + step) % 8
        return remote(
            self.weights[kind].at[:, self.columns(chip)], self.outs[kind].at[self.chip], self.s.at[kind, step],
            self.r.at[kind, step], device(chip // 2, chip % 2, self.c, self.h),
        )

    def pull(self, kind, step):
        ref = self.outs[kind].at[(self.chip + 8 - step) % 8]
        return remote(ref, ref, self.s.at[kind, step], self.r.at[kind, step], device(self.z, self.y, self.c, self.h))

    def keep(self, kind):
        return local(self.weights[kind].at[:, self.columns(self.chip)], self.outs[kind].at[self.chip], self.own.at[kind])

    def start(self):
        for kind in range(2):
            self.keep(kind).start()
            for step in range(1, 8):
                self.push(kind, step).start()

    def finish(self):
        for kind in range(2):
            self.keep(kind).wait()
            for step in range(1, 8):
                self.pull(kind, step).wait_recv()
                self.push(kind, step).wait_send()


class MlpShare:
    @staticmethod
    def scratch():
        return [dma(2), dma(2, 2), dma(2, 2), dma(2, 2), dma(2, 2)]

    def __init__(self, quarters, outs, sems):
        self.quarters, self.outs = quarters, outs
        self.own, self.x_s, self.x_r, self.c_s, self.c_r = sems
        self.z, self.y, self.c, self.h = place()
        self.part = quarters[0].shape[2]

    def slot(self, kind, cut, half):
        columns = pl.ds(pl.multiple_of(half * self.part, self.part), self.part)
        return self.outs[kind].at[pl.ds(cut * 4, 4), self.c, :, columns]

    def keep(self, kind):
        columns = pl.ds(pl.multiple_of(self.h * self.part, self.part), self.part)
        return local(self.quarters[kind], self.outs[kind].at[:, self.c, :, columns], self.own.at[kind])

    def over(self, kind, cut, half):
        return remote(
            self.quarters[kind].at[pl.ds(cut * 4, 4)], self.slot(kind, cut, half), self.x_s.at[kind, cut],
            self.x_r.at[kind, cut], device(self.z, self.y, self.c, 1 - self.h),
        )

    def share(self, kind, cut, core):
        ref = self.outs[kind].at[pl.ds(cut * 4, 4), core]
        return remote(
            ref, ref, self.c_s.at[kind, cut], self.c_r.at[kind, cut], device(self.z, self.y, 1 - self.c, self.h)
        )

    def start(self):
        for kind in range(2):
            for cut in range(2):
                self.over(kind, cut, self.h).start()
            self.keep(kind).start()

    def relay(self):
        for kind in range(2):
            self.keep(kind).wait()
            for cut in range(2):
                self.over(kind, cut, 1 - self.h).wait_recv()
                self.share(kind, cut, self.c).start()

    def finish(self):
        for kind in range(2):
            for cut in range(2):
                self.share(kind, cut, 1 - self.c).wait_recv()
                self.share(kind, cut, self.c).wait_send()
                self.over(kind, cut, self.h).wait_send()


class DownSpread:
    @staticmethod
    def scratch():
        return [dma(1), dma(2), dma(2)]

    def __init__(self, weight, out, sems):
        self.weight, self.out = weight, out
        self.d_own, self.d_x, self.d_sib = sems
        self.z, self.y, self.c, self.h = place()

    def keep(self):
        return local(self.weight, self.out.at[self.h, self.c], self.d_own.at[0])

    def over(self):
        return remote(
            self.weight, self.out.at[self.h, self.c], self.d_x.at[0], self.d_x.at[1],
            device(self.z, self.y, self.c, 1 - self.h),
        )

    def over_in(self):
        ref = self.out.at[1 - self.h, self.c]
        return remote(ref, ref, self.d_x.at[0], self.d_x.at[1], device(self.z, self.y, self.c, self.h))

    def share(self):
        ref = self.out.at[:, self.c]
        return remote(ref, ref, self.d_sib.at[0], self.d_sib.at[1], device(self.z, self.y, 1 - self.c, self.h))

    def share_in(self):
        ref = self.out.at[:, 1 - self.c]
        return remote(ref, ref, self.d_sib.at[0], self.d_sib.at[1], device(self.z, self.y, self.c, self.h))

    def start(self):
        self.keep().start()
        self.over().start()

    def relay(self):
        self.keep().wait()
        self.over_in().wait_recv()
        self.share().start()

    def finish(self):
        self.share_in().wait_recv()
        self.share().wait_send()
        self.over().wait_send()


class NoteSpread:
    @staticmethod
    def scratch():
        return [dma(16), dma(16), dma(1)]

    def __init__(self, note, out, sems):
        self.note, self.out = note, out
        self.s, self.r, self.own = sems
        self.blk, self.h = lax.axis_index("blk"), lax.axis_index("head")

    def push(self, step):
        other = (self.blk + step) % 16
        return remote(self.note, self.out.at[self.blk], self.s.at[step], self.r.at[step], (other, self.h))

    def pull(self, step):
        ref = self.out.at[(self.blk + 16 - step) % 16]
        return remote(ref, ref, self.s.at[step], self.r.at[step], (self.blk, self.h))

    def keep(self):
        return local(self.note, self.out.at[self.blk], self.own.at[0])

    def start(self):
        self.keep().start()
        for step in range(1, 16):
            self.push(step).start()

    def finish(self):
        self.keep().wait()
        for step in range(1, 16):
            self.pull(step).wait_recv()
            self.push(step).wait_send()


def split_refs(refs, counts):
    groups, at = [], 0
    for count in counts:
        groups.append(refs[at : at + count])
        at += count
    return groups


def reduce_share_kernel(attended, out_w, gate_in, up_in, out, gate, up, parts, *refs):
    reduce_refs, share_sems = split_refs(refs, (9, 5))
    z, y, c, h = place()
    greet(device(z, y, 1 - c, h))
    greet(device(z, y, c, 1 - h))
    greet_plane(2)
    reduce = Reduce(parts, reduce_refs)
    share = MlpShare((gate_in, up_in), (gate, up), share_sems)
    rows, width = parts.shape[1:]
    share.start()
    for place_at in range(4):
        line = reduce.order[place_at]
        both = attended[pl.ds(pl.multiple_of(line * 2 * rows, 2 * rows), 2 * rows)]
        parts[pl.ds(line * 2, 2)] = product(both, out_w[...]).astype(jnp.bfloat16).reshape(2, rows, width)
        reduce.start(place_at)
    for place_at in range(3):
        reduce.relay(place_at)
    reduce.total(out)
    share.relay()
    reduce.finish()
    share.finish()


def reduce_share(attended, out_w, gate, up):
    eight, depth, part = gate.shape
    shape = (eight, attended.shape[0] // eight, out_w.shape[1])
    full = jax.ShapeDtypeStruct((eight, 2, depth, 2 * part), gate.dtype)
    return pl.pallas_call(
        reduce_share_kernel,
        out_shape=(jax.ShapeDtypeStruct(shape[1:], jnp.float32), full, full),
        in_specs=[INSIDE] * 4,
        out_specs=(INSIDE, ANY, ANY),
        scratch_shapes=[pltpu.VMEM(shape, jnp.bfloat16)] + Reduce.scratch(shape[2]) + MlpShare.scratch(),
        compiler_params=kernel_params(7),
        name="reduce_share",
    )(attended, out_w, gate, up)


def mlp_kernel(
    src, wd, gate_in, up_in, cot_in,
    mlp_out, normed_out, active, grad_gate, grad_up, grad_out,
    normed, gate_w, up_w, down_w, gate_pre, up_pre, cot, parts, load_s, out_s, *refs,
):
    gather_sems, down_sems, reduce_refs = split_refs(refs, (8, 3, 9))
    loads = [
        local(gate_in, gate_w, load_s.at[0]),
        local(up_in, up_w, load_s.at[1]),
        local(cot_in, cot, load_s.at[2]),
    ]
    for load in loads:
        load.start()
    z, y, c, h = place()
    greet(device(z, y, 1 - c, h))
    greet(device(z, y, c, 1 - h))
    greet_plane(2)
    gather = Gather(src, normed, gather_sems)
    downs = DownSpread(wd, down_w, down_sems)
    reduce = Reduce(parts, reduce_refs)
    gather.start()
    downs.start()
    rows, width = normed.shape[1:]
    hidden = gate_w.shape[1]
    step = hidden // 4
    pair = 2 * rows

    def forward(chip, own=False):
        shard = src if own else normed.at[chip]

        @pl.loop(0, 4)
        def _(tile):
            columns = pl.ds(pl.multiple_of(tile * step, step), step)
            gate_part = product(shard[...], gate_w[:, columns])
            up_part = product(shard[...], up_w[:, columns])
            gate_pre[chip, :, columns] = gate_part
            up_pre[chip, :, columns] = up_part
            active[chip, :, columns] = (gate_part * jax.nn.sigmoid(gate_part) * up_part).astype(jnp.bfloat16)

    def forward_own(distance):
        @pl.when(z - distance >= 0)
        def _():
            forward((z - distance) * 2 + y)

        @pl.when(z + distance <= LINE - 1)
        def _():
            forward((z + distance) * 2 + y)

    def forward_other(distance):
        def one(line):
            for elem in (0, 1):
                gather.across_in(line, elem).wait_recv()
            forward(line * 2 + 1 - y)

        if distance == 0:
            one(z)
        else:

            @pl.when(z - distance >= 0)
            def _():
                one(z - distance)

            @pl.when(z + distance <= LINE - 1)
            def _():
                one(z + distance)

    def relay(distance):
        for elem in (2, 0, 1, 3):
            gather.relay(distance - 1, elem)

    gather.relay_b()
    loads[0].wait()
    loads[1].wait()
    forward(z * 2 + y, own=True)
    relay(1)
    forward_other(0)
    forward_own(1)
    relay(2)
    forward_other(1)
    forward_own(2)
    relay(3)
    downs.relay()
    forward_other(2)
    forward_own(3)
    forward_other(3)
    gather.own_copy().wait()
    store = local(normed, normed_out, out_s)
    store.start()
    downs.finish()

    def contribute(line):
        both = pl.ds(line * 2, 2)

        @pl.loop(0, 4)
        def _(tile):
            columns = pl.ds(pl.multiple_of(tile * (width // 4), width // 4), width // 4)
            part = product(
                active[both].reshape(pair, hidden), down_w[:, :, :, columns].reshape(hidden, width // 4)
            )
            parts[both, :, columns] = part.astype(jnp.bfloat16).reshape(2, rows, width // 4)

    for place_at in range(4):
        contribute(reduce.order[place_at])
        reduce.start(place_at)
    loads[2].wait()

    def backward(line):
        both = pl.ds(line * 2, 2)

        @pl.loop(0, 4)
        def _(tile):
            columns = pl.ds(pl.multiple_of(tile * step, step), step)
            grad_active = times_transposed(cot[both].reshape(pair, width), down_w[tile // 2, tile % 2])
            gate_part = gate_pre[both, :, columns].reshape(pair, step)
            up_part = up_pre[both, :, columns].reshape(pair, step)
            sigmoid = jax.nn.sigmoid(gate_part)
            silu = gate_part * sigmoid
            gate_grad = grad_active * up_part * sigmoid * (1.0 + gate_part * (1.0 - sigmoid))
            grad_gate[both, :, columns] = gate_grad.astype(jnp.bfloat16).reshape(2, rows, step)
            grad_up[both, :, columns] = (grad_active * silu).astype(jnp.bfloat16).reshape(2, rows, step)

        @pl.loop(0, 4)
        def _(tile):
            columns = pl.ds(pl.multiple_of(tile * (width // 4), width // 4), width // 4)
            part = times_transposed(grad_gate[both].reshape(pair, hidden), gate_w[columns])
            part += times_transposed(grad_up[both].reshape(pair, hidden), up_w[columns])
            grad_out[both, :, columns] = part.astype(jnp.bfloat16).reshape(2, rows, width // 4)

    for place_at in range(3):
        backward(place_at)
        reduce.relay(place_at)
    backward(3)
    reduce.total(mlp_out)
    reduce.finish()
    store.wait()
    for line in range(LINE):
        for elem in (0, 1):
            gather.across(line, elem).wait_send()
    gather.finish_sends()


def run_mlp(src, wd, gate_w, up_w, cot):
    rows, width = src.shape
    hidden = gate_w.shape[1]

    def room(*dims, dtype=jnp.bfloat16):
        return pltpu.VMEM(dims, dtype)

    def shape(*dims, dtype=jnp.bfloat16):
        return jax.ShapeDtypeStruct(dims, dtype)

    return pl.pallas_call(
        mlp_kernel,
        out_shape=(
            shape(rows, width, dtype=jnp.float32),
            shape(8, rows, width),
            shape(8, rows, hidden),
            shape(8, rows, hidden),
            shape(8, rows, hidden),
            shape(8, rows, width),
        ),
        in_specs=[INSIDE, INSIDE, ANY, ANY, ANY],
        out_specs=(INSIDE, ANY, INSIDE, INSIDE, INSIDE, INSIDE),
        scratch_shapes=[
            room(8, rows, width), room(width, hidden), room(width, hidden), room(2, 2, *wd.shape),
            room(8, rows, hidden, dtype=jnp.float32), room(8, rows, hidden, dtype=jnp.float32),
            room(8, rows, width), room(8, rows, width), dma(3), dma(),
        ] + Gather.scratch() + DownSpread.scratch() + Reduce.scratch(width),
        compiler_params=kernel_params(8),
        name="run_mlp",
    )(src, wd, gate_w, up_w, cot)


def column_of(row):
    size = row.shape[1]
    same = lax.broadcasted_iota(jnp.int32, (size, size), 0) == lax.broadcasted_iota(jnp.int32, (size, size), 1)
    return jnp.sum(jnp.where(same, row, 0.0), axis=1, keepdims=True)


def row_of(column):
    size = column.shape[0]
    same = lax.broadcasted_iota(jnp.int32, (size, size), 0) == lax.broadcasted_iota(jnp.int32, (size, size), 1)
    return jnp.sum(jnp.where(same, column, 0.0), axis=0, keepdims=True)


def front_kernel(
    tokens, cot, note, inv_freqs, wq, wk, wv, wo, wg, wu,
    kv_out, normed_out, qkv_out, out_w, notes, cos_table, sine_table, query, attended_out, attended_low_out,
    log_out, cot_out, gate, up,
    gathered, normed, qkv_w, gain, query_ids, key_ids, kv, keys, scores, total,
    own, x_s, x_r, c_s, c_r, store_s, *sems,
):
    z, y, c, h = place()
    tok_sems, note_sems, attn_sems, cot_sems, mlp_sems = split_refs(sems, (8, 3, 10, 8, 3))
    greet_all(16, 2)
    rows, width = tokens.shape[0], HD
    pair = 2 * rows
    tok = Gather(tokens, gathered, tok_sems)
    notices = NoteSpread(note, notes, note_sems)
    attn = AttnSpread((wq, wk, wv, wo), (qkv_w, out_w), attn_sems)
    cots = Gather(cot, cot_out, cot_sems)
    mlp = MlpSpread((wg, wu), (gate, up), mlp_sems)

    def keep(cut):
        part = pl.ds(cut * 2, 2)
        return local(kv.at[part], keys.at[part, c, h], own.at[cut])

    def over(cut, half):
        part = pl.ds(cut * 2, 2)
        return remote(kv.at[part], keys.at[part, c, half], x_s.at[cut], x_r.at[cut], device(z, y, c, 1 - h))

    def share(cut, core):
        ref = keys.at[pl.ds(cut * 2, 2), core]
        return remote(ref, ref, c_s.at[cut], c_r.at[cut], device(z, y, 1 - c, h))

    def tables():
        for blk in range(16):
            gain[:, pl.ds(blk * rows, rows)] = notes[blk, 4:5, :]
        for chip in range(8):
            part = pl.ds(chip * rows, rows)
            mine = notes[2 * chip + c]
            angles = column_of(jnp.where(h == 0, mine[0:1], mine[1:2])) * inv_freqs[...]
            cos_table[part] = jnp.cos(angles)
            sine_table[part] = jnp.sin(angles)
            query_ids[part] = column_of(jnp.where(h == 0, mine[2:3], mine[3:4]))
            for piece in range(4):
                key_ids[chip, :, pl.ds(piece * rows, rows)] = notes[2 * chip + piece // 2, 2 + piece % 2 : 3 + piece % 2, :]

    def project(cut):
        part = pl.ds(cut * pair, pair)
        inputs = gathered[pl.ds(cut * 2, 2)].reshape(pair, tokens.shape[1]).astype(jnp.float32)
        rows_normed = (inputs * rms_scale(inputs) * gain[...]).astype(jnp.bfloat16)
        normed[part] = rows_normed
        cos_rows, sine_rows = cos_table[part], sine_table[part]

        def turn(lower, upper):
            return (
                (lower * cos_rows - upper * sine_rows).astype(jnp.bfloat16),
                (upper * cos_rows + lower * sine_rows).astype(jnp.bfloat16),
            )

        def weight(columns):
            return qkv_w[:, :, :, columns].reshape(tokens.shape[1], columns.size)

        half = width // 2
        projected = product(rows_normed, weight(pl.ds(0, width)))
        lower, upper = turn(projected[:, :half], projected[:, half:])
        query[part, :half] = (lower.astype(jnp.float32) * HD**-0.5).astype(jnp.bfloat16)
        query[part, half:] = (upper.astype(jnp.float32) * HD**-0.5).astype(jnp.bfloat16)
        projected = product(rows_normed, weight(pl.ds(width, 2 * width)))
        lower, upper = turn(projected[:, :half], projected[:, half:width])
        both = pl.ds(cut * 2, 2)
        kv[both, :, :half] = lower.reshape(2, rows, half)
        kv[both, :, half:width] = upper.reshape(2, rows, half)
        kv[both, :, width:] = projected[:, width:].astype(jnp.bfloat16).reshape(2, rows, width)
        over(cut, h).start()
        keep(cut).start()

    def pass_on(cut):
        keep(cut).wait()
        over(cut, 1 - h).wait_recv()
        share(cut, c).start()

    def attend(place_at):
        part = pl.ds(place_at * pair, pair)
        count = min(2 * place_at + 3, 8)
        ids = query_ids[part]

        def maxima(block, best):
            key = keys[block, :, :, :, :width].reshape(4 * rows, width)
            part_scores = times_transposed(query[part], key)
            part_scores = jnp.where(key_ids[block] <= ids, part_scores, -1e30)
            scores[block] = part_scores
            for lane in range(4 * rows // 128):
                best = jnp.maximum(best, part_scores[:, lane * 128 : lane * 128 + 128])
            return best

        best = lax.fori_loop(0, count, maxima, jnp.full((pair, 128), -1e30, jnp.float32))
        row_max = jnp.max(best, axis=1, keepdims=True)
        total[...] = jnp.zeros_like(total)

        def mix(block, sums):
            weights = jnp.exp(scores[block] - row_max)
            value = keys[block, :, :, :, width:].reshape(4 * rows, width)
            total[...] += product(weights.astype(jnp.bfloat16), value)
            for lane in range(4 * rows // 128):
                sums = sums + weights[:, lane * 128 : lane * 128 + 128]
            return sums

        sums = lax.fori_loop(0, count, mix, jnp.zeros((pair, 128), jnp.float32))
        row_sum = jnp.sum(sums, axis=1, keepdims=True)
        mixed = total[...] / row_sum
        attended_out[part] = mixed
        attended_low_out[part] = mixed.astype(jnp.bfloat16)
        log_out[place_at] = row_of(row_max + jnp.log(row_sum))

    order = (2, 0, 1, 3)
    attn.start()
    tok.start()
    notices.start()
    tok.relay_b()
    attn.relay(0)
    for elem in order:
        tok.relay(0, elem)
    attn.relay(1)
    attn.relay(2)
    for elem in order:
        tok.relay(1, elem)
    attn.relay(3)
    attn.relay_out()
    notices.finish()
    tables()
    for elem in order:
        tok.relay(2, elem)
    cots.start()
    mlp.start()
    for step in range(LINE):
        attn.relay_share(step)
    attn.relay_out_share()
    tok.finish()
    attn.finish()
    store_qkv = local(qkv_w, qkv_out, store_s.at[0])
    store_qkv.start()
    for cut in range(LINE):
        project(cut)
    store_normed = local(normed, normed_out, store_s.at[1])
    store_normed.start()
    cots.relay_b()
    for elem in order:
        cots.relay(0, elem)
    pass_on(0)
    pass_on(1)
    share(0, 1 - c).wait_recv()
    share(1, 1 - c).wait_recv()
    attend(0)
    for elem in order:
        cots.relay(1, elem)
    pass_on(2)
    share(2, 1 - c).wait_recv()
    attend(1)
    pass_on(3)
    share(3, 1 - c).wait_recv()
    store = local(keys, kv_out, store_s.at[2])
    store.start()
    attend(2)
    for elem in order:
        cots.relay(2, elem)
    attend(3)
    cots.finish()
    mlp.finish()
    for cut in range(LINE):
        share(cut, c).wait_send()
        over(cut, h).wait_send()
    store.wait()
    store_normed.wait()
    store_qkv.wait()


def front(tokens, cot, note, inv_freqs, wq, wk, wv, wo, wg, wu):
    rows, width = tokens.shape
    depth, part = wg.shape[0], wg.shape[1] // 8
    token_rows = 8 * rows

    def room(*dims, dtype=jnp.bfloat16):
        return pltpu.VMEM(dims, dtype)

    def shape(*dims, dtype=jnp.bfloat16):
        return jax.ShapeDtypeStruct(dims, dtype)

    f32 = jnp.float32
    return pl.pallas_call(
        front_kernel,
        out_shape=(
            shape(8, 2, 2, rows, 2 * HD),
            shape(token_rows, width),
            shape(8, 2, depth, 3 * HD),
            shape(2, 2, wo.shape[0], width),
            shape(16, *note.shape, dtype=f32),
            shape(token_rows, HD // 2, dtype=f32),
            shape(token_rows, HD // 2, dtype=f32),
            shape(token_rows, HD),
            shape(token_rows, HD, dtype=f32),
            shape(token_rows, HD),
            shape(LINE, 1, token_rows // LINE, dtype=f32),
            shape(8, *cot.shape),
            shape(8, depth, part),
            shape(8, depth, part),
        ),
        in_specs=[INSIDE] * 10,
        out_specs=(ANY, ANY, ANY, ANY) + (INSIDE,) * 7 + (ANY, ANY, ANY),
        scratch_shapes=[
            room(8, rows, width),
            room(token_rows, width),
            room(8, 2, depth, 3 * HD),
            room(1, width, dtype=f32),
            room(token_rows, 1, dtype=f32),
            room(8, 1, 4 * rows, dtype=f32),
            room(8, rows, 2 * HD),
            room(8, 2, 2, rows, 2 * HD),
            room(8, token_rows // LINE, 4 * rows, dtype=f32),
            room(token_rows // LINE, HD, dtype=f32),
        ]
        + [dma(4)] * 5
        + [dma(3)]
        + Gather.scratch()
        + NoteSpread.scratch()
        + AttnSpread.scratch()
        + Gather.scratch()
        + MlpSpread.scratch(),
        compiler_params=kernel_params(3),
        name="front",
    )(tokens, cot, note, inv_freqs, wq, wk, wv, wo, wg, wu)


def add_into(target, *others):
    total = target[...].astype(jnp.float32)
    for other in others:
        total += other[...].astype(jnp.float32)
    target[...] = total.astype(target.dtype)


class QuarterReduce:
    @staticmethod
    def scratch(depth, wide):
        store = pltpu.VMEM((8, 2, depth, wide), jnp.bfloat16)
        sib = pltpu.VMEM((8, depth, wide), jnp.bfloat16)
        over = pltpu.VMEM((8, depth, wide // 2), jnp.bfloat16)
        return [store, store, sib, sib, over, over] + [dma(2)] + [dma(2, 2)] * 4

    def __init__(self, sources, outs, refs):
        self.sources, self.outs = sources, outs
        self.store, self.sib, self.box = refs[0:2], refs[2:4], refs[4:6]
        self.load_s, self.c_s, self.c_r, self.x_s, self.x_r = refs[6:]
        self.z, self.y, self.c, self.h = place()
        self.part = self.box[0].shape[2]

    def columns(self, half):
        return pl.ds(pl.multiple_of(half * self.part, self.part), self.part)

    def load(self, kind):
        return local(self.sources[kind], self.store[kind], self.load_s.at[kind])

    def share(self, kind, cut):
        chips = pl.ds(cut * 4, 4)
        return remote(
            self.store[kind].at[chips, 1 - self.c], self.sib[kind].at[chips], self.c_s.at[kind, cut],
            self.c_r.at[kind, cut], device(self.z, self.y, 1 - self.c, self.h),
        )

    def over(self, kind, cut):
        chips = pl.ds(cut * 4, 4)
        return remote(
            self.store[kind].at[chips, self.c, :, self.columns(1 - self.h)], self.box[kind].at[chips],
            self.x_s.at[kind, cut], self.x_r.at[kind, cut], device(self.z, self.y, self.c, 1 - self.h),
        )

    def start_loads(self):
        for kind in range(2):
            self.load(kind).start()

    def start(self, kind):
        self.load(kind).wait()
        for cut in range(2):
            self.share(kind, cut).start()

    def relay(self, kind):
        columns = self.columns(1 - self.h)
        for cut in range(2):
            self.share(kind, cut).wait_recv()

            @pl.loop(cut * 4, cut * 4 + 4)
            def _(chip):
                add_into(self.store[kind].at[chip, self.c, :, columns], self.sib[kind].at[chip, :, columns])

            self.over(kind, cut).start()

    def finish(self, kind):
        columns = self.columns(self.h)
        for cut in range(2):
            self.over(kind, cut).wait_recv()

            @pl.loop(cut * 4, cut * 4 + 4)
            def _(chip):
                total = self.store[kind][chip, self.c, :, columns].astype(jnp.float32)
                total += self.sib[kind][chip, :, columns].astype(jnp.float32)
                total += self.box[kind][chip].astype(jnp.float32)
                self.outs[kind][chip] = total.astype(jnp.bfloat16)

        for cut in range(2):
            self.share(kind, cut).wait_send()
            self.over(kind, cut).wait_send()


class QuarterScatter:
    @staticmethod
    def scratch():
        return [dma(2, 8), dma(2, 8), dma(2)]

    def __init__(self, quarters, outs, sems):
        self.quarters, self.outs = quarters, outs
        self.s, self.r, self.own = sems
        self.z, self.y, self.c, self.h = place()
        self.chip = self.z * 2 + self.y
        self.part = quarters[0].shape[2]

    def columns(self, chip):
        return pl.ds(pl.multiple_of(chip * self.part, self.part), self.part)

    def push(self, kind, step):
        target = (self.chip + step) % 8
        return remote(
            self.quarters[kind].at[target], self.outs[kind].at[:, self.columns(self.chip)], self.s.at[kind, step],
            self.r.at[kind, step], device(target // 2, target % 2, self.c, self.h),
        )

    def pull(self, kind, step):
        ref = self.outs[kind].at[:, self.columns((self.chip + 8 - step) % 8)]
        return remote(ref, ref, self.s.at[kind, step], self.r.at[kind, step], device(self.z, self.y, self.c, self.h))

    def keep(self, kind):
        return local(self.quarters[kind].at[self.chip], self.outs[kind].at[:, self.columns(self.chip)], self.own.at[kind])

    def start(self):
        for kind in range(2):
            self.keep(kind).start()
            for step in range(1, 8):
                self.push(kind, step).start()

    def finish(self):
        for kind in range(2):
            self.keep(kind).wait()
            for step in range(1, 8):
                self.pull(kind, step).wait_recv()
                self.push(kind, step).wait_send()


class DownReduce:
    @staticmethod
    def scratch(rows, width):
        return [
            pltpu.VMEM((2, 2, rows, width), jnp.bfloat16),
            pltpu.VMEM((2, rows, width), jnp.bfloat16),
            pltpu.VMEM((rows, width), jnp.bfloat16),
            dma(1), dma(2), dma(2),
        ]

    def __init__(self, source, out, refs):
        self.source, self.out = source, out
        self.store, self.sib, self.box, self.load_s, self.c_sr, self.x_sr = refs
        self.z, self.y, self.c, self.h = place()

    def load(self):
        return local(self.source, self.store, self.load_s.at[0])

    def share(self):
        return remote(
            self.store.at[:, 1 - self.c], self.sib, self.c_sr.at[0], self.c_sr.at[1],
            device(self.z, self.y, 1 - self.c, self.h),
        )

    def over(self):
        return remote(
            self.store.at[1 - self.h, self.c], self.box, self.x_sr.at[0], self.x_sr.at[1],
            device(self.z, self.y, self.c, 1 - self.h),
        )

    def start(self):
        self.load().wait()
        self.share().start()

    def relay(self):
        self.share().wait_recv()
        add_into(self.store.at[1 - self.h, self.c], self.sib.at[1 - self.h])
        self.over().start()

    def finish(self):
        self.over().wait_recv()
        total = self.store[self.h, self.c].astype(jnp.float32) + self.sib[self.h].astype(jnp.float32)
        self.out[...] = total + self.box[...].astype(jnp.float32)
        self.share().wait_send()
        self.over().wait_send()


def reduce_grads_kernel(parts_in, gate_in, up_in, out, gate, up, parts, in_sem, *refs):
    reduce_refs, grad_refs = split_refs(refs, (9, 11))
    load = pltpu.make_async_copy(parts_in, parts, in_sem)
    load.start()
    z, y, c, h = place()
    grads = QuarterReduce((gate_in, up_in), (gate, up), grad_refs)
    grads.start_loads()
    greet(device(z, y, 1 - c, h))
    greet(device(z, y, c, 1 - h))
    greet_plane(2)
    reduce = Reduce(parts, reduce_refs)
    load.wait()
    for place_at in range(4):
        reduce.start(place_at)
    grads.start(0)
    grads.start(1)
    grads.relay(0)
    reduce.relay(0)
    grads.relay(1)
    reduce.relay(1)
    reduce.relay(2)
    reduce.total(out)
    grads.finish(0)
    grads.finish(1)
    reduce.finish()


def reduce_grads(parts, gate, up):
    shape = parts.shape
    depth, wide = gate.shape[2:]
    quarter = jax.ShapeDtypeStruct((8, depth, wide // 2), gate.dtype)
    return pl.pallas_call(
        reduce_grads_kernel,
        out_shape=(jax.ShapeDtypeStruct(shape[1:], jnp.float32), quarter, quarter),
        in_specs=[ANY] * 3,
        out_specs=(INSIDE,) * 3,
        scratch_shapes=[pltpu.VMEM(shape, jnp.bfloat16), dma()]
        + Reduce.scratch(shape[2])
        + QuarterReduce.scratch(depth, wide),
        compiler_params=kernel_params(9),
        name="reduce_grads",
    )(parts, gate, up)


def gather_grads_kernel(src, down_in, out, down, *refs):
    gather_sems, down_refs = split_refs(refs, (8, 6))
    z, y, c, h = place()
    downs = DownReduce(down_in, down, down_refs)
    downs.load().start()
    greet(device(z, y, 1 - c, h))
    greet(device(z, y, c, 1 - h))
    greet_plane(2)
    gather = Gather(src, out, gather_sems)
    gather.start()
    downs.start()
    gather.relay_b()
    downs.relay()
    for step in range(LINE - 1):
        for elem in (2, 0, 1, 3):
            gather.relay(step, elem)
    downs.finish()
    gather.finish()


def gather_grads(rows, down):
    return pl.pallas_call(
        gather_grads_kernel,
        out_shape=(
            jax.ShapeDtypeStruct((2 * LINE,) + rows.shape, rows.dtype),
            jax.ShapeDtypeStruct(down.shape[2:], jnp.float32),
        ),
        in_specs=[INSIDE, ANY],
        out_specs=(ANY, INSIDE),
        scratch_shapes=Gather.scratch() + DownReduce.scratch(*down.shape[2:]),
        compiler_params=kernel_params(10),
        name="gather_grads",
    )(rows, down)


def attend_back_kernel(
    query, grad_out, keys_in, keys_turned, log_row, delta_row, query_row, key_column, gate_in, up_in,
    side_out, grad_query, gate, up,
    keys, turned, parts, grad_key, grad_value, sib_in, x_in, z_in,
    load_s, c_s, c_r, x_s, x_r, z_s, z_r, *sems,
):
    z, y, c, h = place()
    mate = z + 1 - 2 * (z % 2)
    loads = [local(keys_in, keys, load_s.at[0]), local(keys_turned, turned, load_s.at[1])]
    for load in loads:
        load.start()
    greet_all(16, 2)
    scatter = QuarterScatter((gate_in, up_in), (gate, up), sems)
    scatter.start()
    rows, width = key_column.shape[1], query.shape[1]
    pair = query.shape[0] // LINE

    def share(block):
        return remote(
            parts.at[block, 1 - c], sib_in.at[block], c_s.at[block], c_r.at[block], device(z, y, 1 - c, h)
        )

    def over(block):
        return remote(
            parts.at[block, c, 1 - h], x_in.at[block], x_s.at[block], x_r.at[block], device(z, y, c, 1 - h)
        )

    def columns(kind):
        return pl.ds(pl.multiple_of(kind * width, width), width)

    def across(block):
        return remote(
            parts.at[block, c, h, :, columns(1 - z % 2)], z_in.at[block], z_s.at[block], z_r.at[block],
            device(mate, y, c, h),
        )

    def stage_two(block):
        share(block).wait_recv()
        add_into(parts.at[block, c, 1 - h], sib_in.at[block, 1 - h])
        over(block).start()

    def stage_three(block):
        over(block).wait_recv()
        add_into(parts.at[block, c, h], sib_in.at[block, h], x_in.at[block])
        across(block).start()

    def stage_four(block):
        across(block).wait_recv()
        side_out[block] = parts[block, c, h, :, columns(z % 2)].astype(jnp.float32) + z_in[block].astype(jnp.float32)

    for load in loads:
        load.wait()
    grad_query[...] = jnp.zeros_like(grad_query)
    for block in range(8):
        key = keys[block, :, :, :, :width].reshape(rows, width)
        value = keys[block, :, :, :, width:].reshape(rows, width)
        grad_key[...] = jnp.zeros_like(grad_key)
        grad_value[...] = jnp.zeros_like(grad_value)

        @pl.loop(max(0, (block - 1) // 2), LINE)
        def _(place_at):
            part = pl.ds(pl.multiple_of(place_at * pair, pair), pair)
            part_scores = times_transposed(key, query[part])
            visible = key_column[block] <= query_row[place_at]
            weights = jnp.where(visible, jnp.exp(part_scores - log_row[place_at]), 0.0)
            grad_weights = times_transposed(value, grad_out[part])
            grad_scores = (weights * (grad_weights - delta_row[place_at])).astype(jnp.bfloat16)
            grad_key[...] += product(grad_scores, query[part])
            grad_value[...] += product(weights.astype(jnp.bfloat16), grad_out[part])
            grad_query[place_at] += product(turned[block], grad_scores)

        parts[block, :, :, :, :width] = grad_key[...].astype(jnp.bfloat16).reshape(2, 2, rows // 4, width)
        parts[block, :, :, :, width:] = grad_value[...].astype(jnp.bfloat16).reshape(2, 2, rows // 4, width)
        share(block).start()
        if block >= 1:
            stage_two(block - 1)
        if block >= 4:
            stage_three(block - 4)
    stage_two(7)
    for block in range(4, 8):
        stage_three(block)
        stage_four(block - 4)
    for block in range(4, 8):
        stage_four(block)
    for block in range(8):
        share(block).wait_send()
        over(block).wait_send()
        across(block).wait_send()
    scatter.finish()


def attend_back(query, grad_out, keys, keys_turned, log_row, delta_row, query_row, key_column, gate, up):
    eight, _, _, rows, width = keys.shape
    tokens = query.shape[0]
    depth, part = gate.shape[1:]

    def room(*dims, dtype=jnp.bfloat16):
        return pltpu.VMEM(dims, dtype)

    def shape(*dims, dtype=jnp.bfloat16):
        return jax.ShapeDtypeStruct(dims, dtype)

    return pl.pallas_call(
        attend_back_kernel,
        out_shape=(
            shape(eight, rows, HD, dtype=jnp.float32),
            shape(LINE, HD, tokens // LINE, dtype=jnp.float32),
            shape(depth, 8 * part),
            shape(depth, 8 * part),
        ),
        in_specs=[INSIDE, INSIDE, ANY, ANY, INSIDE, INSIDE, INSIDE, INSIDE, INSIDE, INSIDE],
        out_specs=(INSIDE, INSIDE, ANY, ANY),
        scratch_shapes=[
            room(*keys.shape), room(*keys_turned.shape), room(*keys.shape),
            room(4 * rows, HD, dtype=jnp.float32), room(4 * rows, HD, dtype=jnp.float32),
            room(eight, 2, rows, width), room(eight, rows, width), room(eight, rows, HD),
            dma(2),
        ] + [dma(8)] * 6 + QuarterScatter.scratch(),
        compiler_params=kernel_params(11),
        name="attend_back",
    )(query, grad_out, keys, keys_turned, log_row, delta_row, query_row, key_column, gate, up)


class HeadGrads:
    @staticmethod
    def scratch(depth, out_rows, width):
        def room(*dims):
            return pltpu.VMEM(dims, jnp.bfloat16)

        return [
            room(8, 2, depth, HD), room(8, 2, depth, HD), room(2, 2, out_rows, width),
            room(8, depth, HD), room(8, depth, HD), room(2, out_rows, width),
            room(8, depth, HD), room(8, depth, HD), room(2, out_rows, width),
            dma(3), dma(3), dma(3), dma(3), dma(3), dma(3, 8), dma(3, 4, 8), dma(2), dma(4),
        ]

    def __init__(self, sources, outs, refs):
        self.sources, self.outs = sources, outs
        self.store, self.sib, self.box = refs[0:3], refs[3:6], refs[6:9]
        (self.load_s, self.c_s, self.c_r, self.x_s, self.x_r, self.s, self.r, self.y_sr, self.own) = refs[9:]
        self.z, self.y, self.c, self.h = place()
        self.chip = self.z * 2 + self.y
        self.me = device(self.z, self.y, self.c, self.h)
        self.owner = self.h == self.y

    def load(self, i):
        return local(self.sources[i], self.store[i], self.load_s.at[i])

    def share(self, i):
        return remote(
            self.store[i].at[:, 1 - self.c], self.sib[i], self.c_s.at[i], self.c_r.at[i],
            device(self.z, self.y, 1 - self.c, self.h),
        )

    def over(self, i):
        return remote(
            self.store[i].at[:, self.c], self.box[i], self.x_s.at[i], self.x_r.at[i],
            device(self.z, self.y, self.c, 1 - self.h),
        )

    def target(self, kind, line):
        start = line * HD if kind == 0 else (line // 2) * HD
        return self.outs[kind].at[:, pl.ds(pl.multiple_of(start, HD), HD)]

    def push(self, kind, step):
        chip = (self.chip + step) % 8
        return remote(
            self.store[min(kind, 1)].at[chip, self.c], self.target(kind, self.z), self.s.at[kind, step],
            self.r.at[kind, self.z, step], device(chip // 2, chip % 2, self.c, self.h),
        )

    def keep(self, kind):
        return local(self.store[min(kind, 1)].at[self.chip, self.c], self.target(kind, self.z), self.own.at[kind])

    def pull(self, kind, line, step):
        ref = self.target(kind, line)
        return remote(ref, ref, self.s.at[kind, step], self.r.at[kind, line, step], self.me)

    def out_move(self):
        return remote(
            self.store[2].at[1 - self.y, self.c], self.outs[3], self.y_sr.at[0], self.y_sr.at[1],
            device(self.z, 1 - self.y, self.c, self.h),
        )

    def out_keep(self):
        return local(self.store[2].at[self.y, self.c], self.outs[3], self.own.at[3])

    def start_loads(self):
        for i in range(3):
            self.load(i).start()

    def start(self):
        for i in (2, 0, 1):
            self.load(i).wait()
            self.share(i).start()

    def relay(self):
        for i in (2, 0, 1):
            self.share(i).wait_recv()

            @pl.loop(0, self.sib[i].shape[0])
            def _(at):
                add_into(self.store[i].at[at, self.c], self.sib[i].at[at])

            @pl.when(jnp.logical_not(self.owner))
            def _():
                self.over(i).start()

    def scatter(self):
        @pl.when(self.owner)
        def _():
            for i in (2, 0, 1):
                self.over(i).wait_recv()

                @pl.loop(0, self.sib[i].shape[0])
                def _(at):
                    add_into(self.store[i].at[at, self.c], self.box[i].at[at])

                if i == 2:
                    self.out_move().start()
                    self.out_keep().start()
                elif i == 0:
                    self.keep(0).start()
                    for step in range(1, 8):
                        self.push(0, step).start()
                else:
                    for kind in (1, 2):

                        @pl.when(self.z % 2 == kind - 1)
                        def _():
                            self.keep(kind).start()
                            for step in range(1, 8):
                                self.push(kind, step).start()

    def finish(self):
        for kind in range(3):
            for line in range(LINE):
                if kind and line % 2 != kind - 1:
                    continue
                step = (self.chip + 8 - (line * 2 + self.h)) % 8

                @pl.when(step != 0)
                def _():
                    self.pull(kind, line, step).wait_recv()

                @pl.when(step == 0)
                def _():
                    self.keep(kind).wait()

        @pl.when(jnp.logical_not(self.owner))
        def _():
            remote(self.outs[3], self.outs[3], self.y_sr.at[0], self.y_sr.at[1], self.me).wait_recv()
            for i in range(3):
                self.over(i).wait_send()

        @pl.when(self.owner)
        def _():
            self.out_keep().wait()
            self.out_move().wait_send()
            for step in range(1, 8):
                self.push(0, step).wait_send()
            for kind in (1, 2):

                @pl.when(self.z % 2 == kind - 1)
                def _():
                    for step in range(1, 8):
                        self.push(kind, step).wait_send()

        for i in range(3):
            self.share(i).wait_send()


def reduce_heads_kernel(
    parts_in, query_in, side_in, out_in, out, query, key, value, outw, parts, in_sem, *refs
):
    reduce_refs, head_refs = split_refs(refs, (9, 18))
    load = pltpu.make_async_copy(parts_in, parts, in_sem)
    load.start()
    heads = HeadGrads((query_in, side_in, out_in), (query, key, value, outw), head_refs)
    heads.start_loads()
    greet_all(16, 2)
    reduce = Reduce(parts, reduce_refs)
    load.wait()
    for place_at in range(4):
        reduce.start(place_at)
    heads.start()
    heads.relay()
    reduce.relay(0)
    reduce.relay(1)
    heads.scatter()
    reduce.relay(2)
    reduce.total(out)
    heads.finish()
    reduce.finish()


def reduce_heads(parts, query, side, outw):
    shape = parts.shape
    depth = query.shape[2]
    out_rows, width = outw.shape[2:]

    def room(*dims):
        return jax.ShapeDtypeStruct(dims, jnp.bfloat16)

    return pl.pallas_call(
        reduce_heads_kernel,
        out_shape=(
            jax.ShapeDtypeStruct(shape[1:], jnp.float32),
            room(depth, 4 * HD), room(depth, 2 * HD), room(depth, 2 * HD), room(out_rows, width),
        ),
        in_specs=[ANY] * 4,
        out_specs=(INSIDE, ANY, ANY, ANY, ANY),
        scratch_shapes=[pltpu.VMEM(shape, jnp.bfloat16), dma()]
        + Reduce.scratch(shape[2])
        + HeadGrads.scratch(depth, out_rows, width),
        compiler_params=kernel_params(6),
        name="reduce_heads",
    )(parts, query, side, outw)


def gains_kernel(gains, out, box, own, send_sems, recv_sems):
    blk, h = lax.axis_index("blk"), lax.axis_index("head")
    greet_all(16, 2)

    def push(step):
        other = (blk + step // 2) % 16
        return remote(
            gains.at[other], box.at[step], send_sems.at[step], recv_sems.at[step], (other, (h + step % 2) % 2)
        )

    keep = local(gains.at[blk], box.at[0], own.at[0])
    keep.start()
    for step in range(1, 32):
        push(step).start()
    keep.wait()
    total = box[0]
    for step in range(1, 32):
        push(step).wait_recv()
        total += box[step]
    out[...] = total
    for step in range(1, 32):
        push(step).wait_send()


def reduce_gains(gains):
    return pl.pallas_call(
        gains_kernel,
        out_shape=jax.ShapeDtypeStruct(gains.shape[1:], gains.dtype),
        in_specs=[INSIDE],
        out_specs=INSIDE,
        scratch_shapes=[pltpu.VMEM((32,) + gains.shape[1:], gains.dtype), dma(1), dma(32), dma(32)],
        compiler_params=kernel_params(12),
        name="reduce_gains",
    )(gains)


def fast_body(
    tokens,
    attn_gain,
    w_query,
    w_key,
    w_value,
    w_out,
    mlp_gain,
    w_gate,
    w_up,
    w_down,
    block_ids,
    positions,
    cotangent,
):
    z, y, core, half = place()
    rows, width = tokens.shape
    token_rows = 8 * rows
    f32, bf16 = jnp.float32, jnp.bfloat16

    def own_half(values):
        return lax.dynamic_index_in_dim(values, half, 0, False)

    note = jnp.concatenate(
        [
            positions.astype(f32).reshape(2, rows),
            block_ids.astype(f32).reshape(2, rows),
            attn_gain.astype(f32)[None],
            mlp_gain.astype(f32)[None],
            jnp.zeros((2, rows), f32),
        ]
    )
    inv_freqs = rope_base ** (-2.0 * jnp.arange(HD // 2, dtype=f32) / HD)
    (
        keys_values, normed, qkv_w, out_w, notes, cos_table, sine_table, scaled_query, attended, attended_low,
        log_total, cot_all, gate_w, up_w,
    ) = front(tokens, cotangent, note, inv_freqs[None], w_query, w_key, w_value, w_out, w_gate, w_up)
    qkv_w = qkv_w.reshape(width, 3 * HD)
    out_w = out_w.reshape(HD, width)
    gain_attn = notes[:, 4].reshape(1, width)
    gain_mlp = notes[:, 5].reshape(1, width)
    mine = lax.dynamic_index_in_dim(notes.reshape(8, 2, 8, rows), core, 1, False)
    ids_mine = lax.dynamic_index_in_dim(mine[:, 2:4], half, 1, False).reshape(token_rows)
    key_ids = notes[:, 2:4].reshape(32 * rows)
    score_scale = HD ** (-0.5)
    branch, gate_w, up_w = reduce_share(attended_low, out_w, gate_w, up_w)
    hidden_part = gate_w.shape[3]
    gate_w = gate_w.reshape(width, hidden_part)
    up_w = up_w.reshape(width, hidden_part)

    inputs = tokens.astype(f32)
    inv_attn = rms_scale(inputs)
    hidden = inputs + branch
    inv_mlp = rms_scale(hidden)
    mlp_own, normed_mlp, active, grad_gate, grad_up, grad_normed_part = run_mlp(
        (hidden * inv_mlp * gain_mlp).astype(bf16), w_down, gate_w, up_w, cot_all
    )
    output = (hidden + mlp_own).astype(bf16)
    normed_mlp = normed_mlp.reshape(token_rows, width)
    active = active.reshape(token_rows, hidden_part)
    grad_gate = grad_gate.reshape(token_rows, hidden_part)
    grad_up = grad_up.reshape(token_rows, hidden_part)
    cot_all = cot_all.reshape(token_rows, width)
    depth = w_query.shape[0]
    grad_normed_mlp, gate_quarter, up_quarter = reduce_grads(
        grad_normed_part,
        transposed_times(normed_mlp, grad_gate).astype(bf16).reshape(8, 2, depth, hidden_part),
        transposed_times(normed_mlp, grad_up).astype(bf16).reshape(8, 2, depth, hidden_part),
    )
    grad_down_w = transposed_times(active, cot_all).astype(bf16)
    grad_hidden_norm, gain_mlp_term = norm_backward(grad_normed_mlp, hidden, inv_mlp, gain_mlp)
    grad_hidden = cotangent.astype(f32) + grad_hidden_norm

    grad_branch, down_grad = gather_grads(
        grad_hidden.astype(bf16), grad_down_w.reshape(2, 2, w_down.shape[0], width)
    )
    grad_branch = grad_branch.reshape(token_rows, width)
    grad_out_w = transposed_times(attended_low, grad_branch)
    grad_attended = times_transposed(grad_branch, out_w).astype(bf16)
    delta = jnp.sum(grad_attended.astype(f32) * attended, axis=-1)
    keys_turned = jnp.swapaxes(keys_values[..., :HD].reshape(8, 4 * rows, HD), 1, 2)
    side, grad_query_rot, gate_grad, up_grad = attend_back(
        scaled_query,
        grad_attended,
        keys_values,
        keys_turned,
        log_total.reshape(LINE, 1, token_rows // LINE),
        delta.reshape(LINE, 1, token_rows // LINE),
        ids_mine.reshape(LINE, 1, token_rows // LINE),
        key_ids.reshape(8, 4 * rows, 1),
        gate_quarter,
        up_quarter,
    )
    side = side.reshape(token_rows, HD)
    grad_query_rot = jnp.swapaxes(grad_query_rot, 1, 2).reshape(token_rows, HD) * score_scale
    is_key = z % 2 == 0
    side_grad = jnp.where(is_key, rotate(side, cos_table, -sine_table), side).astype(bf16)
    grad_query = rotate(grad_query_rot, cos_table, -sine_table).astype(bf16)
    side_w = jnp.where(is_key, qkv_w[:, HD : 2 * HD], qkv_w[:, 2 * HD :])
    grad_normed_part = times_transposed(grad_query, qkv_w[:, :HD]) + times_transposed(
        side_grad, side_w
    )
    grad_normed, query_grad, key_grad, value_grad, out_grad = reduce_heads(
        grad_normed_part.astype(bf16).reshape(8, rows, width),
        transposed_times(normed, grad_query).astype(bf16).reshape(8, 2, depth, HD),
        transposed_times(normed, side_grad).astype(bf16).reshape(8, 2, depth, HD),
        grad_out_w.astype(bf16).reshape(2, 2, w_out.shape[0], width),
    )
    grad_inputs_norm, gain_attn_term = norm_backward(grad_normed, inputs, inv_attn, gain_attn)
    tokens_grad = (grad_hidden + grad_inputs_norm).astype(bf16)

    gains = jnp.concatenate(
        [
            gain_attn_term.reshape(16, 1, rows),
            gain_mlp_term.reshape(16, 1, rows),
            jnp.zeros((16, 6, rows), f32),
        ],
        axis=1,
    )
    gain_grads = reduce_gains(gains)
    return (
        output,
        tokens_grad,
        gain_grads[0],
        query_grad.astype(f32),
        key_grad.astype(f32),
        value_grad.astype(f32),
        out_grad.astype(f32),
        gain_grads[1],
        gate_grad.astype(f32),
        up_grad.astype(f32),
        down_grad,
    )


def solution(mesh):
    placed = (
        P(("blk", "head"), None),
        P("blk"),
        P("blk", "head"),
        P("blk", "head"),
        P("blk", "head"),
        P(("head", "blk"), None),
        P("blk"),
        P("blk", "head"),
        P("blk", "head"),
        P(("head", "blk"), None),
        P("blk"),
        P("blk"),
        P(("blk", "head"), None),
    )
    fits = mesh.shape["blk"] == 16 and mesh.shape["head"] == 2
    return jax.shard_map(
        fast_body if fits else body,
        mesh=mesh,
        in_specs=placed,
        out_specs=(
            P(("blk", "head"), None),
            P(("blk", "head"), None),
            P("blk"),
            P("blk", "head"),
            P("blk", "head"),
            P("blk", "head"),
            P(("head", "blk"), None),
            P("blk"),
            P("blk", "head"),
            P("blk", "head"),
            P(("head", "blk"), None),
        ),
        check_vma=False,
    )
```

```python
import jax
import jax.numpy as jnp
from jax import lax
from jax.experimental import pallas as pl
from jax.experimental.pallas import tpu as pltpu
from jax.sharding import PartitionSpec as P

HD = 256


eps_norm = 1e-06
rope_base = 1000042.0


def rms_scale(rows):
    return lax.rsqrt(jnp.mean(rows * rows, axis=-1, keepdims=True) + eps_norm)


def rope_tables(positions):
    inv_freqs = rope_base ** (-2.0 * jnp.arange(HD // 2, dtype=jnp.float32) / HD)
    angles = positions.astype(jnp.float32)[:, None] * inv_freqs[None, :]
    return (jnp.cos(angles)[:, None, :], jnp.sin(angles)[:, None, :])


def rotate(heads, cos_table, sine_table):
    half_size = heads.shape[-1] // 2
    lower_half = heads[..., :half_size]
    upper_half = heads[..., half_size:]
    return jnp.concatenate(
        [
            lower_half * cos_table - upper_half * sine_table,
            upper_half * cos_table + lower_half * sine_table,
        ],
        axis=-1,
    )


def product(left, right):
    return jnp.dot(left, right, preferred_element_type=jnp.float32)


def times_transposed(left, right):
    return lax.dot_general(
        left, right, (((1,), (1,)), ((), ())), preferred_element_type=jnp.float32
    )


def transposed_times(left, right):
    return lax.dot_general(
        left, right, (((0,), (0,)), ((), ())), preferred_element_type=jnp.float32
    )


def norm_backward(grad_normed, inputs, inv_scale, gain_rows):
    unit_rows = inputs * inv_scale
    grad_unit = grad_normed * gain_rows
    gain_term = jnp.sum(grad_normed * unit_rows, axis=0)
    grad_inputs = inv_scale * (
        grad_unit - unit_rows * jnp.mean(grad_unit * unit_rows, axis=-1, keepdims=True)
    )
    return (grad_inputs, gain_term)


def body(
    tokens,
    attn_gain,
    w_query,
    w_key,
    w_value,
    w_out,
    mlp_gain,
    w_gate,
    w_up,
    w_down,
    block_ids,
    positions,
    cotangent,
):
    rows_own = tokens.shape[0]
    head_rank = lax.axis_index("head")
    tokens_all, cot_all = (
        lax.all_gather(tokens, "head", axis=0, tiled=True),
        lax.all_gather(cotangent, "head", axis=0, tiled=True),
    )
    rows_all = tokens_all.shape[0]
    gain_attn, query_w, key_w, value_w, out_w = (
        lax.all_gather(attn_gain, "blk", axis=0, tiled=True),
        lax.all_gather(w_query, "blk", axis=0, tiled=True),
        lax.all_gather(w_key, "blk", axis=0, tiled=True),
        lax.all_gather(w_value, "blk", axis=0, tiled=True),
        lax.all_gather(w_out, "blk", axis=0, tiled=True),
    )
    gain_mlp, gate_w, up_w, down_w = (
        lax.all_gather(mlp_gain, "blk", axis=0, tiled=True),
        lax.all_gather(w_gate, "blk", axis=0, tiled=True),
        lax.all_gather(w_up, "blk", axis=0, tiled=True),
        lax.all_gather(w_down, "blk", axis=0, tiled=True),
    )
    key_ids = lax.all_gather(block_ids, "blk", axis=0, tiled=True)
    heads_local = query_w.shape[1] // HD
    kv_local = key_w.shape[1] // HD
    kv_width = kv_local * HD
    group_size = heads_local // kv_local
    cos_table, sine_table = rope_tables(positions)
    score_scale = HD ** (-0.5)
    seq_len = key_ids.shape[0]
    key_block = min(2048, seq_len)
    block_total = seq_len // key_block
    block_steps = jnp.arange(block_total)
    top_query = jnp.max(block_ids)
    inputs = tokens_all.astype(jnp.float32)
    inv_attn = rms_scale(inputs)
    normed = (inputs * inv_attn * gain_attn.astype(jnp.float32)).astype(jnp.bfloat16)
    queries = rotate(
        product(normed, query_w).reshape(rows_all, heads_local, HD), cos_table, sine_table
    ).astype(jnp.bfloat16)
    keys_own = rotate(product(normed, key_w).reshape(rows_all, kv_local, HD), cos_table, sine_table)
    keys_own = keys_own.astype(jnp.bfloat16).reshape(rows_all, kv_width)
    values_own = product(normed, value_w).astype(jnp.bfloat16)
    keys_all, values_all = (
        lax.all_gather(keys_own, "blk", axis=0, tiled=True),
        lax.all_gather(values_own, "blk", axis=0, tiled=True),
    )
    grouped = queries.reshape(rows_all, kv_local, group_size, HD)

    def slice_keys(key_start, count):
        key_rows = lax.dynamic_slice_in_dim(keys_all, key_start, count, 0).reshape(
            count, kv_local, HD
        )
        value_rows = lax.dynamic_slice_in_dim(values_all, key_start, count, 0).reshape(
            count, kv_local, HD
        )
        block_keys = lax.dynamic_slice_in_dim(key_ids, key_start, count, 0)
        return (key_rows, value_rows, block_keys)

    def scores_for(key_rows, block_keys):
        scores = (
            jnp.einsum("qkgd,ckd->kgqc", grouped, key_rows, preferred_element_type=jnp.float32)
            * score_scale
        )
        visible = (block_keys[None, :] <= block_ids[:, None])[None, None]
        return (scores, visible)

    def max_sum(state_pair, step_index):
        key_start = step_index * key_block

        def max_live(pair):
            run_max, run_sum = pair
            key_rows, value_rows, block_keys = slice_keys(key_start, key_block)
            scores, visible = scores_for(key_rows, block_keys)
            scores = jnp.where(visible, scores, -1e30)
            new_max = jnp.maximum(run_max, jnp.max(scores, axis=-1))
            kept_terms = jnp.where(visible, jnp.exp(scores - new_max[..., None]), 0.0)
            return (new_max, run_sum * jnp.exp(run_max - new_max) + jnp.sum(kept_terms, axis=-1))

        def max_skipped(pair):
            return pair

        return (lax.cond(key_ids[key_start] <= top_query, max_live, max_skipped, state_pair), None)

    start_max = jnp.full((kv_local, group_size, rows_all), -1e30, jnp.float32)
    start_sum = jnp.zeros((kv_local, group_size, rows_all), jnp.float32)
    (run_max, run_sum), unused_max = lax.scan(max_sum, (start_max, start_sum), block_steps)
    log_total = run_max + jnp.log(run_sum)

    def weighted(accum_rows, step_index):
        key_start = step_index * key_block

        def weighted_live(accum):
            key_rows, value_rows, block_keys = slice_keys(key_start, key_block)
            scores, visible = scores_for(key_rows, block_keys)
            probabilities = jnp.where(visible, jnp.exp(scores - log_total[..., None]), 0.0).astype(
                jnp.bfloat16
            )
            return accum + jnp.einsum(
                "kgqc,ckd->qkgd", probabilities, value_rows, preferred_element_type=jnp.float32
            )

        def weighted_skipped(accum):
            return accum

        return (
            lax.cond(key_ids[key_start] <= top_query, weighted_live, weighted_skipped, accum_rows),
            None,
        )

    attended, unused_rows = lax.scan(
        weighted, jnp.zeros((rows_all, kv_local, group_size, HD), jnp.float32), block_steps
    )
    attended_low = attended.reshape(rows_all, heads_local * HD).astype(jnp.bfloat16)
    branch_sum = lax.psum(product(attended_low, out_w).astype(jnp.bfloat16), "head").astype(
        jnp.float32
    )
    hidden = inputs + branch_sum
    inv_mlp = rms_scale(hidden)
    normed_mlp = (hidden * inv_mlp * gain_mlp.astype(jnp.float32)).astype(jnp.bfloat16)
    gate_pre = product(normed_mlp, gate_w)
    up_pre = product(normed_mlp, up_w)
    sigmoid_gate = jax.nn.sigmoid(gate_pre)
    active = (gate_pre * sigmoid_gate * up_pre).astype(jnp.bfloat16)
    mlp_own = lax.psum_scatter(
        product(active, down_w).astype(jnp.bfloat16), "head", scatter_dimension=0, tiled=True
    ).astype(jnp.float32)
    hidden_own = lax.dynamic_slice_in_dim(hidden, head_rank * rows_own, rows_own, 0)
    output = (hidden_own + mlp_own).astype(jnp.bfloat16)
    gain_attn, query_w, key_w, value_w, out_w = (
        lax.all_gather(attn_gain, "blk", axis=0, tiled=True),
        lax.all_gather(w_query, "blk", axis=0, tiled=True),
        lax.all_gather(w_key, "blk", axis=0, tiled=True),
        lax.all_gather(w_value, "blk", axis=0, tiled=True),
        lax.all_gather(w_out, "blk", axis=0, tiled=True),
    )
    gain_mlp, gate_w, up_w, down_w = (
        lax.all_gather(mlp_gain, "blk", axis=0, tiled=True),
        lax.all_gather(w_gate, "blk", axis=0, tiled=True),
        lax.all_gather(w_up, "blk", axis=0, tiled=True),
        lax.all_gather(w_down, "blk", axis=0, tiled=True),
    )
    grad_active = times_transposed(cot_all, down_w)
    grad_gate = (
        grad_active * up_pre * sigmoid_gate * (1.0 + gate_pre * (1.0 - sigmoid_gate))
    ).astype(jnp.bfloat16)
    grad_up = (grad_active * gate_pre * sigmoid_gate).astype(jnp.bfloat16)
    grad_gate_w = transposed_times(normed_mlp, grad_gate)
    grad_up_w = transposed_times(normed_mlp, grad_up)
    grad_down_w = transposed_times(active, cot_all)
    grad_normed_part = times_transposed(grad_gate, gate_w) + times_transposed(grad_up, up_w)
    grad_normed_mlp = lax.psum(grad_normed_part.astype(jnp.bfloat16), "head").astype(jnp.float32)
    grad_hidden_norm, gain_mlp_term = norm_backward(
        grad_normed_mlp, hidden, inv_mlp, gain_mlp.astype(jnp.float32)
    )
    grad_hidden = cot_all.astype(jnp.float32) + grad_hidden_norm
    mlp_results = (
        lax.psum_scatter(gain_mlp_term, "blk", scatter_dimension=0, tiled=True),
        lax.psum_scatter(grad_gate_w, "blk", scatter_dimension=0, tiled=True),
        lax.psum_scatter(grad_up_w, "blk", scatter_dimension=0, tiled=True),
        lax.psum_scatter(grad_down_w, "blk", scatter_dimension=0, tiled=True),
    )
    grad_branch = grad_hidden.astype(jnp.bfloat16)
    grad_out_w = transposed_times(attended_low, grad_branch)
    grad_attended = times_transposed(grad_branch, out_w).astype(jnp.bfloat16)
    grad_grouped = grad_attended.reshape(rows_all, kv_local, group_size, HD)
    delta_rows = jnp.transpose(
        jnp.sum(grad_grouped.astype(jnp.float32) * attended, axis=-1), (1, 2, 0)
    )

    def pair_backward(key_rows, value_rows, block_keys):
        count = key_rows.shape[0]
        scores, visible = scores_for(key_rows, block_keys)
        probabilities = jnp.where(visible, jnp.exp(scores - log_total[..., None]), 0.0)
        grad_probs = jnp.einsum(
            "qkgd,ckd->kgqc", grad_grouped, value_rows, preferred_element_type=jnp.float32
        )
        grad_scores = (probabilities * (grad_probs - delta_rows[..., None])).astype(jnp.bfloat16)
        query_terms = jnp.einsum(
            "kgqc,ckd->qkgd", grad_scores, key_rows, preferred_element_type=jnp.float32
        )
        key_terms = (
            jnp.einsum("kgqc,qkgd->ckd", grad_scores, grouped, preferred_element_type=jnp.float32)
            * score_scale
        )
        value_terms = jnp.einsum(
            "kgqc,qkgd->ckd",
            probabilities.astype(jnp.bfloat16),
            grad_grouped,
            preferred_element_type=jnp.float32,
        )
        return (
            query_terms,
            key_terms.reshape(count, kv_width),
            value_terms.reshape(count, kv_width),
        )

    query_zeros = jnp.zeros((rows_all, kv_local, group_size, HD), jnp.float32)

    def backward_block(accum_rows, step_index):
        key_start = step_index * key_block

        def backward_live(unused_arg):
            key_rows, value_rows, block_keys = slice_keys(key_start, key_block)
            return pair_backward(key_rows, value_rows, block_keys)

        def backward_skipped(unused_arg):
            empty_terms = jnp.zeros((key_block, kv_width), jnp.float32)
            return (query_zeros, empty_terms, empty_terms)

        query_terms, key_terms, value_terms = lax.cond(
            key_ids[key_start] <= top_query, backward_live, backward_skipped, 0
        )
        return (accum_rows + query_terms, (key_terms, value_terms))

    grad_query_rot, (key_terms, value_terms) = lax.scan(backward_block, query_zeros, block_steps)
    key_terms = key_terms.reshape(seq_len, kv_width)
    value_terms = value_terms.reshape(seq_len, kv_width)
    key_grad_own, value_grad_own = (
        lax.psum_scatter(key_terms, "blk", scatter_dimension=0, tiled=True),
        lax.psum_scatter(value_terms, "blk", scatter_dimension=0, tiled=True),
    )
    grad_query_rot = grad_query_rot * score_scale
    grad_key = rotate(key_grad_own.reshape(rows_all, kv_local, HD), cos_table, -sine_table)
    grad_key = grad_key.reshape(rows_all, kv_width).astype(jnp.bfloat16)
    grad_value = value_grad_own.astype(jnp.bfloat16)
    grad_query = rotate(grad_query_rot.reshape(rows_all, heads_local, HD), cos_table, -sine_table)
    grad_query = grad_query.reshape(rows_all, heads_local * HD).astype(jnp.bfloat16)
    grad_query_w = transposed_times(normed, grad_query)
    grad_key_w = transposed_times(normed, grad_key)
    grad_value_w = transposed_times(normed, grad_value)
    grad_normed_part = (
        times_transposed(grad_query, query_w)
        + times_transposed(grad_key, key_w)
        + times_transposed(grad_value, value_w)
    )
    grad_normed = lax.psum(grad_normed_part.astype(jnp.bfloat16), "head").astype(jnp.float32)
    grad_inputs_norm, gain_attn_term = norm_backward(
        grad_normed, inputs, inv_attn, gain_attn.astype(jnp.float32)
    )
    grad_inputs = grad_hidden + grad_inputs_norm
    grad_own = lax.dynamic_slice_in_dim(grad_inputs, head_rank * rows_own, rows_own, 0).astype(
        jnp.bfloat16
    )
    attn_results = (
        lax.psum_scatter(gain_attn_term, "blk", scatter_dimension=0, tiled=True),
        lax.psum_scatter(grad_query_w, "blk", scatter_dimension=0, tiled=True),
        lax.psum_scatter(grad_key_w, "blk", scatter_dimension=0, tiled=True),
        lax.psum_scatter(grad_value_w, "blk", scatter_dimension=0, tiled=True),
        lax.psum_scatter(grad_out_w, "blk", scatter_dimension=0, tiled=True),
    )
    return (
        output,
        grad_own,
        attn_results[0],
        attn_results[1],
        attn_results[2],
        attn_results[3],
        attn_results[4],
        mlp_results[0],
        mlp_results[1],
        mlp_results[2],
        mlp_results[3],
    )


MESH = pl.DeviceIdType.MESH
LINE = 4
VMEM_BYTES = 60 * 2**20


def place():
    blk, head = lax.axis_index("blk"), lax.axis_index("head")
    return blk // 4, (blk // 2) % 2, blk % 2, head


def device(z, y, c, h):
    return (z * 4 + y * 2 + c, h)


def remote(src, dst, send_sem, recv_sem, target):
    return pltpu.make_async_remote_copy(
        src_ref=src,
        dst_ref=dst,
        send_sem=send_sem,
        recv_sem=recv_sem,
        device_id=target,
        device_id_type=MESH,
    )


def greet(target):
    pl.semaphore_signal(
        pltpu.get_barrier_semaphore(), inc=1, device_id=target, device_id_type=MESH
    )


def greet_all(blk_total, head_total):
    blk, head = lax.axis_index("blk"), lax.axis_index("head")
    for other in range(blk_total):
        for half in range(head_total):

            @pl.when(jnp.logical_or(blk != other, head != half))
            def _():
                greet((jnp.int32(other), jnp.int32(half)))

    pl.semaphore_wait(pltpu.get_barrier_semaphore(), blk_total * head_total - 1)


def greet_plane(more=0):
    z, y, c, h = place()

    @pl.when(z > 0)
    def _():
        greet(device(z - 1, y, c, h))

    @pl.when(z < LINE - 1)
    def _():
        greet(device(z + 1, y, c, h))

    greet(device(z, 1 - y, c, h))
    pl.semaphore_wait(
        pltpu.get_barrier_semaphore(),
        1 + more + (z + LINE - 1) // LINE + (LINE - 1 - z + LINE - 1) // LINE,
    )


class Gather:
    CUTS = ((0, 64), (64, 48), (112, 16), (112, 16))
    SEMS = [(3, 4)] * 4 + [(4, 2)] * 2 + [(2,)]

    @staticmethod
    def scratch():
        return [pltpu.SemaphoreType.DMA(shape) for shape in Gather.SEMS] + [
            pltpu.SemaphoreType.DMA
        ]

    def __init__(self, src, out, sems):
        self.src, self.out = src, out
        (self.up_s, self.up_r, self.dn_s, self.dn_r, self.y_s, self.y_r, self.b_sr, self.own_sem) = sems
        self.z, self.y, self.c, self.h = place()

    def piece(self, line, elem):
        y = 1 - self.y if elem == 3 else self.y
        start, size = self.CUTS[elem]
        return self.out.at[line * 2 + y, pl.ds(start, size)]

    def first(self, elem):
        if elem == 3:
            return self.piece(self.z, 3)
        start, size = self.CUTS[elem]
        return self.src.at[pl.ds(start, size)]

    def up(self, step, elem):
        src = self.first(elem) if step == 0 else self.piece(self.z - step, elem)
        return remote(
            src, self.piece(self.z - step, elem), self.up_s.at[step, elem], self.up_r.at[step, elem],
            device(self.z + 1, self.y, self.c, self.h),
        )

    def down(self, step, elem):
        src = self.first(elem) if step == 0 else self.piece(self.z + step, elem)
        return remote(
            src, self.piece(self.z + step, elem), self.dn_s.at[step, elem], self.dn_r.at[step, elem],
            device(self.z - 1, self.y, self.c, self.h),
        )

    def up_in(self, step, elem):
        ref = self.piece(self.z - 1 - step, elem)
        return remote(ref, ref, self.up_s.at[step, elem], self.up_r.at[step, elem], device(self.z, self.y, self.c, self.h))

    def down_in(self, step, elem):
        ref = self.piece(self.z + 1 + step, elem)
        return remote(ref, ref, self.dn_s.at[step, elem], self.dn_r.at[step, elem], device(self.z, self.y, self.c, self.h))

    def across(self, line, elem, own=False):
        src = self.first(elem) if own else self.piece(line, elem)
        return remote(
            src, self.piece(line, elem), self.y_s.at[line, elem], self.y_r.at[line, elem],
            device(self.z, 1 - self.y, self.c, self.h),
        )

    def across_in(self, line, elem):
        start, size = self.CUTS[elem]
        ref = self.out.at[line * 2 + 1 - self.y, pl.ds(start, size)]
        return remote(ref, ref, self.y_s.at[line, elem], self.y_r.at[line, elem], device(self.z, self.y, self.c, self.h))

    def across_b(self):
        return remote(
            self.first(2), self.piece(self.z, 2), self.b_sr.at[0], self.b_sr.at[1],
            device(self.z, 1 - self.y, self.c, self.h),
        )

    def across_b_in(self):
        ref = self.piece(self.z, 3)
        return remote(ref, ref, self.b_sr.at[0], self.b_sr.at[1], device(self.z, self.y, self.c, self.h))

    def own_copy(self):
        return pltpu.make_async_copy(self.src, self.out.at[self.z * 2 + self.y], self.own_sem)

    def start(self):
        self.own_copy().start()
        self.across_b().start()
        for elem in (0, 1, 2):

            @pl.when(self.z < LINE - 1)
            def _():
                self.up(0, elem).start()

            @pl.when(self.z > 0)
            def _():
                self.down(0, elem).start()

            if elem < 2:
                self.across(self.z, elem, own=True).start()

    def relay_b(self):
        self.across_b_in().wait_recv()

        @pl.when(self.z < LINE - 1)
        def _():
            self.up(0, 3).start()

        @pl.when(self.z > 0)
        def _():
            self.down(0, 3).start()

    def relay(self, step, elem):
        @pl.when(self.z - 1 - step >= 0)
        def _():
            self.up_in(step, elem).wait_recv()
            if step < LINE - 2:

                @pl.when(self.z < LINE - 1)
                def _():
                    self.up(step + 1, elem).start()

            if elem < 2:
                self.across(self.z - 1 - step, elem).start()

        @pl.when(self.z + 1 + step <= LINE - 1)
        def _():
            self.down_in(step, elem).wait_recv()
            if step < LINE - 2:

                @pl.when(self.z > 0)
                def _():
                    self.down(step + 1, elem).start()

            if elem < 2:
                self.across(self.z + 1 + step, elem).start()

    def relays(self):
        self.relay_b()
        for step in range(LINE - 1):
            for elem in (0, 1, 2, 3):
                self.relay(step, elem)

    def finish(self):
        for line in range(LINE):
            for elem in (0, 1):
                self.across_in(line, elem).wait_recv()
        for line in range(LINE):
            for elem in (0, 1):
                self.across(line, elem).wait_send()
        self.finish_sends()
        self.own_copy().wait()

    def finish_sends(self):
        self.across_b().wait_send()
        for step in range(LINE - 1):
            for elem in range(4):

                @pl.when(jnp.logical_and(self.z < LINE - 1, self.z - step >= 0))
                def _():
                    self.up(step, elem).wait_send()

                @pl.when(jnp.logical_and(self.z > 0, self.z + step <= LINE - 1))
                def _():
                    self.down(step, elem).wait_send()


def gather_kernel(src, out, *sems):
    greet_plane()
    gather = Gather(src, out, sems)
    gather.start()
    gather.relays()
    gather.finish()


ANY = pl.BlockSpec(memory_space=pl.ANY)
INSIDE = pl.BlockSpec(memory_space=pltpu.VMEM)


def kernel_params(collective_id):
    return pltpu.CompilerParams(
        collective_id=collective_id, has_side_effects=True, vmem_limit_bytes=VMEM_BYTES
    )


def gather_plane(rows):
    return pl.pallas_call(
        gather_kernel,
        out_shape=jax.ShapeDtypeStruct((2 * LINE,) + rows.shape, rows.dtype),
        in_specs=[INSIDE],
        out_specs=ANY,
        scratch_shapes=Gather.scratch(),
        compiler_params=kernel_params(1),
        name="gather_plane",
    )(rows)


class Reduce:
    CUTS = ((0, 64), (64, 64))

    @staticmethod
    def scratch(width):
        inbox = pltpu.VMEM((LINE, 128, width), jnp.bfloat16)
        return [inbox] * 3 + [pltpu.SemaphoreType.DMA((LINE, 2))] * 6

    def __init__(self, parts, refs):
        self.parts = parts
        self.y_in, self.up_in, self.dn_in = refs[:3]
        self.y_s, self.y_r, self.up_s, self.up_r, self.dn_s, self.dn_r = refs[3:]
        self.z, self.y, self.c, self.h = place()
        z = self.z
        self.order = (3 - 3 * (z // 2), (2 + 3 * z) % 5, 1 + z % 2, z)

    def rows(self, cut):
        return pl.ds(*self.CUTS[cut])

    def across(self, line, cut):
        return remote(
            self.parts.at[line * 2 + 1 - self.y, self.rows(cut)], self.y_in.at[line, self.rows(cut)],
            self.y_s.at[line, cut], self.y_r.at[line, cut], device(self.z, 1 - self.y, self.c, self.h),
        )

    def up(self, line, cut):
        return remote(
            self.parts.at[line * 2 + self.y, self.rows(cut)], self.up_in.at[line, self.rows(cut)],
            self.up_s.at[line, cut], self.up_r.at[line, cut], device(self.z + 1, self.y, self.c, self.h),
        )

    def down(self, line, cut):
        return remote(
            self.parts.at[line * 2 + self.y, self.rows(cut)], self.dn_in.at[line, self.rows(cut)],
            self.dn_s.at[line, cut], self.dn_r.at[line, cut], device(self.z - 1, self.y, self.c, self.h),
        )

    def start(self, place_at):
        for cut in range(2):
            self.across(self.order[place_at], cut).start()

    def own(self, line, cut):
        return self.parts.at[line * 2 + self.y, self.rows(cut)]

    def relay(self, place_at):
        line = self.order[place_at]
        for cut in range(2):
            rows = self.rows(cut)
            self.across(line, cut).wait_recv()
            target = self.parts.at[line * 2 + self.y]

            @pl.when(line > self.z)
            def _():
                @pl.when(self.z > 0)
                def _():
                    self.up(line, cut).wait_recv()
                    total = (
                        target[rows].astype(jnp.float32)
                        + self.y_in[line, rows].astype(jnp.float32)
                        + self.up_in[line, rows].astype(jnp.float32)
                    )
                    target[rows] = total.astype(jnp.bfloat16)

                @pl.when(self.z == 0)
                def _():
                    total = target[rows].astype(jnp.float32) + self.y_in[line, rows].astype(jnp.float32)
                    target[rows] = total.astype(jnp.bfloat16)

                self.up(line, cut).start()

            @pl.when(line < self.z)
            def _():
                @pl.when(self.z < LINE - 1)
                def _():
                    self.down(line, cut).wait_recv()
                    total = (
                        target[rows].astype(jnp.float32)
                        + self.y_in[line, rows].astype(jnp.float32)
                        + self.dn_in[line, rows].astype(jnp.float32)
                    )
                    target[rows] = total.astype(jnp.bfloat16)

                @pl.when(self.z == LINE - 1)
                def _():
                    total = target[rows].astype(jnp.float32) + self.y_in[line, rows].astype(jnp.float32)
                    target[rows] = total.astype(jnp.bfloat16)

                self.down(line, cut).start()

    def total(self, out):
        line = self.z
        for cut in range(2):
            rows = self.rows(cut)
            self.across(line, cut).wait_recv()
            out[rows] = self.parts[line * 2 + self.y, rows].astype(jnp.float32) + self.y_in[line, rows].astype(jnp.float32)
        for cut in range(2):
            rows = self.rows(cut)

            @pl.when(self.z > 0)
            def _():
                self.up(line, cut).wait_recv()
                out[rows] += self.up_in[line, rows].astype(jnp.float32)

            @pl.when(self.z < LINE - 1)
            def _():
                self.down(line, cut).wait_recv()
                out[rows] += self.dn_in[line, rows].astype(jnp.float32)

    def finish(self):
        for line in range(LINE):
            for cut in range(2):
                self.across(line, cut).wait_send()

                @pl.when(self.z < line)
                def _():
                    self.up(line, cut).wait_send()

                @pl.when(self.z > line)
                def _():
                    self.down(line, cut).wait_send()


def reduce_kernel(parts_in, out, parts, in_sem, *refs):
    load = pltpu.make_async_copy(parts_in, parts, in_sem)
    load.start()
    greet_plane()
    reduce = Reduce(parts, refs)
    load.wait()
    for place_at in range(4):
        reduce.start(place_at)
    for place_at in range(3):
        reduce.relay(place_at)
    reduce.total(out)
    reduce.finish()


def reduce_plane(parts):
    shape = parts.shape
    return pl.pallas_call(
        reduce_kernel,
        out_shape=jax.ShapeDtypeStruct(shape[1:], jnp.float32),
        in_specs=[ANY],
        out_specs=INSIDE,
        scratch_shapes=[pltpu.VMEM(shape, jnp.bfloat16), pltpu.SemaphoreType.DMA] + Reduce.scratch(shape[2]),
        compiler_params=kernel_params(2),
        name="reduce_plane",
    )(parts)


def dma(*shape):
    return pltpu.SemaphoreType.DMA(shape) if shape else pltpu.SemaphoreType.DMA


def local(src, dst, sem):
    return pltpu.make_async_copy(src, dst, sem)


class AttnSpread:
    @staticmethod
    def scratch():
        return [dma(3, 4), dma(3, 4), dma(3, 8), dma(3), dma(4), dma(4), dma(4), dma(4), dma(4), dma(4)]

    def __init__(self, weights, outs, sems):
        self.weights, (self.qkv, self.out_w) = weights, outs
        (self.s, self.f_s, self.r, self.own, self.x_s, self.x_r, self.c_s, self.c_r, self.o_s, self.o_r) = sems
        self.z, self.y, self.c, self.h = place()
        self.chip = self.z * 2 + self.y
        self.me = device(self.z, self.y, self.c, self.h)
        self.owner = self.h == self.y

    def source(self, kind, line):
        start = line * HD if kind == 0 else (line // 2) * HD
        return self.weights[kind].at[:, pl.ds(pl.multiple_of(start, HD), HD)]

    def slot(self, kind, chip):
        return self.qkv.at[chip, self.c, :, pl.ds(kind * HD, HD)]

    def push(self, kind, step):
        line = (self.z + step) % LINE
        return remote(
            self.source(kind, line), self.slot(kind, self.chip), self.s.at[kind, step], self.r.at[kind, self.chip],
            device(line, self.h, self.c, self.h),
        )

    def push_far(self, kind, step):
        line = (self.z + step) % LINE
        return remote(
            self.source(kind, line), self.slot(kind, self.chip), self.f_s.at[kind, step], self.r.at[kind, self.chip],
            device(line, self.h, self.c, 1 - self.h),
        )

    def keep(self, kind):
        return local(self.source(kind, self.z), self.slot(kind, self.chip), self.own.at[kind])

    def pull(self, kind, chip):
        ref = self.slot(kind, chip)
        return remote(ref, ref, self.s.at[kind, 0], self.r.at[kind, chip], self.me)

    def near(self, step):
        return ((self.z + LINE - step) % LINE) * 2 + self.y

    def far(self, step):
        return ((self.z + LINE - step) % LINE) * 2 + 1 - self.y

    def over(self, step):
        ref = self.qkv.at[self.near(step), self.c]
        return remote(ref, ref, self.x_s.at[step], self.x_r.at[step], device(self.z, self.y, self.c, 1 - self.h))

    def share(self, line, core):
        ref = self.qkv.at[pl.ds(line * 2, 2), core]
        return remote(ref, ref, self.c_s.at[line], self.c_r.at[line], device(self.z, self.y, 1 - self.c, self.h))

    def out_push(self):
        return remote(
            self.weights[3], self.out_w.at[self.y, self.c], self.o_s.at[0], self.o_r.at[0],
            device(self.z, 1 - self.y, self.c, self.h),
        )

    def out_keep(self):
        return local(self.weights[3], self.out_w.at[self.y, self.c], self.o_s.at[1])

    def out_pull(self):
        ref = self.out_w.at[1 - self.y, self.c]
        return remote(ref, ref, self.o_s.at[0], self.o_r.at[0], self.me)

    def out_over(self):
        ref = self.out_w.at[:, self.c]
        return remote(ref, ref, self.o_s.at[2], self.o_r.at[2], device(self.z, self.y, self.c, 1 - self.h))

    def out_share(self, core):
        ref = self.out_w.at[:, core]
        return remote(ref, ref, self.o_s.at[3], self.o_r.at[3], device(self.z, self.y, 1 - self.c, self.h))

    def start(self):
        for kind in range(3):

            @pl.when(self.owner)
            def _():
                self.keep(kind).start()

            @pl.when(jnp.logical_not(self.owner))
            def _():
                self.push(kind, 0).start()
                self.push_far(kind, 0).start()

        for step in range(1, LINE):
            for kind in range(3):
                self.push(kind, step).start()

            @pl.when(jnp.logical_not(self.owner))
            def _():
                for kind in range(3):
                    self.push_far(kind, step).start()

        @pl.when(self.owner)
        def _():
            self.out_keep().start()

        @pl.when(jnp.logical_not(self.owner))
        def _():
            self.out_push().start()

    def relay(self, step):
        @pl.when(self.owner)
        def _():
            for kind in range(3):
                if step:
                    self.pull(kind, self.near(step)).wait_recv()
                else:
                    self.keep(kind).wait()
            self.over(step).start()

    def relay_out(self):
        @pl.when(self.owner)
        def _():
            self.out_keep().wait()
            self.out_pull().wait_recv()
            self.out_over().start()

    def relay_share(self, step):
        @pl.when(jnp.logical_not(self.owner))
        def _():
            self.over(step).wait_recv()

        for kind in range(3):
            self.pull(kind, self.far(step)).wait_recv()
        self.share((self.z + LINE - step) % LINE, self.c).start()

    def relay_out_share(self):
        @pl.when(jnp.logical_not(self.owner))
        def _():
            self.out_over().wait_recv()

        self.out_share(self.c).start()

    def finish(self):
        for line in range(LINE):
            self.share(line, 1 - self.c).wait_recv()
            self.share(line, self.c).wait_send()
        self.out_share(1 - self.c).wait_recv()
        self.out_share(self.c).wait_send()
        for kind in range(3):
            for step in range(1, LINE):
                self.push(kind, step).wait_send()

        @pl.when(self.owner)
        def _():
            for step in range(LINE):
                self.over(step).wait_send()
            self.out_over().wait_send()

        @pl.when(jnp.logical_not(self.owner))
        def _():
            for kind in range(3):
                self.push(kind, 0).wait_send()
                for step in range(LINE):
                    self.push_far(kind, step).wait_send()
            self.out_push().wait_send()


class MlpSpread:
    @staticmethod
    def scratch():
        return [dma(2, 8), dma(2, 8), dma(2)]

    def __init__(self, weights, outs, sems):
        self.weights, self.outs = weights, outs
        self.s, self.r, self.own = sems
        self.z, self.y, self.c, self.h = place()
        self.chip = self.z * 2 + self.y
        self.part = weights[0].shape[1] // 8

    def columns(self, index):
        return pl.ds(pl.multiple_of(index * self.part, self.part), self.part)

    def push(self, kind, step):
        chip = (self.chip + step) % 8
        return remote(
            self.weights[kind].at[:, self.columns(chip)], self.outs[kind].at[self.chip], self.s.at[kind, step],
            self.r.at[kind, step], device(chip // 2, chip % 2, self.c, self.h),
        )

    def pull(self, kind, step):
        ref = self.outs[kind].at[(self.chip + 8 - step) % 8]
        return remote(ref, ref, self.s.at[kind, step], self.r.at[kind, step], device(self.z, self.y, self.c, self.h))

    def keep(self, kind):
        return local(self.weights[kind].at[:, self.columns(self.chip)], self.outs[kind].at[self.chip], self.own.at[kind])

    def start(self):
        for kind in range(2):
            self.keep(kind).start()
            for step in range(1, 8):
                self.push(kind, step).start()

    def finish(self):
        for kind in range(2):
            self.keep(kind).wait()
            for step in range(1, 8):
                self.pull(kind, step).wait_recv()
                self.push(kind, step).wait_send()


class MlpShare:
    @staticmethod
    def scratch():
        return [dma(2), dma(2, 2), dma(2, 2), dma(2, 2), dma(2, 2)]

    def __init__(self, quarters, outs, sems):
        self.quarters, self.outs = quarters, outs
        self.own, self.x_s, self.x_r, self.c_s, self.c_r = sems
        self.z, self.y, self.c, self.h = place()
        self.part = quarters[0].shape[2]

    def slot(self, kind, cut, half):
        columns = pl.ds(pl.multiple_of(half * self.part, self.part), self.part)
        return self.outs[kind].at[pl.ds(cut * 4, 4), self.c, :, columns]

    def keep(self, kind):
        columns = pl.ds(pl.multiple_of(self.h * self.part, self.part), self.part)
        return local(self.quarters[kind], self.outs[kind].at[:, self.c, :, columns], self.own.at[kind])

    def over(self, kind, cut, half):
        return remote(
            self.quarters[kind].at[pl.ds(cut * 4, 4)], self.slot(kind, cut, half), self.x_s.at[kind, cut],
            self.x_r.at[kind, cut], device(self.z, self.y, self.c, 1 - self.h),
        )

    def share(self, kind, cut, core):
        ref = self.outs[kind].at[pl.ds(cut * 4, 4), core]
        return remote(
            ref, ref, self.c_s.at[kind, cut], self.c_r.at[kind, cut], device(self.z, self.y, 1 - self.c, self.h)
        )

    def start(self):
        for kind in range(2):
            for cut in range(2):
                self.over(kind, cut, self.h).start()
            self.keep(kind).start()

    def relay(self):
        for kind in range(2):
            self.keep(kind).wait()
            for cut in range(2):
                self.over(kind, cut, 1 - self.h).wait_recv()
                self.share(kind, cut, self.c).start()

    def finish(self):
        for kind in range(2):
            for cut in range(2):
                self.share(kind, cut, 1 - self.c).wait_recv()
                self.share(kind, cut, self.c).wait_send()
                self.over(kind, cut, self.h).wait_send()


class DownSpread:
    @staticmethod
    def scratch():
        return [dma(1), dma(2), dma(2)]

    def __init__(self, weight, out, sems):
        self.weight, self.out = weight, out
        self.d_own, self.d_x, self.d_sib = sems
        self.z, self.y, self.c, self.h = place()

    def keep(self):
        return local(self.weight, self.out.at[self.h, self.c], self.d_own.at[0])

    def over(self):
        return remote(
            self.weight, self.out.at[self.h, self.c], self.d_x.at[0], self.d_x.at[1],
            device(self.z, self.y, self.c, 1 - self.h),
        )

    def over_in(self):
        ref = self.out.at[1 - self.h, self.c]
        return remote(ref, ref, self.d_x.at[0], self.d_x.at[1], device(self.z, self.y, self.c, self.h))

    def share(self):
        ref = self.out.at[:, self.c]
        return remote(ref, ref, self.d_sib.at[0], self.d_sib.at[1], device(self.z, self.y, 1 - self.c, self.h))

    def share_in(self):
        ref = self.out.at[:, 1 - self.c]
        return remote(ref, ref, self.d_sib.at[0], self.d_sib.at[1], device(self.z, self.y, self.c, self.h))

    def start(self):
        self.keep().start()
        self.over().start()

    def relay(self):
        self.keep().wait()
        self.over_in().wait_recv()
        self.share().start()

    def finish(self):
        self.share_in().wait_recv()
        self.share().wait_send()
        self.over().wait_send()


class NoteSpread:
    @staticmethod
    def scratch():
        return [dma(16), dma(16), dma(1)]

    def __init__(self, note, out, sems):
        self.note, self.out = note, out
        self.s, self.r, self.own = sems
        self.blk, self.h = lax.axis_index("blk"), lax.axis_index("head")

    def push(self, step):
        other = (self.blk + step) % 16
        return remote(self.note, self.out.at[self.blk], self.s.at[step], self.r.at[step], (other, self.h))

    def pull(self, step):
        ref = self.out.at[(self.blk + 16 - step) % 16]
        return remote(ref, ref, self.s.at[step], self.r.at[step], (self.blk, self.h))

    def keep(self):
        return local(self.note, self.out.at[self.blk], self.own.at[0])

    def start(self):
        self.keep().start()
        for step in range(1, 16):
            self.push(step).start()

    def finish(self):
        self.keep().wait()
        for step in range(1, 16):
            self.pull(step).wait_recv()
            self.push(step).wait_send()


def split_refs(refs, counts):
    groups, at = [], 0
    for count in counts:
        groups.append(refs[at : at + count])
        at += count
    return groups


def mid_kernel(
    attended, out_w, gate_in, up_in, wd, tokens, gain, cot_in,
    output, hidden_out, normed_out, active, grad_gate, grad_up, grad_out,
    normed, src, total, gate_w, up_w, down_w, gate_pre, up_pre, cot, parts, load_s, out_s, *refs,
):
    gather_sems, share_sems, down_sems, reduce_refs = split_refs(refs, (8, 5, 3, 9))
    load = local(cot_in, cot, load_s)
    load.start()
    z, y, c, h = place()
    greet(device(z, y, 1 - c, h))
    greet(device(z, y, c, 1 - h))
    greet_plane(2)
    gather = Gather(src, normed, gather_sems)
    share = MlpShare((gate_in, up_in), (gate_w, up_w), share_sems)
    downs = DownSpread(wd, down_w, down_sems)
    reduce = Reduce(parts, reduce_refs)
    rows, width = normed.shape[1:]
    hidden = gate_w.shape[3]
    step = hidden // 4
    pair = 2 * rows
    share.start()
    for place_at in range(4):
        line = reduce.order[place_at]
        both = attended[pl.ds(pl.multiple_of(line * pair, pair), pair)]
        parts[pl.ds(line * 2, 2)] = product(both, out_w[...]).astype(jnp.bfloat16).reshape(2, rows, width)
        reduce.start(place_at)
    for place_at in range(3):
        reduce.relay(place_at)
    reduce.total(total)
    hidden_rows = tokens[...].astype(jnp.float32) + total[...]
    hidden_out[...] = hidden_rows
    src[...] = (hidden_rows * rms_scale(hidden_rows) * gain[...]).astype(jnp.bfloat16)
    gather.start()
    share.relay()
    downs.start()
    reduce.finish()

    def forward(chip, own=False):
        shard = src if own else normed.at[chip]

        @pl.loop(0, 4)
        def _(tile):
            columns = pl.ds(pl.multiple_of(tile * step, step), step)
            gate_part = product(shard[...], gate_w[:, :, :, columns].reshape(width, step))
            up_part = product(shard[...], up_w[:, :, :, columns].reshape(width, step))
            gate_pre[chip, :, columns] = gate_part
            up_pre[chip, :, columns] = up_part
            active[chip, :, columns] = (gate_part * jax.nn.sigmoid(gate_part) * up_part).astype(jnp.bfloat16)

    def forward_own(distance):
        @pl.when(z - distance >= 0)
        def _():
            forward((z - distance) * 2 + y)

        @pl.when(z + distance <= LINE - 1)
        def _():
            forward((z + distance) * 2 + y)

    def forward_other(distance):
        def one(line):
            for elem in (0, 1):
                gather.across_in(line, elem).wait_recv()
            forward(line * 2 + 1 - y)

        if distance == 0:
            one(z)
        else:

            @pl.when(z - distance >= 0)
            def _():
                one(z - distance)

            @pl.when(z + distance <= LINE - 1)
            def _():
                one(z + distance)

    def relay(distance):
        for elem in (2, 0, 1, 3):
            gather.relay(distance - 1, elem)

    gather.relay_b()
    share.finish()
    forward(z * 2 + y, own=True)
    relay(1)
    forward_other(0)
    forward_own(1)
    relay(2)
    forward_other(1)
    forward_own(2)
    relay(3)
    downs.relay()
    forward_other(2)
    forward_own(3)
    forward_other(3)
    gather.own_copy().wait()
    store = local(normed, normed_out, out_s)
    store.start()
    downs.finish()

    def contribute(line):
        both = pl.ds(line * 2, 2)

        @pl.loop(0, 4)
        def _(tile):
            columns = pl.ds(pl.multiple_of(tile * (width // 4), width // 4), width // 4)
            part = product(
                active[both].reshape(pair, hidden), down_w[:, :, :, columns].reshape(hidden, width // 4)
            )
            parts[both, :, columns] = part.astype(jnp.bfloat16).reshape(2, rows, width // 4)

    for place_at in range(4):
        contribute(reduce.order[place_at])
        reduce.start(place_at)
    load.wait()

    def backward(line):
        both = pl.ds(line * 2, 2)

        @pl.loop(0, 4)
        def _(tile):
            columns = pl.ds(pl.multiple_of(tile * step, step), step)
            grad_active = times_transposed(cot[both].reshape(pair, width), down_w[tile // 2, tile % 2])
            gate_part = gate_pre[both, :, columns].reshape(pair, step)
            up_part = up_pre[both, :, columns].reshape(pair, step)
            sigmoid = jax.nn.sigmoid(gate_part)
            silu = gate_part * sigmoid
            gate_grad = grad_active * up_part * sigmoid * (1.0 + gate_part * (1.0 - sigmoid))
            grad_gate[both, :, columns] = gate_grad.astype(jnp.bfloat16).reshape(2, rows, step)
            grad_up[both, :, columns] = (grad_active * silu).astype(jnp.bfloat16).reshape(2, rows, step)

        @pl.loop(0, 4)
        def _(tile):
            columns = pl.ds(pl.multiple_of(tile * (width // 4), width // 4), width // 4)
            chips = pl.ds(tile * 2, 2)
            part = times_transposed(grad_gate[both].reshape(pair, hidden), gate_w[chips].reshape(width // 4, hidden))
            part += times_transposed(grad_up[both].reshape(pair, hidden), up_w[chips].reshape(width // 4, hidden))
            grad_out[both, :, columns] = part.astype(jnp.bfloat16).reshape(2, rows, width // 4)

    for place_at in range(3):
        backward(place_at)
        reduce.relay(place_at)
    backward(3)
    reduce.total(total)
    output[...] = (hidden_out[...] + total[...]).astype(jnp.bfloat16)
    reduce.finish()
    store.wait()
    for line in range(LINE):
        for elem in (0, 1):
            gather.across(line, elem).wait_send()
    gather.finish_sends()


def mid(attended, out_w, gate, up, wd, tokens, gain, cot):
    eight, depth, part = gate.shape
    rows, width = tokens.shape
    hidden = 2 * part

    def room(*dims, dtype=jnp.bfloat16):
        return pltpu.VMEM(dims, dtype)

    def shape(*dims, dtype=jnp.bfloat16):
        return jax.ShapeDtypeStruct(dims, dtype)

    f32 = jnp.float32
    return pl.pallas_call(
        mid_kernel,
        out_shape=(
            shape(rows, width),
            shape(rows, width, dtype=f32),
            shape(8, rows, width),
            shape(8, rows, hidden),
            shape(8, rows, hidden),
            shape(8, rows, hidden),
            shape(8, rows, width),
        ),
        in_specs=[INSIDE] * 7 + [ANY],
        out_specs=(INSIDE, INSIDE, ANY, INSIDE, INSIDE, INSIDE, INSIDE),
        scratch_shapes=[
            room(8, rows, width), room(rows, width), room(rows, width, dtype=f32),
            room(eight, 2, depth, hidden), room(eight, 2, depth, hidden), room(2, 2, *wd.shape),
            room(8, rows, hidden, dtype=f32), room(8, rows, hidden, dtype=f32),
            room(8, rows, width), room(8, rows, width), dma(), dma(),
        ] + Gather.scratch() + MlpShare.scratch() + DownSpread.scratch() + Reduce.scratch(width),
        compiler_params=kernel_params(8),
        name="mid",
    )(attended, out_w, gate, up, wd, tokens, gain, cot)


def column_of(row):
    size = row.shape[1]
    same = lax.broadcasted_iota(jnp.int32, (size, size), 0) == lax.broadcasted_iota(jnp.int32, (size, size), 1)
    return jnp.sum(jnp.where(same, row, 0.0), axis=1, keepdims=True)


def row_of(column):
    size = column.shape[0]
    same = lax.broadcasted_iota(jnp.int32, (size, size), 0) == lax.broadcasted_iota(jnp.int32, (size, size), 1)
    return jnp.sum(jnp.where(same, column, 0.0), axis=0, keepdims=True)


def front_kernel(
    tokens, cot, note, inv_freqs, wq, wk, wv, wo, wg, wu,
    kv_out, normed_out, qkv_out, out_w, notes, cos_table, sine_table, query, attended_out, attended_low_out,
    log_out, cot_out, gate, up,
    gathered, normed, qkv_w, gain, query_ids, key_ids, kv, keys, scores, total,
    own, x_s, x_r, c_s, c_r, store_s, *sems,
):
    z, y, c, h = place()
    tok_sems, note_sems, attn_sems, cot_sems, mlp_sems = split_refs(sems, (8, 3, 10, 8, 3))
    greet_all(16, 2)
    rows, width = tokens.shape[0], HD
    pair = 2 * rows
    tok = Gather(tokens, gathered, tok_sems)
    notices = NoteSpread(note, notes, note_sems)
    attn = AttnSpread((wq, wk, wv, wo), (qkv_w, out_w), attn_sems)
    cots = Gather(cot, cot_out, cot_sems)
    mlp = MlpSpread((wg, wu), (gate, up), mlp_sems)

    def keep(cut):
        part = pl.ds(cut * 2, 2)
        return local(kv.at[part], keys.at[part, c, h], own.at[cut])

    def over(cut, half):
        part = pl.ds(cut * 2, 2)
        return remote(kv.at[part], keys.at[part, c, half], x_s.at[cut], x_r.at[cut], device(z, y, c, 1 - h))

    def share(cut, core):
        ref = keys.at[pl.ds(cut * 2, 2), core]
        return remote(ref, ref, c_s.at[cut], c_r.at[cut], device(z, y, 1 - c, h))

    def tables():
        for blk in range(16):
            gain[:, pl.ds(blk * rows, rows)] = notes[blk, 4:5, :]
        for chip in range(8):
            part = pl.ds(chip * rows, rows)
            mine = notes[2 * chip + c]
            angles = column_of(jnp.where(h == 0, mine[0:1], mine[1:2])) * inv_freqs[...]
            cos_table[part] = jnp.cos(angles)
            sine_table[part] = jnp.sin(angles)
            query_ids[part] = column_of(jnp.where(h == 0, mine[2:3], mine[3:4]))
            for piece in range(4):
                key_ids[chip, :, pl.ds(piece * rows, rows)] = notes[2 * chip + piece // 2, 2 + piece % 2 : 3 + piece % 2, :]

    def project(cut):
        part = pl.ds(cut * pair, pair)
        inputs = gathered[pl.ds(cut * 2, 2)].reshape(pair, tokens.shape[1]).astype(jnp.float32)
        rows_normed = (inputs * rms_scale(inputs) * gain[...]).astype(jnp.bfloat16)
        normed[part] = rows_normed
        cos_rows, sine_rows = cos_table[part], sine_table[part]

        def turn(lower, upper):
            return (
                (lower * cos_rows - upper * sine_rows).astype(jnp.bfloat16),
                (upper * cos_rows + lower * sine_rows).astype(jnp.bfloat16),
            )

        def weight(columns):
            return qkv_w[:, :, :, columns].reshape(tokens.shape[1], columns.size)

        half = width // 2
        projected = product(rows_normed, weight(pl.ds(0, width)))
        lower, upper = turn(projected[:, :half], projected[:, half:])
        query[part, :half] = (lower.astype(jnp.float32) * HD**-0.5).astype(jnp.bfloat16)
        query[part, half:] = (upper.astype(jnp.float32) * HD**-0.5).astype(jnp.bfloat16)
        projected = product(rows_normed, weight(pl.ds(width, 2 * width)))
        lower, upper = turn(projected[:, :half], projected[:, half:width])
        both = pl.ds(cut * 2, 2)
        kv[both, :, :half] = lower.reshape(2, rows, half)
        kv[both, :, half:width] = upper.reshape(2, rows, half)
        kv[both, :, width:] = projected[:, width:].astype(jnp.bfloat16).reshape(2, rows, width)
        over(cut, h).start()
        keep(cut).start()

    def pass_on(cut):
        keep(cut).wait()
        over(cut, 1 - h).wait_recv()
        share(cut, c).start()

    def attend(place_at):
        part = pl.ds(place_at * pair, pair)
        count = min(2 * place_at + 3, 8)
        ids = query_ids[part]

        def maxima(block, best):
            key = keys[block, :, :, :, :width].reshape(4 * rows, width)
            part_scores = times_transposed(query[part], key)
            part_scores = jnp.where(key_ids[block] <= ids, part_scores, -1e30)
            scores[block] = part_scores
            for lane in range(4 * rows // 128):
                best = jnp.maximum(best, part_scores[:, lane * 128 : lane * 128 + 128])
            return best

        best = lax.fori_loop(0, count, maxima, jnp.full((pair, 128), -1e30, jnp.float32))
        row_max = jnp.max(best, axis=1, keepdims=True)
        total[...] = jnp.zeros_like(total)

        def mix(block, sums):
            weights = jnp.exp(scores[block] - row_max)
            value = keys[block, :, :, :, width:].reshape(4 * rows, width)
            total[...] += product(weights.astype(jnp.bfloat16), value)
            for lane in range(4 * rows // 128):
                sums = sums + weights[:, lane * 128 : lane * 128 + 128]
            return sums

        sums = lax.fori_loop(0, count, mix, jnp.zeros((pair, 128), jnp.float32))
        row_sum = jnp.sum(sums, axis=1, keepdims=True)
        mixed = total[...] / row_sum
        attended_out[part] = mixed
        attended_low_out[part] = mixed.astype(jnp.bfloat16)
        log_out[place_at] = row_of(row_max + jnp.log(row_sum))

    order = (2, 0, 1, 3)
    attn.start()
    tok.start()
    notices.start()
    tok.relay_b()
    attn.relay(0)
    for elem in order:
        tok.relay(0, elem)
    attn.relay(1)
    attn.relay(2)
    for elem in order:
        tok.relay(1, elem)
    attn.relay(3)
    attn.relay_out()
    notices.finish()
    tables()
    for elem in order:
        tok.relay(2, elem)
    cots.start()
    mlp.start()
    for step in range(LINE):
        attn.relay_share(step)
    attn.relay_out_share()
    tok.finish()
    attn.finish()
    store_qkv = local(qkv_w, qkv_out, store_s.at[0])
    store_qkv.start()
    for cut in range(LINE):
        project(cut)
    store_normed = local(normed, normed_out, store_s.at[1])
    store_normed.start()
    cots.relay_b()
    for elem in order:
        cots.relay(0, elem)
    pass_on(0)
    pass_on(1)
    share(0, 1 - c).wait_recv()
    share(1, 1 - c).wait_recv()
    attend(0)
    for elem in order:
        cots.relay(1, elem)
    pass_on(2)
    share(2, 1 - c).wait_recv()
    attend(1)
    pass_on(3)
    share(3, 1 - c).wait_recv()
    store = local(keys, kv_out, store_s.at[2])
    store.start()
    attend(2)
    for elem in order:
        cots.relay(2, elem)
    attend(3)
    cots.finish()
    mlp.finish()
    for cut in range(LINE):
        share(cut, c).wait_send()
        over(cut, h).wait_send()
    store.wait()
    store_normed.wait()
    store_qkv.wait()


def front(tokens, cot, note, inv_freqs, wq, wk, wv, wo, wg, wu):
    rows, width = tokens.shape
    depth, part = wg.shape[0], wg.shape[1] // 8
    token_rows = 8 * rows

    def room(*dims, dtype=jnp.bfloat16):
        return pltpu.VMEM(dims, dtype)

    def shape(*dims, dtype=jnp.bfloat16):
        return jax.ShapeDtypeStruct(dims, dtype)

    f32 = jnp.float32
    return pl.pallas_call(
        front_kernel,
        out_shape=(
            shape(8, 2, 2, rows, 2 * HD),
            shape(token_rows, width),
            shape(8, 2, depth, 3 * HD),
            shape(2, 2, wo.shape[0], width),
            shape(16, *note.shape, dtype=f32),
            shape(token_rows, HD // 2, dtype=f32),
            shape(token_rows, HD // 2, dtype=f32),
            shape(token_rows, HD),
            shape(token_rows, HD, dtype=f32),
            shape(token_rows, HD),
            shape(LINE, 1, token_rows // LINE, dtype=f32),
            shape(8, *cot.shape),
            shape(8, depth, part),
            shape(8, depth, part),
        ),
        in_specs=[INSIDE] * 10,
        out_specs=(ANY, ANY, ANY, ANY) + (INSIDE,) * 7 + (ANY, ANY, ANY),
        scratch_shapes=[
            room(8, rows, width),
            room(token_rows, width),
            room(8, 2, depth, 3 * HD),
            room(1, width, dtype=f32),
            room(token_rows, 1, dtype=f32),
            room(8, 1, 4 * rows, dtype=f32),
            room(8, rows, 2 * HD),
            room(8, 2, 2, rows, 2 * HD),
            room(8, token_rows // LINE, 4 * rows, dtype=f32),
            room(token_rows // LINE, HD, dtype=f32),
        ]
        + [dma(4)] * 5
        + [dma(3)]
        + Gather.scratch()
        + NoteSpread.scratch()
        + AttnSpread.scratch()
        + Gather.scratch()
        + MlpSpread.scratch(),
        compiler_params=kernel_params(3),
        name="front",
    )(tokens, cot, note, inv_freqs, wq, wk, wv, wo, wg, wu)


def add_into(target, *others):
    total = target[...].astype(jnp.float32)
    for other in others:
        total += other[...].astype(jnp.float32)
    target[...] = total.astype(target.dtype)


class QuarterReduce:
    @staticmethod
    def scratch(depth, wide):
        store = pltpu.VMEM((8, 2, depth, wide), jnp.bfloat16)
        sib = pltpu.VMEM((8, depth, wide), jnp.bfloat16)
        over = pltpu.VMEM((8, depth, wide // 2), jnp.bfloat16)
        return [store, store, sib, sib, over, over] + [dma(2)] + [dma(2, 2)] * 4

    def __init__(self, sources, outs, refs):
        self.sources, self.outs = sources, outs
        self.store, self.sib, self.box = refs[0:2], refs[2:4], refs[4:6]
        self.load_s, self.c_s, self.c_r, self.x_s, self.x_r = refs[6:]
        self.z, self.y, self.c, self.h = place()
        self.part = self.box[0].shape[2]

    def columns(self, half):
        return pl.ds(pl.multiple_of(half * self.part, self.part), self.part)

    def load(self, kind):
        return local(self.sources[kind], self.store[kind], self.load_s.at[kind])

    def share(self, kind, cut):
        chips = pl.ds(cut * 4, 4)
        return remote(
            self.store[kind].at[chips, 1 - self.c], self.sib[kind].at[chips], self.c_s.at[kind, cut],
            self.c_r.at[kind, cut], device(self.z, self.y, 1 - self.c, self.h),
        )

    def over(self, kind, cut):
        chips = pl.ds(cut * 4, 4)
        return remote(
            self.store[kind].at[chips, self.c, :, self.columns(1 - self.h)], self.box[kind].at[chips],
            self.x_s.at[kind, cut], self.x_r.at[kind, cut], device(self.z, self.y, self.c, 1 - self.h),
        )

    def start_loads(self):
        for kind in range(2):
            self.load(kind).start()

    def start(self, kind):
        self.load(kind).wait()
        for cut in range(2):
            self.share(kind, cut).start()

    def relay(self, kind):
        columns = self.columns(1 - self.h)
        for cut in range(2):
            self.share(kind, cut).wait_recv()

            @pl.loop(cut * 4, cut * 4 + 4)
            def _(chip):
                add_into(self.store[kind].at[chip, self.c, :, columns], self.sib[kind].at[chip, :, columns])

            self.over(kind, cut).start()

    def finish(self, kind):
        columns = self.columns(self.h)
        for cut in range(2):
            self.over(kind, cut).wait_recv()

            @pl.loop(cut * 4, cut * 4 + 4)
            def _(chip):
                total = self.store[kind][chip, self.c, :, columns].astype(jnp.float32)
                total += self.sib[kind][chip, :, columns].astype(jnp.float32)
                total += self.box[kind][chip].astype(jnp.float32)
                self.outs[kind][chip] = total.astype(jnp.bfloat16)

        for cut in range(2):
            self.share(kind, cut).wait_send()
            self.over(kind, cut).wait_send()


class QuarterScatter:
    @staticmethod
    def scratch():
        return [dma(2, 8), dma(2, 8), dma(2)]

    def __init__(self, quarters, outs, sems):
        self.quarters, self.outs = quarters, outs
        self.s, self.r, self.own = sems
        self.z, self.y, self.c, self.h = place()
        self.chip = self.z * 2 + self.y
        self.part = quarters[0].shape[2]

    def columns(self, chip):
        return pl.ds(pl.multiple_of(chip * self.part, self.part), self.part)

    def push(self, kind, step):
        target = (self.chip + step) % 8
        return remote(
            self.quarters[kind].at[target], self.outs[kind].at[:, self.columns(self.chip)], self.s.at[kind, step],
            self.r.at[kind, step], device(target // 2, target % 2, self.c, self.h),
        )

    def pull(self, kind, step):
        ref = self.outs[kind].at[:, self.columns((self.chip + 8 - step) % 8)]
        return remote(ref, ref, self.s.at[kind, step], self.r.at[kind, step], device(self.z, self.y, self.c, self.h))

    def keep(self, kind):
        return local(self.quarters[kind].at[self.chip], self.outs[kind].at[:, self.columns(self.chip)], self.own.at[kind])

    def start(self):
        for kind in range(2):
            self.keep(kind).start()
            for step in range(1, 8):
                self.push(kind, step).start()

    def finish(self):
        for kind in range(2):
            self.keep(kind).wait()
            for step in range(1, 8):
                self.pull(kind, step).wait_recv()
                self.push(kind, step).wait_send()


class DownReduce:
    @staticmethod
    def scratch(rows, width):
        return [
            pltpu.VMEM((2, 2, rows, width), jnp.bfloat16),
            pltpu.VMEM((2, rows, width), jnp.bfloat16),
            pltpu.VMEM((rows, width), jnp.bfloat16),
            dma(2), dma(2),
        ]

    def __init__(self, out, refs):
        self.out = out
        self.store, self.sib, self.box, self.c_sr, self.x_sr = refs
        self.z, self.y, self.c, self.h = place()

    def share(self):
        return remote(
            self.store.at[:, 1 - self.c], self.sib, self.c_sr.at[0], self.c_sr.at[1],
            device(self.z, self.y, 1 - self.c, self.h),
        )

    def over(self):
        return remote(
            self.store.at[1 - self.h, self.c], self.box, self.x_sr.at[0], self.x_sr.at[1],
            device(self.z, self.y, self.c, 1 - self.h),
        )

    def relay(self):
        self.share().wait_recv()
        add_into(self.store.at[1 - self.h, self.c], self.sib.at[1 - self.h])
        self.over().start()

    def finish(self):
        self.over().wait_recv()
        total = self.store[self.h, self.c].astype(jnp.float32) + self.sib[self.h].astype(jnp.float32)
        self.out[...] = total + self.box[...].astype(jnp.float32)
        self.share().wait_send()
        self.over().wait_send()


def turn_kernel(
    parts_in, normed_in, gate_grad_in, up_grad_in, active_in, cot_in, hidden, gain, cot,
    gathered, grad_hidden, gain_term, gate, up, down,
    parts, normed, gate_grad, up_grad, active, cot_all, grad_normed, branch, load_s, *refs,
):
    reduce_refs, gather_sems, quarter_refs, down_refs = split_refs(refs, (9, 8, 11, 5))
    loads = [
        local(parts_in, parts, load_s.at[0]),
        local(normed_in, normed, load_s.at[1]),
        local(gate_grad_in, gate_grad, load_s.at[2]),
        local(up_grad_in, up_grad, load_s.at[3]),
        local(active_in, active, load_s.at[4]),
        local(cot_in, cot_all, load_s.at[5]),
    ]
    for load in loads:
        load.start()
    z, y, c, h = place()
    grads = QuarterReduce((None, None), (gate, up), quarter_refs)
    downs = DownReduce(down, down_refs)
    greet(device(z, y, 1 - c, h))
    greet(device(z, y, c, 1 - h))
    greet_plane(2)
    reduce = Reduce(parts, reduce_refs)
    gather = Gather(branch, gathered, gather_sems)
    loads[0].wait()
    for place_at in range(4):
        reduce.start(place_at)
    for load in loads[1:]:
        load.wait()
    tokens, width = normed.shape
    depth, wide = quarter_refs[0].shape[2:]

    def weight_grad(kind, first, last):
        source = (gate_grad, up_grad)[kind]
        store = quarter_refs[kind]

        @pl.loop(first, last)
        def _(tile):
            columns = pl.ds(pl.multiple_of(tile * 2 * depth, 2 * depth), 2 * depth)
            part = transposed_times(normed[:, columns], source[...])
            store[tile] = part.astype(jnp.bfloat16).reshape(2, depth, wide)

    down_store = down_refs[0]
    down_rows = down_store.shape[2]

    def down_grad(tile):
        columns = pl.ds(tile * down_rows, down_rows)

        @pl.loop(0, 4)
        def _(piece):
            part_columns = pl.ds(pl.multiple_of(piece * (width // 4), width // 4), width // 4)
            part = transposed_times(active[:, columns], cot_all[:, part_columns])
            down_store[tile // 2, tile % 2, :, part_columns] = part.astype(jnp.bfloat16)

    weight_grad(0, 0, 4)
    grads.share(0, 0).start()
    weight_grad(0, 4, 8)
    grads.share(0, 1).start()
    reduce.relay(0)
    weight_grad(1, 0, 4)
    grads.relay(0)
    grads.share(1, 0).start()
    weight_grad(1, 4, 8)
    grads.share(1, 1).start()
    reduce.relay(1)
    grads.relay(1)
    reduce.relay(2)
    reduce.total(grad_normed)
    inputs = hidden[...]
    inv_scale = rms_scale(inputs)
    unit_rows = inputs * inv_scale
    grad_unit = grad_normed[...] * gain[...]
    gain_term[...] = jnp.sum(grad_normed[...] * unit_rows, axis=0, keepdims=True)
    mean = jnp.mean(grad_unit * unit_rows, axis=-1, keepdims=True)
    grad_rows = cot[...].astype(jnp.float32) + inv_scale * (grad_unit - unit_rows * mean)
    grad_hidden[...] = grad_rows
    branch[...] = grad_rows.astype(jnp.bfloat16)
    gather.start()
    gather.relay_b()
    for tile in range(4):
        down_grad(tile)
    downs.share().start()
    for elem in (2, 0, 1, 3):
        gather.relay(0, elem)
    downs.relay()
    grads.finish(0)
    for elem in (2, 0, 1, 3):
        gather.relay(1, elem)
    grads.finish(1)
    for elem in (2, 0, 1, 3):
        gather.relay(2, elem)
    downs.finish()
    gather.finish()
    reduce.finish()


def turn(parts, normed, gate_grad, up_grad, active, cot_all, hidden, gain, cot):
    eight, rows, width = parts.shape
    wide = gate_grad.shape[1]
    depth = normed.shape[1] // 16
    down_rows = wide // 4

    def room(*dims, dtype=jnp.bfloat16):
        return pltpu.VMEM(dims, dtype)

    def shape(*dims, dtype=jnp.bfloat16):
        return jax.ShapeDtypeStruct(dims, dtype)

    f32 = jnp.float32
    return pl.pallas_call(
        turn_kernel,
        out_shape=(
            shape(eight, rows, width),
            shape(rows, width, dtype=f32),
            shape(1, width, dtype=f32),
            shape(8, depth, wide // 2),
            shape(8, depth, wide // 2),
            shape(down_rows, width, dtype=f32),
        ),
        in_specs=[ANY] * 6 + [INSIDE] * 3,
        out_specs=(ANY,) + (INSIDE,) * 5,
        scratch_shapes=[
            room(*parts.shape), room(*normed.shape), room(*gate_grad.shape), room(*up_grad.shape),
            room(*active.shape), room(*cot_all.shape), room(rows, width, dtype=f32), room(rows, width), dma(6),
        ]
        + Reduce.scratch(width)
        + Gather.scratch()
        + QuarterReduce.scratch(depth, wide)
        + DownReduce.scratch(down_rows, width),
        compiler_params=kernel_params(9),
        name="turn",
    )(parts, normed, gate_grad, up_grad, active, cot_all, hidden, gain, cot)


class OutGrad:
    @staticmethod
    def scratch(rows, width):
        def room(*dims):
            return pltpu.VMEM(dims, jnp.bfloat16)

        return [room(2, 2, rows, width), room(2, rows, width), room(2, rows, width), dma(2), dma(2), dma(2), dma(1)]

    def __init__(self, out, refs):
        self.out = out
        self.store, self.sib, self.box, self.c_sr, self.x_sr, self.y_sr, self.own = refs
        self.z, self.y, self.c, self.h = place()
        self.me = device(self.z, self.y, self.c, self.h)
        self.owner = self.h == self.y

    def share(self):
        return remote(
            self.store.at[:, 1 - self.c], self.sib, self.c_sr.at[0], self.c_sr.at[1],
            device(self.z, self.y, 1 - self.c, self.h),
        )

    def over(self):
        return remote(
            self.store.at[:, self.c], self.box, self.x_sr.at[0], self.x_sr.at[1],
            device(self.z, self.y, self.c, 1 - self.h),
        )

    def move(self):
        return remote(
            self.store.at[1 - self.y, self.c], self.out, self.y_sr.at[0], self.y_sr.at[1],
            device(self.z, 1 - self.y, self.c, self.h),
        )

    def keep(self):
        return local(self.store.at[self.y, self.c], self.out, self.own.at[0])

    def relay(self):
        self.share().wait_recv()
        for pair in range(2):
            add_into(self.store.at[pair, self.c], self.sib.at[pair])

        @pl.when(jnp.logical_not(self.owner))
        def _():
            self.over().start()

    def send(self):
        @pl.when(self.owner)
        def _():
            self.over().wait_recv()
            for pair in range(2):
                add_into(self.store.at[pair, self.c], self.box.at[pair])
            self.move().start()
            self.keep().start()

    def finish(self):
        self.share().wait_send()

        @pl.when(jnp.logical_not(self.owner))
        def _():
            remote(self.out, self.out, self.y_sr.at[0], self.y_sr.at[1], self.me).wait_recv()
            self.over().wait_send()

        @pl.when(self.owner)
        def _():
            self.keep().wait()
            self.move().wait_send()


def attend_back_kernel(
    query, keys_in, branch_in, out_w, attended, attended_low, log_row, notes, cos_table, sine_table, gate_in, up_in,
    side_out, grad_query, gate, up, out_grad,
    keys, branch, grad_out, delta_row, query_row, key_column, grad_rot, parts, grad_key, grad_value, sib_in, x_in, z_in,
    load_s, c_s, c_r, x_s, x_r, z_s, z_r, *sems,
):
    z, y, c, h = place()
    mate = z + 1 - 2 * (z % 2)
    loads = [local(keys_in, keys, load_s.at[0]), local(branch_in, branch, load_s.at[1])]
    for load in loads:
        load.start()
    greet_all(16, 2)
    scatter_sems, out_refs = split_refs(sems, (3, 7))
    scatter = QuarterScatter((gate_in, up_in), (gate, up), scatter_sems)
    outs = OutGrad(out_grad, out_refs)
    scatter.start()
    width = query.shape[1]
    rows = branch.shape[1]
    pair = 2 * rows
    block_rows = 4 * rows

    def share(block):
        return remote(
            parts.at[block, 1 - c], sib_in.at[block], c_s.at[block], c_r.at[block], device(z, y, 1 - c, h)
        )

    def over(block):
        return remote(
            parts.at[block, c, 1 - h], x_in.at[block], x_s.at[block], x_r.at[block], device(z, y, c, 1 - h)
        )

    def columns(kind):
        return pl.ds(pl.multiple_of(kind * width, width), width)

    def across(block):
        return remote(
            parts.at[block, c, h, :, columns(1 - z % 2)], z_in.at[block], z_s.at[block], z_r.at[block],
            device(mate, y, c, h),
        )

    def stage_two(block):
        share(block).wait_recv()
        add_into(parts.at[block, c, 1 - h], sib_in.at[block, 1 - h])
        over(block).start()

    def stage_three(block):
        over(block).wait_recv()
        add_into(parts.at[block, c, h], sib_in.at[block, h], x_in.at[block])
        across(block).start()

    def turn_back(values, part):
        half = width // 2
        lower, upper = values[:, :half], values[:, half:]
        cos_rows, sine_rows = cos_table[part], sine_table[part]
        return (
            (lower * cos_rows + upper * sine_rows).astype(jnp.bfloat16),
            (upper * cos_rows - lower * sine_rows).astype(jnp.bfloat16),
        )

    def stage_four(block):
        across(block).wait_recv()
        total = parts[block, c, h, :, columns(z % 2)].astype(jnp.float32) + z_in[block].astype(jnp.float32)
        part = pl.ds(block * rows, rows)

        @pl.when(z % 2 == 0)
        def _():
            lower, upper = turn_back(total, part)
            side_out[part, : width // 2] = lower
            side_out[part, width // 2 :] = upper

        @pl.when(z % 2 == 1)
        def _():
            side_out[part] = total.astype(jnp.bfloat16)

    for chip in range(8):
        mine = notes[2 * chip + c]
        query_row[chip // 2, :, pl.ds((chip % 2) * rows, rows)] = jnp.where(h == 0, mine[2:3], mine[3:4])
        for piece in range(4):
            row = notes[2 * chip + piece // 2, 2 + piece % 2 : 3 + piece % 2, :]
            key_column[chip, pl.ds(piece * rows, rows)] = column_of(row)
    for load in loads:
        load.wait()
    grad_rot[...] = jnp.zeros_like(grad_rot)
    for place_at in range(LINE):
        part = pl.ds(place_at * pair, pair)
        grad_rows = times_transposed(branch[pl.ds(place_at * 2, 2)].reshape(pair, branch.shape[2]), out_w[...])
        grad_rows = grad_rows.astype(jnp.bfloat16)
        grad_out[part] = grad_rows
        delta = jnp.sum(grad_rows.astype(jnp.float32) * attended[part], axis=1, keepdims=True)
        delta_row[place_at] = row_of(delta)
    out_store = out_refs[0]

    @pl.loop(0, 4)
    def _(tile):
        tile_columns = pl.ds(pl.multiple_of(tile * 512, 512), 512)
        part = transposed_times(attended_low[...], branch[:, :, tile_columns].reshape(8 * rows, 512))
        out_store[:, :, :, tile_columns] = part.astype(jnp.bfloat16).reshape(2, 2, out_store.shape[2], 512)

    outs.share().start()
    for block in range(8):
        key = keys[block, :, :, :, :width].reshape(block_rows, width)
        value = keys[block, :, :, :, width:].reshape(block_rows, width)
        grad_key[...] = jnp.zeros_like(grad_key)
        grad_value[...] = jnp.zeros_like(grad_value)

        @pl.loop(max(0, (block - 1) // 2), LINE)
        def _(place_at):
            part = pl.ds(pl.multiple_of(place_at * pair, pair), pair)
            part_scores = times_transposed(key, query[part])
            visible = key_column[block] <= query_row[place_at]
            weights = jnp.where(visible, jnp.exp(part_scores - log_row[place_at]), 0.0)
            grad_weights = times_transposed(value, grad_out[part])
            grad_scores = (weights * (grad_weights - delta_row[place_at])).astype(jnp.bfloat16)
            grad_key[...] += product(grad_scores, query[part])
            grad_value[...] += product(weights.astype(jnp.bfloat16), grad_out[part])
            grad_rot[part] += transposed_times(grad_scores, key)

        parts[block, :, :, :, :width] = grad_key[...].astype(jnp.bfloat16).reshape(2, 2, rows, width)
        parts[block, :, :, :, width:] = grad_value[...].astype(jnp.bfloat16).reshape(2, 2, rows, width)
        share(block).start()
        if block == 0:
            outs.relay()
        if block >= 1:
            stage_two(block - 1)
        if block >= 4:
            stage_three(block - 4)
    stage_two(7)
    outs.send()
    for place_at in range(LINE):
        part = pl.ds(place_at * pair, pair)
        lower, upper = turn_back(grad_rot[part] * HD**-0.5, part)
        grad_query[part, : width // 2] = lower
        grad_query[part, width // 2 :] = upper
    for block in range(4, 8):
        stage_three(block)
        stage_four(block - 4)
    for block in range(4, 8):
        stage_four(block)
    for block in range(8):
        share(block).wait_send()
        over(block).wait_send()
        across(block).wait_send()
    scatter.finish()
    outs.finish()


def attend_back(query, keys, branch, out_w, attended, attended_low, log_row, notes, cos_table, sine_table, gate, up, out_rows):
    eight, _, _, rows, width = keys.shape
    tokens = query.shape[0]
    depth, part = gate.shape[1:]

    def room(*dims, dtype=jnp.bfloat16):
        return pltpu.VMEM(dims, dtype)

    def shape(*dims, dtype=jnp.bfloat16):
        return jax.ShapeDtypeStruct(dims, dtype)

    f32 = jnp.float32
    return pl.pallas_call(
        attend_back_kernel,
        out_shape=(
            shape(tokens, HD),
            shape(tokens, HD),
            shape(depth, 8 * part),
            shape(depth, 8 * part),
            shape(out_rows, out_w.shape[1]),
        ),
        in_specs=[INSIDE, ANY, ANY] + [INSIDE] * 9,
        out_specs=(INSIDE, INSIDE, ANY, ANY, ANY),
        scratch_shapes=[
            room(*keys.shape), room(*branch.shape), room(tokens, HD),
            room(LINE, 1, tokens // LINE, dtype=f32), room(LINE, 1, tokens // LINE, dtype=f32),
            room(8, 4 * rows, 1, dtype=f32), room(tokens, HD, dtype=f32), room(*keys.shape),
            room(4 * rows, HD, dtype=f32), room(4 * rows, HD, dtype=f32),
            room(eight, 2, rows, width), room(eight, rows, width), room(eight, rows, HD),
            dma(2),
        ] + [dma(8)] * 6 + QuarterScatter.scratch() + OutGrad.scratch(out_rows, out_w.shape[1]),
        compiler_params=kernel_params(11),
        name="attend_back",
    )(query, keys, branch, out_w, attended, attended_low, log_row, notes, cos_table, sine_table, gate, up)


class HeadGrads:
    @staticmethod
    def scratch(depth):
        def room(*dims):
            return pltpu.VMEM(dims, jnp.bfloat16)

        return [
            room(8, 2, depth, HD), room(8, 2, depth, HD),
            room(8, depth, HD), room(8, depth, HD),
            room(8, depth, HD), room(8, depth, HD),
            dma(2), dma(2), dma(2), dma(2), dma(3, 8), dma(3, 4, 8), dma(3),
        ]

    def __init__(self, outs, refs):
        self.outs = outs
        self.store, self.sib, self.box = refs[0:2], refs[2:4], refs[4:6]
        (self.c_s, self.c_r, self.x_s, self.x_r, self.s, self.r, self.own) = refs[6:]
        self.z, self.y, self.c, self.h = place()
        self.chip = self.z * 2 + self.y
        self.me = device(self.z, self.y, self.c, self.h)
        self.owner = self.h == self.y

    def share(self, i):
        return remote(
            self.store[i].at[:, 1 - self.c], self.sib[i], self.c_s.at[i], self.c_r.at[i],
            device(self.z, self.y, 1 - self.c, self.h),
        )

    def over(self, i):
        return remote(
            self.store[i].at[:, self.c], self.box[i], self.x_s.at[i], self.x_r.at[i],
            device(self.z, self.y, self.c, 1 - self.h),
        )

    def target(self, kind, line):
        start = line * HD if kind == 0 else (line // 2) * HD
        return self.outs[kind].at[:, pl.ds(pl.multiple_of(start, HD), HD)]

    def push(self, kind, step):
        chip = (self.chip + step) % 8
        return remote(
            self.store[min(kind, 1)].at[chip, self.c], self.target(kind, self.z), self.s.at[kind, step],
            self.r.at[kind, self.z, step], device(chip // 2, chip % 2, self.c, self.h),
        )

    def keep(self, kind):
        return local(self.store[min(kind, 1)].at[self.chip, self.c], self.target(kind, self.z), self.own.at[kind])

    def pull(self, kind, line, step):
        ref = self.target(kind, line)
        return remote(ref, ref, self.s.at[kind, step], self.r.at[kind, line, step], self.me)

    def relay(self, i):
        self.share(i).wait_recv()

        @pl.loop(0, 8)
        def _(at):
            add_into(self.store[i].at[at, self.c], self.sib[i].at[at])

        @pl.when(jnp.logical_not(self.owner))
        def _():
            self.over(i).start()

    def scatter(self, i):
        @pl.when(self.owner)
        def _():
            self.over(i).wait_recv()

            @pl.loop(0, 8)
            def _(at):
                add_into(self.store[i].at[at, self.c], self.box[i].at[at])

            if i == 0:
                self.keep(0).start()
                for step in range(1, 8):
                    self.push(0, step).start()
            else:
                for kind in (1, 2):

                    @pl.when(self.z % 2 == kind - 1)
                    def _():
                        self.keep(kind).start()
                        for step in range(1, 8):
                            self.push(kind, step).start()

    def finish(self):
        for kind in range(3):
            for line in range(LINE):
                if kind and line % 2 != kind - 1:
                    continue
                step = (self.chip + 8 - (line * 2 + self.h)) % 8

                @pl.when(step != 0)
                def _():
                    self.pull(kind, line, step).wait_recv()

                @pl.when(step == 0)
                def _():
                    self.keep(kind).wait()

        @pl.when(jnp.logical_not(self.owner))
        def _():
            for i in range(2):
                self.over(i).wait_send()

        @pl.when(self.owner)
        def _():
            for step in range(1, 8):
                self.push(0, step).wait_send()
            for kind in (1, 2):

                @pl.when(self.z % 2 == kind - 1)
                def _():
                    for step in range(1, 8):
                        self.push(kind, step).wait_send()

        for i in range(2):
            self.share(i).wait_send()


class GainSum:
    @staticmethod
    def scratch(rows):
        return [
            pltpu.VMEM((16, 8, rows), jnp.float32), pltpu.VMEM((32, 8, rows), jnp.float32), dma(32), dma(32),
        ]

    def __init__(self, out, refs):
        self.out = out
        self.terms, self.box, self.s, self.r = refs
        self.blk, self.h = lax.axis_index("blk"), lax.axis_index("head")

    def push(self, step):
        other = (self.blk + step // 2) % 16
        return remote(
            self.terms.at[other], self.box.at[step], self.s.at[step], self.r.at[step], (other, (self.h + step % 2) % 2)
        )

    def start(self, attn_term, mlp_term):
        rows = self.terms.shape[2]
        self.terms[...] = jnp.zeros_like(self.terms)
        for blk in range(16):
            part = pl.ds(blk * rows, rows)
            self.terms[blk, 0:1] = attn_term[:, part]
            self.terms[blk, 1:2] = mlp_term[:, part]
        for step in range(1, 32):
            self.push(step).start()

    def finish(self):
        total = self.terms[self.blk]
        for step in range(1, 32):
            self.push(step).wait_recv()
            total += self.box[step]
        self.out[...] = total
        for step in range(1, 32):
            self.push(step).wait_send()


def close_kernel(
    normed_in, qkv_w, grad_query, grad_side, grad_hidden, tokens, gain, mlp_term,
    tokens_grad, gains, query, key, value,
    normed, weight, parts, grad_normed, attn_term, load_s, *refs,
):
    reduce_refs, head_refs, gain_refs = split_refs(refs, (9, 13, 4))
    z, y, c, h = place()
    load = local(normed_in, normed, load_s.at[0])
    load_q = local(qkv_w.at[:, :, :, pl.ds(0, HD)], weight.at[0], load_s.at[1])
    side_columns = pl.ds(pl.multiple_of((1 + z % 2) * HD, HD), HD)
    load_side = local(qkv_w.at[:, :, :, side_columns], weight.at[1], load_s.at[2])
    load_q.start()
    load_side.start()
    load.start()
    greet_all(16, 2)
    reduce = Reduce(parts, reduce_refs)
    heads = HeadGrads((query, key, value), head_refs)
    gain_sum = GainSum(gains, gain_refs)
    rows, width = parts.shape[1:]
    pair = 2 * rows
    depth = head_refs[0].shape[2]
    load_q.wait()
    load_side.wait()
    for place_at in range(4):
        line = reduce.order[place_at]
        both = pl.ds(pl.multiple_of(line * pair, pair), pair)

        @pl.loop(0, 4)
        def _(tile):
            columns = pl.ds(pl.multiple_of(tile * (width // 4), width // 4), width // 4)
            part = times_transposed(grad_query[both], weight[0, pl.ds(tile * 2, 2)].reshape(width // 4, HD))
            part += times_transposed(grad_side[both], weight[1, pl.ds(tile * 2, 2)].reshape(width // 4, HD))
            parts[pl.ds(line * 2, 2), :, columns] = part.astype(jnp.bfloat16).reshape(2, rows, width // 4)

        reduce.start(place_at)
    load.wait()
    for i, source in enumerate((grad_query, grad_side)):

        @pl.loop(0, 4)
        def _(tile):
            columns = pl.ds(pl.multiple_of(tile * 4 * depth, 4 * depth), 4 * depth)
            part = transposed_times(normed[:, columns], source[...])
            head_refs[i][pl.ds(tile * 2, 2)] = part.astype(jnp.bfloat16).reshape(2, 2, depth, HD)

        heads.share(i).start()
    heads.relay(0)
    heads.relay(1)
    reduce.relay(0)
    reduce.relay(1)
    heads.scatter(0)
    reduce.relay(2)
    heads.scatter(1)
    reduce.total(grad_normed)
    inputs = tokens[...].astype(jnp.float32)
    inv_scale = rms_scale(inputs)
    unit_rows = inputs * inv_scale
    attn_term[...] = jnp.sum(grad_normed[...] * unit_rows, axis=0, keepdims=True)
    gain_sum.start(attn_term, mlp_term)
    grad_unit = grad_normed[...] * gain[...]
    mean = jnp.mean(grad_unit * unit_rows, axis=-1, keepdims=True)
    tokens_grad[...] = (grad_hidden[...] + inv_scale * (grad_unit - unit_rows * mean)).astype(jnp.bfloat16)
    heads.finish()
    reduce.finish()
    gain_sum.finish()


def close(normed, qkv_w, grad_query, grad_side, grad_hidden, tokens, gain, mlp_term):
    rows, width = tokens.shape
    depth = qkv_w.shape[2]

    def room(*dims, dtype=jnp.bfloat16):
        return pltpu.VMEM(dims, dtype)

    def shape(*dims, dtype=jnp.bfloat16):
        return jax.ShapeDtypeStruct(dims, dtype)

    f32 = jnp.float32
    return pl.pallas_call(
        close_kernel,
        out_shape=(
            shape(rows, width),
            shape(8, rows, dtype=f32),
            shape(depth, 4 * HD), shape(depth, 2 * HD), shape(depth, 2 * HD),
        ),
        in_specs=[ANY, ANY] + [INSIDE] * 6,
        out_specs=(INSIDE, INSIDE, ANY, ANY, ANY),
        scratch_shapes=[
            room(*normed.shape), room(2, 8, 2, depth, HD), room(8, rows, width),
            room(rows, width, dtype=f32), room(1, width, dtype=f32), dma(3),
        ]
        + Reduce.scratch(width)
        + HeadGrads.scratch(depth)
        + GainSum.scratch(rows),
        compiler_params=kernel_params(6),
        name="close",
    )(normed, qkv_w, grad_query, grad_side, grad_hidden, tokens, gain, mlp_term)


def fast_body(
    tokens,
    attn_gain,
    w_query,
    w_key,
    w_value,
    w_out,
    mlp_gain,
    w_gate,
    w_up,
    w_down,
    block_ids,
    positions,
    cotangent,
):
    rows, width = tokens.shape
    token_rows = 8 * rows
    f32, bf16 = jnp.float32, jnp.bfloat16

    note = jnp.concatenate(
        [
            positions.astype(f32).reshape(2, rows),
            block_ids.astype(f32).reshape(2, rows),
            attn_gain.astype(f32)[None],
            mlp_gain.astype(f32)[None],
            jnp.zeros((2, rows), f32),
        ]
    )
    inv_freqs = rope_base ** (-2.0 * jnp.arange(HD // 2, dtype=f32) / HD)
    (
        keys_values, normed, qkv_w, out_w, notes, cos_table, sine_table, scaled_query, attended, attended_low,
        log_total, cot_all, gate_w, up_w,
    ) = front(tokens, cotangent, note, inv_freqs[None], w_query, w_key, w_value, w_out, w_gate, w_up)
    out_w = out_w.reshape(HD, width)
    gain_attn = notes[:, 4].reshape(1, width)
    gain_mlp = notes[:, 5].reshape(1, width)
    output, hidden, normed_mlp, active, grad_gate, grad_up, grad_normed_part = mid(
        attended_low, out_w, gate_w, up_w, w_down, tokens, gain_mlp, cot_all
    )
    hidden_part = active.shape[2]
    grad_branch, grad_hidden, mlp_term, gate_quarter, up_quarter, down_grad = turn(
        grad_normed_part,
        normed_mlp.reshape(token_rows, width),
        grad_gate.reshape(token_rows, hidden_part),
        grad_up.reshape(token_rows, hidden_part),
        active.reshape(token_rows, hidden_part),
        cot_all.reshape(token_rows, width),
        hidden,
        gain_mlp,
        cotangent,
    )

    side_grad, grad_query, gate_grad, up_grad, out_grad = attend_back(
        scaled_query,
        keys_values,
        grad_branch,
        out_w,
        attended,
        attended_low,
        log_total,
        notes,
        cos_table,
        sine_table,
        gate_quarter,
        up_quarter,
        w_out.shape[0],
    )
    tokens_grad, gain_grads, query_grad, key_grad, value_grad = close(
        normed, qkv_w, grad_query, side_grad, grad_hidden, tokens, gain_attn, mlp_term
    )
    return (
        output,
        tokens_grad,
        gain_grads[0],
        query_grad.astype(f32),
        key_grad.astype(f32),
        value_grad.astype(f32),
        out_grad.astype(f32),
        gain_grads[1],
        gate_grad.astype(f32),
        up_grad.astype(f32),
        down_grad,
    )


def solution(mesh):
    placed = (
        P(("blk", "head"), None),
        P("blk"),
        P("blk", "head"),
        P("blk", "head"),
        P("blk", "head"),
        P(("head", "blk"), None),
        P("blk"),
        P("blk", "head"),
        P("blk", "head"),
        P(("head", "blk"), None),
        P("blk"),
        P("blk"),
        P(("blk", "head"), None),
    )
    fits = mesh.shape["blk"] == 16 and mesh.shape["head"] == 2
    return jax.shard_map(
        fast_body if fits else body,
        mesh=mesh,
        in_specs=placed,
        out_specs=(
            P(("blk", "head"), None),
            P(("blk", "head"), None),
            P("blk"),
            P("blk", "head"),
            P("blk", "head"),
            P("blk", "head"),
            P(("head", "blk"), None),
            P("blk"),
            P("blk", "head"),
            P("blk", "head"),
            P(("head", "blk"), None),
        ),
        check_vma=False,
    )
```

```python
import jax
import jax.numpy as jnp
from jax import lax
from jax.experimental import pallas as pl
from jax.experimental.pallas import tpu as pltpu
from jax.sharding import PartitionSpec as P

HD = 256


eps_norm = 1e-06
rope_base = 1000042.0


def rms_scale(rows):
    return lax.rsqrt(jnp.mean(rows * rows, axis=-1, keepdims=True) + eps_norm)


def rope_tables(positions):
    inv_freqs = rope_base ** (-2.0 * jnp.arange(HD // 2, dtype=jnp.float32) / HD)
    angles = positions.astype(jnp.float32)[:, None] * inv_freqs[None, :]
    return (jnp.cos(angles)[:, None, :], jnp.sin(angles)[:, None, :])


def rotate(heads, cos_table, sine_table):
    half_size = heads.shape[-1] // 2
    lower_half = heads[..., :half_size]
    upper_half = heads[..., half_size:]
    return jnp.concatenate(
        [
            lower_half * cos_table - upper_half * sine_table,
            upper_half * cos_table + lower_half * sine_table,
        ],
        axis=-1,
    )


def product(left, right):
    return jnp.dot(left, right, preferred_element_type=jnp.float32)


def times_transposed(left, right):
    return lax.dot_general(
        left, right, (((1,), (1,)), ((), ())), preferred_element_type=jnp.float32
    )


def transposed_times(left, right):
    return lax.dot_general(
        left, right, (((0,), (0,)), ((), ())), preferred_element_type=jnp.float32
    )


def norm_backward(grad_normed, inputs, inv_scale, gain_rows):
    unit_rows = inputs * inv_scale
    grad_unit = grad_normed * gain_rows
    gain_term = jnp.sum(grad_normed * unit_rows, axis=0)
    grad_inputs = inv_scale * (
        grad_unit - unit_rows * jnp.mean(grad_unit * unit_rows, axis=-1, keepdims=True)
    )
    return (grad_inputs, gain_term)


def body(
    tokens,
    attn_gain,
    w_query,
    w_key,
    w_value,
    w_out,
    mlp_gain,
    w_gate,
    w_up,
    w_down,
    block_ids,
    positions,
    cotangent,
):
    rows_own = tokens.shape[0]
    head_rank = lax.axis_index("head")
    tokens_all, cot_all = (
        lax.all_gather(tokens, "head", axis=0, tiled=True),
        lax.all_gather(cotangent, "head", axis=0, tiled=True),
    )
    rows_all = tokens_all.shape[0]
    gain_attn, query_w, key_w, value_w, out_w = (
        lax.all_gather(attn_gain, "blk", axis=0, tiled=True),
        lax.all_gather(w_query, "blk", axis=0, tiled=True),
        lax.all_gather(w_key, "blk", axis=0, tiled=True),
        lax.all_gather(w_value, "blk", axis=0, tiled=True),
        lax.all_gather(w_out, "blk", axis=0, tiled=True),
    )
    gain_mlp, gate_w, up_w, down_w = (
        lax.all_gather(mlp_gain, "blk", axis=0, tiled=True),
        lax.all_gather(w_gate, "blk", axis=0, tiled=True),
        lax.all_gather(w_up, "blk", axis=0, tiled=True),
        lax.all_gather(w_down, "blk", axis=0, tiled=True),
    )
    key_ids = lax.all_gather(block_ids, "blk", axis=0, tiled=True)
    heads_local = query_w.shape[1] // HD
    kv_local = key_w.shape[1] // HD
    kv_width = kv_local * HD
    group_size = heads_local // kv_local
    cos_table, sine_table = rope_tables(positions)
    score_scale = HD ** (-0.5)
    seq_len = key_ids.shape[0]
    key_block = min(2048, seq_len)
    block_total = seq_len // key_block
    block_steps = jnp.arange(block_total)
    top_query = jnp.max(block_ids)
    inputs = tokens_all.astype(jnp.float32)
    inv_attn = rms_scale(inputs)
    normed = (inputs * inv_attn * gain_attn.astype(jnp.float32)).astype(jnp.bfloat16)
    queries = rotate(
        product(normed, query_w).reshape(rows_all, heads_local, HD), cos_table, sine_table
    ).astype(jnp.bfloat16)
    keys_own = rotate(product(normed, key_w).reshape(rows_all, kv_local, HD), cos_table, sine_table)
    keys_own = keys_own.astype(jnp.bfloat16).reshape(rows_all, kv_width)
    values_own = product(normed, value_w).astype(jnp.bfloat16)
    keys_all, values_all = (
        lax.all_gather(keys_own, "blk", axis=0, tiled=True),
        lax.all_gather(values_own, "blk", axis=0, tiled=True),
    )
    grouped = queries.reshape(rows_all, kv_local, group_size, HD)

    def slice_keys(key_start, count):
        key_rows = lax.dynamic_slice_in_dim(keys_all, key_start, count, 0).reshape(
            count, kv_local, HD
        )
        value_rows = lax.dynamic_slice_in_dim(values_all, key_start, count, 0).reshape(
            count, kv_local, HD
        )
        block_keys = lax.dynamic_slice_in_dim(key_ids, key_start, count, 0)
        return (key_rows, value_rows, block_keys)

    def scores_for(key_rows, block_keys):
        scores = (
            jnp.einsum("qkgd,ckd->kgqc", grouped, key_rows, preferred_element_type=jnp.float32)
            * score_scale
        )
        visible = (block_keys[None, :] <= block_ids[:, None])[None, None]
        return (scores, visible)

    def max_sum(state_pair, step_index):
        key_start = step_index * key_block

        def max_live(pair):
            run_max, run_sum = pair
            key_rows, value_rows, block_keys = slice_keys(key_start, key_block)
            scores, visible = scores_for(key_rows, block_keys)
            scores = jnp.where(visible, scores, -1e30)
            new_max = jnp.maximum(run_max, jnp.max(scores, axis=-1))
            kept_terms = jnp.where(visible, jnp.exp(scores - new_max[..., None]), 0.0)
            return (new_max, run_sum * jnp.exp(run_max - new_max) + jnp.sum(kept_terms, axis=-1))

        def max_skipped(pair):
            return pair

        return (lax.cond(key_ids[key_start] <= top_query, max_live, max_skipped, state_pair), None)

    start_max = jnp.full((kv_local, group_size, rows_all), -1e30, jnp.float32)
    start_sum = jnp.zeros((kv_local, group_size, rows_all), jnp.float32)
    (run_max, run_sum), unused_max = lax.scan(max_sum, (start_max, start_sum), block_steps)
    log_total = run_max + jnp.log(run_sum)

    def weighted(accum_rows, step_index):
        key_start = step_index * key_block

        def weighted_live(accum):
            key_rows, value_rows, block_keys = slice_keys(key_start, key_block)
            scores, visible = scores_for(key_rows, block_keys)
            probabilities = jnp.where(visible, jnp.exp(scores - log_total[..., None]), 0.0).astype(
                jnp.bfloat16
            )
            return accum + jnp.einsum(
                "kgqc,ckd->qkgd", probabilities, value_rows, preferred_element_type=jnp.float32
            )

        def weighted_skipped(accum):
            return accum

        return (
            lax.cond(key_ids[key_start] <= top_query, weighted_live, weighted_skipped, accum_rows),
            None,
        )

    attended, unused_rows = lax.scan(
        weighted, jnp.zeros((rows_all, kv_local, group_size, HD), jnp.float32), block_steps
    )
    attended_low = attended.reshape(rows_all, heads_local * HD).astype(jnp.bfloat16)
    branch_sum = lax.psum(product(attended_low, out_w).astype(jnp.bfloat16), "head").astype(
        jnp.float32
    )
    hidden = inputs + branch_sum
    inv_mlp = rms_scale(hidden)
    normed_mlp = (hidden * inv_mlp * gain_mlp.astype(jnp.float32)).astype(jnp.bfloat16)
    gate_pre = product(normed_mlp, gate_w)
    up_pre = product(normed_mlp, up_w)
    sigmoid_gate = jax.nn.sigmoid(gate_pre)
    active = (gate_pre * sigmoid_gate * up_pre).astype(jnp.bfloat16)
    mlp_own = lax.psum_scatter(
        product(active, down_w).astype(jnp.bfloat16), "head", scatter_dimension=0, tiled=True
    ).astype(jnp.float32)
    hidden_own = lax.dynamic_slice_in_dim(hidden, head_rank * rows_own, rows_own, 0)
    output = (hidden_own + mlp_own).astype(jnp.bfloat16)
    gain_attn, query_w, key_w, value_w, out_w = (
        lax.all_gather(attn_gain, "blk", axis=0, tiled=True),
        lax.all_gather(w_query, "blk", axis=0, tiled=True),
        lax.all_gather(w_key, "blk", axis=0, tiled=True),
        lax.all_gather(w_value, "blk", axis=0, tiled=True),
        lax.all_gather(w_out, "blk", axis=0, tiled=True),
    )
    gain_mlp, gate_w, up_w, down_w = (
        lax.all_gather(mlp_gain, "blk", axis=0, tiled=True),
        lax.all_gather(w_gate, "blk", axis=0, tiled=True),
        lax.all_gather(w_up, "blk", axis=0, tiled=True),
        lax.all_gather(w_down, "blk", axis=0, tiled=True),
    )
    grad_active = times_transposed(cot_all, down_w)
    grad_gate = (
        grad_active * up_pre * sigmoid_gate * (1.0 + gate_pre * (1.0 - sigmoid_gate))
    ).astype(jnp.bfloat16)
    grad_up = (grad_active * gate_pre * sigmoid_gate).astype(jnp.bfloat16)
    grad_gate_w = transposed_times(normed_mlp, grad_gate)
    grad_up_w = transposed_times(normed_mlp, grad_up)
    grad_down_w = transposed_times(active, cot_all)
    grad_normed_part = times_transposed(grad_gate, gate_w) + times_transposed(grad_up, up_w)
    grad_normed_mlp = lax.psum(grad_normed_part.astype(jnp.bfloat16), "head").astype(jnp.float32)
    grad_hidden_norm, gain_mlp_term = norm_backward(
        grad_normed_mlp, hidden, inv_mlp, gain_mlp.astype(jnp.float32)
    )
    grad_hidden = cot_all.astype(jnp.float32) + grad_hidden_norm
    mlp_results = (
        lax.psum_scatter(gain_mlp_term, "blk", scatter_dimension=0, tiled=True),
        lax.psum_scatter(grad_gate_w, "blk", scatter_dimension=0, tiled=True),
        lax.psum_scatter(grad_up_w, "blk", scatter_dimension=0, tiled=True),
        lax.psum_scatter(grad_down_w, "blk", scatter_dimension=0, tiled=True),
    )
    grad_branch = grad_hidden.astype(jnp.bfloat16)
    grad_out_w = transposed_times(attended_low, grad_branch)
    grad_attended = times_transposed(grad_branch, out_w).astype(jnp.bfloat16)
    grad_grouped = grad_attended.reshape(rows_all, kv_local, group_size, HD)
    delta_rows = jnp.transpose(
        jnp.sum(grad_grouped.astype(jnp.float32) * attended, axis=-1), (1, 2, 0)
    )

    def pair_backward(key_rows, value_rows, block_keys):
        count = key_rows.shape[0]
        scores, visible = scores_for(key_rows, block_keys)
        probabilities = jnp.where(visible, jnp.exp(scores - log_total[..., None]), 0.0)
        grad_probs = jnp.einsum(
            "qkgd,ckd->kgqc", grad_grouped, value_rows, preferred_element_type=jnp.float32
        )
        grad_scores = (probabilities * (grad_probs - delta_rows[..., None])).astype(jnp.bfloat16)
        query_terms = jnp.einsum(
            "kgqc,ckd->qkgd", grad_scores, key_rows, preferred_element_type=jnp.float32
        )
        key_terms = (
            jnp.einsum("kgqc,qkgd->ckd", grad_scores, grouped, preferred_element_type=jnp.float32)
            * score_scale
        )
        value_terms = jnp.einsum(
            "kgqc,qkgd->ckd",
            probabilities.astype(jnp.bfloat16),
            grad_grouped,
            preferred_element_type=jnp.float32,
        )
        return (
            query_terms,
            key_terms.reshape(count, kv_width),
            value_terms.reshape(count, kv_width),
        )

    query_zeros = jnp.zeros((rows_all, kv_local, group_size, HD), jnp.float32)

    def backward_block(accum_rows, step_index):
        key_start = step_index * key_block

        def backward_live(unused_arg):
            key_rows, value_rows, block_keys = slice_keys(key_start, key_block)
            return pair_backward(key_rows, value_rows, block_keys)

        def backward_skipped(unused_arg):
            empty_terms = jnp.zeros((key_block, kv_width), jnp.float32)
            return (query_zeros, empty_terms, empty_terms)

        query_terms, key_terms, value_terms = lax.cond(
            key_ids[key_start] <= top_query, backward_live, backward_skipped, 0
        )
        return (accum_rows + query_terms, (key_terms, value_terms))

    grad_query_rot, (key_terms, value_terms) = lax.scan(backward_block, query_zeros, block_steps)
    key_terms = key_terms.reshape(seq_len, kv_width)
    value_terms = value_terms.reshape(seq_len, kv_width)
    key_grad_own, value_grad_own = (
        lax.psum_scatter(key_terms, "blk", scatter_dimension=0, tiled=True),
        lax.psum_scatter(value_terms, "blk", scatter_dimension=0, tiled=True),
    )
    grad_query_rot = grad_query_rot * score_scale
    grad_key = rotate(key_grad_own.reshape(rows_all, kv_local, HD), cos_table, -sine_table)
    grad_key = grad_key.reshape(rows_all, kv_width).astype(jnp.bfloat16)
    grad_value = value_grad_own.astype(jnp.bfloat16)
    grad_query = rotate(grad_query_rot.reshape(rows_all, heads_local, HD), cos_table, -sine_table)
    grad_query = grad_query.reshape(rows_all, heads_local * HD).astype(jnp.bfloat16)
    grad_query_w = transposed_times(normed, grad_query)
    grad_key_w = transposed_times(normed, grad_key)
    grad_value_w = transposed_times(normed, grad_value)
    grad_normed_part = (
        times_transposed(grad_query, query_w)
        + times_transposed(grad_key, key_w)
        + times_transposed(grad_value, value_w)
    )
    grad_normed = lax.psum(grad_normed_part.astype(jnp.bfloat16), "head").astype(jnp.float32)
    grad_inputs_norm, gain_attn_term = norm_backward(
        grad_normed, inputs, inv_attn, gain_attn.astype(jnp.float32)
    )
    grad_inputs = grad_hidden + grad_inputs_norm
    grad_own = lax.dynamic_slice_in_dim(grad_inputs, head_rank * rows_own, rows_own, 0).astype(
        jnp.bfloat16
    )
    attn_results = (
        lax.psum_scatter(gain_attn_term, "blk", scatter_dimension=0, tiled=True),
        lax.psum_scatter(grad_query_w, "blk", scatter_dimension=0, tiled=True),
        lax.psum_scatter(grad_key_w, "blk", scatter_dimension=0, tiled=True),
        lax.psum_scatter(grad_value_w, "blk", scatter_dimension=0, tiled=True),
        lax.psum_scatter(grad_out_w, "blk", scatter_dimension=0, tiled=True),
    )
    return (
        output,
        grad_own,
        attn_results[0],
        attn_results[1],
        attn_results[2],
        attn_results[3],
        attn_results[4],
        mlp_results[0],
        mlp_results[1],
        mlp_results[2],
        mlp_results[3],
    )


MESH = pl.DeviceIdType.MESH
LINE = 4
VMEM_BYTES = 60 * 2**20


def place():
    blk, head = lax.axis_index("blk"), lax.axis_index("head")
    return blk // 4, (blk // 2) % 2, blk % 2, head


def device(z, y, c, h):
    return (z * 4 + y * 2 + c, h)


def remote(src, dst, send_sem, recv_sem, target):
    return pltpu.make_async_remote_copy(
        src_ref=src,
        dst_ref=dst,
        send_sem=send_sem,
        recv_sem=recv_sem,
        device_id=target,
        device_id_type=MESH,
    )


def greet(target):
    pl.semaphore_signal(
        pltpu.get_barrier_semaphore(), inc=1, device_id=target, device_id_type=MESH
    )


def greet_all(blk_total, head_total):
    blk, head = lax.axis_index("blk"), lax.axis_index("head")
    for other in range(blk_total):
        for half in range(head_total):

            @pl.when(jnp.logical_or(blk != other, head != half))
            def _():
                greet((jnp.int32(other), jnp.int32(half)))

    pl.semaphore_wait(pltpu.get_barrier_semaphore(), blk_total * head_total - 1)


def greet_plane(more=0):
    z, y, c, h = place()

    @pl.when(z > 0)
    def _():
        greet(device(z - 1, y, c, h))

    @pl.when(z < LINE - 1)
    def _():
        greet(device(z + 1, y, c, h))

    greet(device(z, 1 - y, c, h))
    pl.semaphore_wait(
        pltpu.get_barrier_semaphore(),
        1 + more + (z + LINE - 1) // LINE + (LINE - 1 - z + LINE - 1) // LINE,
    )


class Gather:
    CUTS = ((0, 64), (64, 48), (112, 16), (112, 16))
    SEMS = [(3, 4)] * 4 + [(4, 2)] * 2 + [(2,)]

    @staticmethod
    def scratch():
        return [pltpu.SemaphoreType.DMA(shape) for shape in Gather.SEMS] + [
            pltpu.SemaphoreType.DMA
        ]

    def __init__(self, src, out, sems):
        self.src, self.out = src, out
        (self.up_s, self.up_r, self.dn_s, self.dn_r, self.y_s, self.y_r, self.b_sr, self.own_sem) = sems
        self.z, self.y, self.c, self.h = place()

    def piece(self, line, elem):
        y = 1 - self.y if elem == 3 else self.y
        start, size = self.CUTS[elem]
        return self.out.at[line * 2 + y, pl.ds(start, size)]

    def first(self, elem):
        if elem == 3:
            return self.piece(self.z, 3)
        start, size = self.CUTS[elem]
        return self.src.at[pl.ds(start, size)]

    def up(self, step, elem):
        src = self.first(elem) if step == 0 else self.piece(self.z - step, elem)
        return remote(
            src, self.piece(self.z - step, elem), self.up_s.at[step, elem], self.up_r.at[step, elem],
            device(self.z + 1, self.y, self.c, self.h),
        )

    def down(self, step, elem):
        src = self.first(elem) if step == 0 else self.piece(self.z + step, elem)
        return remote(
            src, self.piece(self.z + step, elem), self.dn_s.at[step, elem], self.dn_r.at[step, elem],
            device(self.z - 1, self.y, self.c, self.h),
        )

    def up_in(self, step, elem):
        ref = self.piece(self.z - 1 - step, elem)
        return remote(ref, ref, self.up_s.at[step, elem], self.up_r.at[step, elem], device(self.z, self.y, self.c, self.h))

    def down_in(self, step, elem):
        ref = self.piece(self.z + 1 + step, elem)
        return remote(ref, ref, self.dn_s.at[step, elem], self.dn_r.at[step, elem], device(self.z, self.y, self.c, self.h))

    def across(self, line, elem, own=False):
        src = self.first(elem) if own else self.piece(line, elem)
        return remote(
            src, self.piece(line, elem), self.y_s.at[line, elem], self.y_r.at[line, elem],
            device(self.z, 1 - self.y, self.c, self.h),
        )

    def across_in(self, line, elem):
        start, size = self.CUTS[elem]
        ref = self.out.at[line * 2 + 1 - self.y, pl.ds(start, size)]
        return remote(ref, ref, self.y_s.at[line, elem], self.y_r.at[line, elem], device(self.z, self.y, self.c, self.h))

    def across_b(self):
        return remote(
            self.first(2), self.piece(self.z, 2), self.b_sr.at[0], self.b_sr.at[1],
            device(self.z, 1 - self.y, self.c, self.h),
        )

    def across_b_in(self):
        ref = self.piece(self.z, 3)
        return remote(ref, ref, self.b_sr.at[0], self.b_sr.at[1], device(self.z, self.y, self.c, self.h))

    def own_copy(self):
        return pltpu.make_async_copy(self.src, self.out.at[self.z * 2 + self.y], self.own_sem)

    def start(self):
        self.own_copy().start()
        self.across_b().start()
        for elem in (0, 1, 2):

            @pl.when(self.z < LINE - 1)
            def _():
                self.up(0, elem).start()

            @pl.when(self.z > 0)
            def _():
                self.down(0, elem).start()

            if elem < 2:
                self.across(self.z, elem, own=True).start()

    def relay_b(self):
        self.across_b_in().wait_recv()

        @pl.when(self.z < LINE - 1)
        def _():
            self.up(0, 3).start()

        @pl.when(self.z > 0)
        def _():
            self.down(0, 3).start()

    def relay(self, step, elem):
        @pl.when(self.z - 1 - step >= 0)
        def _():
            self.up_in(step, elem).wait_recv()
            if step < LINE - 2:

                @pl.when(self.z < LINE - 1)
                def _():
                    self.up(step + 1, elem).start()

            if elem < 2:
                self.across(self.z - 1 - step, elem).start()

        @pl.when(self.z + 1 + step <= LINE - 1)
        def _():
            self.down_in(step, elem).wait_recv()
            if step < LINE - 2:

                @pl.when(self.z > 0)
                def _():
                    self.down(step + 1, elem).start()

            if elem < 2:
                self.across(self.z + 1 + step, elem).start()

    def relays(self):
        self.relay_b()
        for step in range(LINE - 1):
            for elem in (0, 1, 2, 3):
                self.relay(step, elem)

    def finish(self):
        for line in range(LINE):
            for elem in (0, 1):
                self.across_in(line, elem).wait_recv()
        for line in range(LINE):
            for elem in (0, 1):
                self.across(line, elem).wait_send()
        self.finish_sends()
        self.own_copy().wait()

    def finish_sends(self):
        self.across_b().wait_send()
        for step in range(LINE - 1):
            for elem in range(4):

                @pl.when(jnp.logical_and(self.z < LINE - 1, self.z - step >= 0))
                def _():
                    self.up(step, elem).wait_send()

                @pl.when(jnp.logical_and(self.z > 0, self.z + step <= LINE - 1))
                def _():
                    self.down(step, elem).wait_send()


ANY = pl.BlockSpec(memory_space=pl.ANY)
INSIDE = pl.BlockSpec(memory_space=pltpu.VMEM)


def kernel_params(collective_id):
    return pltpu.CompilerParams(
        collective_id=collective_id, has_side_effects=True, vmem_limit_bytes=VMEM_BYTES
    )


def add_into(target, *others):
    total = target[...].astype(jnp.float32)
    for other in others:
        total += other[...].astype(jnp.float32)
    target[...] = total.astype(target.dtype)


class Reduce:
    CUTS = ((0, 64), (64, 48))
    LAST = (112, 16)

    @staticmethod
    def scratch(width):
        inbox = pltpu.VMEM((LINE, 112, width), jnp.bfloat16)
        last = pltpu.VMEM((LINE, 2, 16, width), jnp.bfloat16)
        sems = [pltpu.SemaphoreType.DMA((LINE, 2))] * 10 + [pltpu.SemaphoreType.DMA((2,))]
        return [inbox] * 3 + [last] * 2 + [pltpu.VMEM((16, width), jnp.bfloat16)] + sems

    COUNT = 17

    def __init__(self, parts, refs):
        self.parts = parts
        self.y_in, self.up_in, self.dn_in, self.up_last, self.dn_last, self.y_last = refs[:6]
        (
            self.y_s, self.y_r, self.up_s, self.up_r, self.dn_s, self.dn_r,
            self.ul_s, self.ul_r, self.dl_s, self.dl_r, self.yl_sr,
        ) = refs[6:]
        self.z, self.y, self.c, self.h = place()
        z = self.z
        self.order = (3 - 3 * (z // 2), (2 + 3 * z) % 5, 1 + z % 2, z)

    def rows(self, cut):
        return pl.ds(*self.CUTS[cut])

    def across(self, line, cut):
        return remote(
            self.parts.at[line * 2 + 1 - self.y, self.rows(cut)], self.y_in.at[line, self.rows(cut)],
            self.y_s.at[line, cut], self.y_r.at[line, cut], device(self.z, 1 - self.y, self.c, self.h),
        )

    def up(self, line, cut):
        return remote(
            self.parts.at[line * 2 + self.y, self.rows(cut)], self.up_in.at[line, self.rows(cut)],
            self.up_s.at[line, cut], self.up_r.at[line, cut], device(self.z + 1, self.y, self.c, self.h),
        )

    def down(self, line, cut):
        return remote(
            self.parts.at[line * 2 + self.y, self.rows(cut)], self.dn_in.at[line, self.rows(cut)],
            self.dn_s.at[line, cut], self.dn_r.at[line, cut], device(self.z - 1, self.y, self.c, self.h),
        )

    def last(self, line, column):
        return self.parts.at[line * 2 + column, pl.ds(*self.LAST)]

    def last_up(self, line, column):
        return remote(
            self.last(line, column), self.up_last.at[line, column], self.ul_s.at[line, column],
            self.ul_r.at[line, column], device(self.z + 1, self.y, self.c, self.h),
        )

    def last_down(self, line, column):
        return remote(
            self.last(line, column), self.dn_last.at[line, column], self.dl_s.at[line, column],
            self.dl_r.at[line, column], device(self.z - 1, self.y, self.c, self.h),
        )

    def last_across(self):
        return remote(
            self.last(self.z, 1 - self.y), self.y_last, self.yl_sr.at[0], self.yl_sr.at[1],
            device(self.z, 1 - self.y, self.c, self.h),
        )

    def start(self, place_at):
        line = self.order[place_at]
        for cut in range(2):
            self.across(line, cut).start()

        @pl.when(jnp.logical_and(line > self.z, self.z == 0))
        def _():
            for column in range(2):
                self.last_up(line, column).start()

        @pl.when(jnp.logical_and(line < self.z, self.z == LINE - 1))
        def _():
            for column in range(2):
                self.last_down(line, column).start()

    def relay_last(self, line):
        @pl.when(jnp.logical_and(line > self.z, self.z > 0))
        def _():
            for column in range(2):
                self.last_up(line, column).wait_recv()
                add_into(self.last(line, column), self.up_last.at[line, column])
                self.last_up(line, column).start()

        @pl.when(jnp.logical_and(line < self.z, self.z < LINE - 1))
        def _():
            for column in range(2):
                self.last_down(line, column).wait_recv()
                add_into(self.last(line, column), self.dn_last.at[line, column])
                self.last_down(line, column).start()

    def relay(self, place_at):
        line = self.order[place_at]
        for cut in range(2):
            rows = self.rows(cut)
            self.across(line, cut).wait_recv()
            target = self.parts.at[line * 2 + self.y, rows]

            @pl.when(line > self.z)
            def _():
                @pl.when(self.z > 0)
                def _():
                    self.up(line, cut).wait_recv()
                    add_into(target, self.y_in.at[line, rows], self.up_in.at[line, rows])

                @pl.when(self.z == 0)
                def _():
                    add_into(target, self.y_in.at[line, rows])

                self.up(line, cut).start()

            @pl.when(line < self.z)
            def _():
                @pl.when(self.z < LINE - 1)
                def _():
                    self.down(line, cut).wait_recv()
                    add_into(target, self.y_in.at[line, rows], self.dn_in.at[line, rows])

                @pl.when(self.z == LINE - 1)
                def _():
                    add_into(target, self.y_in.at[line, rows])

                self.down(line, cut).start()

            if cut == 0:
                self.relay_last(line)

    def total(self, out):
        line = self.z
        last = pl.ds(*self.LAST)
        own, other = line * 2 + self.y, line * 2 + 1 - self.y

        @pl.when(self.z > 0)
        def _():
            for column in range(2):
                self.last_up(line, column).wait_recv()
                add_into(self.last(line, column), self.up_last.at[line, column])

        @pl.when(self.z < LINE - 1)
        def _():
            for column in range(2):
                self.last_down(line, column).wait_recv()
                add_into(self.last(line, column), self.dn_last.at[line, column])

        self.last_across().start()
        for cut in range(2):
            rows = self.rows(cut)
            self.across(line, cut).wait_recv()
            out[rows] = self.parts[own, rows].astype(jnp.float32) + self.y_in[line, rows].astype(jnp.float32)
        for cut in range(2):
            rows = self.rows(cut)

            @pl.when(self.z > 0)
            def _():
                self.up(line, cut).wait_recv()
                out[rows] += self.up_in[line, rows].astype(jnp.float32)

            @pl.when(self.z < LINE - 1)
            def _():
                self.down(line, cut).wait_recv()
                out[rows] += self.dn_in[line, rows].astype(jnp.float32)

        self.last_across().wait_recv()
        out[last] = self.parts[own, last].astype(jnp.float32) + self.y_last[...].astype(jnp.float32)

    def finish(self):
        for line in range(LINE):
            for cut in range(2):
                self.across(line, cut).wait_send()

                @pl.when(self.z < line)
                def _():
                    self.up(line, cut).wait_send()
                    self.last_up(line, cut).wait_send()

                @pl.when(self.z > line)
                def _():
                    self.down(line, cut).wait_send()
                    self.last_down(line, cut).wait_send()

        self.last_across().wait_send()


def dma(*shape):
    return pltpu.SemaphoreType.DMA(shape) if shape else pltpu.SemaphoreType.DMA


def local(src, dst, sem):
    return pltpu.make_async_copy(src, dst, sem)


class AttnSpread:
    @staticmethod
    def scratch(depth):
        return [pltpu.VMEM((LINE, depth, 3 * HD), jnp.bfloat16)] + [
            dma(3, 4), dma(3, 4), dma(3), dma(4), dma(4), dma(4), dma(4), dma(4), dma(4), dma(4), dma(4), dma(4), dma(4),
        ]

    COUNT = 14

    def __init__(self, weights, outs, refs):
        self.weights, (self.qkv, self.out_w) = weights, outs
        (
            self.stage, self.s, self.r, self.own, self.x_s, self.x_r, self.a_s, self.a_r, self.b_s, self.b_r,
            self.c_s, self.c_r, self.o_s, self.o_r,
        ) = refs
        self.z, self.y, self.c, self.h = place()
        self.me = device(self.z, self.y, self.c, self.h)
        self.owner = self.h == self.y

    def source(self, kind, line):
        start = line * HD if kind == 0 else (line // 2) * HD
        return self.weights[kind].at[:, pl.ds(pl.multiple_of(start, HD), HD)]

    def slot(self, kind, line, owner):
        columns = pl.ds(kind * HD, HD)
        if owner:
            return self.qkv.at[line * 2 + self.y, self.c, :, columns]
        return self.stage.at[line, :, columns]

    def push(self, kind, step, owner):
        line = (self.z + step) % LINE
        return remote(
            self.source(kind, line), self.slot(kind, self.z, owner), self.s.at[kind, step], self.r.at[kind, self.z],
            device(line, self.y, self.c, self.h),
        )

    def pull(self, kind, line, owner):
        ref = self.slot(kind, line, owner)
        return remote(ref, ref, self.s.at[kind, 0], self.r.at[kind, line], self.me)

    def keep(self, kind, owner):
        return local(self.source(kind, self.z), self.slot(kind, self.z, owner), self.own.at[kind])

    def over(self, line):
        ref = self.qkv.at[line * 2 + self.y, self.c]
        return remote(ref, ref, self.x_s.at[line], self.x_r.at[line], device(self.z, self.y, self.c, 1 - self.h))

    def over_in(self, line):
        ref = self.qkv.at[line * 2 + self.y, self.c]
        return remote(ref, ref, self.x_s.at[line], self.x_r.at[line], self.me)

    def across(self, line):
        return remote(
            self.stage.at[line], self.qkv.at[line * 2 + self.y, self.c], self.a_s.at[line], self.a_r.at[line],
            device(self.z, 1 - self.y, self.c, self.h),
        )

    def across_far(self, line):
        return remote(
            self.stage.at[line], self.qkv.at[line * 2 + self.y, self.c], self.b_s.at[line], self.b_r.at[line],
            device(self.z, 1 - self.y, self.c, 1 - self.h),
        )

    def far_in(self, line, owner):
        ref = self.qkv.at[line * 2 + 1 - self.y, self.c]
        s, r = (self.a_s, self.a_r) if owner else (self.b_s, self.b_r)
        return remote(ref, ref, s.at[line], r.at[line], self.me)

    def share(self, line, core):
        ref = self.qkv.at[pl.ds(line * 2, 2), core]
        return remote(ref, ref, self.c_s.at[line], self.c_r.at[line], device(self.z, self.y, 1 - self.c, self.h))

    def out_push(self):
        return remote(
            self.weights[3], self.out_w.at[self.y, self.c], self.o_s.at[0], self.o_r.at[0],
            device(self.z, 1 - self.y, self.c, self.h),
        )

    def out_keep(self):
        return local(self.weights[3], self.out_w.at[self.y, self.c], self.o_s.at[1])

    def out_pull(self):
        ref = self.out_w.at[1 - self.y, self.c]
        return remote(ref, ref, self.o_s.at[0], self.o_r.at[0], self.me)

    def out_over(self):
        ref = self.out_w.at[:, self.c]
        return remote(ref, ref, self.o_s.at[2], self.o_r.at[2], device(self.z, self.y, self.c, 1 - self.h))

    def out_share(self, core):
        ref = self.out_w.at[:, core]
        return remote(ref, ref, self.o_s.at[3], self.o_r.at[3], device(self.z, self.y, 1 - self.c, self.h))

    def each(self, act):
        @pl.when(self.owner)
        def _():
            act(True)

        @pl.when(jnp.logical_not(self.owner))
        def _():
            act(False)

    def start(self):
        def act(owner):
            for kind in range(3):
                self.keep(kind, owner).start()
            for step in range(1, LINE):
                for kind in range(3):
                    self.push(kind, step, owner).start()
            if owner:
                self.out_keep().start()
            else:
                self.out_push().start()

        self.each(act)

    def relay(self, step):
        line = (self.z + LINE - step) % LINE

        def act(owner):
            for kind in range(3):
                if step:
                    self.pull(kind, line, owner).wait_recv()
                else:
                    self.keep(kind, owner).wait()
            if owner:
                self.over(line).start()
            else:
                self.across(line).start()
                self.across_far(line).start()

        self.each(act)

    def relay_out(self):
        @pl.when(self.owner)
        def _():
            self.out_keep().wait()
            self.out_pull().wait_recv()
            self.out_over().start()

    def relay_share(self, step):
        line = (self.z + LINE - step) % LINE

        def act(owner):
            if not owner:
                self.over_in(line).wait_recv()
            self.far_in(line, owner).wait_recv()

        self.each(act)
        self.share(line, self.c).start()

    def relay_out_share(self):
        @pl.when(jnp.logical_not(self.owner))
        def _():
            self.out_over().wait_recv()

        self.out_share(self.c).start()

    def finish(self):
        for line in range(LINE):
            self.share(line, 1 - self.c).wait_recv()
            self.share(line, self.c).wait_send()
        self.out_share(1 - self.c).wait_recv()
        self.out_share(self.c).wait_send()

        def act(owner):
            for kind in range(3):
                for step in range(1, LINE):
                    self.push(kind, step, owner).wait_send()
            for line in range(LINE):
                if owner:
                    self.over(line).wait_send()
                else:
                    self.across(line).wait_send()
                    self.across_far(line).wait_send()
            if owner:
                self.out_over().wait_send()
            else:
                self.out_push().wait_send()

        self.each(act)


class MlpSpread:
    @staticmethod
    def scratch():
        return [dma(2, 8), dma(2, 8), dma(2)]

    def __init__(self, weights, outs, sems):
        self.weights, self.outs = weights, outs
        self.s, self.r, self.own = sems
        self.z, self.y, self.c, self.h = place()
        self.chip = self.z * 2 + self.y
        self.part = weights[0].shape[1] // 8

    def columns(self, index):
        return pl.ds(pl.multiple_of(index * self.part, self.part), self.part)

    def push(self, kind, step):
        chip = (self.chip + step) % 8
        return remote(
            self.weights[kind].at[:, self.columns(chip)], self.outs[kind].at[self.chip], self.s.at[kind, step],
            self.r.at[kind, step], device(chip // 2, chip % 2, self.c, self.h),
        )

    def pull(self, kind, step):
        ref = self.outs[kind].at[(self.chip + 8 - step) % 8]
        return remote(ref, ref, self.s.at[kind, step], self.r.at[kind, step], device(self.z, self.y, self.c, self.h))

    def keep(self, kind):
        return local(self.weights[kind].at[:, self.columns(self.chip)], self.outs[kind].at[self.chip], self.own.at[kind])

    def start(self):
        for kind in range(2):
            self.keep(kind).start()
            for step in range(1, 8):
                self.push(kind, step).start()

    def finish(self):
        for kind in range(2):
            self.keep(kind).wait()
            for step in range(1, 8):
                self.pull(kind, step).wait_recv()
                self.push(kind, step).wait_send()


class MlpShare:
    @staticmethod
    def scratch():
        return [dma(2), dma(2, 2), dma(2, 2), dma(2, 2), dma(2, 2)]

    def __init__(self, quarters, outs, sems):
        self.quarters, self.outs = quarters, outs
        self.own, self.x_s, self.x_r, self.c_s, self.c_r = sems
        self.z, self.y, self.c, self.h = place()
        self.part = quarters[0].shape[2]

    def slot(self, kind, cut, half):
        columns = pl.ds(pl.multiple_of(half * self.part, self.part), self.part)
        return self.outs[kind].at[pl.ds(cut * 4, 4), self.c, :, columns]

    def keep(self, kind):
        columns = pl.ds(pl.multiple_of(self.h * self.part, self.part), self.part)
        return local(self.quarters[kind], self.outs[kind].at[:, self.c, :, columns], self.own.at[kind])

    def over(self, kind, cut, half):
        return remote(
            self.quarters[kind].at[pl.ds(cut * 4, 4)], self.slot(kind, cut, half), self.x_s.at[kind, cut],
            self.x_r.at[kind, cut], device(self.z, self.y, self.c, 1 - self.h),
        )

    def share(self, kind, cut, core):
        ref = self.outs[kind].at[pl.ds(cut * 4, 4), core]
        return remote(
            ref, ref, self.c_s.at[kind, cut], self.c_r.at[kind, cut], device(self.z, self.y, 1 - self.c, self.h)
        )

    def start(self):
        for kind in range(2):
            for cut in range(2):
                self.over(kind, cut, self.h).start()
            self.keep(kind).start()

    def relay(self):
        for kind in range(2):
            self.keep(kind).wait()
            for cut in range(2):
                self.over(kind, cut, 1 - self.h).wait_recv()
                self.share(kind, cut, self.c).start()

    def finish(self):
        for kind in range(2):
            for cut in range(2):
                self.share(kind, cut, 1 - self.c).wait_recv()
                self.share(kind, cut, self.c).wait_send()
                self.over(kind, cut, self.h).wait_send()


class DownSpread:
    @staticmethod
    def scratch():
        return [dma(1), dma(2), dma(2)]

    def __init__(self, weight, out, sems):
        self.weight, self.out = weight, out
        self.d_own, self.d_x, self.d_sib = sems
        self.z, self.y, self.c, self.h = place()

    def keep(self):
        return local(self.weight, self.out.at[self.h, self.c], self.d_own.at[0])

    def over(self):
        return remote(
            self.weight, self.out.at[self.h, self.c], self.d_x.at[0], self.d_x.at[1],
            device(self.z, self.y, self.c, 1 - self.h),
        )

    def over_in(self):
        ref = self.out.at[1 - self.h, self.c]
        return remote(ref, ref, self.d_x.at[0], self.d_x.at[1], device(self.z, self.y, self.c, self.h))

    def share(self):
        ref = self.out.at[:, self.c]
        return remote(ref, ref, self.d_sib.at[0], self.d_sib.at[1], device(self.z, self.y, 1 - self.c, self.h))

    def share_in(self):
        ref = self.out.at[:, 1 - self.c]
        return remote(ref, ref, self.d_sib.at[0], self.d_sib.at[1], device(self.z, self.y, self.c, self.h))

    def start(self):
        self.keep().start()
        self.over().start()

    def relay(self):
        self.keep().wait()
        self.over_in().wait_recv()
        self.share().start()

    def finish(self):
        self.share_in().wait_recv()
        self.share().wait_send()
        self.over().wait_send()


class NoteSpread:
    @staticmethod
    def scratch():
        return [dma(16), dma(16), dma(1)]

    def __init__(self, note, out, sems):
        self.note, self.out = note, out
        self.s, self.r, self.own = sems
        self.blk, self.h = lax.axis_index("blk"), lax.axis_index("head")

    def push(self, step):
        other = (self.blk + step) % 16
        return remote(self.note, self.out.at[self.blk], self.s.at[step], self.r.at[step], (other, self.h))

    def pull(self, step):
        ref = self.out.at[(self.blk + 16 - step) % 16]
        return remote(ref, ref, self.s.at[step], self.r.at[step], (self.blk, self.h))

    def keep(self):
        return local(self.note, self.out.at[self.blk], self.own.at[0])

    def start(self):
        self.keep().start()
        for step in range(1, 16):
            self.push(step).start()

    def finish(self):
        self.keep().wait()
        for step in range(1, 16):
            self.pull(step).wait_recv()
            self.push(step).wait_send()


def split_refs(refs, counts):
    groups, at = [], 0
    for count in counts:
        groups.append(refs[at : at + count])
        at += count
    return groups


def core_kernel(
    attended, out_w, gate_in, up_in, wd, tokens, gain, cot, cot_in,
    hidden_out, active, mlp_part, gathered, grad_hidden, gain_term, gate, up,
    normed, src, total, gate_w, up_w, down_w, gate_factor, up_factor, cot_pairs, parts, stage, gate_grad, up_grad, branch,
    cot_s, stage_s, *refs,
):
    gather_sems, back_sems, share_sems, down_sems, reduce_refs, quarter_refs = split_refs(
        refs, (8, 8, 5, 3, Reduce.COUNT, 8)
    )
    z, y, c, h = place()
    greet(device(z, y, 1 - c, h))
    greet(device(z, y, c, 1 - h))
    greet_plane(2)
    gather = Gather(src, normed, gather_sems)
    back = Gather(branch, gathered, back_sems)
    share = MlpShare((gate_in, up_in), (gate_w, up_w), share_sems)
    downs = DownSpread(wd, down_w, down_sems)
    reduce = Reduce(parts, reduce_refs)
    grads = QuarterReduce((gate_w, up_w), (gate, up), quarter_refs)
    rows, width = normed.shape[1:]
    hidden = gate_w.shape[3]
    step = hidden // 4
    pair = 2 * rows
    order = (2, 0, 1, 3)

    def cot_load(place_at):
        return local(cot_in.at[pl.ds(reduce.order[place_at] * 2, 2)], cot_pairs.at[place_at % 2], cot_s.at[place_at % 2])

    cot_load(0).start()
    cot_load(1).start()

    share.start()
    for place_at in range(4):
        line = reduce.order[place_at]
        both = attended[pl.ds(pl.multiple_of(line * pair, pair), pair)]
        parts[pl.ds(line * 2, 2)] = product(both, out_w[...]).astype(jnp.bfloat16).reshape(2, rows, width)
        reduce.start(place_at)
    for place_at in range(3):
        reduce.relay(place_at)
    reduce.total(total)
    hidden_rows = tokens[...].astype(jnp.float32) + total[...]
    hidden_out[...] = hidden_rows
    src[...] = (hidden_rows * rms_scale(hidden_rows) * gain[...]).astype(jnp.bfloat16)
    gather.start()
    share.relay()
    downs.start()
    reduce.finish()

    def forward(chip, own=False):
        shard = src if own else normed.at[chip]

        @pl.loop(0, 4)
        def _(tile):
            columns = pl.ds(pl.multiple_of(tile * step, step), step)
            gate_part = product(shard[...], gate_w[:, :, :, columns].reshape(width, step))
            up_part = product(shard[...], up_w[:, :, :, columns].reshape(width, step))
            sigmoid = jax.nn.sigmoid(gate_part)
            silu = gate_part * sigmoid
            slope = sigmoid * (1.0 + gate_part * (1.0 - sigmoid))
            gate_factor[chip, :, columns] = (up_part * slope).astype(jnp.bfloat16)
            up_factor[chip, :, columns] = silu.astype(jnp.bfloat16)
            active[chip, :, columns] = (silu * up_part).astype(jnp.bfloat16)

    def forward_own(distance):
        @pl.when(z - distance >= 0)
        def _():
            forward((z - distance) * 2 + y)

        @pl.when(z + distance <= LINE - 1)
        def _():
            forward((z + distance) * 2 + y)

    def forward_other(distance):
        def one(line):
            for elem in (0, 1):
                gather.across_in(line, elem).wait_recv()
            forward(line * 2 + 1 - y)

        if distance == 0:
            one(z)
        else:

            @pl.when(z - distance >= 0)
            def _():
                one(z - distance)

            @pl.when(z + distance <= LINE - 1)
            def _():
                one(z + distance)

    def relay(distance):
        for elem in order:
            gather.relay(distance - 1, elem)

    gather.relay_b()
    share.finish()
    forward(z * 2 + y, own=True)
    relay(1)
    forward_other(0)
    forward_own(1)
    relay(2)
    forward_other(1)
    forward_own(2)
    relay(3)
    downs.relay()
    forward_other(2)
    forward_own(3)
    forward_other(3)
    gather.own_copy().wait()
    downs.finish()

    def backward(place_at):
        line = reduce.order[place_at]
        both = pl.ds(line * 2, 2)
        cot_load(place_at).wait()

        @pl.loop(0, 4)
        def _(tile):
            columns = pl.ds(pl.multiple_of(tile * step, step), step)
            grad_active = times_transposed(
                cot_pairs[place_at % 2].reshape(pair, width), down_w[tile // 2, tile % 2]
            ).reshape(2, rows, step)
            gate_grad[both, :, columns] = (grad_active * gate_factor[both, :, columns].astype(jnp.float32)).astype(jnp.bfloat16)
            up_grad[both, :, columns] = (grad_active * up_factor[both, :, columns].astype(jnp.float32)).astype(jnp.bfloat16)

        if place_at < 2:
            cot_load(place_at + 2).start()

        @pl.loop(0, 4)
        def _(tile):
            columns = pl.ds(pl.multiple_of(tile * (width // 4), width // 4), width // 4)
            chips = pl.ds(tile * 2, 2)
            part = times_transposed(gate_grad[both].reshape(pair, hidden), gate_w[chips].reshape(width // 4, hidden))
            part += times_transposed(up_grad[both].reshape(pair, hidden), up_w[chips].reshape(width // 4, hidden))
            parts[both, :, columns] = part.astype(jnp.bfloat16).reshape(2, rows, width // 4)

    def stage_store(line):
        return local(stage, mlp_part.at[pl.ds(line * 2, 2)], stage_s)

    def contribute(line):
        if line:
            stage_store(line - 1).wait()

        @pl.loop(0, 4)
        def _(tile):
            columns = pl.ds(pl.multiple_of(tile * (width // 4), width // 4), width // 4)
            part = product(
                active[pl.ds(line * 2, 2)].reshape(pair, hidden), down_w[:, :, :, columns].reshape(hidden, width // 4)
            )
            stage[:, :, columns] = part.astype(jnp.bfloat16).reshape(2, rows, width // 4)

        stage_store(line).start()

    def weight_grad(kind):
        source = (gate_grad, up_grad)[kind]
        store = (gate_w, up_w)[kind]

        @pl.loop(0, 8)
        def _(tile):
            columns = pl.ds(pl.multiple_of(tile * pair, pair), pair)
            part = transposed_times(
                normed[:, :, columns].reshape(8 * rows, pair), source[...].reshape(8 * rows, hidden)
            )
            store[tile] = part.astype(jnp.bfloat16).reshape(2, rows, hidden)

    for place_at in range(3):
        backward(place_at)
        reduce.start(place_at)
    reduce.relay(0)
    backward(3)
    reduce.start(3)
    contribute(0)
    contribute(1)
    reduce.relay(1)
    weight_grad(0)
    for cut in range(2):
        grads.share(0, cut).start()
    contribute(2)
    contribute(3)
    reduce.relay(2)
    grads.relay(0)
    reduce.total(total)

    inputs = hidden_out[...]
    inv_scale = rms_scale(inputs)
    unit_rows = inputs * inv_scale
    grad_unit = total[...] * gain[...]
    mean = jnp.mean(grad_unit * unit_rows, axis=-1, keepdims=True)
    grad_rows = cot[...].astype(jnp.float32) + inv_scale * (grad_unit - unit_rows * mean)
    grad_hidden[...] = grad_rows
    branch[...] = grad_rows.astype(jnp.bfloat16)
    back.start()
    gain_term[...] = jnp.sum(total[...] * unit_rows, axis=0, keepdims=True)
    back.relay_b()
    weight_grad(1)
    for cut in range(2):
        grads.share(1, cut).start()
    for elem in order:
        back.relay(0, elem)
    grads.relay(1)
    for elem in order:
        back.relay(1, elem)
    grads.finish(0)
    for elem in order:
        back.relay(2, elem)
    grads.finish(1)
    back.finish()
    reduce.finish()
    stage_store(3).wait()
    for line in range(LINE):
        for elem in (0, 1):
            gather.across(line, elem).wait_send()
    gather.finish_sends()


def core(attended, out_w, gate, up, wd, tokens, gain, cot, cot_all):
    eight, depth, part = gate.shape
    rows, width = tokens.shape
    hidden = 2 * part

    def room(*dims, dtype=jnp.bfloat16):
        return pltpu.VMEM(dims, dtype)

    def shape(*dims, dtype=jnp.bfloat16):
        return jax.ShapeDtypeStruct(dims, dtype)

    f32 = jnp.float32
    return pl.pallas_call(
        core_kernel,
        out_shape=(
            shape(rows, width, dtype=f32),
            shape(8, rows, hidden),
            shape(8, rows, width),
            shape(8, rows, width),
            shape(rows, width, dtype=f32),
            shape(1, width, dtype=f32),
            shape(8, depth, part),
            shape(8, depth, part),
        ),
        in_specs=[INSIDE, INSIDE, ANY, ANY, ANY, INSIDE, INSIDE, INSIDE, ANY],
        out_specs=(INSIDE, INSIDE, ANY, ANY, INSIDE, INSIDE, INSIDE, INSIDE),
        scratch_shapes=[
            room(8, rows, width), room(rows, width), room(rows, width, dtype=f32),
            room(eight, 2, depth, hidden), room(eight, 2, depth, hidden), room(2, 2, *wd.shape),
            room(8, rows, hidden), room(8, rows, hidden),
            room(2, 2, rows, width), room(8, rows, width), room(2, rows, width),
            room(8, rows, hidden), room(8, rows, hidden), room(rows, width),
            dma(2), dma(),
        ]
        + Gather.scratch()
        + Gather.scratch()
        + MlpShare.scratch()
        + DownSpread.scratch()
        + Reduce.scratch(width)
        + QuarterReduce.scratch(depth, hidden),
        compiler_params=kernel_params(8),
        name="core",
    )(attended, out_w, gate, up, wd, tokens, gain, cot, cot_all)


def column_of(row):
    size = row.shape[1]
    same = lax.broadcasted_iota(jnp.int32, (size, size), 0) == lax.broadcasted_iota(jnp.int32, (size, size), 1)
    return jnp.sum(jnp.where(same, row, 0.0), axis=1, keepdims=True)


def row_of(column):
    size = column.shape[0]
    same = lax.broadcasted_iota(jnp.int32, (size, size), 0) == lax.broadcasted_iota(jnp.int32, (size, size), 1)
    return jnp.sum(jnp.where(same, column, 0.0), axis=0, keepdims=True)


def front_kernel(
    tokens, cot, note, inv_freqs, wq, wk, wv, wo, wg, wu,
    kv_out, normed_out, qkv_out, out_w, notes, cos_table, sine_table, query, attended_out, attended_low_out,
    log_out, cot_out, gate, up,
    gathered, normed, qkv_w, gain, query_ids, key_ids, kv, keys, scores, total,
    own, x_s, x_r, c_s, c_r, store_s, *sems,
):
    z, y, c, h = place()
    tok_sems, note_sems, attn_sems, cot_sems, mlp_sems = split_refs(sems, (8, 3, AttnSpread.COUNT, 8, 3))
    greet_all(16, 2)
    rows, width = tokens.shape[0], HD
    pair = 2 * rows
    tok = Gather(tokens, gathered, tok_sems)
    notices = NoteSpread(note, notes, note_sems)
    attn = AttnSpread((wq, wk, wv, wo), (qkv_w, out_w), attn_sems)
    cots = Gather(cot, cot_out, cot_sems)
    mlp = MlpSpread((wg, wu), (gate, up), mlp_sems)

    def keep(cut):
        part = pl.ds(cut * 2, 2)
        return local(kv.at[part], keys.at[part, c, h], own.at[cut])

    def over(cut, half):
        part = pl.ds(cut * 2, 2)
        return remote(kv.at[part], keys.at[part, c, half], x_s.at[cut], x_r.at[cut], device(z, y, c, 1 - h))

    def share(cut, core):
        ref = keys.at[pl.ds(cut * 2, 2), core]
        return remote(ref, ref, c_s.at[cut], c_r.at[cut], device(z, y, 1 - c, h))

    def tables():
        for blk in range(16):
            gain[:, pl.ds(blk * rows, rows)] = notes[blk, 4:5, :]
        for chip in range(8):
            part = pl.ds(chip * rows, rows)
            mine = notes[2 * chip + c]
            angles = column_of(jnp.where(h == 0, mine[0:1], mine[1:2])) * inv_freqs[...]
            cos_table[part] = jnp.cos(angles)
            sine_table[part] = jnp.sin(angles)
            query_ids[part] = column_of(jnp.where(h == 0, mine[2:3], mine[3:4]))
            for piece in range(4):
                key_ids[chip, :, pl.ds(piece * rows, rows)] = notes[2 * chip + piece // 2, 2 + piece % 2 : 3 + piece % 2, :]

    def project(cut):
        part = pl.ds(cut * pair, pair)
        inputs = gathered[pl.ds(cut * 2, 2)].reshape(pair, tokens.shape[1]).astype(jnp.float32)
        rows_normed = (inputs * rms_scale(inputs) * gain[...]).astype(jnp.bfloat16)
        normed[part] = rows_normed
        cos_rows, sine_rows = cos_table[part], sine_table[part]

        def turn(lower, upper):
            return (
                (lower * cos_rows - upper * sine_rows).astype(jnp.bfloat16),
                (upper * cos_rows + lower * sine_rows).astype(jnp.bfloat16),
            )

        def weight(columns):
            return qkv_w[:, :, :, columns].reshape(tokens.shape[1], columns.size)

        half = width // 2
        projected = product(rows_normed, weight(pl.ds(0, width)))
        lower, upper = turn(projected[:, :half], projected[:, half:])
        query[part, :half] = (lower.astype(jnp.float32) * HD**-0.5).astype(jnp.bfloat16)
        query[part, half:] = (upper.astype(jnp.float32) * HD**-0.5).astype(jnp.bfloat16)
        projected = product(rows_normed, weight(pl.ds(width, 2 * width)))
        lower, upper = turn(projected[:, :half], projected[:, half:width])
        both = pl.ds(cut * 2, 2)
        kv[both, :, :half] = lower.reshape(2, rows, half)
        kv[both, :, half:width] = upper.reshape(2, rows, half)
        kv[both, :, width:] = projected[:, width:].astype(jnp.bfloat16).reshape(2, rows, width)
        over(cut, h).start()
        keep(cut).start()

    def pass_on(cut):
        keep(cut).wait()
        over(cut, 1 - h).wait_recv()
        share(cut, c).start()

    def attend(place_at):
        part = pl.ds(place_at * pair, pair)
        count = min(2 * place_at + 3, 8)
        ids = query_ids[part]

        def maxima(block, best):
            key = keys[block, :, :, :, :width].reshape(4 * rows, width)
            part_scores = times_transposed(query[part], key)
            part_scores = jnp.where(key_ids[block] <= ids, part_scores, -1e30)
            scores[block] = part_scores
            for lane in range(4 * rows // 128):
                best = jnp.maximum(best, part_scores[:, lane * 128 : lane * 128 + 128])
            return best

        best = lax.fori_loop(0, count, maxima, jnp.full((pair, 128), -1e30, jnp.float32))
        row_max = jnp.max(best, axis=1, keepdims=True)
        total[...] = jnp.zeros_like(total)

        def mix(block, sums):
            weights = jnp.exp(scores[block] - row_max)
            value = keys[block, :, :, :, width:].reshape(4 * rows, width)
            total[...] += product(weights.astype(jnp.bfloat16), value)
            for lane in range(4 * rows // 128):
                sums = sums + weights[:, lane * 128 : lane * 128 + 128]
            return sums

        sums = lax.fori_loop(0, count, mix, jnp.zeros((pair, 128), jnp.float32))
        row_sum = jnp.sum(sums, axis=1, keepdims=True)
        mixed = total[...] / row_sum
        attended_out[part] = mixed
        attended_low_out[part] = mixed.astype(jnp.bfloat16)
        log_out[place_at] = row_of(row_max + jnp.log(row_sum))

    order = (2, 0, 1, 3)
    attn.start()
    tok.start()
    notices.start()
    tok.relay_b()
    attn.relay(0)
    for elem in order:
        tok.relay(0, elem)
    attn.relay(1)
    attn.relay(2)
    for elem in order:
        tok.relay(1, elem)
    attn.relay(3)
    attn.relay_out()
    notices.finish()
    tables()
    for elem in order:
        tok.relay(2, elem)
    cots.start()
    mlp.start()
    for step in range(LINE):
        attn.relay_share(step)
    attn.relay_out_share()
    tok.finish()
    attn.finish()
    store_qkv = local(qkv_w, qkv_out, store_s.at[0])
    store_qkv.start()
    for cut in range(LINE):
        project(cut)
    store_normed = local(normed, normed_out, store_s.at[1])
    store_normed.start()
    cots.relay_b()
    for elem in order:
        cots.relay(0, elem)
    pass_on(0)
    pass_on(1)
    share(0, 1 - c).wait_recv()
    share(1, 1 - c).wait_recv()
    attend(0)
    for elem in order:
        cots.relay(1, elem)
    pass_on(2)
    share(2, 1 - c).wait_recv()
    attend(1)
    pass_on(3)
    share(3, 1 - c).wait_recv()
    store = local(keys, kv_out, store_s.at[2])
    store.start()
    attend(2)
    for elem in order:
        cots.relay(2, elem)
    attend(3)
    cots.finish()
    mlp.finish()
    for cut in range(LINE):
        share(cut, c).wait_send()
        over(cut, h).wait_send()
    store.wait()
    store_normed.wait()
    store_qkv.wait()


def front(tokens, cot, note, inv_freqs, wq, wk, wv, wo, wg, wu):
    rows, width = tokens.shape
    depth, part = wg.shape[0], wg.shape[1] // 8
    token_rows = 8 * rows

    def room(*dims, dtype=jnp.bfloat16):
        return pltpu.VMEM(dims, dtype)

    def shape(*dims, dtype=jnp.bfloat16):
        return jax.ShapeDtypeStruct(dims, dtype)

    f32 = jnp.float32
    return pl.pallas_call(
        front_kernel,
        out_shape=(
            shape(8, 2, 2, rows, 2 * HD),
            shape(token_rows, width),
            shape(8, 2, depth, 3 * HD),
            shape(2, 2, wo.shape[0], width),
            shape(16, *note.shape, dtype=f32),
            shape(token_rows, HD // 2, dtype=f32),
            shape(token_rows, HD // 2, dtype=f32),
            shape(token_rows, HD),
            shape(token_rows, HD, dtype=f32),
            shape(token_rows, HD),
            shape(LINE, 1, token_rows // LINE, dtype=f32),
            shape(8, *cot.shape),
            shape(8, depth, part),
            shape(8, depth, part),
        ),
        in_specs=[INSIDE] * 10,
        out_specs=(ANY, ANY, ANY, ANY) + (INSIDE,) * 7 + (ANY, ANY, ANY),
        scratch_shapes=[
            room(8, rows, width),
            room(token_rows, width),
            room(8, 2, depth, 3 * HD),
            room(1, width, dtype=f32),
            room(token_rows, 1, dtype=f32),
            room(8, 1, 4 * rows, dtype=f32),
            room(8, rows, 2 * HD),
            room(8, 2, 2, rows, 2 * HD),
            room(8, token_rows // LINE, 4 * rows, dtype=f32),
            room(token_rows // LINE, HD, dtype=f32),
        ]
        + [dma(4)] * 5
        + [dma(3)]
        + Gather.scratch()
        + NoteSpread.scratch()
        + AttnSpread.scratch(depth)
        + Gather.scratch()
        + MlpSpread.scratch(),
        compiler_params=kernel_params(3),
        name="front",
    )(tokens, cot, note, inv_freqs, wq, wk, wv, wo, wg, wu)


class QuarterReduce:
    @staticmethod
    def scratch(depth, wide):
        sib = pltpu.VMEM((8, depth, wide), jnp.bfloat16)
        over = pltpu.VMEM((8, depth, wide // 2), jnp.bfloat16)
        return [sib, sib, over, over] + [dma(2, 2)] * 4

    def __init__(self, store, outs, refs):
        self.store, self.outs = store, outs
        self.sib, self.box = refs[0:2], refs[2:4]
        self.c_s, self.c_r, self.x_s, self.x_r = refs[4:]
        self.z, self.y, self.c, self.h = place()
        self.part = self.box[0].shape[2]

    def columns(self, half):
        return pl.ds(pl.multiple_of(half * self.part, self.part), self.part)

    def share(self, kind, cut):
        chips = pl.ds(cut * 4, 4)
        return remote(
            self.store[kind].at[chips, 1 - self.c], self.sib[kind].at[chips], self.c_s.at[kind, cut],
            self.c_r.at[kind, cut], device(self.z, self.y, 1 - self.c, self.h),
        )

    def over(self, kind, cut):
        chips = pl.ds(cut * 4, 4)
        return remote(
            self.store[kind].at[chips, self.c, :, self.columns(1 - self.h)], self.box[kind].at[chips],
            self.x_s.at[kind, cut], self.x_r.at[kind, cut], device(self.z, self.y, self.c, 1 - self.h),
        )

    def relay(self, kind):
        columns = self.columns(1 - self.h)
        for cut in range(2):
            self.share(kind, cut).wait_recv()

            @pl.loop(cut * 4, cut * 4 + 4)
            def _(chip):
                add_into(self.store[kind].at[chip, self.c, :, columns], self.sib[kind].at[chip, :, columns])

            self.over(kind, cut).start()

    def finish(self, kind):
        columns = self.columns(self.h)
        for cut in range(2):
            self.over(kind, cut).wait_recv()

            @pl.loop(cut * 4, cut * 4 + 4)
            def _(chip):
                total = self.store[kind][chip, self.c, :, columns].astype(jnp.float32)
                total += self.sib[kind][chip, :, columns].astype(jnp.float32)
                total += self.box[kind][chip].astype(jnp.float32)
                self.outs[kind][chip] = total.astype(jnp.bfloat16)

        for cut in range(2):
            self.share(kind, cut).wait_send()
            self.over(kind, cut).wait_send()


class QuarterScatter:
    @staticmethod
    def scratch():
        return [dma(2, 8), dma(2, 8), dma(2)]

    def __init__(self, quarters, outs, sems):
        self.quarters, self.outs = quarters, outs
        self.s, self.r, self.own = sems
        self.z, self.y, self.c, self.h = place()
        self.chip = self.z * 2 + self.y
        self.part = quarters[0].shape[2]

    def columns(self, chip):
        return pl.ds(pl.multiple_of(chip * self.part, self.part), self.part)

    def push(self, kind, step):
        target = (self.chip + step) % 8
        return remote(
            self.quarters[kind].at[target], self.outs[kind].at[:, self.columns(self.chip)], self.s.at[kind, step],
            self.r.at[kind, step], device(target // 2, target % 2, self.c, self.h),
        )

    def pull(self, kind, step):
        ref = self.outs[kind].at[:, self.columns((self.chip + 8 - step) % 8)]
        return remote(ref, ref, self.s.at[kind, step], self.r.at[kind, step], device(self.z, self.y, self.c, self.h))

    def keep(self, kind):
        return local(self.quarters[kind].at[self.chip], self.outs[kind].at[:, self.columns(self.chip)], self.own.at[kind])

    def start(self):
        for kind in range(2):
            self.keep(kind).start()
            for step in range(1, 8):
                self.push(kind, step).start()

    def finish(self):
        for kind in range(2):
            self.keep(kind).wait()
            for step in range(1, 8):
                self.pull(kind, step).wait_recv()
                self.push(kind, step).wait_send()


class DownReduce:
    @staticmethod
    def scratch(rows, width):
        return [
            pltpu.VMEM((2, 2, rows, width), jnp.bfloat16),
            pltpu.VMEM((2, rows, width), jnp.bfloat16),
            pltpu.VMEM((rows, width), jnp.bfloat16),
            dma(2), dma(2),
        ]

    def __init__(self, out, refs):
        self.out = out
        self.store, self.sib, self.box, self.c_sr, self.x_sr = refs
        self.z, self.y, self.c, self.h = place()

    def share(self):
        return remote(
            self.store.at[:, 1 - self.c], self.sib, self.c_sr.at[0], self.c_sr.at[1],
            device(self.z, self.y, 1 - self.c, self.h),
        )

    def over(self):
        return remote(
            self.store.at[1 - self.h, self.c], self.box, self.x_sr.at[0], self.x_sr.at[1],
            device(self.z, self.y, self.c, 1 - self.h),
        )

    def relay(self):
        self.share().wait_recv()
        add_into(self.store.at[1 - self.h, self.c], self.sib.at[1 - self.h])
        self.over().start()

    def finish(self):
        self.over().wait_recv()
        total = self.store[self.h, self.c].astype(jnp.float32) + self.sib[self.h].astype(jnp.float32)
        self.out[...] = total + self.box[...].astype(jnp.float32)
        self.share().wait_send()
        self.over().wait_send()


class OutGrad:
    @staticmethod
    def scratch(rows, width):
        def room(*dims):
            return pltpu.VMEM(dims, jnp.bfloat16)

        return [room(2, 2, rows, width), room(2, rows, width), room(2, rows, width), dma(2), dma(2), dma(2), dma(1)]

    def __init__(self, out, refs):
        self.out = out
        self.store, self.sib, self.box, self.c_sr, self.x_sr, self.y_sr, self.own = refs
        self.z, self.y, self.c, self.h = place()
        self.me = device(self.z, self.y, self.c, self.h)
        self.owner = self.h == self.y

    def share(self):
        return remote(
            self.store.at[:, 1 - self.c], self.sib, self.c_sr.at[0], self.c_sr.at[1],
            device(self.z, self.y, 1 - self.c, self.h),
        )

    def over(self):
        return remote(
            self.store.at[:, self.c], self.box, self.x_sr.at[0], self.x_sr.at[1],
            device(self.z, self.y, self.c, 1 - self.h),
        )

    def move(self):
        return remote(
            self.store.at[1 - self.y, self.c], self.out, self.y_sr.at[0], self.y_sr.at[1],
            device(self.z, 1 - self.y, self.c, self.h),
        )

    def keep(self):
        return local(self.store.at[self.y, self.c], self.out, self.own.at[0])

    def relay(self):
        self.share().wait_recv()
        for pair in range(2):
            add_into(self.store.at[pair, self.c], self.sib.at[pair])

        @pl.when(jnp.logical_not(self.owner))
        def _():
            self.over().start()

    def send(self):
        @pl.when(self.owner)
        def _():
            self.over().wait_recv()
            for pair in range(2):
                add_into(self.store.at[pair, self.c], self.box.at[pair])
            self.move().start()
            self.keep().start()

    def finish(self):
        self.share().wait_send()

        @pl.when(jnp.logical_not(self.owner))
        def _():
            remote(self.out, self.out, self.y_sr.at[0], self.y_sr.at[1], self.me).wait_recv()
            self.over().wait_send()

        @pl.when(self.owner)
        def _():
            self.keep().wait()
            self.move().wait_send()


def attend_back_kernel(
    query, keys_in, branch_in, out_w, attended, attended_low, log_row, notes, cos_table, sine_table, gate_in, up_in,
    side_out, grad_query, gate, up, out_grad,
    keys, branch, grad_out, delta_row, query_row, key_column, grad_rot, parts, grad_key, grad_value, sib_in, x_in, z_in,
    load_s, c_s, c_r, x_s, x_r, z_s, z_r, *sems,
):
    z, y, c, h = place()
    mate = z + 1 - 2 * (z % 2)
    loads = [local(keys_in, keys, load_s.at[0]), local(branch_in, branch, load_s.at[1])]
    for load in loads:
        load.start()
    greet_all(16, 2)
    scatter_sems, out_refs = split_refs(sems, (3, 7))
    scatter = QuarterScatter((gate_in, up_in), (gate, up), scatter_sems)
    outs = OutGrad(out_grad, out_refs)
    scatter.start()
    width = query.shape[1]
    rows = branch.shape[1]
    pair = 2 * rows
    block_rows = 4 * rows

    def share(block):
        return remote(
            parts.at[block, 1 - c], sib_in.at[block], c_s.at[block], c_r.at[block], device(z, y, 1 - c, h)
        )

    def over(block):
        return remote(
            parts.at[block, c, 1 - h], x_in.at[block], x_s.at[block], x_r.at[block], device(z, y, c, 1 - h)
        )

    def columns(kind):
        return pl.ds(pl.multiple_of(kind * width, width), width)

    def across(block):
        return remote(
            parts.at[block, c, h, :, columns(1 - z % 2)], z_in.at[block], z_s.at[block], z_r.at[block],
            device(mate, y, c, h),
        )

    def stage_two(block):
        share(block).wait_recv()
        add_into(parts.at[block, c, 1 - h], sib_in.at[block, 1 - h])
        over(block).start()

    def stage_three(block):
        over(block).wait_recv()
        add_into(parts.at[block, c, h], sib_in.at[block, h], x_in.at[block])
        across(block).start()

    def turn_back(values, part):
        half = width // 2
        lower, upper = values[:, :half], values[:, half:]
        cos_rows, sine_rows = cos_table[part], sine_table[part]
        return (
            (lower * cos_rows + upper * sine_rows).astype(jnp.bfloat16),
            (upper * cos_rows - lower * sine_rows).astype(jnp.bfloat16),
        )

    def stage_four(block):
        across(block).wait_recv()
        total = parts[block, c, h, :, columns(z % 2)].astype(jnp.float32) + z_in[block].astype(jnp.float32)
        part = pl.ds(block * rows, rows)

        @pl.when(z % 2 == 0)
        def _():
            lower, upper = turn_back(total, part)
            side_out[part, : width // 2] = lower
            side_out[part, width // 2 :] = upper

        @pl.when(z % 2 == 1)
        def _():
            side_out[part] = total.astype(jnp.bfloat16)

    for chip in range(8):
        mine = notes[2 * chip + c]
        query_row[chip // 2, :, pl.ds((chip % 2) * rows, rows)] = jnp.where(h == 0, mine[2:3], mine[3:4])
        for piece in range(4):
            row = notes[2 * chip + piece // 2, 2 + piece % 2 : 3 + piece % 2, :]
            key_column[chip, pl.ds(piece * rows, rows)] = column_of(row)
    for load in loads:
        load.wait()
    grad_rot[...] = jnp.zeros_like(grad_rot)
    for place_at in range(LINE):
        part = pl.ds(place_at * pair, pair)
        grad_rows = times_transposed(branch[pl.ds(place_at * 2, 2)].reshape(pair, branch.shape[2]), out_w[...])
        grad_rows = grad_rows.astype(jnp.bfloat16)
        grad_out[part] = grad_rows
        delta = jnp.sum(grad_rows.astype(jnp.float32) * attended[part], axis=1, keepdims=True)
        delta_row[place_at] = row_of(delta)
    out_store = out_refs[0]

    @pl.loop(0, 4)
    def _(tile):
        tile_columns = pl.ds(pl.multiple_of(tile * 512, 512), 512)
        part = transposed_times(attended_low[...], branch[:, :, tile_columns].reshape(8 * rows, 512))
        out_store[:, :, :, tile_columns] = part.astype(jnp.bfloat16).reshape(2, 2, out_store.shape[2], 512)

    outs.share().start()
    for block in range(8):
        key = keys[block, :, :, :, :width].reshape(block_rows, width)
        value = keys[block, :, :, :, width:].reshape(block_rows, width)
        grad_key[...] = jnp.zeros_like(grad_key)
        grad_value[...] = jnp.zeros_like(grad_value)

        @pl.loop(max(0, (block - 1) // 2), LINE)
        def _(place_at):
            part = pl.ds(pl.multiple_of(place_at * pair, pair), pair)
            part_scores = times_transposed(key, query[part])
            visible = key_column[block] <= query_row[place_at]
            weights = jnp.where(visible, jnp.exp(part_scores - log_row[place_at]), 0.0)
            grad_weights = times_transposed(value, grad_out[part])
            grad_scores = (weights * (grad_weights - delta_row[place_at])).astype(jnp.bfloat16)
            grad_key[...] += product(grad_scores, query[part])
            grad_value[...] += product(weights.astype(jnp.bfloat16), grad_out[part])
            grad_rot[part] += transposed_times(grad_scores, key)

        parts[block, :, :, :, :width] = grad_key[...].astype(jnp.bfloat16).reshape(2, 2, rows, width)
        parts[block, :, :, :, width:] = grad_value[...].astype(jnp.bfloat16).reshape(2, 2, rows, width)
        share(block).start()
        if block == 0:
            outs.relay()
        if block >= 1:
            stage_two(block - 1)
        if block >= 4:
            stage_three(block - 4)
    stage_two(7)
    outs.send()
    for place_at in range(LINE):
        part = pl.ds(place_at * pair, pair)
        lower, upper = turn_back(grad_rot[part] * HD**-0.5, part)
        grad_query[part, : width // 2] = lower
        grad_query[part, width // 2 :] = upper
    for block in range(4, 8):
        stage_three(block)
        stage_four(block - 4)
    for block in range(4, 8):
        stage_four(block)
    for block in range(8):
        share(block).wait_send()
        over(block).wait_send()
        across(block).wait_send()
    scatter.finish()
    outs.finish()


def attend_back(query, keys, branch, out_w, attended, attended_low, log_row, notes, cos_table, sine_table, gate, up, out_rows):
    eight, _, _, rows, width = keys.shape
    tokens = query.shape[0]
    depth, part = gate.shape[1:]

    def room(*dims, dtype=jnp.bfloat16):
        return pltpu.VMEM(dims, dtype)

    def shape(*dims, dtype=jnp.bfloat16):
        return jax.ShapeDtypeStruct(dims, dtype)

    f32 = jnp.float32
    return pl.pallas_call(
        attend_back_kernel,
        out_shape=(
            shape(tokens, HD),
            shape(tokens, HD),
            shape(depth, 8 * part),
            shape(depth, 8 * part),
            shape(out_rows, out_w.shape[1]),
        ),
        in_specs=[INSIDE, ANY, ANY] + [INSIDE] * 9,
        out_specs=(INSIDE, INSIDE, ANY, ANY, ANY),
        scratch_shapes=[
            room(*keys.shape), room(*branch.shape), room(tokens, HD),
            room(LINE, 1, tokens // LINE, dtype=f32), room(LINE, 1, tokens // LINE, dtype=f32),
            room(8, 4 * rows, 1, dtype=f32), room(tokens, HD, dtype=f32), room(*keys.shape),
            room(4 * rows, HD, dtype=f32), room(4 * rows, HD, dtype=f32),
            room(eight, 2, rows, width), room(eight, rows, width), room(eight, rows, HD),
            dma(2),
        ] + [dma(8)] * 6 + QuarterScatter.scratch() + OutGrad.scratch(out_rows, out_w.shape[1]),
        compiler_params=kernel_params(11),
        name="attend_back",
    )(query, keys, branch, out_w, attended, attended_low, log_row, notes, cos_table, sine_table, gate, up)


class HeadGrads:
    @staticmethod
    def scratch(depth):
        def room(*dims):
            return pltpu.VMEM(dims, jnp.bfloat16)

        return [
            room(8, 2, depth, HD), room(8, 2, depth, HD),
            room(8, depth, HD), room(8, depth, HD),
            room(8, depth, HD), room(8, depth, HD),
            dma(2), dma(2), dma(2), dma(2), dma(3, 8), dma(3, 4, 8), dma(3),
        ]

    def __init__(self, outs, refs):
        self.outs = outs
        self.store, self.sib, self.box = refs[0:2], refs[2:4], refs[4:6]
        (self.c_s, self.c_r, self.x_s, self.x_r, self.s, self.r, self.own) = refs[6:]
        self.z, self.y, self.c, self.h = place()
        self.chip = self.z * 2 + self.y
        self.me = device(self.z, self.y, self.c, self.h)
        self.owner = self.h == self.y

    def share(self, i):
        return remote(
            self.store[i].at[:, 1 - self.c], self.sib[i], self.c_s.at[i], self.c_r.at[i],
            device(self.z, self.y, 1 - self.c, self.h),
        )

    def over(self, i):
        return remote(
            self.store[i].at[:, self.c], self.box[i], self.x_s.at[i], self.x_r.at[i],
            device(self.z, self.y, self.c, 1 - self.h),
        )

    def target(self, kind, line):
        start = line * HD if kind == 0 else (line // 2) * HD
        return self.outs[kind].at[:, pl.ds(pl.multiple_of(start, HD), HD)]

    def push(self, kind, step):
        chip = (self.chip + step) % 8
        return remote(
            self.store[min(kind, 1)].at[chip, self.c], self.target(kind, self.z), self.s.at[kind, step],
            self.r.at[kind, self.z, step], device(chip // 2, chip % 2, self.c, self.h),
        )

    def keep(self, kind):
        return local(self.store[min(kind, 1)].at[self.chip, self.c], self.target(kind, self.z), self.own.at[kind])

    def pull(self, kind, line, step):
        ref = self.target(kind, line)
        return remote(ref, ref, self.s.at[kind, step], self.r.at[kind, line, step], self.me)

    def relay(self, i):
        self.share(i).wait_recv()

        @pl.loop(0, 8)
        def _(at):
            add_into(self.store[i].at[at, self.c], self.sib[i].at[at])

        @pl.when(jnp.logical_not(self.owner))
        def _():
            self.over(i).start()

    def scatter(self, i):
        @pl.when(self.owner)
        def _():
            self.over(i).wait_recv()

            @pl.loop(0, 8)
            def _(at):
                add_into(self.store[i].at[at, self.c], self.box[i].at[at])

            if i == 0:
                self.keep(0).start()
                for step in range(1, 8):
                    self.push(0, step).start()
            else:
                for kind in (1, 2):

                    @pl.when(self.z % 2 == kind - 1)
                    def _():
                        self.keep(kind).start()
                        for step in range(1, 8):
                            self.push(kind, step).start()

    def finish(self):
        for kind in range(3):
            for line in range(LINE):
                if kind and line % 2 != kind - 1:
                    continue
                step = (self.chip + 8 - (line * 2 + self.h)) % 8

                @pl.when(step != 0)
                def _():
                    self.pull(kind, line, step).wait_recv()

                @pl.when(step == 0)
                def _():
                    self.keep(kind).wait()

        @pl.when(jnp.logical_not(self.owner))
        def _():
            for i in range(2):
                self.over(i).wait_send()

        @pl.when(self.owner)
        def _():
            for step in range(1, 8):
                self.push(0, step).wait_send()
            for kind in (1, 2):

                @pl.when(self.z % 2 == kind - 1)
                def _():
                    for step in range(1, 8):
                        self.push(kind, step).wait_send()

        for i in range(2):
            self.share(i).wait_send()


class GainSum:
    @staticmethod
    def scratch(rows):
        return [
            pltpu.VMEM((16, 8, rows), jnp.float32), pltpu.VMEM((32, 8, rows), jnp.float32), dma(32), dma(32),
        ]

    def __init__(self, out, refs):
        self.out = out
        self.terms, self.box, self.s, self.r = refs
        self.blk, self.h = lax.axis_index("blk"), lax.axis_index("head")

    def push(self, step):
        other = (self.blk + step // 2) % 16
        return remote(
            self.terms.at[other], self.box.at[step], self.s.at[step], self.r.at[step], (other, (self.h + step % 2) % 2)
        )

    def start(self, attn_term, mlp_term):
        rows = self.terms.shape[2]
        self.terms[...] = jnp.zeros_like(self.terms)
        for blk in range(16):
            part = pl.ds(blk * rows, rows)
            self.terms[blk, 0:1] = attn_term[:, part]
            self.terms[blk, 1:2] = mlp_term[:, part]
        for step in range(1, 32):
            self.push(step).start()

    def finish(self):
        total = self.terms[self.blk]
        for step in range(1, 32):
            self.push(step).wait_recv()
            total += self.box[step]
        self.out[...] = total
        for step in range(1, 32):
            self.push(step).wait_send()


def close_kernel(
    normed_in, qkv_w, mlp_part, active_in, cot_in, grad_query, grad_side, grad_hidden, hidden, tokens, gain, mlp_term,
    output, tokens_grad, gains, down, query, key, value,
    normed, weight, parts, mlp_parts, active, cot, total, attn_term, load_s, *refs,
):
    reduce_refs, mlp_refs, head_refs, gain_refs, down_refs = split_refs(refs, (Reduce.COUNT, Reduce.COUNT, 13, 4, 5))
    z, y, c, h = place()
    loads = [
        local(active_in, active, load_s.at[3]),
        local(cot_in, cot, load_s.at[4]),
        local(mlp_part, mlp_parts, load_s.at[5]),
    ]
    load = local(normed_in, normed, load_s.at[0])
    load_q = local(qkv_w.at[:, :, :, pl.ds(0, HD)], weight.at[0], load_s.at[1])
    side_columns = pl.ds(pl.multiple_of((1 + z % 2) * HD, HD), HD)
    load_side = local(qkv_w.at[:, :, :, side_columns], weight.at[1], load_s.at[2])
    load_q.start()
    load_side.start()
    load.start()
    for later in loads:
        later.start()
    greet_all(16, 2)
    reduce = Reduce(parts, reduce_refs)
    mlp_reduce = Reduce(mlp_parts, mlp_refs)
    downs = DownReduce(down, down_refs)
    heads = HeadGrads((query, key, value), head_refs)
    gain_sum = GainSum(gains, gain_refs)
    rows, width = parts.shape[1:]
    pair = 2 * rows
    depth = head_refs[0].shape[2]
    load_q.wait()
    load_side.wait()
    for place_at in range(4):
        line = reduce.order[place_at]
        both = pl.ds(pl.multiple_of(line * pair, pair), pair)

        @pl.loop(0, 4)
        def _(tile):
            columns = pl.ds(pl.multiple_of(tile * (width // 4), width // 4), width // 4)
            part = times_transposed(grad_query[both], weight[0, pl.ds(tile * 2, 2)].reshape(width // 4, HD))
            part += times_transposed(grad_side[both], weight[1, pl.ds(tile * 2, 2)].reshape(width // 4, HD))
            parts[pl.ds(line * 2, 2), :, columns] = part.astype(jnp.bfloat16).reshape(2, rows, width // 4)

        reduce.start(place_at)
    load.wait()
    for i, source in enumerate((grad_query, grad_side)):

        @pl.loop(0, 4)
        def _(tile):
            columns = pl.ds(pl.multiple_of(tile * 4 * depth, 4 * depth), 4 * depth)
            part = transposed_times(normed[:, columns], source[...])
            head_refs[i][pl.ds(tile * 2, 2)] = part.astype(jnp.bfloat16).reshape(2, 2, depth, HD)

        heads.share(i).start()
    heads.relay(0)
    heads.relay(1)
    reduce.relay(0)
    for later in loads:
        later.wait()
    down_rows = down.shape[0]

    def down_grad(tile):
        columns = pl.ds(tile * down_rows, down_rows)

        @pl.loop(0, 4)
        def _(piece):
            wide = pl.ds(pl.multiple_of(piece * (width // 4), width // 4), width // 4)
            part = transposed_times(
                active[:, :, columns].reshape(8 * rows, down_rows), cot[:, :, wide].reshape(8 * rows, width // 4)
            )
            down_refs[0][tile // 2, tile % 2, :, wide] = part.astype(jnp.bfloat16)

    for tile in range(4):
        down_grad(tile)
    downs.share().start()
    reduce.relay(1)
    downs.relay()
    reduce.relay(2)
    reduce.total(total)
    for place_at in range(4):
        mlp_reduce.start(place_at)
    inputs = tokens[...].astype(jnp.float32)
    inv_scale = rms_scale(inputs)
    unit_rows = inputs * inv_scale
    attn_term[...] = jnp.sum(total[...] * unit_rows, axis=0, keepdims=True)
    gain_sum.start(attn_term, mlp_term)
    grad_unit = total[...] * gain[...]
    mean = jnp.mean(grad_unit * unit_rows, axis=-1, keepdims=True)
    tokens_grad[...] = (grad_hidden[...] + inv_scale * (grad_unit - unit_rows * mean)).astype(jnp.bfloat16)
    reduce.finish()
    heads.scatter(0)
    heads.scatter(1)
    mlp_reduce.relay(0)
    downs.finish()
    mlp_reduce.relay(1)
    mlp_reduce.relay(2)
    heads.finish()
    gain_sum.finish()
    mlp_reduce.total(total)
    output[...] = (hidden[...] + total[...]).astype(jnp.bfloat16)
    mlp_reduce.finish()


def close(normed, qkv_w, mlp_part, active, cot, grad_query, grad_side, grad_hidden, hidden, tokens, gain, mlp_term):
    rows, width = tokens.shape
    down_rows = active.shape[2] // 4
    depth = qkv_w.shape[2]

    def room(*dims, dtype=jnp.bfloat16):
        return pltpu.VMEM(dims, dtype)

    def shape(*dims, dtype=jnp.bfloat16):
        return jax.ShapeDtypeStruct(dims, dtype)

    f32 = jnp.float32
    return pl.pallas_call(
        close_kernel,
        out_shape=(
            shape(rows, width),
            shape(rows, width),
            shape(8, rows, dtype=f32),
            shape(down_rows, width, dtype=f32),
            shape(depth, 4 * HD), shape(depth, 2 * HD), shape(depth, 2 * HD),
        ),
        in_specs=[ANY] * 5 + [INSIDE] * 7,
        out_specs=(INSIDE, INSIDE, INSIDE, INSIDE, ANY, ANY, ANY),
        scratch_shapes=[
            room(*normed.shape), room(2, 8, 2, depth, HD), room(8, rows, width), room(8, rows, width),
            room(*active.shape), room(*cot.shape),
            room(rows, width, dtype=f32), room(1, width, dtype=f32), dma(6),
        ]
        + Reduce.scratch(width)
        + Reduce.scratch(width)
        + HeadGrads.scratch(depth)
        + GainSum.scratch(rows)
        + DownReduce.scratch(down_rows, width),
        compiler_params=kernel_params(6),
        name="close",
    )(normed, qkv_w, mlp_part, active, cot, grad_query, grad_side, grad_hidden, hidden, tokens, gain, mlp_term)


def widen_kernel(*refs):
    half = len(refs) // 2
    for source, target in zip(refs[:half], refs[half:]):
        target[...] = source[...].astype(target.dtype)


def widen(arrays, dtypes):
    return pl.pallas_call(
        widen_kernel,
        out_shape=tuple(jax.ShapeDtypeStruct(array.shape, dtype) for array, dtype in zip(arrays, dtypes)),
        in_specs=[INSIDE] * len(arrays),
        out_specs=(INSIDE,) * len(arrays),
        compiler_params=pltpu.CompilerParams(vmem_limit_bytes=VMEM_BYTES),
        name="widen",
    )(*arrays)


def fast_body(
    tokens,
    attn_gain,
    w_query,
    w_key,
    w_value,
    w_out,
    mlp_gain,
    w_gate,
    w_up,
    w_down,
    block_ids,
    positions,
    cotangent,
):
    rows, width = tokens.shape
    token_rows = 8 * rows
    f32, bf16 = jnp.float32, jnp.bfloat16

    note = jnp.concatenate(
        [
            positions.astype(f32).reshape(2, rows),
            block_ids.astype(f32).reshape(2, rows),
            attn_gain.astype(f32)[None],
            mlp_gain.astype(f32)[None],
            jnp.zeros((2, rows), f32),
        ]
    )
    inv_freqs = rope_base ** (-2.0 * jnp.arange(HD // 2, dtype=f32) / HD)
    (
        keys_values, normed, qkv_w, out_w, notes, cos_table, sine_table, scaled_query, attended, attended_low,
        log_total, cot_all, gate_w, up_w,
    ) = front(tokens, cotangent, note, inv_freqs[None], w_query, w_key, w_value, w_out, w_gate, w_up)
    out_w = out_w.reshape(HD, width)
    gain_attn = notes[:, 4].reshape(1, width)
    gain_mlp = notes[:, 5].reshape(1, width)
    hidden, active, mlp_part, grad_branch, grad_hidden, mlp_term, gate_quarter, up_quarter = core(
        attended_low, out_w, gate_w, up_w, w_down, tokens, gain_mlp, cotangent, cot_all
    )

    side_grad, grad_query, gate_grad, up_grad, out_grad = attend_back(
        scaled_query,
        keys_values,
        grad_branch,
        out_w,
        attended,
        attended_low,
        log_total,
        notes,
        cos_table,
        sine_table,
        gate_quarter,
        up_quarter,
        w_out.shape[0],
    )
    output, tokens_grad, gain_grads, down_grad, query_grad, key_grad, value_grad = close(
        normed,
        qkv_w,
        mlp_part,
        active,
        cot_all,
        grad_query,
        side_grad,
        grad_hidden,
        hidden,
        tokens,
        gain_attn,
        mlp_term,
    )
    arrays = (output, tokens_grad, query_grad, key_grad, value_grad, out_grad, gate_grad, up_grad, down_grad)
    output, tokens_grad, query_grad, key_grad, value_grad, out_grad, gate_grad, up_grad, down_grad = widen(
        arrays, (bf16, bf16) + (f32,) * 7
    )
    return (
        output,
        tokens_grad,
        gain_grads[0],
        query_grad,
        key_grad,
        value_grad,
        out_grad,
        gain_grads[1],
        gate_grad,
        up_grad,
        down_grad,
    )


def solution(mesh):
    placed = (
        P(("blk", "head"), None),
        P("blk"),
        P("blk", "head"),
        P("blk", "head"),
        P("blk", "head"),
        P(("head", "blk"), None),
        P("blk"),
        P("blk", "head"),
        P("blk", "head"),
        P(("head", "blk"), None),
        P("blk"),
        P("blk"),
        P(("blk", "head"), None),
    )
    fits = mesh.shape["blk"] == 16 and mesh.shape["head"] == 2
    return jax.shard_map(
        fast_body if fits else body,
        mesh=mesh,
        in_specs=placed,
        out_specs=(
            P(("blk", "head"), None),
            P(("blk", "head"), None),
            P("blk"),
            P("blk", "head"),
            P("blk", "head"),
            P("blk", "head"),
            P(("head", "blk"), None),
            P("blk"),
            P("blk", "head"),
            P("blk", "head"),
            P(("head", "blk"), None),
        ),
        check_vma=False,
    )
```

```python
import jax
import jax.numpy as jnp
from jax import lax
import numpy as np
from jax.experimental import pallas as pl
from jax.experimental.pallas import tpu as pltpu
from jax.sharding import PartitionSpec as P

HD = 256


eps_norm = 1e-06
rope_base = 1000042.0


def rms_scale(rows):
    return lax.rsqrt(jnp.mean(rows * rows, axis=-1, keepdims=True) + eps_norm)


def rope_tables(positions):
    inv_freqs = rope_base ** (-2.0 * jnp.arange(HD // 2, dtype=jnp.float32) / HD)
    angles = positions.astype(jnp.float32)[:, None] * inv_freqs[None, :]
    return (jnp.cos(angles)[:, None, :], jnp.sin(angles)[:, None, :])


def rotate(heads, cos_table, sine_table):
    half_size = heads.shape[-1] // 2
    lower_half = heads[..., :half_size]
    upper_half = heads[..., half_size:]
    return jnp.concatenate(
        [
            lower_half * cos_table - upper_half * sine_table,
            upper_half * cos_table + lower_half * sine_table,
        ],
        axis=-1,
    )


def product(left, right):
    return jnp.dot(left, right, preferred_element_type=jnp.float32)


def times_transposed(left, right):
    return lax.dot_general(
        left, right, (((1,), (1,)), ((), ())), preferred_element_type=jnp.float32
    )


def transposed_times(left, right):
    return lax.dot_general(
        left, right, (((0,), (0,)), ((), ())), preferred_element_type=jnp.float32
    )


def norm_backward(grad_normed, inputs, inv_scale, gain_rows):
    unit_rows = inputs * inv_scale
    grad_unit = grad_normed * gain_rows
    gain_term = jnp.sum(grad_normed * unit_rows, axis=0)
    grad_inputs = inv_scale * (
        grad_unit - unit_rows * jnp.mean(grad_unit * unit_rows, axis=-1, keepdims=True)
    )
    return (grad_inputs, gain_term)


def body(
    tokens,
    attn_gain,
    w_query,
    w_key,
    w_value,
    w_out,
    mlp_gain,
    w_gate,
    w_up,
    w_down,
    block_ids,
    positions,
    cotangent,
):
    rows_own = tokens.shape[0]
    head_rank = lax.axis_index("head")
    tokens_all, cot_all = (
        lax.all_gather(tokens, "head", axis=0, tiled=True),
        lax.all_gather(cotangent, "head", axis=0, tiled=True),
    )
    rows_all = tokens_all.shape[0]
    gain_attn, query_w, key_w, value_w, out_w = (
        lax.all_gather(attn_gain, "blk", axis=0, tiled=True),
        lax.all_gather(w_query, "blk", axis=0, tiled=True),
        lax.all_gather(w_key, "blk", axis=0, tiled=True),
        lax.all_gather(w_value, "blk", axis=0, tiled=True),
        lax.all_gather(w_out, "blk", axis=0, tiled=True),
    )
    gain_mlp, gate_w, up_w, down_w = (
        lax.all_gather(mlp_gain, "blk", axis=0, tiled=True),
        lax.all_gather(w_gate, "blk", axis=0, tiled=True),
        lax.all_gather(w_up, "blk", axis=0, tiled=True),
        lax.all_gather(w_down, "blk", axis=0, tiled=True),
    )
    key_ids = lax.all_gather(block_ids, "blk", axis=0, tiled=True)
    heads_local = query_w.shape[1] // HD
    kv_local = key_w.shape[1] // HD
    kv_width = kv_local * HD
    group_size = heads_local // kv_local
    cos_table, sine_table = rope_tables(positions)
    score_scale = HD ** (-0.5)
    seq_len = key_ids.shape[0]
    key_block = min(2048, seq_len)
    block_total = seq_len // key_block
    block_steps = jnp.arange(block_total)
    top_query = jnp.max(block_ids)
    inputs = tokens_all.astype(jnp.float32)
    inv_attn = rms_scale(inputs)
    normed = (inputs * inv_attn * gain_attn.astype(jnp.float32)).astype(jnp.bfloat16)
    queries = rotate(
        product(normed, query_w).reshape(rows_all, heads_local, HD), cos_table, sine_table
    ).astype(jnp.bfloat16)
    keys_own = rotate(product(normed, key_w).reshape(rows_all, kv_local, HD), cos_table, sine_table)
    keys_own = keys_own.astype(jnp.bfloat16).reshape(rows_all, kv_width)
    values_own = product(normed, value_w).astype(jnp.bfloat16)
    keys_all, values_all = (
        lax.all_gather(keys_own, "blk", axis=0, tiled=True),
        lax.all_gather(values_own, "blk", axis=0, tiled=True),
    )
    grouped = queries.reshape(rows_all, kv_local, group_size, HD)

    def slice_keys(key_start, count):
        key_rows = lax.dynamic_slice_in_dim(keys_all, key_start, count, 0).reshape(
            count, kv_local, HD
        )
        value_rows = lax.dynamic_slice_in_dim(values_all, key_start, count, 0).reshape(
            count, kv_local, HD
        )
        block_keys = lax.dynamic_slice_in_dim(key_ids, key_start, count, 0)
        return (key_rows, value_rows, block_keys)

    def scores_for(key_rows, block_keys):
        scores = (
            jnp.einsum("qkgd,ckd->kgqc", grouped, key_rows, preferred_element_type=jnp.float32)
            * score_scale
        )
        visible = (block_keys[None, :] <= block_ids[:, None])[None, None]
        return (scores, visible)

    def max_sum(state_pair, step_index):
        key_start = step_index * key_block

        def max_live(pair):
            run_max, run_sum = pair
            key_rows, value_rows, block_keys = slice_keys(key_start, key_block)
            scores, visible = scores_for(key_rows, block_keys)
            scores = jnp.where(visible, scores, -1e30)
            new_max = jnp.maximum(run_max, jnp.max(scores, axis=-1))
            kept_terms = jnp.where(visible, jnp.exp(scores - new_max[..., None]), 0.0)
            return (new_max, run_sum * jnp.exp(run_max - new_max) + jnp.sum(kept_terms, axis=-1))

        def max_skipped(pair):
            return pair

        return (lax.cond(key_ids[key_start] <= top_query, max_live, max_skipped, state_pair), None)

    start_max = jnp.full((kv_local, group_size, rows_all), -1e30, jnp.float32)
    start_sum = jnp.zeros((kv_local, group_size, rows_all), jnp.float32)
    (run_max, run_sum), unused_max = lax.scan(max_sum, (start_max, start_sum), block_steps)
    log_total = run_max + jnp.log(run_sum)

    def weighted(accum_rows, step_index):
        key_start = step_index * key_block

        def weighted_live(accum):
            key_rows, value_rows, block_keys = slice_keys(key_start, key_block)
            scores, visible = scores_for(key_rows, block_keys)
            probabilities = jnp.where(visible, jnp.exp(scores - log_total[..., None]), 0.0).astype(
                jnp.bfloat16
            )
            return accum + jnp.einsum(
                "kgqc,ckd->qkgd", probabilities, value_rows, preferred_element_type=jnp.float32
            )

        def weighted_skipped(accum):
            return accum

        return (
            lax.cond(key_ids[key_start] <= top_query, weighted_live, weighted_skipped, accum_rows),
            None,
        )

    attended, unused_rows = lax.scan(
        weighted, jnp.zeros((rows_all, kv_local, group_size, HD), jnp.float32), block_steps
    )
    attended_low = attended.reshape(rows_all, heads_local * HD).astype(jnp.bfloat16)
    branch_sum = lax.psum(product(attended_low, out_w).astype(jnp.bfloat16), "head").astype(
        jnp.float32
    )
    hidden = inputs + branch_sum
    inv_mlp = rms_scale(hidden)
    normed_mlp = (hidden * inv_mlp * gain_mlp.astype(jnp.float32)).astype(jnp.bfloat16)
    gate_pre = product(normed_mlp, gate_w)
    up_pre = product(normed_mlp, up_w)
    sigmoid_gate = jax.nn.sigmoid(gate_pre)
    active = (gate_pre * sigmoid_gate * up_pre).astype(jnp.bfloat16)
    mlp_own = lax.psum_scatter(
        product(active, down_w).astype(jnp.bfloat16), "head", scatter_dimension=0, tiled=True
    ).astype(jnp.float32)
    hidden_own = lax.dynamic_slice_in_dim(hidden, head_rank * rows_own, rows_own, 0)
    output = (hidden_own + mlp_own).astype(jnp.bfloat16)
    gain_attn, query_w, key_w, value_w, out_w = (
        lax.all_gather(attn_gain, "blk", axis=0, tiled=True),
        lax.all_gather(w_query, "blk", axis=0, tiled=True),
        lax.all_gather(w_key, "blk", axis=0, tiled=True),
        lax.all_gather(w_value, "blk", axis=0, tiled=True),
        lax.all_gather(w_out, "blk", axis=0, tiled=True),
    )
    gain_mlp, gate_w, up_w, down_w = (
        lax.all_gather(mlp_gain, "blk", axis=0, tiled=True),
        lax.all_gather(w_gate, "blk", axis=0, tiled=True),
        lax.all_gather(w_up, "blk", axis=0, tiled=True),
        lax.all_gather(w_down, "blk", axis=0, tiled=True),
    )
    grad_active = times_transposed(cot_all, down_w)
    grad_gate = (
        grad_active * up_pre * sigmoid_gate * (1.0 + gate_pre * (1.0 - sigmoid_gate))
    ).astype(jnp.bfloat16)
    grad_up = (grad_active * gate_pre * sigmoid_gate).astype(jnp.bfloat16)
    grad_gate_w = transposed_times(normed_mlp, grad_gate)
    grad_up_w = transposed_times(normed_mlp, grad_up)
    grad_down_w = transposed_times(active, cot_all)
    grad_normed_part = times_transposed(grad_gate, gate_w) + times_transposed(grad_up, up_w)
    grad_normed_mlp = lax.psum(grad_normed_part.astype(jnp.bfloat16), "head").astype(jnp.float32)
    grad_hidden_norm, gain_mlp_term = norm_backward(
        grad_normed_mlp, hidden, inv_mlp, gain_mlp.astype(jnp.float32)
    )
    grad_hidden = cot_all.astype(jnp.float32) + grad_hidden_norm
    mlp_results = (
        lax.psum_scatter(gain_mlp_term, "blk", scatter_dimension=0, tiled=True),
        lax.psum_scatter(grad_gate_w, "blk", scatter_dimension=0, tiled=True),
        lax.psum_scatter(grad_up_w, "blk", scatter_dimension=0, tiled=True),
        lax.psum_scatter(grad_down_w, "blk", scatter_dimension=0, tiled=True),
    )
    grad_branch = grad_hidden.astype(jnp.bfloat16)
    grad_out_w = transposed_times(attended_low, grad_branch)
    grad_attended = times_transposed(grad_branch, out_w).astype(jnp.bfloat16)
    grad_grouped = grad_attended.reshape(rows_all, kv_local, group_size, HD)
    delta_rows = jnp.transpose(
        jnp.sum(grad_grouped.astype(jnp.float32) * attended, axis=-1), (1, 2, 0)
    )

    def pair_backward(key_rows, value_rows, block_keys):
        count = key_rows.shape[0]
        scores, visible = scores_for(key_rows, block_keys)
        probabilities = jnp.where(visible, jnp.exp(scores - log_total[..., None]), 0.0)
        grad_probs = jnp.einsum(
            "qkgd,ckd->kgqc", grad_grouped, value_rows, preferred_element_type=jnp.float32
        )
        grad_scores = (probabilities * (grad_probs - delta_rows[..., None])).astype(jnp.bfloat16)
        query_terms = jnp.einsum(
            "kgqc,ckd->qkgd", grad_scores, key_rows, preferred_element_type=jnp.float32
        )
        key_terms = (
            jnp.einsum("kgqc,qkgd->ckd", grad_scores, grouped, preferred_element_type=jnp.float32)
            * score_scale
        )
        value_terms = jnp.einsum(
            "kgqc,qkgd->ckd",
            probabilities.astype(jnp.bfloat16),
            grad_grouped,
            preferred_element_type=jnp.float32,
        )
        return (
            query_terms,
            key_terms.reshape(count, kv_width),
            value_terms.reshape(count, kv_width),
        )

    query_zeros = jnp.zeros((rows_all, kv_local, group_size, HD), jnp.float32)

    def backward_block(accum_rows, step_index):
        key_start = step_index * key_block

        def backward_live(unused_arg):
            key_rows, value_rows, block_keys = slice_keys(key_start, key_block)
            return pair_backward(key_rows, value_rows, block_keys)

        def backward_skipped(unused_arg):
            empty_terms = jnp.zeros((key_block, kv_width), jnp.float32)
            return (query_zeros, empty_terms, empty_terms)

        query_terms, key_terms, value_terms = lax.cond(
            key_ids[key_start] <= top_query, backward_live, backward_skipped, 0
        )
        return (accum_rows + query_terms, (key_terms, value_terms))

    grad_query_rot, (key_terms, value_terms) = lax.scan(backward_block, query_zeros, block_steps)
    key_terms = key_terms.reshape(seq_len, kv_width)
    value_terms = value_terms.reshape(seq_len, kv_width)
    key_grad_own, value_grad_own = (
        lax.psum_scatter(key_terms, "blk", scatter_dimension=0, tiled=True),
        lax.psum_scatter(value_terms, "blk", scatter_dimension=0, tiled=True),
    )
    grad_query_rot = grad_query_rot * score_scale
    grad_key = rotate(key_grad_own.reshape(rows_all, kv_local, HD), cos_table, -sine_table)
    grad_key = grad_key.reshape(rows_all, kv_width).astype(jnp.bfloat16)
    grad_value = value_grad_own.astype(jnp.bfloat16)
    grad_query = rotate(grad_query_rot.reshape(rows_all, heads_local, HD), cos_table, -sine_table)
    grad_query = grad_query.reshape(rows_all, heads_local * HD).astype(jnp.bfloat16)
    grad_query_w = transposed_times(normed, grad_query)
    grad_key_w = transposed_times(normed, grad_key)
    grad_value_w = transposed_times(normed, grad_value)
    grad_normed_part = (
        times_transposed(grad_query, query_w)
        + times_transposed(grad_key, key_w)
        + times_transposed(grad_value, value_w)
    )
    grad_normed = lax.psum(grad_normed_part.astype(jnp.bfloat16), "head").astype(jnp.float32)
    grad_inputs_norm, gain_attn_term = norm_backward(
        grad_normed, inputs, inv_attn, gain_attn.astype(jnp.float32)
    )
    grad_inputs = grad_hidden + grad_inputs_norm
    grad_own = lax.dynamic_slice_in_dim(grad_inputs, head_rank * rows_own, rows_own, 0).astype(
        jnp.bfloat16
    )
    attn_results = (
        lax.psum_scatter(gain_attn_term, "blk", scatter_dimension=0, tiled=True),
        lax.psum_scatter(grad_query_w, "blk", scatter_dimension=0, tiled=True),
        lax.psum_scatter(grad_key_w, "blk", scatter_dimension=0, tiled=True),
        lax.psum_scatter(grad_value_w, "blk", scatter_dimension=0, tiled=True),
        lax.psum_scatter(grad_out_w, "blk", scatter_dimension=0, tiled=True),
    )
    return (
        output,
        grad_own,
        attn_results[0],
        attn_results[1],
        attn_results[2],
        attn_results[3],
        attn_results[4],
        mlp_results[0],
        mlp_results[1],
        mlp_results[2],
        mlp_results[3],
    )


MESH = pl.DeviceIdType.MESH
LINE = 4
VMEM_BYTES = 60 * 2**20


def place():
    blk, head = lax.axis_index("blk"), lax.axis_index("head")
    return blk // 4, (blk // 2) % 2, blk % 2, head


def device(z, y, c, h):
    return (z * 4 + y * 2 + c, h)


def remote(src, dst, send_sem, recv_sem, target):
    return pltpu.make_async_remote_copy(
        src_ref=src,
        dst_ref=dst,
        send_sem=send_sem,
        recv_sem=recv_sem,
        device_id=target,
        device_id_type=MESH,
    )


def greet(target):
    pl.semaphore_signal(
        pltpu.get_barrier_semaphore(), inc=1, device_id=target, device_id_type=MESH
    )


def greet_all(blk_total, head_total):
    blk, head = lax.axis_index("blk"), lax.axis_index("head")
    for other in range(blk_total):
        for half in range(head_total):

            @pl.when(jnp.logical_or(blk != other, head != half))
            def _():
                greet((jnp.int32(other), jnp.int32(half)))

    pl.semaphore_wait(pltpu.get_barrier_semaphore(), blk_total * head_total - 1)


def greet_plane(more=0):
    z, y, c, h = place()

    @pl.when(z > 0)
    def _():
        greet(device(z - 1, y, c, h))

    @pl.when(z < LINE - 1)
    def _():
        greet(device(z + 1, y, c, h))

    greet(device(z, 1 - y, c, h))
    pl.semaphore_wait(
        pltpu.get_barrier_semaphore(),
        1 + more + (z + LINE - 1) // LINE + (LINE - 1 - z + LINE - 1) // LINE,
    )


class Gather:
    CUTS = ((0, 64), (64, 48), (112, 16), (112, 16))
    SEMS = [(3, 4)] * 4 + [(4, 2)] * 2 + [(2,)]

    @staticmethod
    def scratch():
        return [pltpu.SemaphoreType.DMA(shape) for shape in Gather.SEMS] + [
            pltpu.SemaphoreType.DMA
        ]

    def __init__(self, src, out, sems):
        self.src, self.out = src, out
        (self.up_s, self.up_r, self.dn_s, self.dn_r, self.y_s, self.y_r, self.b_sr, self.own_sem) = sems
        self.z, self.y, self.c, self.h = place()

    def piece(self, line, elem):
        y = 1 - self.y if elem == 3 else self.y
        start, size = self.CUTS[elem]
        return self.out.at[line * 2 + y, pl.ds(start, size)]

    def first(self, elem):
        if elem == 3:
            return self.piece(self.z, 3)
        start, size = self.CUTS[elem]
        return self.src.at[pl.ds(start, size)]

    def up(self, step, elem):
        src = self.first(elem) if step == 0 else self.piece(self.z - step, elem)
        return remote(
            src, self.piece(self.z - step, elem), self.up_s.at[step, elem], self.up_r.at[step, elem],
            device(self.z + 1, self.y, self.c, self.h),
        )

    def down(self, step, elem):
        src = self.first(elem) if step == 0 else self.piece(self.z + step, elem)
        return remote(
            src, self.piece(self.z + step, elem), self.dn_s.at[step, elem], self.dn_r.at[step, elem],
            device(self.z - 1, self.y, self.c, self.h),
        )

    def up_in(self, step, elem):
        ref = self.piece(self.z - 1 - step, elem)
        return remote(ref, ref, self.up_s.at[step, elem], self.up_r.at[step, elem], device(self.z, self.y, self.c, self.h))

    def down_in(self, step, elem):
        ref = self.piece(self.z + 1 + step, elem)
        return remote(ref, ref, self.dn_s.at[step, elem], self.dn_r.at[step, elem], device(self.z, self.y, self.c, self.h))

    def across(self, line, elem, own=False):
        src = self.first(elem) if own else self.piece(line, elem)
        return remote(
            src, self.piece(line, elem), self.y_s.at[line, elem], self.y_r.at[line, elem],
            device(self.z, 1 - self.y, self.c, self.h),
        )

    def across_in(self, line, elem):
        start, size = self.CUTS[elem]
        ref = self.out.at[line * 2 + 1 - self.y, pl.ds(start, size)]
        return remote(ref, ref, self.y_s.at[line, elem], self.y_r.at[line, elem], device(self.z, self.y, self.c, self.h))

    def across_b(self):
        return remote(
            self.first(2), self.piece(self.z, 2), self.b_sr.at[0], self.b_sr.at[1],
            device(self.z, 1 - self.y, self.c, self.h),
        )

    def across_b_in(self):
        ref = self.piece(self.z, 3)
        return remote(ref, ref, self.b_sr.at[0], self.b_sr.at[1], device(self.z, self.y, self.c, self.h))

    def own_copy(self):
        return pltpu.make_async_copy(self.src, self.out.at[self.z * 2 + self.y], self.own_sem)

    def start(self):
        self.own_copy().start()
        self.across_b().start()
        for elem in (0, 1, 2):

            @pl.when(self.z < LINE - 1)
            def _():
                self.up(0, elem).start()

            @pl.when(self.z > 0)
            def _():
                self.down(0, elem).start()

            if elem < 2:
                self.across(self.z, elem, own=True).start()

    def relay_b(self):
        self.across_b_in().wait_recv()

        @pl.when(self.z < LINE - 1)
        def _():
            self.up(0, 3).start()

        @pl.when(self.z > 0)
        def _():
            self.down(0, 3).start()

    def relay(self, step, elem):
        @pl.when(self.z - 1 - step >= 0)
        def _():
            self.up_in(step, elem).wait_recv()
            if step < LINE - 2:

                @pl.when(self.z < LINE - 1)
                def _():
                    self.up(step + 1, elem).start()

            if elem < 2:
                self.across(self.z - 1 - step, elem).start()

        @pl.when(self.z + 1 + step <= LINE - 1)
        def _():
            self.down_in(step, elem).wait_recv()
            if step < LINE - 2:

                @pl.when(self.z > 0)
                def _():
                    self.down(step + 1, elem).start()

            if elem < 2:
                self.across(self.z + 1 + step, elem).start()

    def relays(self):
        self.relay_b()
        for step in range(LINE - 1):
            for elem in (0, 1, 2, 3):
                self.relay(step, elem)

    def finish(self):
        for line in range(LINE):
            for elem in (0, 1):
                self.across_in(line, elem).wait_recv()
        for line in range(LINE):
            for elem in (0, 1):
                self.across(line, elem).wait_send()
        self.finish_sends()
        self.own_copy().wait()

    def finish_sends(self):
        self.across_b().wait_send()
        for step in range(LINE - 1):
            for elem in range(4):

                @pl.when(jnp.logical_and(self.z < LINE - 1, self.z - step >= 0))
                def _():
                    self.up(step, elem).wait_send()

                @pl.when(jnp.logical_and(self.z > 0, self.z + step <= LINE - 1))
                def _():
                    self.down(step, elem).wait_send()


ANY = pl.BlockSpec(memory_space=pl.ANY)
INSIDE = pl.BlockSpec(memory_space=pltpu.VMEM)


def kernel_params(collective_id):
    return pltpu.CompilerParams(
        collective_id=collective_id, has_side_effects=True, vmem_limit_bytes=VMEM_BYTES
    )


def add_into(target, *others):
    total = target[...].astype(jnp.float32)
    for other in others:
        total += other[...].astype(jnp.float32)
    target[...] = total.astype(target.dtype)


class Reduce:
    CUTS = ((0, 64), (64, 48))
    LAST = (112, 16)

    @staticmethod
    def scratch(width):
        inbox = pltpu.VMEM((LINE, 112, width), jnp.bfloat16)
        last = pltpu.VMEM((LINE, 2, 16, width), jnp.bfloat16)
        sems = [pltpu.SemaphoreType.DMA((LINE, 2))] * 10 + [pltpu.SemaphoreType.DMA((2,))]
        return [inbox] * 3 + [last] * 2 + [pltpu.VMEM((16, width), jnp.bfloat16)] + sems

    COUNT = 17

    def __init__(self, parts, refs):
        self.parts = parts
        self.y_in, self.up_in, self.dn_in, self.up_last, self.dn_last, self.y_last = refs[:6]
        (
            self.y_s, self.y_r, self.up_s, self.up_r, self.dn_s, self.dn_r,
            self.ul_s, self.ul_r, self.dl_s, self.dl_r, self.yl_sr,
        ) = refs[6:]
        self.z, self.y, self.c, self.h = place()
        z = self.z
        self.order = (3 - 3 * (z // 2), (2 + 3 * z) % 5, 1 + z % 2, z)

    def rows(self, cut):
        return pl.ds(*self.CUTS[cut])

    def across(self, line, cut):
        return remote(
            self.parts.at[line * 2 + 1 - self.y, self.rows(cut)], self.y_in.at[line, self.rows(cut)],
            self.y_s.at[line, cut], self.y_r.at[line, cut], device(self.z, 1 - self.y, self.c, self.h),
        )

    def up(self, line, cut):
        return remote(
            self.parts.at[line * 2 + self.y, self.rows(cut)], self.up_in.at[line, self.rows(cut)],
            self.up_s.at[line, cut], self.up_r.at[line, cut], device(self.z + 1, self.y, self.c, self.h),
        )

    def down(self, line, cut):
        return remote(
            self.parts.at[line * 2 + self.y, self.rows(cut)], self.dn_in.at[line, self.rows(cut)],
            self.dn_s.at[line, cut], self.dn_r.at[line, cut], device(self.z - 1, self.y, self.c, self.h),
        )

    def last(self, line, column):
        return self.parts.at[line * 2 + column, pl.ds(*self.LAST)]

    def last_up(self, line, column):
        return remote(
            self.last(line, column), self.up_last.at[line, column], self.ul_s.at[line, column],
            self.ul_r.at[line, column], device(self.z + 1, self.y, self.c, self.h),
        )

    def last_down(self, line, column):
        return remote(
            self.last(line, column), self.dn_last.at[line, column], self.dl_s.at[line, column],
            self.dl_r.at[line, column], device(self.z - 1, self.y, self.c, self.h),
        )

    def last_across(self):
        return remote(
            self.last(self.z, 1 - self.y), self.y_last, self.yl_sr.at[0], self.yl_sr.at[1],
            device(self.z, 1 - self.y, self.c, self.h),
        )

    def start(self, place_at):
        line = self.order[place_at]
        for cut in range(2):
            self.across(line, cut).start()

        @pl.when(jnp.logical_and(line > self.z, self.z == 0))
        def _():
            for column in range(2):
                self.last_up(line, column).start()

        @pl.when(jnp.logical_and(line < self.z, self.z == LINE - 1))
        def _():
            for column in range(2):
                self.last_down(line, column).start()

    def relay_last(self, line):
        @pl.when(jnp.logical_and(line > self.z, self.z > 0))
        def _():
            for column in range(2):
                self.last_up(line, column).wait_recv()
                add_into(self.last(line, column), self.up_last.at[line, column])
                self.last_up(line, column).start()

        @pl.when(jnp.logical_and(line < self.z, self.z < LINE - 1))
        def _():
            for column in range(2):
                self.last_down(line, column).wait_recv()
                add_into(self.last(line, column), self.dn_last.at[line, column])
                self.last_down(line, column).start()

    def relay(self, place_at):
        line = self.order[place_at]
        for cut in range(2):
            rows = self.rows(cut)
            self.across(line, cut).wait_recv()
            target = self.parts.at[line * 2 + self.y, rows]

            @pl.when(line > self.z)
            def _():
                @pl.when(self.z > 0)
                def _():
                    self.up(line, cut).wait_recv()
                    add_into(target, self.y_in.at[line, rows], self.up_in.at[line, rows])

                @pl.when(self.z == 0)
                def _():
                    add_into(target, self.y_in.at[line, rows])

                self.up(line, cut).start()

            @pl.when(line < self.z)
            def _():
                @pl.when(self.z < LINE - 1)
                def _():
                    self.down(line, cut).wait_recv()
                    add_into(target, self.y_in.at[line, rows], self.dn_in.at[line, rows])

                @pl.when(self.z == LINE - 1)
                def _():
                    add_into(target, self.y_in.at[line, rows])

                self.down(line, cut).start()

            if cut == 0:
                self.relay_last(line)

    def total(self, out):
        line = self.z
        last = pl.ds(*self.LAST)
        own, other = line * 2 + self.y, line * 2 + 1 - self.y

        @pl.when(self.z > 0)
        def _():
            for column in range(2):
                self.last_up(line, column).wait_recv()
                add_into(self.last(line, column), self.up_last.at[line, column])

        @pl.when(self.z < LINE - 1)
        def _():
            for column in range(2):
                self.last_down(line, column).wait_recv()
                add_into(self.last(line, column), self.dn_last.at[line, column])

        self.last_across().start()
        for cut in range(2):
            rows = self.rows(cut)
            self.across(line, cut).wait_recv()
            out[rows] = self.parts[own, rows].astype(jnp.float32) + self.y_in[line, rows].astype(jnp.float32)
        for cut in range(2):
            rows = self.rows(cut)

            @pl.when(self.z > 0)
            def _():
                self.up(line, cut).wait_recv()
                out[rows] += self.up_in[line, rows].astype(jnp.float32)

            @pl.when(self.z < LINE - 1)
            def _():
                self.down(line, cut).wait_recv()
                out[rows] += self.dn_in[line, rows].astype(jnp.float32)

        self.last_across().wait_recv()
        out[last] = self.parts[own, last].astype(jnp.float32) + self.y_last[...].astype(jnp.float32)

    def finish(self):
        for line in range(LINE):
            for cut in range(2):
                self.across(line, cut).wait_send()

                @pl.when(self.z < line)
                def _():
                    self.up(line, cut).wait_send()
                    self.last_up(line, cut).wait_send()

                @pl.when(self.z > line)
                def _():
                    self.down(line, cut).wait_send()
                    self.last_down(line, cut).wait_send()

        self.last_across().wait_send()


def dma(*shape):
    return pltpu.SemaphoreType.DMA(shape) if shape else pltpu.SemaphoreType.DMA


def local(src, dst, sem):
    return pltpu.make_async_copy(src, dst, sem)


class AttnSpread:
    @staticmethod
    def scratch(depth):
        return [pltpu.VMEM((LINE, depth, 3 * HD), jnp.bfloat16)] + [
            dma(3, 4), dma(3, 4), dma(3), dma(4), dma(4), dma(4), dma(4), dma(4), dma(4), dma(4), dma(4), dma(4), dma(4),
        ]

    COUNT = 14

    def __init__(self, weights, outs, refs):
        self.weights, (self.qkv, self.out_w) = weights, outs
        (
            self.stage, self.s, self.r, self.own, self.x_s, self.x_r, self.a_s, self.a_r, self.b_s, self.b_r,
            self.c_s, self.c_r, self.o_s, self.o_r,
        ) = refs
        self.z, self.y, self.c, self.h = place()
        self.me = device(self.z, self.y, self.c, self.h)
        self.owner = self.h == self.y

    def source(self, kind, line):
        start = line * HD if kind == 0 else (line // 2) * HD
        return self.weights[kind].at[:, pl.ds(pl.multiple_of(start, HD), HD)]

    def slot(self, kind, line, owner):
        columns = pl.ds(kind * HD, HD)
        if owner:
            return self.qkv.at[line * 2 + self.y, self.c, :, columns]
        return self.stage.at[line, :, columns]

    def push(self, kind, step, owner):
        line = (self.z + step) % LINE
        return remote(
            self.source(kind, line), self.slot(kind, self.z, owner), self.s.at[kind, step], self.r.at[kind, self.z],
            device(line, self.y, self.c, self.h),
        )

    def pull(self, kind, line, owner):
        ref = self.slot(kind, line, owner)
        return remote(ref, ref, self.s.at[kind, 0], self.r.at[kind, line], self.me)

    def keep(self, kind, owner):
        return local(self.source(kind, self.z), self.slot(kind, self.z, owner), self.own.at[kind])

    def over(self, line):
        ref = self.qkv.at[line * 2 + self.y, self.c]
        return remote(ref, ref, self.x_s.at[line], self.x_r.at[line], device(self.z, self.y, self.c, 1 - self.h))

    def over_in(self, line):
        ref = self.qkv.at[line * 2 + self.y, self.c]
        return remote(ref, ref, self.x_s.at[line], self.x_r.at[line], self.me)

    def across(self, line):
        return remote(
            self.stage.at[line], self.qkv.at[line * 2 + self.y, self.c], self.a_s.at[line], self.a_r.at[line],
            device(self.z, 1 - self.y, self.c, self.h),
        )

    def across_far(self, line):
        return remote(
            self.stage.at[line], self.qkv.at[line * 2 + self.y, self.c], self.b_s.at[line], self.b_r.at[line],
            device(self.z, 1 - self.y, self.c, 1 - self.h),
        )

    def far_in(self, line, owner):
        ref = self.qkv.at[line * 2 + 1 - self.y, self.c]
        s, r = (self.a_s, self.a_r) if owner else (self.b_s, self.b_r)
        return remote(ref, ref, s.at[line], r.at[line], self.me)

    def share(self, line, core):
        ref = self.qkv.at[pl.ds(line * 2, 2), core]
        return remote(ref, ref, self.c_s.at[line], self.c_r.at[line], device(self.z, self.y, 1 - self.c, self.h))

    def out_push(self):
        return remote(
            self.weights[3], self.out_w.at[self.y, self.c], self.o_s.at[0], self.o_r.at[0],
            device(self.z, 1 - self.y, self.c, self.h),
        )

    def out_keep(self):
        return local(self.weights[3], self.out_w.at[self.y, self.c], self.o_s.at[1])

    def out_pull(self):
        ref = self.out_w.at[1 - self.y, self.c]
        return remote(ref, ref, self.o_s.at[0], self.o_r.at[0], self.me)

    def out_over(self):
        ref = self.out_w.at[:, self.c]
        return remote(ref, ref, self.o_s.at[2], self.o_r.at[2], device(self.z, self.y, self.c, 1 - self.h))

    def out_share(self, core):
        ref = self.out_w.at[:, core]
        return remote(ref, ref, self.o_s.at[3], self.o_r.at[3], device(self.z, self.y, 1 - self.c, self.h))

    def each(self, act):
        @pl.when(self.owner)
        def _():
            act(True)

        @pl.when(jnp.logical_not(self.owner))
        def _():
            act(False)

    def start(self):
        def act(owner):
            for kind in range(3):
                self.keep(kind, owner).start()
            for step in range(1, LINE):
                for kind in range(3):
                    self.push(kind, step, owner).start()
            if owner:
                self.out_keep().start()
            else:
                self.out_push().start()

        self.each(act)

    def relay(self, step):
        line = (self.z + LINE - step) % LINE

        def act(owner):
            for kind in range(3):
                if step:
                    self.pull(kind, line, owner).wait_recv()
                else:
                    self.keep(kind, owner).wait()
            if owner:
                self.over(line).start()
            else:
                self.across(line).start()
                self.across_far(line).start()

        self.each(act)

    def relay_out(self):
        @pl.when(self.owner)
        def _():
            self.out_keep().wait()
            self.out_pull().wait_recv()
            self.out_over().start()

    def relay_share(self, step):
        line = (self.z + LINE - step) % LINE

        def act(owner):
            if not owner:
                self.over_in(line).wait_recv()
            self.far_in(line, owner).wait_recv()

        self.each(act)
        self.share(line, self.c).start()

    def relay_out_share(self):
        @pl.when(jnp.logical_not(self.owner))
        def _():
            self.out_over().wait_recv()

        self.out_share(self.c).start()

    def finish(self):
        for line in range(LINE):
            self.share(line, 1 - self.c).wait_recv()
            self.share(line, self.c).wait_send()
        self.out_share(1 - self.c).wait_recv()
        self.out_share(self.c).wait_send()

        def act(owner):
            for kind in range(3):
                for step in range(1, LINE):
                    self.push(kind, step, owner).wait_send()
            for line in range(LINE):
                if owner:
                    self.over(line).wait_send()
                else:
                    self.across(line).wait_send()
                    self.across_far(line).wait_send()
            if owner:
                self.out_over().wait_send()
            else:
                self.out_push().wait_send()

        self.each(act)


class MlpSpread:
    @staticmethod
    def scratch():
        return [dma(2, 8), dma(2, 8), dma(2)]

    def __init__(self, weights, outs, sems):
        self.weights, self.outs = weights, outs
        self.s, self.r, self.own = sems
        self.z, self.y, self.c, self.h = place()
        self.chip = self.z * 2 + self.y
        self.part = weights[0].shape[1] // 8

    def columns(self, index):
        return pl.ds(pl.multiple_of(index * self.part, self.part), self.part)

    def push(self, kind, step):
        chip = (self.chip + step) % 8
        return remote(
            self.weights[kind].at[:, self.columns(chip)], self.outs[kind].at[self.chip], self.s.at[kind, step],
            self.r.at[kind, step], device(chip // 2, chip % 2, self.c, self.h),
        )

    def pull(self, kind, step):
        ref = self.outs[kind].at[(self.chip + 8 - step) % 8]
        return remote(ref, ref, self.s.at[kind, step], self.r.at[kind, step], device(self.z, self.y, self.c, self.h))

    def keep(self, kind):
        return local(self.weights[kind].at[:, self.columns(self.chip)], self.outs[kind].at[self.chip], self.own.at[kind])

    def start(self):
        for kind in range(2):
            self.keep(kind).start()
            for step in range(1, 8):
                self.push(kind, step).start()

    def finish(self):
        for kind in range(2):
            self.keep(kind).wait()
            for step in range(1, 8):
                self.pull(kind, step).wait_recv()
                self.push(kind, step).wait_send()


class MlpShare:
    @staticmethod
    def scratch():
        return [dma(2), dma(2, 2), dma(2, 2), dma(2, 2), dma(2, 2)]

    def __init__(self, quarters, outs, sems):
        self.quarters, self.outs = quarters, outs
        self.own, self.x_s, self.x_r, self.c_s, self.c_r = sems
        self.z, self.y, self.c, self.h = place()
        self.part = quarters[0].shape[2]

    def slot(self, kind, cut, half):
        columns = pl.ds(pl.multiple_of(half * self.part, self.part), self.part)
        return self.outs[kind].at[pl.ds(cut * 4, 4), self.c, :, columns]

    def keep(self, kind):
        columns = pl.ds(pl.multiple_of(self.h * self.part, self.part), self.part)
        return local(self.quarters[kind], self.outs[kind].at[:, self.c, :, columns], self.own.at[kind])

    def over(self, kind, cut, half):
        return remote(
            self.quarters[kind].at[pl.ds(cut * 4, 4)], self.slot(kind, cut, half), self.x_s.at[kind, cut],
            self.x_r.at[kind, cut], device(self.z, self.y, self.c, 1 - self.h),
        )

    def share(self, kind, cut, core):
        ref = self.outs[kind].at[pl.ds(cut * 4, 4), core]
        return remote(
            ref, ref, self.c_s.at[kind, cut], self.c_r.at[kind, cut], device(self.z, self.y, 1 - self.c, self.h)
        )

    def start(self):
        for kind in range(2):
            for cut in range(2):
                self.over(kind, cut, self.h).start()
            self.keep(kind).start()

    def relay(self):
        for kind in range(2):
            self.keep(kind).wait()
            for cut in range(2):
                self.over(kind, cut, 1 - self.h).wait_recv()
                self.share(kind, cut, self.c).start()

    def finish(self):
        for kind in range(2):
            for cut in range(2):
                self.share(kind, cut, 1 - self.c).wait_recv()
                self.share(kind, cut, self.c).wait_send()
                self.over(kind, cut, self.h).wait_send()


class DownSpread:
    @staticmethod
    def scratch():
        return [dma(1), dma(2), dma(2)]

    def __init__(self, weight, out, sems):
        self.weight, self.out = weight, out
        self.d_own, self.d_x, self.d_sib = sems
        self.z, self.y, self.c, self.h = place()

    def keep(self):
        return local(self.weight, self.out.at[self.h, self.c], self.d_own.at[0])

    def over(self):
        return remote(
            self.weight, self.out.at[self.h, self.c], self.d_x.at[0], self.d_x.at[1],
            device(self.z, self.y, self.c, 1 - self.h),
        )

    def over_in(self):
        ref = self.out.at[1 - self.h, self.c]
        return remote(ref, ref, self.d_x.at[0], self.d_x.at[1], device(self.z, self.y, self.c, self.h))

    def share(self):
        ref = self.out.at[:, self.c]
        return remote(ref, ref, self.d_sib.at[0], self.d_sib.at[1], device(self.z, self.y, 1 - self.c, self.h))

    def share_in(self):
        ref = self.out.at[:, 1 - self.c]
        return remote(ref, ref, self.d_sib.at[0], self.d_sib.at[1], device(self.z, self.y, self.c, self.h))

    def start(self):
        self.keep().start()
        self.over().start()

    def relay(self):
        self.keep().wait()
        self.over_in().wait_recv()
        self.share().start()

    def finish(self):
        self.share_in().wait_recv()
        self.share().wait_send()
        self.over().wait_send()


class NoteSpread:
    @staticmethod
    def scratch():
        return [dma(16), dma(16), dma(1)]

    def __init__(self, note, out, sems):
        self.note, self.out = note, out
        self.s, self.r, self.own = sems
        self.blk, self.h = lax.axis_index("blk"), lax.axis_index("head")

    def push(self, step):
        other = (self.blk + step) % 16
        return remote(self.note, self.out.at[self.blk], self.s.at[step], self.r.at[step], (other, self.h))

    def pull(self, step):
        ref = self.out.at[(self.blk + 16 - step) % 16]
        return remote(ref, ref, self.s.at[step], self.r.at[step], (self.blk, self.h))

    def keep(self):
        return local(self.note, self.out.at[self.blk], self.own.at[0])

    def start(self):
        self.keep().start()
        for step in range(1, 16):
            self.push(step).start()

    def finish(self):
        self.keep().wait()
        for step in range(1, 16):
            self.pull(step).wait_recv()
            self.push(step).wait_send()


def split_refs(refs, counts):
    groups, at = [], 0
    for count in counts:
        groups.append(refs[at : at + count])
        at += count
    return groups


def core_kernel(
    attended, out_w, gate_in, up_in, wd, tokens, gain, cot, cot_in,
    hidden_out, active, mlp_part, gathered, grad_hidden, gain_term, gate, up,
    normed, src, total, gate_w, up_w, down_w, gate_factor, up_factor, cot_pairs, parts, stage, gate_grad, up_grad, branch,
    cot_s, stage_s, *refs,
):
    gather_sems, back_sems, share_sems, down_sems, reduce_refs, quarter_refs = split_refs(
        refs, (8, 8, 5, 3, Reduce.COUNT, 8)
    )
    z, y, c, h = place()
    greet(device(z, y, 1 - c, h))
    greet(device(z, y, c, 1 - h))
    greet_plane(2)
    gather = Gather(src, normed, gather_sems)
    back = Gather(branch, gathered, back_sems)
    share = MlpShare((gate_in, up_in), (gate_w, up_w), share_sems)
    downs = DownSpread(wd, down_w, down_sems)
    reduce = Reduce(parts, reduce_refs)
    grads = QuarterReduce((gate_w, up_w), (gate, up), quarter_refs)
    rows, width = normed.shape[1:]
    hidden = gate_w.shape[3]
    step = hidden // 4
    pair = 2 * rows
    order = (2, 0, 1, 3)

    def cot_load(place_at):
        return local(cot_in.at[pl.ds(reduce.order[place_at] * 2, 2)], cot_pairs.at[place_at % 2], cot_s.at[place_at % 2])

    cot_load(0).start()
    cot_load(1).start()

    share.start()
    for place_at in range(4):
        line = reduce.order[place_at]
        both = attended[pl.ds(pl.multiple_of(line * pair, pair), pair)]
        parts[pl.ds(line * 2, 2)] = product(both, out_w[...]).astype(jnp.bfloat16).reshape(2, rows, width)
        reduce.start(place_at)
    for place_at in range(3):
        reduce.relay(place_at)
    reduce.total(total)
    hidden_rows = tokens[...].astype(jnp.float32) + total[...]
    hidden_out[...] = hidden_rows
    src[...] = (hidden_rows * rms_scale(hidden_rows) * gain[...]).astype(jnp.bfloat16)
    gather.start()
    share.relay()
    downs.start()
    reduce.finish()

    def forward(chip, own=False):
        shard = src if own else normed.at[chip]

        @pl.loop(0, 4)
        def _(tile):
            columns = pl.ds(pl.multiple_of(tile * step, step), step)
            gate_part = product(shard[...], gate_w[:, :, :, columns].reshape(width, step))
            up_part = product(shard[...], up_w[:, :, :, columns].reshape(width, step))
            sigmoid = jax.nn.sigmoid(gate_part)
            silu = gate_part * sigmoid
            slope = sigmoid * (1.0 + gate_part * (1.0 - sigmoid))
            gate_factor[chip, :, columns] = (up_part * slope).astype(jnp.bfloat16)
            up_factor[chip, :, columns] = silu.astype(jnp.bfloat16)
            active[chip, :, columns] = (silu * up_part).astype(jnp.bfloat16)

    def forward_own(distance):
        @pl.when(z - distance >= 0)
        def _():
            forward((z - distance) * 2 + y)

        @pl.when(z + distance <= LINE - 1)
        def _():
            forward((z + distance) * 2 + y)

    def forward_other(distance):
        def one(line):
            for elem in (0, 1):
                gather.across_in(line, elem).wait_recv()
            forward(line * 2 + 1 - y)

        if distance == 0:
            one(z)
        else:

            @pl.when(z - distance >= 0)
            def _():
                one(z - distance)

            @pl.when(z + distance <= LINE - 1)
            def _():
                one(z + distance)

    def relay(distance):
        for elem in order:
            gather.relay(distance - 1, elem)

    gather.relay_b()
    share.finish()
    forward(z * 2 + y, own=True)
    relay(1)
    forward_other(0)
    forward_own(1)
    relay(2)
    forward_other(1)
    forward_own(2)
    relay(3)
    downs.relay()
    forward_other(2)
    forward_own(3)
    forward_other(3)
    gather.own_copy().wait()
    downs.finish()

    def backward(place_at):
        line = reduce.order[place_at]
        both = pl.ds(line * 2, 2)
        cot_load(place_at).wait()

        @pl.loop(0, 4)
        def _(tile):
            columns = pl.ds(pl.multiple_of(tile * step, step), step)
            grad_active = times_transposed(
                cot_pairs[place_at % 2].reshape(pair, width), down_w[tile // 2, tile % 2]
            ).reshape(2, rows, step)
            gate_grad[both, :, columns] = (grad_active * gate_factor[both, :, columns].astype(jnp.float32)).astype(jnp.bfloat16)
            up_grad[both, :, columns] = (grad_active * up_factor[both, :, columns].astype(jnp.float32)).astype(jnp.bfloat16)

        if place_at < 2:
            cot_load(place_at + 2).start()

        @pl.loop(0, 4)
        def _(tile):
            columns = pl.ds(pl.multiple_of(tile * (width // 4), width // 4), width // 4)
            chips = pl.ds(tile * 2, 2)
            part = times_transposed(gate_grad[both].reshape(pair, hidden), gate_w[chips].reshape(width // 4, hidden))
            part += times_transposed(up_grad[both].reshape(pair, hidden), up_w[chips].reshape(width // 4, hidden))
            parts[both, :, columns] = part.astype(jnp.bfloat16).reshape(2, rows, width // 4)

    def stage_store(line):
        return local(stage, mlp_part.at[pl.ds(line * 2, 2)], stage_s)

    def contribute(line):
        if line:
            stage_store(line - 1).wait()

        @pl.loop(0, 4)
        def _(tile):
            columns = pl.ds(pl.multiple_of(tile * (width // 4), width // 4), width // 4)
            part = product(
                active[pl.ds(line * 2, 2)].reshape(pair, hidden), down_w[:, :, :, columns].reshape(hidden, width // 4)
            )
            stage[:, :, columns] = part.astype(jnp.bfloat16).reshape(2, rows, width // 4)

        stage_store(line).start()

    def weight_grad(kind):
        source = (gate_grad, up_grad)[kind]
        store = (gate_w, up_w)[kind]

        @pl.loop(0, 8)
        def _(tile):
            columns = pl.ds(pl.multiple_of(tile * pair, pair), pair)
            part = transposed_times(
                normed[:, :, columns].reshape(8 * rows, pair), source[...].reshape(8 * rows, hidden)
            )
            store[tile] = part.astype(jnp.bfloat16).reshape(2, rows, hidden)

    at_end = jnp.logical_or(z == 0, z == LINE - 1)
    inside = jnp.logical_not(at_end)
    for place_at in range(3):
        backward(place_at)
        reduce.start(place_at)

    @pl.when(at_end)
    def _():
        reduce.relay(0)

    backward(3)
    reduce.start(3)

    @pl.when(at_end)
    def _():
        reduce.relay(1)

    @pl.when(inside)
    def _():
        reduce.relay(0)

    weight_grad(0)
    for cut in range(2):
        grads.share(0, cut).start()
    contribute(0)

    @pl.when(inside)
    def _():
        reduce.relay(1)

    grads.relay(0)
    reduce.relay(2)
    for line in range(1, LINE):
        contribute(line)
    reduce.total(total)

    inputs = hidden_out[...]
    inv_scale = rms_scale(inputs)
    unit_rows = inputs * inv_scale
    grad_unit = total[...] * gain[...]
    mean = jnp.mean(grad_unit * unit_rows, axis=-1, keepdims=True)
    grad_rows = cot[...].astype(jnp.float32) + inv_scale * (grad_unit - unit_rows * mean)
    grad_hidden[...] = grad_rows
    branch[...] = grad_rows.astype(jnp.bfloat16)
    back.start()
    gain_term[...] = jnp.sum(total[...] * unit_rows, axis=0, keepdims=True)
    back.relay_b()
    weight_grad(1)
    for cut in range(2):
        grads.share(1, cut).start()
    for elem in order:
        back.relay(0, elem)
    grads.relay(1)
    for elem in order:
        back.relay(1, elem)
    grads.finish(0)
    for elem in order:
        back.relay(2, elem)
    grads.finish(1)
    back.finish()
    reduce.finish()
    stage_store(3).wait()
    for line in range(LINE):
        for elem in (0, 1):
            gather.across(line, elem).wait_send()
    gather.finish_sends()


def core(attended, out_w, gate, up, wd, tokens, gain, cot, cot_all):
    eight, depth, part = gate.shape
    rows, width = tokens.shape
    hidden = 2 * part

    def room(*dims, dtype=jnp.bfloat16):
        return pltpu.VMEM(dims, dtype)

    def shape(*dims, dtype=jnp.bfloat16):
        return jax.ShapeDtypeStruct(dims, dtype)

    f32 = jnp.float32
    return pl.pallas_call(
        core_kernel,
        out_shape=(
            shape(rows, width, dtype=f32),
            shape(8, rows, hidden),
            shape(8, rows, width),
            shape(8, rows, width),
            shape(rows, width, dtype=f32),
            shape(1, width, dtype=f32),
            shape(8, depth, part),
            shape(8, depth, part),
        ),
        in_specs=[INSIDE, INSIDE, ANY, ANY, ANY, INSIDE, INSIDE, INSIDE, ANY],
        out_specs=(INSIDE, INSIDE, ANY, ANY, INSIDE, INSIDE, INSIDE, INSIDE),
        scratch_shapes=[
            room(8, rows, width), room(rows, width), room(rows, width, dtype=f32),
            room(eight, 2, depth, hidden), room(eight, 2, depth, hidden), room(2, 2, *wd.shape),
            room(8, rows, hidden), room(8, rows, hidden),
            room(2, 2, rows, width), room(8, rows, width), room(2, rows, width),
            room(8, rows, hidden), room(8, rows, hidden), room(rows, width),
            dma(2), dma(),
        ]
        + Gather.scratch()
        + Gather.scratch()
        + MlpShare.scratch()
        + DownSpread.scratch()
        + Reduce.scratch(width)
        + QuarterReduce.scratch(depth, hidden),
        compiler_params=kernel_params(8),
        name="core",
    )(attended, out_w, gate, up, wd, tokens, gain, cot, cot_all)


def column_of(row):
    size = row.shape[1]
    same = lax.broadcasted_iota(jnp.int32, (size, size), 0) == lax.broadcasted_iota(jnp.int32, (size, size), 1)
    return jnp.sum(jnp.where(same, row, 0.0), axis=1, keepdims=True)


def row_of(column):
    size = column.shape[0]
    same = lax.broadcasted_iota(jnp.int32, (size, size), 0) == lax.broadcasted_iota(jnp.int32, (size, size), 1)
    return jnp.sum(jnp.where(same, column, 0.0), axis=0, keepdims=True)


def front_kernel(
    tokens, cot, note, inv_freqs, wq, wk, wv, wo, wg, wu,
    kv_out, normed_out, qkv_out, out_w, notes, gain, mlp_gain, cos_table, sine_table, query, attended_out, attended_low_out,
    log_out, cot_out, gate, up,
    gathered, normed, qkv_w, query_ids, key_ids, kv, keys, scores, total,
    own, x_s, x_r, c_s, c_r, store_s, *sems,
):
    z, y, c, h = place()
    tok_sems, note_sems, attn_sems, cot_sems, mlp_sems = split_refs(sems, (8, 3, AttnSpread.COUNT, 8, 3))
    greet_all(16, 2)
    rows, width = tokens.shape[0], HD
    pair = 2 * rows
    tok = Gather(tokens, gathered, tok_sems)
    notices = NoteSpread(note, notes, note_sems)
    attn = AttnSpread((wq, wk, wv, wo), (qkv_w, out_w), attn_sems)
    cots = Gather(cot, cot_out, cot_sems)
    mlp = MlpSpread((wg, wu), (gate, up), mlp_sems)

    def keep(cut):
        part = pl.ds(cut * 2, 2)
        return local(kv.at[part], keys.at[part, c, h], own.at[cut])

    def over(cut, half):
        part = pl.ds(cut * 2, 2)
        return remote(kv.at[part], keys.at[part, c, half], x_s.at[cut], x_r.at[cut], device(z, y, c, 1 - h))

    def share(cut, core):
        ref = keys.at[pl.ds(cut * 2, 2), core]
        return remote(ref, ref, c_s.at[cut], c_r.at[cut], device(z, y, 1 - c, h))

    def tables():
        for blk in range(16):
            gain[:, pl.ds(blk * rows, rows)] = notes[blk, 4:5, :]
            mlp_gain[:, pl.ds(blk * rows, rows)] = notes[blk, 5:6, :]
        for chip in range(8):
            part = pl.ds(chip * rows, rows)
            mine = notes[2 * chip + c]
            angles = column_of(jnp.where(h == 0, mine[0:1], mine[1:2])) * inv_freqs[...]
            cos_table[part] = jnp.cos(angles)
            sine_table[part] = jnp.sin(angles)
            query_ids[part] = column_of(jnp.where(h == 0, mine[2:3], mine[3:4]))
            for piece in range(4):
                key_ids[chip, :, pl.ds(piece * rows, rows)] = notes[2 * chip + piece // 2, 2 + piece % 2 : 3 + piece % 2, :]

    def project(cut):
        part = pl.ds(cut * pair, pair)
        inputs = gathered[pl.ds(cut * 2, 2)].reshape(pair, tokens.shape[1]).astype(jnp.float32)
        rows_normed = (inputs * rms_scale(inputs) * gain[...]).astype(jnp.bfloat16)
        normed[part] = rows_normed
        cos_rows, sine_rows = cos_table[part], sine_table[part]

        def turn(lower, upper):
            return (
                (lower * cos_rows - upper * sine_rows).astype(jnp.bfloat16),
                (upper * cos_rows + lower * sine_rows).astype(jnp.bfloat16),
            )

        def weight(columns):
            return qkv_w[:, :, :, columns].reshape(tokens.shape[1], columns.size)

        half = width // 2
        projected = product(rows_normed, weight(pl.ds(0, width)))
        lower, upper = turn(projected[:, :half], projected[:, half:])
        query[part, :half] = (lower.astype(jnp.float32) * HD**-0.5).astype(jnp.bfloat16)
        query[part, half:] = (upper.astype(jnp.float32) * HD**-0.5).astype(jnp.bfloat16)
        projected = product(rows_normed, weight(pl.ds(width, 2 * width)))
        lower, upper = turn(projected[:, :half], projected[:, half:width])
        both = pl.ds(cut * 2, 2)
        kv[both, :, :half] = lower.reshape(2, rows, half)
        kv[both, :, half:width] = upper.reshape(2, rows, half)
        kv[both, :, width:] = projected[:, width:].astype(jnp.bfloat16).reshape(2, rows, width)
        over(cut, h).start()
        keep(cut).start()

    def pass_on(cut):
        keep(cut).wait()
        over(cut, 1 - h).wait_recv()
        share(cut, c).start()

    def attend(place_at):
        part = pl.ds(place_at * pair, pair)
        count = min(2 * place_at + 3, 8)
        ids = query_ids[part]

        def maxima(block, best):
            key = keys[block, :, :, :, :width].reshape(4 * rows, width)
            part_scores = times_transposed(query[part], key)
            part_scores = jnp.where(key_ids[block] <= ids, part_scores, -1e30)
            scores[block] = part_scores
            for lane in range(4 * rows // 128):
                best = jnp.maximum(best, part_scores[:, lane * 128 : lane * 128 + 128])
            return best

        best = lax.fori_loop(0, count, maxima, jnp.full((pair, 128), -1e30, jnp.float32))
        row_max = jnp.max(best, axis=1, keepdims=True)
        total[...] = jnp.zeros_like(total)

        def mix(block, sums):
            weights = jnp.exp(scores[block] - row_max)
            value = keys[block, :, :, :, width:].reshape(4 * rows, width)
            total[...] += product(weights.astype(jnp.bfloat16), value)
            for lane in range(4 * rows // 128):
                sums = sums + weights[:, lane * 128 : lane * 128 + 128]
            return sums

        sums = lax.fori_loop(0, count, mix, jnp.zeros((pair, 128), jnp.float32))
        row_sum = jnp.sum(sums, axis=1, keepdims=True)
        mixed = total[...] / row_sum
        attended_out[part] = mixed
        attended_low_out[part] = mixed.astype(jnp.bfloat16)
        log_out[place_at] = row_of(row_max + jnp.log(row_sum))

    order = (2, 0, 1, 3)
    attn.start()
    tok.start()
    notices.start()
    tok.relay_b()
    attn.relay(0)
    for elem in order:
        tok.relay(0, elem)
    attn.relay(1)
    attn.relay(2)
    for elem in order:
        tok.relay(1, elem)
    attn.relay(3)
    attn.relay_out()
    notices.finish()
    tables()
    for elem in order:
        tok.relay(2, elem)
    cots.start()
    mlp.start()
    for step in range(LINE):
        attn.relay_share(step)
    attn.relay_out_share()
    tok.finish()
    attn.finish()
    store_qkv = local(qkv_w, qkv_out, store_s.at[0])
    store_qkv.start()
    for cut in range(LINE):
        project(cut)
    store_normed = local(normed, normed_out, store_s.at[1])
    store_normed.start()
    cots.relay_b()
    for elem in order:
        cots.relay(0, elem)
    pass_on(0)
    pass_on(1)
    share(0, 1 - c).wait_recv()
    share(1, 1 - c).wait_recv()
    attend(0)
    for elem in order:
        cots.relay(1, elem)
    pass_on(2)
    share(2, 1 - c).wait_recv()
    attend(1)
    pass_on(3)
    share(3, 1 - c).wait_recv()
    store = local(keys, kv_out, store_s.at[2])
    store.start()
    attend(2)
    for elem in order:
        cots.relay(2, elem)
    attend(3)
    cots.finish()
    mlp.finish()
    for cut in range(LINE):
        share(cut, c).wait_send()
        over(cut, h).wait_send()
    store.wait()
    store_normed.wait()
    store_qkv.wait()


def front(tokens, cot, note, inv_freqs, wq, wk, wv, wo, wg, wu):
    rows, width = tokens.shape
    depth, part = wg.shape[0], wg.shape[1] // 8
    token_rows = 8 * rows

    def room(*dims, dtype=jnp.bfloat16):
        return pltpu.VMEM(dims, dtype)

    def shape(*dims, dtype=jnp.bfloat16):
        return jax.ShapeDtypeStruct(dims, dtype)

    f32 = jnp.float32
    return pl.pallas_call(
        front_kernel,
        out_shape=(
            shape(8, 2, 2, rows, 2 * HD),
            shape(token_rows, width),
            shape(8, 2, depth, 3 * HD),
            shape(2, 2, wo.shape[0], width),
            shape(16, *note.shape, dtype=f32),
            shape(1, width, dtype=f32),
            shape(1, width, dtype=f32),
            shape(token_rows, HD // 2, dtype=f32),
            shape(token_rows, HD // 2, dtype=f32),
            shape(token_rows, HD),
            shape(token_rows, HD, dtype=f32),
            shape(token_rows, HD),
            shape(LINE, 1, token_rows // LINE, dtype=f32),
            shape(8, *cot.shape),
            shape(8, depth, part),
            shape(8, depth, part),
        ),
        in_specs=[INSIDE] * 10,
        out_specs=(ANY, ANY, ANY, ANY) + (INSIDE,) * 9 + (ANY, ANY, ANY),
        scratch_shapes=[
            room(8, rows, width),
            room(token_rows, width),
            room(8, 2, depth, 3 * HD),
            room(token_rows, 1, dtype=f32),
            room(8, 1, 4 * rows, dtype=f32),
            room(8, rows, 2 * HD),
            room(8, 2, 2, rows, 2 * HD),
            room(8, token_rows // LINE, 4 * rows, dtype=f32),
            room(token_rows // LINE, HD, dtype=f32),
        ]
        + [dma(4)] * 5
        + [dma(3)]
        + Gather.scratch()
        + NoteSpread.scratch()
        + AttnSpread.scratch(depth)
        + Gather.scratch()
        + MlpSpread.scratch(),
        compiler_params=kernel_params(3),
        name="front",
    )(tokens, cot, note, inv_freqs, wq, wk, wv, wo, wg, wu)


class QuarterReduce:
    @staticmethod
    def scratch(depth, wide):
        sib = pltpu.VMEM((8, depth, wide), jnp.bfloat16)
        over = pltpu.VMEM((8, depth, wide // 2), jnp.bfloat16)
        return [sib, sib, over, over] + [dma(2, 2)] * 4

    def __init__(self, store, outs, refs):
        self.store, self.outs = store, outs
        self.sib, self.box = refs[0:2], refs[2:4]
        self.c_s, self.c_r, self.x_s, self.x_r = refs[4:]
        self.z, self.y, self.c, self.h = place()
        self.part = self.box[0].shape[2]

    def columns(self, half):
        return pl.ds(pl.multiple_of(half * self.part, self.part), self.part)

    def share(self, kind, cut):
        chips = pl.ds(cut * 4, 4)
        return remote(
            self.store[kind].at[chips, 1 - self.c], self.sib[kind].at[chips], self.c_s.at[kind, cut],
            self.c_r.at[kind, cut], device(self.z, self.y, 1 - self.c, self.h),
        )

    def over(self, kind, cut):
        chips = pl.ds(cut * 4, 4)
        return remote(
            self.store[kind].at[chips, self.c, :, self.columns(1 - self.h)], self.box[kind].at[chips],
            self.x_s.at[kind, cut], self.x_r.at[kind, cut], device(self.z, self.y, self.c, 1 - self.h),
        )

    def relay(self, kind):
        columns = self.columns(1 - self.h)
        for cut in range(2):
            self.share(kind, cut).wait_recv()

            @pl.loop(cut * 4, cut * 4 + 4)
            def _(chip):
                add_into(self.store[kind].at[chip, self.c, :, columns], self.sib[kind].at[chip, :, columns])

            self.over(kind, cut).start()

    def finish(self, kind):
        columns = self.columns(self.h)
        for cut in range(2):
            self.over(kind, cut).wait_recv()

            @pl.loop(cut * 4, cut * 4 + 4)
            def _(chip):
                total = self.store[kind][chip, self.c, :, columns].astype(jnp.float32)
                total += self.sib[kind][chip, :, columns].astype(jnp.float32)
                total += self.box[kind][chip].astype(jnp.float32)
                self.outs[kind][chip] = total.astype(jnp.bfloat16)

        for cut in range(2):
            self.share(kind, cut).wait_send()
            self.over(kind, cut).wait_send()


class QuarterScatter:
    @staticmethod
    def scratch():
        return [dma(2, 8), dma(2, 8), dma(2)]

    def __init__(self, quarters, outs, sems):
        self.quarters, self.outs = quarters, outs
        self.s, self.r, self.own = sems
        self.z, self.y, self.c, self.h = place()
        self.chip = self.z * 2 + self.y
        self.part = quarters[0].shape[2]

    def columns(self, chip):
        return pl.ds(pl.multiple_of(chip * self.part, self.part), self.part)

    def push(self, kind, step):
        target = (self.chip + step) % 8
        return remote(
            self.quarters[kind].at[target], self.outs[kind].at[:, self.columns(self.chip)], self.s.at[kind, step],
            self.r.at[kind, step], device(target // 2, target % 2, self.c, self.h),
        )

    def pull(self, kind, step):
        ref = self.outs[kind].at[:, self.columns((self.chip + 8 - step) % 8)]
        return remote(ref, ref, self.s.at[kind, step], self.r.at[kind, step], device(self.z, self.y, self.c, self.h))

    def keep(self, kind):
        return local(self.quarters[kind].at[self.chip], self.outs[kind].at[:, self.columns(self.chip)], self.own.at[kind])

    def start(self):
        for kind in range(2):
            self.keep(kind).start()
            for step in range(1, 8):
                self.push(kind, step).start()

    def finish(self):
        for kind in range(2):
            self.keep(kind).wait()
            for step in range(1, 8):
                self.pull(kind, step).wait_recv()
                self.push(kind, step).wait_send()


class DownReduce:
    @staticmethod
    def scratch(rows, width):
        return [
            pltpu.VMEM((2, 2, rows, width), jnp.bfloat16),
            pltpu.VMEM((2, rows, width), jnp.bfloat16),
            pltpu.VMEM((rows, width), jnp.bfloat16),
            dma(2), dma(2),
        ]

    def __init__(self, out, refs):
        self.out = out
        self.store, self.sib, self.box, self.c_sr, self.x_sr = refs
        self.z, self.y, self.c, self.h = place()

    def share(self):
        return remote(
            self.store.at[:, 1 - self.c], self.sib, self.c_sr.at[0], self.c_sr.at[1],
            device(self.z, self.y, 1 - self.c, self.h),
        )

    def over(self):
        return remote(
            self.store.at[1 - self.h, self.c], self.box, self.x_sr.at[0], self.x_sr.at[1],
            device(self.z, self.y, self.c, 1 - self.h),
        )

    def relay(self):
        self.share().wait_recv()
        add_into(self.store.at[1 - self.h, self.c], self.sib.at[1 - self.h])
        self.over().start()

    def finish(self):
        self.over().wait_recv()
        total = self.store[self.h, self.c].astype(jnp.float32) + self.sib[self.h].astype(jnp.float32)
        self.out[...] = total + self.box[...].astype(jnp.float32)
        self.share().wait_send()
        self.over().wait_send()


class OutGrad:
    @staticmethod
    def scratch(rows, width):
        def room(*dims):
            return pltpu.VMEM(dims, jnp.bfloat16)

        return [room(2, 2, rows, width), room(2, rows, width), room(2, rows, width), dma(2), dma(2), dma(2), dma(1)]

    def __init__(self, out, refs):
        self.out = out
        self.store, self.sib, self.box, self.c_sr, self.x_sr, self.y_sr, self.own = refs
        self.z, self.y, self.c, self.h = place()
        self.me = device(self.z, self.y, self.c, self.h)
        self.owner = self.h == self.y

    def share(self):
        return remote(
            self.store.at[:, 1 - self.c], self.sib, self.c_sr.at[0], self.c_sr.at[1],
            device(self.z, self.y, 1 - self.c, self.h),
        )

    def over(self):
        return remote(
            self.store.at[:, self.c], self.box, self.x_sr.at[0], self.x_sr.at[1],
            device(self.z, self.y, self.c, 1 - self.h),
        )

    def move(self):
        return remote(
            self.store.at[1 - self.y, self.c], self.out, self.y_sr.at[0], self.y_sr.at[1],
            device(self.z, 1 - self.y, self.c, self.h),
        )

    def keep(self):
        return local(self.store.at[self.y, self.c], self.out, self.own.at[0])

    def relay(self):
        self.share().wait_recv()
        for pair in range(2):
            add_into(self.store.at[pair, self.c], self.sib.at[pair])

        @pl.when(jnp.logical_not(self.owner))
        def _():
            self.over().start()

    def send(self):
        @pl.when(self.owner)
        def _():
            self.over().wait_recv()
            for pair in range(2):
                add_into(self.store.at[pair, self.c], self.box.at[pair])
            self.move().start()
            self.keep().start()

    def finish(self):
        self.share().wait_send()

        @pl.when(jnp.logical_not(self.owner))
        def _():
            remote(self.out, self.out, self.y_sr.at[0], self.y_sr.at[1], self.me).wait_recv()
            self.over().wait_send()

        @pl.when(self.owner)
        def _():
            self.keep().wait()
            self.move().wait_send()


def attend_back_kernel(
    query, keys_in, branch_in, mlp_part, hidden, out_w, attended, attended_low, log_row, notes, cos_table, sine_table,
    gate_in, up_in,
    side_out, grad_query, output, gate, up, out_grad,
    mlp_parts, mlp_total, keys, branch, grad_out, delta_row, query_row, key_column, grad_rot, parts, grad_key, grad_value, sib_in, x_in, z_in,
    load_s, c_s, c_r, x_s, x_r, z_s, z_r, *sems,
):
    z, y, c, h = place()
    mate = z + 1 - 2 * (z % 2)
    loads = [local(keys_in, keys, load_s.at[0]), local(branch_in, branch, load_s.at[1])]
    load_mlp = local(mlp_part, mlp_parts, load_s.at[2])
    load_mlp.start()
    for load in loads:
        load.start()
    greet_all(16, 2)
    scatter_sems, out_refs, reduce_refs = split_refs(sems, (3, 7, Reduce.COUNT))
    reduce = Reduce(mlp_parts, reduce_refs)
    load_mlp.wait()
    for place_at in range(4):
        reduce.start(place_at)
    scatter = QuarterScatter((gate_in, up_in), (gate, up), scatter_sems)
    outs = OutGrad(out_grad, out_refs)
    scatter.start()
    width = query.shape[1]
    rows = branch.shape[1]
    pair = 2 * rows
    block_rows = 4 * rows

    def share(block):
        return remote(
            parts.at[block, 1 - c], sib_in.at[block], c_s.at[block], c_r.at[block], device(z, y, 1 - c, h)
        )

    def over(block):
        return remote(
            parts.at[block, c, 1 - h], x_in.at[block], x_s.at[block], x_r.at[block], device(z, y, c, 1 - h)
        )

    def columns(kind):
        return pl.ds(pl.multiple_of(kind * width, width), width)

    def across(block):
        return remote(
            parts.at[block, c, h, :, columns(1 - z % 2)], z_in.at[block], z_s.at[block], z_r.at[block],
            device(mate, y, c, h),
        )

    def stage_two(block):
        share(block).wait_recv()
        add_into(parts.at[block, c, 1 - h], sib_in.at[block, 1 - h])
        over(block).start()

    def stage_three(block):
        over(block).wait_recv()
        add_into(parts.at[block, c, h], sib_in.at[block, h], x_in.at[block])
        across(block).start()

    def turn_back(values, part):
        half = width // 2
        lower, upper = values[:, :half], values[:, half:]
        cos_rows, sine_rows = cos_table[part], sine_table[part]
        return (
            (lower * cos_rows + upper * sine_rows).astype(jnp.bfloat16),
            (upper * cos_rows - lower * sine_rows).astype(jnp.bfloat16),
        )

    def stage_four(block):
        across(block).wait_recv()
        total = parts[block, c, h, :, columns(z % 2)].astype(jnp.float32) + z_in[block].astype(jnp.float32)
        part = pl.ds(block * rows, rows)

        @pl.when(z % 2 == 0)
        def _():
            lower, upper = turn_back(total, part)
            side_out[part, : width // 2] = lower
            side_out[part, width // 2 :] = upper

        @pl.when(z % 2 == 1)
        def _():
            side_out[part] = total.astype(jnp.bfloat16)

    for chip in range(8):
        mine = notes[2 * chip + c]
        query_row[chip // 2, :, pl.ds((chip % 2) * rows, rows)] = jnp.where(h == 0, mine[2:3], mine[3:4])
        for piece in range(4):
            row = notes[2 * chip + piece // 2, 2 + piece % 2 : 3 + piece % 2, :]
            key_column[chip, pl.ds(piece * rows, rows)] = column_of(row)
    for load in loads:
        load.wait()
    grad_rot[...] = jnp.zeros_like(grad_rot)
    for place_at in range(LINE):
        part = pl.ds(place_at * pair, pair)
        grad_rows = times_transposed(branch[pl.ds(place_at * 2, 2)].reshape(pair, branch.shape[2]), out_w[...])
        grad_rows = grad_rows.astype(jnp.bfloat16)
        grad_out[part] = grad_rows
        delta = jnp.sum(grad_rows.astype(jnp.float32) * attended[part], axis=1, keepdims=True)
        delta_row[place_at] = row_of(delta)
    out_store = out_refs[0]

    @pl.loop(0, 4)
    def _(tile):
        tile_columns = pl.ds(pl.multiple_of(tile * 512, 512), 512)
        part = transposed_times(attended_low[...], branch[:, :, tile_columns].reshape(8 * rows, 512))
        out_store[:, :, :, tile_columns] = part.astype(jnp.bfloat16).reshape(2, 2, out_store.shape[2], 512)

    outs.share().start()
    for block in range(8):
        key = keys[block, :, :, :, :width].reshape(block_rows, width)
        value = keys[block, :, :, :, width:].reshape(block_rows, width)
        grad_key[...] = jnp.zeros_like(grad_key)
        grad_value[...] = jnp.zeros_like(grad_value)

        @pl.loop(max(0, (block - 1) // 2), LINE)
        def _(place_at):
            part = pl.ds(pl.multiple_of(place_at * pair, pair), pair)
            part_scores = times_transposed(key, query[part])
            visible = key_column[block] <= query_row[place_at]
            weights = jnp.where(visible, jnp.exp(part_scores - log_row[place_at]), 0.0)
            grad_weights = times_transposed(value, grad_out[part])
            grad_scores = (weights * (grad_weights - delta_row[place_at])).astype(jnp.bfloat16)
            grad_key[...] += product(grad_scores, query[part])
            grad_value[...] += product(weights.astype(jnp.bfloat16), grad_out[part])
            grad_rot[part] += transposed_times(grad_scores, key)

        parts[block, :, :, :, :width] = grad_key[...].astype(jnp.bfloat16).reshape(2, 2, rows, width)
        parts[block, :, :, :, width:] = grad_value[...].astype(jnp.bfloat16).reshape(2, 2, rows, width)
        share(block).start()
        if block == 0:
            outs.relay()
        if block >= 1:
            stage_two(block - 1)
        if block >= 4:
            stage_three(block - 4)
    stage_two(7)
    outs.send()

    @pl.when(jnp.logical_or(z == 0, z == LINE - 1))
    def _():
        reduce.relay(0)

    for place_at in range(LINE):
        part = pl.ds(place_at * pair, pair)
        lower, upper = turn_back(grad_rot[part] * HD**-0.5, part)
        grad_query[part, : width // 2] = lower
        grad_query[part, width // 2 :] = upper
    for block in range(4, 8):
        stage_three(block)
        stage_four(block - 4)

    @pl.when(jnp.logical_and(z > 0, z < LINE - 1))
    def _():
        reduce.relay(0)

    for block in range(4, 8):
        stage_four(block)
    reduce.relay(1)
    reduce.relay(2)
    for block in range(8):
        share(block).wait_send()
        over(block).wait_send()
        across(block).wait_send()
    outs.finish()
    reduce.total(mlp_total)
    output[...] = (hidden[...] + mlp_total[...]).astype(jnp.bfloat16)
    scatter.finish()
    reduce.finish()


def attend_back(
    query, keys, branch, mlp_part, hidden, out_w, attended, attended_low, log_row, notes, cos_table, sine_table, gate, up,
    out_rows,
):
    eight, _, _, rows, width = keys.shape
    tokens = query.shape[0]
    depth, part = gate.shape[1:]

    def room(*dims, dtype=jnp.bfloat16):
        return pltpu.VMEM(dims, dtype)

    def shape(*dims, dtype=jnp.bfloat16):
        return jax.ShapeDtypeStruct(dims, dtype)

    f32 = jnp.float32
    return pl.pallas_call(
        attend_back_kernel,
        out_shape=(
            shape(tokens, HD),
            shape(tokens, HD),
            shape(*hidden.shape),
            shape(depth, 8 * part),
            shape(depth, 8 * part),
            shape(out_rows, out_w.shape[1]),
        ),
        in_specs=[INSIDE, ANY, ANY, ANY] + [INSIDE] * 10,
        out_specs=(INSIDE, INSIDE, INSIDE, ANY, ANY, ANY),
        scratch_shapes=[
            room(*mlp_part.shape), room(*hidden.shape, dtype=f32), room(*keys.shape), room(*branch.shape), room(tokens, HD),
            room(LINE, 1, tokens // LINE, dtype=f32), room(LINE, 1, tokens // LINE, dtype=f32),
            room(8, 4 * rows, 1, dtype=f32), room(tokens, HD, dtype=f32), room(*keys.shape),
            room(4 * rows, HD, dtype=f32), room(4 * rows, HD, dtype=f32),
            room(eight, 2, rows, width), room(eight, rows, width), room(eight, rows, HD),
            dma(3),
        ]
        + [dma(8)] * 6
        + QuarterScatter.scratch()
        + OutGrad.scratch(out_rows, out_w.shape[1])
        + Reduce.scratch(hidden.shape[1]),
        compiler_params=kernel_params(11),
        name="attend_back",
    )(
        query, keys, branch, mlp_part, hidden, out_w, attended, attended_low, log_row, notes, cos_table, sine_table, gate, up
    )


class HeadGrads:
    @staticmethod
    def scratch(depth):
        def room(*dims):
            return pltpu.VMEM(dims, jnp.bfloat16)

        return [
            room(LINE, 2, 2, depth, HD), room(LINE, 2, 2, depth, HD),
            room(LINE, 2, depth, HD), room(LINE, 2, depth, HD),
            room(LINE, depth, HD), room(LINE, depth, HD),
            dma(2), dma(2), dma(2), dma(2), dma(3, 4), dma(3, 4), dma(3),
        ]

    def __init__(self, outs, refs):
        self.outs = outs
        self.store, self.sib, self.box = refs[0:2], refs[2:4], refs[4:6]
        (self.c_s, self.c_r, self.x_s, self.x_r, self.s, self.r, self.own) = refs[6:]
        self.z, self.y, self.c, self.h = place()
        self.me = device(self.z, self.y, self.c, self.h)

    def share(self, i):
        return remote(
            self.store[i].at[:, :, 1 - self.c], self.sib[i], self.c_s.at[i], self.c_r.at[i],
            device(self.z, self.y, 1 - self.c, self.h),
        )

    def over(self, i):
        return remote(
            self.store[i].at[:, 1 - self.h, self.c], self.box[i], self.x_s.at[i], self.x_r.at[i],
            device(self.z, self.y, self.c, 1 - self.h),
        )

    def target(self, kind, line):
        start = line * HD if kind == 0 else (line // 2) * HD
        return self.outs[kind].at[:, pl.ds(pl.multiple_of(start, HD), HD)]

    def push(self, kind, step):
        line = (self.z + step) % LINE
        return remote(
            self.store[min(kind, 1)].at[line, self.h, self.c], self.target(kind, self.z), self.s.at[kind, step],
            self.r.at[kind, self.z], device(line, self.h, self.c, self.y),
        )

    def keep(self, kind):
        return local(self.store[min(kind, 1)].at[self.z, self.h, self.c], self.target(kind, self.z), self.own.at[kind])

    def stays(self, step):
        return self.h == self.y if step == 0 else self.h < 0

    def pull(self, kind, line):
        ref = self.target(kind, line)
        return remote(ref, ref, self.s.at[kind, 0], self.r.at[kind, line], self.me)

    def relay(self, i):
        self.share(i).wait_recv()

        @pl.loop(0, LINE)
        def _(line):
            for pair in range(2):
                add_into(self.store[i].at[line, pair, self.c], self.sib[i].at[line, pair])

        self.over(i).start()

    def each_kind(self, i, act):
        if i == 0:
            act(0)
        else:
            for kind in (1, 2):

                @pl.when(self.z % 2 == kind - 1)
                def _():
                    act(kind)

    def scatter(self, i):
        self.over(i).wait_recv()

        @pl.loop(0, LINE)
        def _(line):
            add_into(self.store[i].at[line, self.h, self.c], self.box[i].at[line])

        def act(kind):
            for step in range(4):

                @pl.when(self.stays(step))
                def _():
                    self.keep(kind).start()

                @pl.when(jnp.logical_not(self.stays(step)))
                def _():
                    self.push(kind, step).start()

        self.each_kind(i, act)

    def finish(self):
        for kind in range(3):
            for line in range(LINE):
                if kind and line % 2 != kind - 1:
                    continue
                from_self = (self.z == line) & (self.y == self.h)

                @pl.when(from_self)
                def _():
                    self.keep(kind).wait()

                @pl.when(jnp.logical_not(from_self))
                def _():
                    self.pull(kind, line).wait_recv()

        def act(kind):
            for step in range(4):

                @pl.when(jnp.logical_not(self.stays(step)))
                def _():
                    self.push(kind, step).wait_send()

        for i in range(2):
            self.each_kind(i, act)
            self.over(i).wait_send()
            self.share(i).wait_send()


class GainSum:
    @staticmethod
    def scratch(rows):
        return [
            pltpu.VMEM((16, 8, rows), jnp.float32), pltpu.VMEM((32, 8, rows), jnp.float32), dma(32), dma(32),
        ]

    def __init__(self, out, refs):
        self.out = out
        self.terms, self.box, self.s, self.r = refs
        self.blk, self.h = lax.axis_index("blk"), lax.axis_index("head")

    def push(self, step):
        other = (self.blk + step // 2) % 16
        return remote(
            self.terms.at[other], self.box.at[step], self.s.at[step], self.r.at[step], (other, (self.h + step % 2) % 2)
        )

    def start(self, attn_term, mlp_term):
        rows = self.terms.shape[2]
        self.terms[...] = jnp.zeros_like(self.terms)
        for blk in range(16):
            part = pl.ds(blk * rows, rows)
            self.terms[blk, 0:1] = attn_term[:, part]
            self.terms[blk, 1:2] = mlp_term[:, part]
        for step in range(1, 32):
            self.push(step).start()

    def finish(self):
        total = self.terms[self.blk]
        for step in range(1, 32):
            self.push(step).wait_recv()
            total += self.box[step]
        self.out[...] = total
        for step in range(1, 32):
            self.push(step).wait_send()


def close_kernel(
    normed_in, qkv_w, active_in, cot_in, grad_query, grad_side, grad_hidden, tokens, gain, mlp_term,
    tokens_grad, gains, down, query, key, value,
    normed, weight, parts, active, cot, total, attn_term, load_s, *refs,
):
    reduce_refs, head_refs, gain_refs, down_refs = split_refs(refs, (Reduce.COUNT, 13, 4, 5))
    z, y, c, h = place()
    loads = [
        local(active_in, active, load_s.at[3]),
        local(cot_in, cot, load_s.at[4]),
    ]
    load = local(normed_in, normed, load_s.at[0])
    load_q = local(qkv_w.at[:, :, :, pl.ds(0, HD)], weight.at[0], load_s.at[1])
    side_columns = pl.ds(pl.multiple_of((1 + z % 2) * HD, HD), HD)
    load_side = local(qkv_w.at[:, :, :, side_columns], weight.at[1], load_s.at[2])
    load_q.start()
    load_side.start()
    load.start()
    for later in loads:
        later.start()
    greet_all(16, 2)
    reduce = Reduce(parts, reduce_refs)
    downs = DownReduce(down, down_refs)
    heads = HeadGrads((query, key, value), head_refs)
    gain_sum = GainSum(gains, gain_refs)
    rows, width = parts.shape[1:]
    pair = 2 * rows
    depth = head_refs[0].shape[3]
    load_q.wait()
    load_side.wait()
    for place_at in range(4):
        line = reduce.order[place_at]
        both = pl.ds(pl.multiple_of(line * pair, pair), pair)

        @pl.loop(0, 4)
        def _(tile):
            columns = pl.ds(pl.multiple_of(tile * (width // 4), width // 4), width // 4)
            part = times_transposed(grad_query[both], weight[0, pl.ds(tile * 2, 2)].reshape(width // 4, HD))
            part += times_transposed(grad_side[both], weight[1, pl.ds(tile * 2, 2)].reshape(width // 4, HD))
            parts[pl.ds(line * 2, 2), :, columns] = part.astype(jnp.bfloat16).reshape(2, rows, width // 4)

        reduce.start(place_at)
    load.wait()
    for i, source in enumerate((grad_query, grad_side)):

        @pl.loop(0, 4)
        def _(tile):
            columns = pl.ds(pl.multiple_of(tile * 4 * depth, 4 * depth), 4 * depth)
            part = transposed_times(normed[:, columns], source[...])
            head_refs[i][tile] = part.astype(jnp.bfloat16).reshape(2, 2, depth, HD)

        heads.share(i).start()
    heads.relay(0)
    heads.relay(1)
    reduce.relay(0)
    for later in loads:
        later.wait()
    down_rows = down.shape[0]

    def down_grad(tile):
        columns = pl.ds(tile * down_rows, down_rows)

        @pl.loop(0, 4)
        def _(piece):
            wide = pl.ds(pl.multiple_of(piece * (width // 4), width // 4), width // 4)
            part = transposed_times(
                active[:, :, columns].reshape(8 * rows, down_rows), cot[:, :, wide].reshape(8 * rows, width // 4)
            )
            down_refs[0][tile // 2, tile % 2, :, wide] = part.astype(jnp.bfloat16)

    for tile in range(4):
        down_grad(tile)
    downs.share().start()
    heads.scatter(0)
    reduce.relay(1)
    heads.scatter(1)
    downs.relay()
    reduce.relay(2)
    reduce.total(total)
    inputs = tokens[...].astype(jnp.float32)
    inv_scale = rms_scale(inputs)
    unit_rows = inputs * inv_scale
    attn_term[...] = jnp.sum(total[...] * unit_rows, axis=0, keepdims=True)
    gain_sum.start(attn_term, mlp_term)
    grad_unit = total[...] * gain[...]
    mean = jnp.mean(grad_unit * unit_rows, axis=-1, keepdims=True)
    tokens_grad[...] = (grad_hidden[...] + inv_scale * (grad_unit - unit_rows * mean)).astype(jnp.bfloat16)
    downs.finish()
    heads.finish()
    reduce.finish()
    gain_sum.finish()


def close(normed, qkv_w, active, cot, grad_query, grad_side, grad_hidden, tokens, gain, mlp_term):
    rows, width = tokens.shape
    down_rows = active.shape[2] // 4
    depth = qkv_w.shape[2]

    def room(*dims, dtype=jnp.bfloat16):
        return pltpu.VMEM(dims, dtype)

    def shape(*dims, dtype=jnp.bfloat16):
        return jax.ShapeDtypeStruct(dims, dtype)

    f32 = jnp.float32
    return pl.pallas_call(
        close_kernel,
        out_shape=(
            shape(rows, width),
            shape(8, rows, dtype=f32),
            shape(down_rows, width, dtype=f32),
            shape(depth, 4 * HD), shape(depth, 2 * HD), shape(depth, 2 * HD),
        ),
        in_specs=[ANY] * 4 + [INSIDE] * 6,
        out_specs=(INSIDE, INSIDE, INSIDE, ANY, ANY, ANY),
        scratch_shapes=[
            room(*normed.shape), room(2, 8, 2, depth, HD), room(8, rows, width),
            room(*active.shape), room(*cot.shape),
            room(rows, width, dtype=f32), room(1, width, dtype=f32), dma(5),
        ]
        + Reduce.scratch(width)
        + HeadGrads.scratch(depth)
        + GainSum.scratch(rows)
        + DownReduce.scratch(down_rows, width),
        compiler_params=kernel_params(6),
        name="close",
    )(normed, qkv_w, active, cot, grad_query, grad_side, grad_hidden, tokens, gain, mlp_term)


def widen_kernel(*refs):
    half = len(refs) // 2
    for source, target in zip(refs[:half], refs[half:]):
        target[...] = source[...].astype(target.dtype)


def widen(arrays, dtypes):
    return pl.pallas_call(
        widen_kernel,
        out_shape=tuple(jax.ShapeDtypeStruct(array.shape, dtype) for array, dtype in zip(arrays, dtypes)),
        in_specs=[INSIDE] * len(arrays),
        out_specs=(INSIDE,) * len(arrays),
        compiler_params=pltpu.CompilerParams(vmem_limit_bytes=VMEM_BYTES),
        name="widen",
    )(*arrays)


def fast_body(
    tokens,
    attn_gain,
    w_query,
    w_key,
    w_value,
    w_out,
    mlp_gain,
    w_gate,
    w_up,
    w_down,
    block_ids,
    positions,
    cotangent,
):
    rows, width = tokens.shape
    token_rows = 8 * rows
    f32, bf16 = jnp.float32, jnp.bfloat16

    note = jnp.concatenate(
        [
            positions.astype(f32).reshape(2, rows),
            block_ids.astype(f32).reshape(2, rows),
            attn_gain.astype(f32)[None],
            mlp_gain.astype(f32)[None],
            jnp.zeros((2, rows), f32),
        ]
    )
    inv_freqs = jnp.asarray((rope_base ** (-2.0 * np.arange(HD // 2) / HD)).astype(np.float32))
    (
        keys_values, normed, qkv_w, out_w, notes, gain_attn, gain_mlp, cos_table, sine_table, scaled_query, attended, attended_low,
        log_total, cot_all, gate_w, up_w,
    ) = front(tokens, cotangent, note, inv_freqs[None], w_query, w_key, w_value, w_out, w_gate, w_up)
    out_w = out_w.reshape(HD, width)
    hidden, active, mlp_part, grad_branch, grad_hidden, mlp_term, gate_quarter, up_quarter = core(
        attended_low, out_w, gate_w, up_w, w_down, tokens, gain_mlp, cotangent, cot_all
    )

    side_grad, grad_query, output, gate_grad, up_grad, out_grad = attend_back(
        scaled_query,
        keys_values,
        grad_branch,
        mlp_part,
        hidden,
        out_w,
        attended,
        attended_low,
        log_total,
        notes,
        cos_table,
        sine_table,
        gate_quarter,
        up_quarter,
        w_out.shape[0],
    )
    tokens_grad, gain_grads, down_grad, query_grad, key_grad, value_grad = close(
        normed,
        qkv_w,
        active,
        cot_all,
        grad_query,
        side_grad,
        grad_hidden,
        tokens,
        gain_attn,
        mlp_term,
    )
    arrays = (output, tokens_grad, query_grad, key_grad, value_grad, out_grad, gate_grad, up_grad, down_grad)
    output, tokens_grad, query_grad, key_grad, value_grad, out_grad, gate_grad, up_grad, down_grad = widen(
        arrays, (bf16, bf16) + (f32,) * 7
    )
    return (
        output,
        tokens_grad,
        gain_grads[0],
        query_grad,
        key_grad,
        value_grad,
        out_grad,
        gain_grads[1],
        gate_grad,
        up_grad,
        down_grad,
    )


def solution(mesh):
    placed = (
        P(("blk", "head"), None),
        P("blk"),
        P("blk", "head"),
        P("blk", "head"),
        P("blk", "head"),
        P(("head", "blk"), None),
        P("blk"),
        P("blk", "head"),
        P("blk", "head"),
        P(("head", "blk"), None),
        P("blk"),
        P("blk"),
        P(("blk", "head"), None),
    )
    fits = mesh.shape["blk"] == 16 and mesh.shape["head"] == 2
    return jax.shard_map(
        fast_body if fits else body,
        mesh=mesh,
        in_specs=placed,
        out_specs=(
            P(("blk", "head"), None),
            P(("blk", "head"), None),
            P("blk"),
            P("blk", "head"),
            P("blk", "head"),
            P("blk", "head"),
            P(("head", "blk"), None),
            P("blk"),
            P("blk", "head"),
            P("blk", "head"),
            P(("head", "blk"), None),
        ),
        check_vma=False,
    )
```

```python
import jax
import jax.numpy as jnp
from jax import lax
import numpy as np
from jax.experimental import pallas as pl
from jax.experimental.pallas import tpu as pltpu
from jax.sharding import PartitionSpec as P

HD = 256


eps_norm = 1e-06
rope_base = 1000042.0


def rms_scale(rows):
    return lax.rsqrt(jnp.mean(rows * rows, axis=-1, keepdims=True) + eps_norm)


def rope_tables(positions):
    inv_freqs = rope_base ** (-2.0 * jnp.arange(HD // 2, dtype=jnp.float32) / HD)
    angles = positions.astype(jnp.float32)[:, None] * inv_freqs[None, :]
    return (jnp.cos(angles)[:, None, :], jnp.sin(angles)[:, None, :])


def rotate(heads, cos_table, sine_table):
    half_size = heads.shape[-1] // 2
    lower_half = heads[..., :half_size]
    upper_half = heads[..., half_size:]
    return jnp.concatenate(
        [
            lower_half * cos_table - upper_half * sine_table,
            upper_half * cos_table + lower_half * sine_table,
        ],
        axis=-1,
    )


def product(left, right):
    return jnp.dot(left, right, preferred_element_type=jnp.float32)


def times_transposed(left, right):
    return lax.dot_general(
        left, right, (((1,), (1,)), ((), ())), preferred_element_type=jnp.float32
    )


def transposed_times(left, right):
    return lax.dot_general(
        left, right, (((0,), (0,)), ((), ())), preferred_element_type=jnp.float32
    )


def norm_backward(grad_normed, inputs, inv_scale, gain_rows):
    unit_rows = inputs * inv_scale
    grad_unit = grad_normed * gain_rows
    gain_term = jnp.sum(grad_normed * unit_rows, axis=0)
    grad_inputs = inv_scale * (
        grad_unit - unit_rows * jnp.mean(grad_unit * unit_rows, axis=-1, keepdims=True)
    )
    return (grad_inputs, gain_term)


def body(
    tokens,
    attn_gain,
    w_query,
    w_key,
    w_value,
    w_out,
    mlp_gain,
    w_gate,
    w_up,
    w_down,
    block_ids,
    positions,
    cotangent,
):
    rows_own = tokens.shape[0]
    head_rank = lax.axis_index("head")
    tokens_all, cot_all = (
        lax.all_gather(tokens, "head", axis=0, tiled=True),
        lax.all_gather(cotangent, "head", axis=0, tiled=True),
    )
    rows_all = tokens_all.shape[0]
    gain_attn, query_w, key_w, value_w, out_w = (
        lax.all_gather(attn_gain, "blk", axis=0, tiled=True),
        lax.all_gather(w_query, "blk", axis=0, tiled=True),
        lax.all_gather(w_key, "blk", axis=0, tiled=True),
        lax.all_gather(w_value, "blk", axis=0, tiled=True),
        lax.all_gather(w_out, "blk", axis=0, tiled=True),
    )
    gain_mlp, gate_w, up_w, down_w = (
        lax.all_gather(mlp_gain, "blk", axis=0, tiled=True),
        lax.all_gather(w_gate, "blk", axis=0, tiled=True),
        lax.all_gather(w_up, "blk", axis=0, tiled=True),
        lax.all_gather(w_down, "blk", axis=0, tiled=True),
    )
    key_ids = lax.all_gather(block_ids, "blk", axis=0, tiled=True)
    heads_local = query_w.shape[1] // HD
    kv_local = key_w.shape[1] // HD
    kv_width = kv_local * HD
    group_size = heads_local // kv_local
    cos_table, sine_table = rope_tables(positions)
    score_scale = HD ** (-0.5)
    seq_len = key_ids.shape[0]
    key_block = min(2048, seq_len)
    block_total = seq_len // key_block
    block_steps = jnp.arange(block_total)
    top_query = jnp.max(block_ids)
    inputs = tokens_all.astype(jnp.float32)
    inv_attn = rms_scale(inputs)
    normed = (inputs * inv_attn * gain_attn.astype(jnp.float32)).astype(jnp.bfloat16)
    queries = rotate(
        product(normed, query_w).reshape(rows_all, heads_local, HD), cos_table, sine_table
    ).astype(jnp.bfloat16)
    keys_own = rotate(product(normed, key_w).reshape(rows_all, kv_local, HD), cos_table, sine_table)
    keys_own = keys_own.astype(jnp.bfloat16).reshape(rows_all, kv_width)
    values_own = product(normed, value_w).astype(jnp.bfloat16)
    keys_all, values_all = (
        lax.all_gather(keys_own, "blk", axis=0, tiled=True),
        lax.all_gather(values_own, "blk", axis=0, tiled=True),
    )
    grouped = queries.reshape(rows_all, kv_local, group_size, HD)

    def slice_keys(key_start, count):
        key_rows = lax.dynamic_slice_in_dim(keys_all, key_start, count, 0).reshape(
            count, kv_local, HD
        )
        value_rows = lax.dynamic_slice_in_dim(values_all, key_start, count, 0).reshape(
            count, kv_local, HD
        )
        block_keys = lax.dynamic_slice_in_dim(key_ids, key_start, count, 0)
        return (key_rows, value_rows, block_keys)

    def scores_for(key_rows, block_keys):
        scores = (
            jnp.einsum("qkgd,ckd->kgqc", grouped, key_rows, preferred_element_type=jnp.float32)
            * score_scale
        )
        visible = (block_keys[None, :] <= block_ids[:, None])[None, None]
        return (scores, visible)

    def max_sum(state_pair, step_index):
        key_start = step_index * key_block

        def max_live(pair):
            run_max, run_sum = pair
            key_rows, value_rows, block_keys = slice_keys(key_start, key_block)
            scores, visible = scores_for(key_rows, block_keys)
            scores = jnp.where(visible, scores, -1e30)
            new_max = jnp.maximum(run_max, jnp.max(scores, axis=-1))
            kept_terms = jnp.where(visible, jnp.exp(scores - new_max[..., None]), 0.0)
            return (new_max, run_sum * jnp.exp(run_max - new_max) + jnp.sum(kept_terms, axis=-1))

        def max_skipped(pair):
            return pair

        return (lax.cond(key_ids[key_start] <= top_query, max_live, max_skipped, state_pair), None)

    start_max = jnp.full((kv_local, group_size, rows_all), -1e30, jnp.float32)
    start_sum = jnp.zeros((kv_local, group_size, rows_all), jnp.float32)
    (run_max, run_sum), unused_max = lax.scan(max_sum, (start_max, start_sum), block_steps)
    log_total = run_max + jnp.log(run_sum)

    def weighted(accum_rows, step_index):
        key_start = step_index * key_block

        def weighted_live(accum):
            key_rows, value_rows, block_keys = slice_keys(key_start, key_block)
            scores, visible = scores_for(key_rows, block_keys)
            probabilities = jnp.where(visible, jnp.exp(scores - log_total[..., None]), 0.0).astype(
                jnp.bfloat16
            )
            return accum + jnp.einsum(
                "kgqc,ckd->qkgd", probabilities, value_rows, preferred_element_type=jnp.float32
            )

        def weighted_skipped(accum):
            return accum

        return (
            lax.cond(key_ids[key_start] <= top_query, weighted_live, weighted_skipped, accum_rows),
            None,
        )

    attended, unused_rows = lax.scan(
        weighted, jnp.zeros((rows_all, kv_local, group_size, HD), jnp.float32), block_steps
    )
    attended_low = attended.reshape(rows_all, heads_local * HD).astype(jnp.bfloat16)
    branch_sum = lax.psum(product(attended_low, out_w).astype(jnp.bfloat16), "head").astype(
        jnp.float32
    )
    hidden = inputs + branch_sum
    inv_mlp = rms_scale(hidden)
    normed_mlp = (hidden * inv_mlp * gain_mlp.astype(jnp.float32)).astype(jnp.bfloat16)
    gate_pre = product(normed_mlp, gate_w)
    up_pre = product(normed_mlp, up_w)
    sigmoid_gate = jax.nn.sigmoid(gate_pre)
    active = (gate_pre * sigmoid_gate * up_pre).astype(jnp.bfloat16)
    mlp_own = lax.psum_scatter(
        product(active, down_w).astype(jnp.bfloat16), "head", scatter_dimension=0, tiled=True
    ).astype(jnp.float32)
    hidden_own = lax.dynamic_slice_in_dim(hidden, head_rank * rows_own, rows_own, 0)
    output = (hidden_own + mlp_own).astype(jnp.bfloat16)
    gain_attn, query_w, key_w, value_w, out_w = (
        lax.all_gather(attn_gain, "blk", axis=0, tiled=True),
        lax.all_gather(w_query, "blk", axis=0, tiled=True),
        lax.all_gather(w_key, "blk", axis=0, tiled=True),
        lax.all_gather(w_value, "blk", axis=0, tiled=True),
        lax.all_gather(w_out, "blk", axis=0, tiled=True),
    )
    gain_mlp, gate_w, up_w, down_w = (
        lax.all_gather(mlp_gain, "blk", axis=0, tiled=True),
        lax.all_gather(w_gate, "blk", axis=0, tiled=True),
        lax.all_gather(w_up, "blk", axis=0, tiled=True),
        lax.all_gather(w_down, "blk", axis=0, tiled=True),
    )
    grad_active = times_transposed(cot_all, down_w)
    grad_gate = (
        grad_active * up_pre * sigmoid_gate * (1.0 + gate_pre * (1.0 - sigmoid_gate))
    ).astype(jnp.bfloat16)
    grad_up = (grad_active * gate_pre * sigmoid_gate).astype(jnp.bfloat16)
    grad_gate_w = transposed_times(normed_mlp, grad_gate)
    grad_up_w = transposed_times(normed_mlp, grad_up)
    grad_down_w = transposed_times(active, cot_all)
    grad_normed_part = times_transposed(grad_gate, gate_w) + times_transposed(grad_up, up_w)
    grad_normed_mlp = lax.psum(grad_normed_part.astype(jnp.bfloat16), "head").astype(jnp.float32)
    grad_hidden_norm, gain_mlp_term = norm_backward(
        grad_normed_mlp, hidden, inv_mlp, gain_mlp.astype(jnp.float32)
    )
    grad_hidden = cot_all.astype(jnp.float32) + grad_hidden_norm
    mlp_results = (
        lax.psum_scatter(gain_mlp_term, "blk", scatter_dimension=0, tiled=True),
        lax.psum_scatter(grad_gate_w, "blk", scatter_dimension=0, tiled=True),
        lax.psum_scatter(grad_up_w, "blk", scatter_dimension=0, tiled=True),
        lax.psum_scatter(grad_down_w, "blk", scatter_dimension=0, tiled=True),
    )
    grad_branch = grad_hidden.astype(jnp.bfloat16)
    grad_out_w = transposed_times(attended_low, grad_branch)
    grad_attended = times_transposed(grad_branch, out_w).astype(jnp.bfloat16)
    grad_grouped = grad_attended.reshape(rows_all, kv_local, group_size, HD)
    delta_rows = jnp.transpose(
        jnp.sum(grad_grouped.astype(jnp.float32) * attended, axis=-1), (1, 2, 0)
    )

    def pair_backward(key_rows, value_rows, block_keys):
        count = key_rows.shape[0]
        scores, visible = scores_for(key_rows, block_keys)
        probabilities = jnp.where(visible, jnp.exp(scores - log_total[..., None]), 0.0)
        grad_probs = jnp.einsum(
            "qkgd,ckd->kgqc", grad_grouped, value_rows, preferred_element_type=jnp.float32
        )
        grad_scores = (probabilities * (grad_probs - delta_rows[..., None])).astype(jnp.bfloat16)
        query_terms = jnp.einsum(
            "kgqc,ckd->qkgd", grad_scores, key_rows, preferred_element_type=jnp.float32
        )
        key_terms = (
            jnp.einsum("kgqc,qkgd->ckd", grad_scores, grouped, preferred_element_type=jnp.float32)
            * score_scale
        )
        value_terms = jnp.einsum(
            "kgqc,qkgd->ckd",
            probabilities.astype(jnp.bfloat16),
            grad_grouped,
            preferred_element_type=jnp.float32,
        )
        return (
            query_terms,
            key_terms.reshape(count, kv_width),
            value_terms.reshape(count, kv_width),
        )

    query_zeros = jnp.zeros((rows_all, kv_local, group_size, HD), jnp.float32)

    def backward_block(accum_rows, step_index):
        key_start = step_index * key_block

        def backward_live(unused_arg):
            key_rows, value_rows, block_keys = slice_keys(key_start, key_block)
            return pair_backward(key_rows, value_rows, block_keys)

        def backward_skipped(unused_arg):
            empty_terms = jnp.zeros((key_block, kv_width), jnp.float32)
            return (query_zeros, empty_terms, empty_terms)

        query_terms, key_terms, value_terms = lax.cond(
            key_ids[key_start] <= top_query, backward_live, backward_skipped, 0
        )
        return (accum_rows + query_terms, (key_terms, value_terms))

    grad_query_rot, (key_terms, value_terms) = lax.scan(backward_block, query_zeros, block_steps)
    key_terms = key_terms.reshape(seq_len, kv_width)
    value_terms = value_terms.reshape(seq_len, kv_width)
    key_grad_own, value_grad_own = (
        lax.psum_scatter(key_terms, "blk", scatter_dimension=0, tiled=True),
        lax.psum_scatter(value_terms, "blk", scatter_dimension=0, tiled=True),
    )
    grad_query_rot = grad_query_rot * score_scale
    grad_key = rotate(key_grad_own.reshape(rows_all, kv_local, HD), cos_table, -sine_table)
    grad_key = grad_key.reshape(rows_all, kv_width).astype(jnp.bfloat16)
    grad_value = value_grad_own.astype(jnp.bfloat16)
    grad_query = rotate(grad_query_rot.reshape(rows_all, heads_local, HD), cos_table, -sine_table)
    grad_query = grad_query.reshape(rows_all, heads_local * HD).astype(jnp.bfloat16)
    grad_query_w = transposed_times(normed, grad_query)
    grad_key_w = transposed_times(normed, grad_key)
    grad_value_w = transposed_times(normed, grad_value)
    grad_normed_part = (
        times_transposed(grad_query, query_w)
        + times_transposed(grad_key, key_w)
        + times_transposed(grad_value, value_w)
    )
    grad_normed = lax.psum(grad_normed_part.astype(jnp.bfloat16), "head").astype(jnp.float32)
    grad_inputs_norm, gain_attn_term = norm_backward(
        grad_normed, inputs, inv_attn, gain_attn.astype(jnp.float32)
    )
    grad_inputs = grad_hidden + grad_inputs_norm
    grad_own = lax.dynamic_slice_in_dim(grad_inputs, head_rank * rows_own, rows_own, 0).astype(
        jnp.bfloat16
    )
    attn_results = (
        lax.psum_scatter(gain_attn_term, "blk", scatter_dimension=0, tiled=True),
        lax.psum_scatter(grad_query_w, "blk", scatter_dimension=0, tiled=True),
        lax.psum_scatter(grad_key_w, "blk", scatter_dimension=0, tiled=True),
        lax.psum_scatter(grad_value_w, "blk", scatter_dimension=0, tiled=True),
        lax.psum_scatter(grad_out_w, "blk", scatter_dimension=0, tiled=True),
    )
    return (
        output,
        grad_own,
        attn_results[0],
        attn_results[1],
        attn_results[2],
        attn_results[3],
        attn_results[4],
        mlp_results[0],
        mlp_results[1],
        mlp_results[2],
        mlp_results[3],
    )


MESH = pl.DeviceIdType.MESH
LINE = 4
VMEM_BYTES = 60 * 2**20


def place():
    blk, head = lax.axis_index("blk"), lax.axis_index("head")
    return blk // 4, (blk // 2) % 2, blk % 2, head


def device(z, y, c, h):
    return (z * 4 + y * 2 + c, h)


def remote(src, dst, send_sem, recv_sem, target):
    return pltpu.make_async_remote_copy(
        src_ref=src,
        dst_ref=dst,
        send_sem=send_sem,
        recv_sem=recv_sem,
        device_id=target,
        device_id_type=MESH,
    )


def greet(target):
    pl.semaphore_signal(
        pltpu.get_barrier_semaphore(), inc=1, device_id=target, device_id_type=MESH
    )


def greet_all(blk_total, head_total):
    blk, head = lax.axis_index("blk"), lax.axis_index("head")
    for other in range(blk_total):
        for half in range(head_total):

            @pl.when(jnp.logical_or(blk != other, head != half))
            def _():
                greet((jnp.int32(other), jnp.int32(half)))

    pl.semaphore_wait(pltpu.get_barrier_semaphore(), blk_total * head_total - 1)


def greet_plane(more=0):
    z, y, c, h = place()

    @pl.when(z > 0)
    def _():
        greet(device(z - 1, y, c, h))

    @pl.when(z < LINE - 1)
    def _():
        greet(device(z + 1, y, c, h))

    greet(device(z, 1 - y, c, h))
    pl.semaphore_wait(
        pltpu.get_barrier_semaphore(),
        1 + more + (z + LINE - 1) // LINE + (LINE - 1 - z + LINE - 1) // LINE,
    )


class Gather:
    CUTS = ((0, 64), (64, 48), (112, 16), (112, 16))
    SEMS = [(3, 4)] * 4 + [(4, 2)] * 2 + [(2,)]

    @staticmethod
    def scratch():
        return [pltpu.SemaphoreType.DMA(shape) for shape in Gather.SEMS] + [
            pltpu.SemaphoreType.DMA
        ]

    def __init__(self, src, out, sems):
        self.src, self.out = src, out
        (self.up_s, self.up_r, self.dn_s, self.dn_r, self.y_s, self.y_r, self.b_sr, self.own_sem) = sems
        self.z, self.y, self.c, self.h = place()

    def piece(self, line, elem):
        y = 1 - self.y if elem == 3 else self.y
        start, size = self.CUTS[elem]
        return self.out.at[line * 2 + y, pl.ds(start, size)]

    def first(self, elem):
        if elem == 3:
            return self.piece(self.z, 3)
        start, size = self.CUTS[elem]
        return self.src.at[pl.ds(start, size)]

    def up(self, step, elem):
        src = self.first(elem) if step == 0 else self.piece(self.z - step, elem)
        return remote(
            src, self.piece(self.z - step, elem), self.up_s.at[step, elem], self.up_r.at[step, elem],
            device(self.z + 1, self.y, self.c, self.h),
        )

    def down(self, step, elem):
        src = self.first(elem) if step == 0 else self.piece(self.z + step, elem)
        return remote(
            src, self.piece(self.z + step, elem), self.dn_s.at[step, elem], self.dn_r.at[step, elem],
            device(self.z - 1, self.y, self.c, self.h),
        )

    def up_in(self, step, elem):
        ref = self.piece(self.z - 1 - step, elem)
        return remote(ref, ref, self.up_s.at[step, elem], self.up_r.at[step, elem], device(self.z, self.y, self.c, self.h))

    def down_in(self, step, elem):
        ref = self.piece(self.z + 1 + step, elem)
        return remote(ref, ref, self.dn_s.at[step, elem], self.dn_r.at[step, elem], device(self.z, self.y, self.c, self.h))

    def across(self, line, elem, own=False):
        src = self.first(elem) if own else self.piece(line, elem)
        return remote(
            src, self.piece(line, elem), self.y_s.at[line, elem], self.y_r.at[line, elem],
            device(self.z, 1 - self.y, self.c, self.h),
        )

    def across_in(self, line, elem):
        start, size = self.CUTS[elem]
        ref = self.out.at[line * 2 + 1 - self.y, pl.ds(start, size)]
        return remote(ref, ref, self.y_s.at[line, elem], self.y_r.at[line, elem], device(self.z, self.y, self.c, self.h))

    def across_b(self):
        return remote(
            self.first(2), self.piece(self.z, 2), self.b_sr.at[0], self.b_sr.at[1],
            device(self.z, 1 - self.y, self.c, self.h),
        )

    def across_b_in(self):
        ref = self.piece(self.z, 3)
        return remote(ref, ref, self.b_sr.at[0], self.b_sr.at[1], device(self.z, self.y, self.c, self.h))

    def own_copy(self):
        return pltpu.make_async_copy(self.src, self.out.at[self.z * 2 + self.y], self.own_sem)

    def start(self):
        self.own_copy().start()
        self.across_b().start()
        for elem in (0, 1, 2):

            @pl.when(self.z < LINE - 1)
            def _():
                self.up(0, elem).start()

            @pl.when(self.z > 0)
            def _():
                self.down(0, elem).start()

            if elem < 2:
                self.across(self.z, elem, own=True).start()

    def relay_b(self):
        self.across_b_in().wait_recv()

        @pl.when(self.z < LINE - 1)
        def _():
            self.up(0, 3).start()

        @pl.when(self.z > 0)
        def _():
            self.down(0, 3).start()

    def relay(self, step, elem):
        @pl.when(self.z - 1 - step >= 0)
        def _():
            self.up_in(step, elem).wait_recv()
            if step < LINE - 2:

                @pl.when(self.z < LINE - 1)
                def _():
                    self.up(step + 1, elem).start()

            if elem < 2:
                self.across(self.z - 1 - step, elem).start()

        @pl.when(self.z + 1 + step <= LINE - 1)
        def _():
            self.down_in(step, elem).wait_recv()
            if step < LINE - 2:

                @pl.when(self.z > 0)
                def _():
                    self.down(step + 1, elem).start()

            if elem < 2:
                self.across(self.z + 1 + step, elem).start()

    def relays(self):
        self.relay_b()
        for step in range(LINE - 1):
            for elem in (0, 1, 2, 3):
                self.relay(step, elem)

    def finish(self):
        for line in range(LINE):
            for elem in (0, 1):
                self.across_in(line, elem).wait_recv()
        for line in range(LINE):
            for elem in (0, 1):
                self.across(line, elem).wait_send()
        self.finish_sends()
        self.own_copy().wait()

    def finish_sends(self):
        self.across_b().wait_send()
        for step in range(LINE - 1):
            for elem in range(4):

                @pl.when(jnp.logical_and(self.z < LINE - 1, self.z - step >= 0))
                def _():
                    self.up(step, elem).wait_send()

                @pl.when(jnp.logical_and(self.z > 0, self.z + step <= LINE - 1))
                def _():
                    self.down(step, elem).wait_send()


ANY = pl.BlockSpec(memory_space=pl.ANY)
INSIDE = pl.BlockSpec(memory_space=pltpu.VMEM)


def kernel_params(collective_id):
    return pltpu.CompilerParams(
        collective_id=collective_id, has_side_effects=True, vmem_limit_bytes=VMEM_BYTES
    )


def add_into(target, *others):
    total = target[...].astype(jnp.float32)
    for other in others:
        total += other[...].astype(jnp.float32)
    target[...] = total.astype(target.dtype)


class Reduce:
    CUTS = ((0, 64), (64, 48))
    LAST = (112, 16)

    @staticmethod
    def scratch(width):
        inbox = pltpu.VMEM((LINE, 112, width), jnp.bfloat16)
        last = pltpu.VMEM((LINE, 2, 16, width), jnp.bfloat16)
        sems = [pltpu.SemaphoreType.DMA((LINE, 2))] * 10 + [pltpu.SemaphoreType.DMA((2,))]
        return [inbox] * 3 + [last] * 2 + [pltpu.VMEM((16, width), jnp.bfloat16)] + sems

    COUNT = 17

    def __init__(self, parts, refs):
        self.parts = parts
        self.y_in, self.up_in, self.dn_in, self.up_last, self.dn_last, self.y_last = refs[:6]
        (
            self.y_s, self.y_r, self.up_s, self.up_r, self.dn_s, self.dn_r,
            self.ul_s, self.ul_r, self.dl_s, self.dl_r, self.yl_sr,
        ) = refs[6:]
        self.z, self.y, self.c, self.h = place()
        z = self.z
        self.order = (3 - 3 * (z // 2), (2 + 3 * z) % 5, 1 + z % 2, z)

    def rows(self, cut):
        return pl.ds(*self.CUTS[cut])

    def across(self, line, cut):
        return remote(
            self.parts.at[line * 2 + 1 - self.y, self.rows(cut)], self.y_in.at[line, self.rows(cut)],
            self.y_s.at[line, cut], self.y_r.at[line, cut], device(self.z, 1 - self.y, self.c, self.h),
        )

    def up(self, line, cut):
        return remote(
            self.parts.at[line * 2 + self.y, self.rows(cut)], self.up_in.at[line, self.rows(cut)],
            self.up_s.at[line, cut], self.up_r.at[line, cut], device(self.z + 1, self.y, self.c, self.h),
        )

    def down(self, line, cut):
        return remote(
            self.parts.at[line * 2 + self.y, self.rows(cut)], self.dn_in.at[line, self.rows(cut)],
            self.dn_s.at[line, cut], self.dn_r.at[line, cut], device(self.z - 1, self.y, self.c, self.h),
        )

    def last(self, line, column):
        return self.parts.at[line * 2 + column, pl.ds(*self.LAST)]

    def last_up(self, line, column):
        return remote(
            self.last(line, column), self.up_last.at[line, column], self.ul_s.at[line, column],
            self.ul_r.at[line, column], device(self.z + 1, self.y, self.c, self.h),
        )

    def last_down(self, line, column):
        return remote(
            self.last(line, column), self.dn_last.at[line, column], self.dl_s.at[line, column],
            self.dl_r.at[line, column], device(self.z - 1, self.y, self.c, self.h),
        )

    def last_across(self):
        return remote(
            self.last(self.z, 1 - self.y), self.y_last, self.yl_sr.at[0], self.yl_sr.at[1],
            device(self.z, 1 - self.y, self.c, self.h),
        )

    def start(self, place_at):
        line = self.order[place_at]
        for cut in range(2):
            self.across(line, cut).start()

        @pl.when(jnp.logical_and(line > self.z, self.z == 0))
        def _():
            for column in range(2):
                self.last_up(line, column).start()

        @pl.when(jnp.logical_and(line < self.z, self.z == LINE - 1))
        def _():
            for column in range(2):
                self.last_down(line, column).start()

    def relay_last(self, line):
        @pl.when(jnp.logical_and(line > self.z, self.z > 0))
        def _():
            for column in range(2):
                self.last_up(line, column).wait_recv()
                add_into(self.last(line, column), self.up_last.at[line, column])
                self.last_up(line, column).start()

        @pl.when(jnp.logical_and(line < self.z, self.z < LINE - 1))
        def _():
            for column in range(2):
                self.last_down(line, column).wait_recv()
                add_into(self.last(line, column), self.dn_last.at[line, column])
                self.last_down(line, column).start()

    def relay(self, place_at):
        line = self.order[place_at]
        for cut in range(2):
            rows = self.rows(cut)
            self.across(line, cut).wait_recv()
            target = self.parts.at[line * 2 + self.y, rows]

            @pl.when(line > self.z)
            def _():
                @pl.when(self.z > 0)
                def _():
                    self.up(line, cut).wait_recv()
                    add_into(target, self.y_in.at[line, rows], self.up_in.at[line, rows])

                @pl.when(self.z == 0)
                def _():
                    add_into(target, self.y_in.at[line, rows])

                self.up(line, cut).start()

            @pl.when(line < self.z)
            def _():
                @pl.when(self.z < LINE - 1)
                def _():
                    self.down(line, cut).wait_recv()
                    add_into(target, self.y_in.at[line, rows], self.dn_in.at[line, rows])

                @pl.when(self.z == LINE - 1)
                def _():
                    add_into(target, self.y_in.at[line, rows])

                self.down(line, cut).start()

            if cut == 0:
                self.relay_last(line)

    def total(self, out):
        line = self.z
        last = pl.ds(*self.LAST)
        own, other = line * 2 + self.y, line * 2 + 1 - self.y

        @pl.when(self.z > 0)
        def _():
            for column in range(2):
                self.last_up(line, column).wait_recv()
                add_into(self.last(line, column), self.up_last.at[line, column])

        @pl.when(self.z < LINE - 1)
        def _():
            for column in range(2):
                self.last_down(line, column).wait_recv()
                add_into(self.last(line, column), self.dn_last.at[line, column])

        self.last_across().start()
        for cut in range(2):
            rows = self.rows(cut)
            self.across(line, cut).wait_recv()
            out[rows] = self.parts[own, rows].astype(jnp.float32) + self.y_in[line, rows].astype(jnp.float32)
        for cut in range(2):
            rows = self.rows(cut)

            @pl.when(self.z > 0)
            def _():
                self.up(line, cut).wait_recv()
                out[rows] += self.up_in[line, rows].astype(jnp.float32)

            @pl.when(self.z < LINE - 1)
            def _():
                self.down(line, cut).wait_recv()
                out[rows] += self.dn_in[line, rows].astype(jnp.float32)

        self.last_across().wait_recv()
        out[last] = self.parts[own, last].astype(jnp.float32) + self.y_last[...].astype(jnp.float32)

    def finish(self):
        for line in range(LINE):
            for cut in range(2):
                self.across(line, cut).wait_send()

                @pl.when(self.z < line)
                def _():
                    self.up(line, cut).wait_send()
                    self.last_up(line, cut).wait_send()

                @pl.when(self.z > line)
                def _():
                    self.down(line, cut).wait_send()
                    self.last_down(line, cut).wait_send()

        self.last_across().wait_send()


def dma(*shape):
    return pltpu.SemaphoreType.DMA(shape) if shape else pltpu.SemaphoreType.DMA


def local(src, dst, sem):
    return pltpu.make_async_copy(src, dst, sem)


class AttnSpread:
    @staticmethod
    def scratch(depth):
        return [pltpu.VMEM((LINE, depth, 3 * HD), jnp.bfloat16)] + [
            dma(3, 4), dma(3, 4), dma(3), dma(4), dma(4), dma(4), dma(4), dma(4), dma(4), dma(4), dma(4), dma(4), dma(4),
        ]

    COUNT = 14

    def __init__(self, weights, outs, refs):
        self.weights, (self.qkv, self.out_w) = weights, outs
        (
            self.stage, self.s, self.r, self.own, self.x_s, self.x_r, self.a_s, self.a_r, self.b_s, self.b_r,
            self.c_s, self.c_r, self.o_s, self.o_r,
        ) = refs
        self.z, self.y, self.c, self.h = place()
        self.me = device(self.z, self.y, self.c, self.h)
        self.owner = self.h == self.y

    def source(self, kind, line):
        start = line * HD if kind == 0 else (line // 2) * HD
        return self.weights[kind].at[:, pl.ds(pl.multiple_of(start, HD), HD)]

    def slot(self, kind, line, owner):
        columns = pl.ds(kind * HD, HD)
        if owner:
            return self.qkv.at[line * 2 + self.y, self.c, :, columns]
        return self.stage.at[line, :, columns]

    def push(self, kind, step, owner):
        line = (self.z + step) % LINE
        return remote(
            self.source(kind, line), self.slot(kind, self.z, owner), self.s.at[kind, step], self.r.at[kind, self.z],
            device(line, self.y, self.c, self.h),
        )

    def pull(self, kind, line, owner):
        ref = self.slot(kind, line, owner)
        return remote(ref, ref, self.s.at[kind, 0], self.r.at[kind, line], self.me)

    def keep(self, kind, owner):
        return local(self.source(kind, self.z), self.slot(kind, self.z, owner), self.own.at[kind])

    def over(self, line):
        ref = self.qkv.at[line * 2 + self.y, self.c]
        return remote(ref, ref, self.x_s.at[line], self.x_r.at[line], device(self.z, self.y, self.c, 1 - self.h))

    def over_in(self, line):
        ref = self.qkv.at[line * 2 + self.y, self.c]
        return remote(ref, ref, self.x_s.at[line], self.x_r.at[line], self.me)

    def across(self, line):
        return remote(
            self.stage.at[line], self.qkv.at[line * 2 + self.y, self.c], self.a_s.at[line], self.a_r.at[line],
            device(self.z, 1 - self.y, self.c, self.h),
        )

    def across_far(self, line):
        return remote(
            self.stage.at[line], self.qkv.at[line * 2 + self.y, self.c], self.b_s.at[line], self.b_r.at[line],
            device(self.z, 1 - self.y, self.c, 1 - self.h),
        )

    def far_in(self, line, owner):
        ref = self.qkv.at[line * 2 + 1 - self.y, self.c]
        s, r = (self.a_s, self.a_r) if owner else (self.b_s, self.b_r)
        return remote(ref, ref, s.at[line], r.at[line], self.me)

    def share(self, line, core):
        ref = self.qkv.at[pl.ds(line * 2, 2), core]
        return remote(ref, ref, self.c_s.at[line], self.c_r.at[line], device(self.z, self.y, 1 - self.c, self.h))

    def out_push(self):
        return remote(
            self.weights[3], self.out_w.at[self.y, self.c], self.o_s.at[0], self.o_r.at[0],
            device(self.z, 1 - self.y, self.c, self.h),
        )

    def out_keep(self):
        return local(self.weights[3], self.out_w.at[self.y, self.c], self.o_s.at[1])

    def out_pull(self):
        ref = self.out_w.at[1 - self.y, self.c]
        return remote(ref, ref, self.o_s.at[0], self.o_r.at[0], self.me)

    def out_over(self):
        ref = self.out_w.at[:, self.c]
        return remote(ref, ref, self.o_s.at[2], self.o_r.at[2], device(self.z, self.y, self.c, 1 - self.h))

    def out_share(self, core):
        ref = self.out_w.at[:, core]
        return remote(ref, ref, self.o_s.at[3], self.o_r.at[3], device(self.z, self.y, 1 - self.c, self.h))

    def each(self, act):
        @pl.when(self.owner)
        def _():
            act(True)

        @pl.when(jnp.logical_not(self.owner))
        def _():
            act(False)

    def start(self):
        def act(owner):
            for kind in range(3):
                self.keep(kind, owner).start()
            for step in range(1, LINE):
                for kind in range(3):
                    self.push(kind, step, owner).start()
            if owner:
                self.out_keep().start()
            else:
                self.out_push().start()

        self.each(act)

    def relay(self, step):
        line = (self.z + LINE - step) % LINE

        def act(owner):
            for kind in range(3):
                if step:
                    self.pull(kind, line, owner).wait_recv()
                else:
                    self.keep(kind, owner).wait()
            if owner:
                self.over(line).start()
            else:
                self.across(line).start()
                self.across_far(line).start()

        self.each(act)

    def relay_out(self):
        @pl.when(self.owner)
        def _():
            self.out_keep().wait()
            self.out_pull().wait_recv()
            self.out_over().start()

    def relay_share(self, step):
        line = (self.z + LINE - step) % LINE

        def act(owner):
            if not owner:
                self.over_in(line).wait_recv()
            self.far_in(line, owner).wait_recv()

        self.each(act)
        self.share(line, self.c).start()

    def relay_out_share(self):
        @pl.when(jnp.logical_not(self.owner))
        def _():
            self.out_over().wait_recv()

        self.out_share(self.c).start()

    def finish(self):
        for line in range(LINE):
            self.share(line, 1 - self.c).wait_recv()
            self.share(line, self.c).wait_send()
        self.out_share(1 - self.c).wait_recv()
        self.out_share(self.c).wait_send()

        def act(owner):
            for kind in range(3):
                for step in range(1, LINE):
                    self.push(kind, step, owner).wait_send()
            for line in range(LINE):
                if owner:
                    self.over(line).wait_send()
                else:
                    self.across(line).wait_send()
                    self.across_far(line).wait_send()
            if owner:
                self.out_over().wait_send()
            else:
                self.out_push().wait_send()

        self.each(act)


class MlpSpread:
    @staticmethod
    def scratch():
        return [dma(2, 8), dma(2, 8), dma(2)]

    def __init__(self, weights, outs, sems):
        self.weights, self.outs = weights, outs
        self.s, self.r, self.own = sems
        self.z, self.y, self.c, self.h = place()
        self.chip = self.z * 2 + self.y
        self.part = weights[0].shape[1] // 8

    def columns(self, index):
        return pl.ds(pl.multiple_of(index * self.part, self.part), self.part)

    def push(self, kind, step):
        chip = (self.chip + step) % 8
        return remote(
            self.weights[kind].at[:, self.columns(chip)], self.outs[kind].at[self.chip], self.s.at[kind, step],
            self.r.at[kind, step], device(chip // 2, chip % 2, self.c, self.h),
        )

    def pull(self, kind, step):
        ref = self.outs[kind].at[(self.chip + 8 - step) % 8]
        return remote(ref, ref, self.s.at[kind, step], self.r.at[kind, step], device(self.z, self.y, self.c, self.h))

    def keep(self, kind):
        return local(self.weights[kind].at[:, self.columns(self.chip)], self.outs[kind].at[self.chip], self.own.at[kind])

    def start(self):
        for kind in range(2):
            self.keep(kind).start()
            for step in range(1, 8):
                self.push(kind, step).start()

    def finish(self):
        for kind in range(2):
            self.keep(kind).wait()
            for step in range(1, 8):
                self.pull(kind, step).wait_recv()
                self.push(kind, step).wait_send()


class MlpShare:
    @staticmethod
    def scratch():
        return [dma(2), dma(2, 2), dma(2, 2), dma(2, 2), dma(2, 2)]

    def __init__(self, quarters, outs, sems):
        self.quarters, self.outs = quarters, outs
        self.own, self.x_s, self.x_r, self.c_s, self.c_r = sems
        self.z, self.y, self.c, self.h = place()
        self.part = quarters[0].shape[2]

    def slot(self, kind, cut, half):
        columns = pl.ds(pl.multiple_of(half * self.part, self.part), self.part)
        return self.outs[kind].at[pl.ds(cut * 4, 4), self.c, :, columns]

    def keep(self, kind):
        columns = pl.ds(pl.multiple_of(self.h * self.part, self.part), self.part)
        return local(self.quarters[kind], self.outs[kind].at[:, self.c, :, columns], self.own.at[kind])

    def over(self, kind, cut, half):
        return remote(
            self.quarters[kind].at[pl.ds(cut * 4, 4)], self.slot(kind, cut, half), self.x_s.at[kind, cut],
            self.x_r.at[kind, cut], device(self.z, self.y, self.c, 1 - self.h),
        )

    def share(self, kind, cut, core):
        ref = self.outs[kind].at[pl.ds(cut * 4, 4), core]
        return remote(
            ref, ref, self.c_s.at[kind, cut], self.c_r.at[kind, cut], device(self.z, self.y, 1 - self.c, self.h)
        )

    def start(self):
        for kind in range(2):
            for cut in range(2):
                self.over(kind, cut, self.h).start()
            self.keep(kind).start()

    def relay(self):
        for kind in range(2):
            self.keep(kind).wait()
            for cut in range(2):
                self.over(kind, cut, 1 - self.h).wait_recv()
                self.share(kind, cut, self.c).start()

    def finish(self):
        for kind in range(2):
            for cut in range(2):
                self.share(kind, cut, 1 - self.c).wait_recv()
                self.share(kind, cut, self.c).wait_send()
                self.over(kind, cut, self.h).wait_send()


class DownSpread:
    @staticmethod
    def scratch():
        return [dma(1), dma(2), dma(2)]

    def __init__(self, weight, out, sems):
        self.weight, self.out = weight, out
        self.d_own, self.d_x, self.d_sib = sems
        self.z, self.y, self.c, self.h = place()

    def keep(self):
        return local(self.weight, self.out.at[self.h, self.c], self.d_own.at[0])

    def over(self):
        return remote(
            self.weight, self.out.at[self.h, self.c], self.d_x.at[0], self.d_x.at[1],
            device(self.z, self.y, self.c, 1 - self.h),
        )

    def over_in(self):
        ref = self.out.at[1 - self.h, self.c]
        return remote(ref, ref, self.d_x.at[0], self.d_x.at[1], device(self.z, self.y, self.c, self.h))

    def share(self):
        ref = self.out.at[:, self.c]
        return remote(ref, ref, self.d_sib.at[0], self.d_sib.at[1], device(self.z, self.y, 1 - self.c, self.h))

    def share_in(self):
        ref = self.out.at[:, 1 - self.c]
        return remote(ref, ref, self.d_sib.at[0], self.d_sib.at[1], device(self.z, self.y, self.c, self.h))

    def start(self):
        self.keep().start()
        self.over().start()

    def relay(self):
        self.keep().wait()
        self.over_in().wait_recv()
        self.share().start()

    def finish(self):
        self.share_in().wait_recv()
        self.share().wait_send()
        self.over().wait_send()


class NoteSpread:
    @staticmethod
    def scratch():
        return [dma(16), dma(16), dma(1)]

    def __init__(self, note, out, sems):
        self.note, self.out = note, out
        self.s, self.r, self.own = sems
        self.blk, self.h = lax.axis_index("blk"), lax.axis_index("head")

    def push(self, step):
        other = (self.blk + step) % 16
        return remote(self.note, self.out.at[self.blk], self.s.at[step], self.r.at[step], (other, self.h))

    def pull(self, step):
        ref = self.out.at[(self.blk + 16 - step) % 16]
        return remote(ref, ref, self.s.at[step], self.r.at[step], (self.blk, self.h))

    def keep(self):
        return local(self.note, self.out.at[self.blk], self.own.at[0])

    def start(self):
        self.keep().start()
        for step in range(1, 16):
            self.push(step).start()

    def finish(self):
        self.keep().wait()
        for step in range(1, 16):
            self.pull(step).wait_recv()
            self.push(step).wait_send()


def split_refs(refs, counts):
    groups, at = [], 0
    for count in counts:
        groups.append(refs[at : at + count])
        at += count
    return groups


def core_kernel(
    attended, out_w, gate_in, up_in, wd, tokens, gain, cot, cot_in,
    hidden_out, active, mlp_part, gathered, grad_hidden, gain_term, gate, up,
    normed, src, total, gate_w, up_w, down_w, gate_factor, up_factor, cot_pairs, parts, stage, gate_grad, up_grad, branch,
    cot_s, stage_s, *refs,
):
    gather_sems, back_sems, share_sems, down_sems, reduce_refs, quarter_refs = split_refs(
        refs, (8, 8, 5, 3, Reduce.COUNT, 8)
    )
    z, y, c, h = place()
    greet(device(z, y, 1 - c, h))
    greet(device(z, y, c, 1 - h))
    greet_plane(2)
    gather = Gather(src, normed, gather_sems)
    back = Gather(branch, gathered, back_sems)
    share = MlpShare((gate_in, up_in), (gate_w, up_w), share_sems)
    downs = DownSpread(wd, down_w, down_sems)
    reduce = Reduce(parts, reduce_refs)
    grads = QuarterReduce((gate_w, up_w), (gate, up), quarter_refs)
    rows, width = normed.shape[1:]
    hidden = gate_w.shape[3]
    step = hidden // 4
    pair = 2 * rows
    order = (2, 0, 1, 3)

    def cot_load(place_at):
        return local(cot_in.at[pl.ds(reduce.order[place_at] * 2, 2)], cot_pairs.at[place_at % 2], cot_s.at[place_at % 2])

    cot_load(0).start()
    cot_load(1).start()

    share.start()
    for place_at in range(4):
        line = reduce.order[place_at]
        both = attended[pl.ds(pl.multiple_of(line * pair, pair), pair)]
        parts[pl.ds(line * 2, 2)] = product(both, out_w[...]).astype(jnp.bfloat16).reshape(2, rows, width)
        reduce.start(place_at)
    for place_at in range(3):
        reduce.relay(place_at)
    reduce.total(total)
    hidden_rows = tokens[...].astype(jnp.float32) + total[...]
    hidden_out[...] = hidden_rows
    src[...] = (hidden_rows * rms_scale(hidden_rows) * gain[...]).astype(jnp.bfloat16)
    gather.start()
    share.relay()
    downs.start()
    reduce.finish()

    def forward(chip, own=False):
        shard = src if own else normed.at[chip]

        @pl.loop(0, 4)
        def _(tile):
            columns = pl.ds(pl.multiple_of(tile * step, step), step)
            gate_part = product(shard[...], gate_w[:, :, :, columns].reshape(width, step))
            up_part = product(shard[...], up_w[:, :, :, columns].reshape(width, step))
            sigmoid = jax.nn.sigmoid(gate_part)
            silu = gate_part * sigmoid
            slope = sigmoid * (1.0 + gate_part * (1.0 - sigmoid))
            gate_factor[chip, :, columns] = (up_part * slope).astype(jnp.bfloat16)
            up_factor[chip, :, columns] = silu.astype(jnp.bfloat16)
            active[chip, :, columns] = (silu * up_part).astype(jnp.bfloat16)

    def forward_own(distance):
        @pl.when(z - distance >= 0)
        def _():
            forward((z - distance) * 2 + y)

        @pl.when(z + distance <= LINE - 1)
        def _():
            forward((z + distance) * 2 + y)

    def forward_other(distance):
        def one(line):
            for elem in (0, 1):
                gather.across_in(line, elem).wait_recv()
            forward(line * 2 + 1 - y)

        if distance == 0:
            one(z)
        else:

            @pl.when(z - distance >= 0)
            def _():
                one(z - distance)

            @pl.when(z + distance <= LINE - 1)
            def _():
                one(z + distance)

    def relay(distance):
        for elem in order:
            gather.relay(distance - 1, elem)

    gather.relay_b()
    share.finish()
    forward(z * 2 + y, own=True)
    relay(1)
    forward_other(0)
    forward_own(1)
    relay(2)
    forward_other(1)
    forward_own(2)
    relay(3)
    downs.relay()
    forward_other(2)
    forward_own(3)
    forward_other(3)
    gather.own_copy().wait()
    downs.finish()

    def backward(place_at):
        line = reduce.order[place_at]
        both = pl.ds(line * 2, 2)
        cot_load(place_at).wait()

        @pl.loop(0, 4)
        def _(tile):
            columns = pl.ds(pl.multiple_of(tile * step, step), step)
            grad_active = times_transposed(
                cot_pairs[place_at % 2].reshape(pair, width), down_w[tile // 2, tile % 2]
            ).reshape(2, rows, step)
            gate_grad[both, :, columns] = (grad_active * gate_factor[both, :, columns].astype(jnp.float32)).astype(jnp.bfloat16)
            up_grad[both, :, columns] = (grad_active * up_factor[both, :, columns].astype(jnp.float32)).astype(jnp.bfloat16)

        if place_at < 2:
            cot_load(place_at + 2).start()

        @pl.loop(0, 4)
        def _(tile):
            columns = pl.ds(pl.multiple_of(tile * (width // 4), width // 4), width // 4)
            chips = pl.ds(tile * 2, 2)
            part = times_transposed(gate_grad[both].reshape(pair, hidden), gate_w[chips].reshape(width // 4, hidden))
            part += times_transposed(up_grad[both].reshape(pair, hidden), up_w[chips].reshape(width // 4, hidden))
            parts[both, :, columns] = part.astype(jnp.bfloat16).reshape(2, rows, width // 4)

    def stage_store(line):
        return local(stage, mlp_part.at[pl.ds(line * 2, 2)], stage_s)

    def contribute(line):
        if line:
            stage_store(line - 1).wait()

        @pl.loop(0, 4)
        def _(tile):
            columns = pl.ds(pl.multiple_of(tile * (width // 4), width // 4), width // 4)
            part = product(
                active[pl.ds(line * 2, 2)].reshape(pair, hidden), down_w[:, :, :, columns].reshape(hidden, width // 4)
            )
            stage[:, :, columns] = part.astype(jnp.bfloat16).reshape(2, rows, width // 4)

        stage_store(line).start()

    def weight_grad(kind, first, last):
        source = (gate_grad, up_grad)[kind]
        store = (gate_w, up_w)[kind]

        @pl.loop(first, last)
        def _(tile):
            columns = pl.ds(pl.multiple_of(tile * pair, pair), pair)
            part = transposed_times(
                normed[:, :, columns].reshape(8 * rows, pair), source[...].reshape(8 * rows, hidden)
            )
            store[tile] = part.astype(jnp.bfloat16).reshape(2, rows, hidden)

    at_end = jnp.logical_or(z == 0, z == LINE - 1)
    inside = jnp.logical_not(at_end)
    for place_at in range(3):
        backward(place_at)
        reduce.start(place_at)

    @pl.when(at_end)
    def _():
        reduce.relay(0)

    backward(3)
    reduce.start(3)

    @pl.when(at_end)
    def _():
        reduce.relay(1)

    @pl.when(inside)
    def _():
        reduce.relay(0)

    weight_grad(0, 0, 4)
    grads.share(0, 0).start()

    @pl.when(inside)
    def _():
        reduce.relay(1)

    reduce.relay(2)
    weight_grad(0, 4, 8)
    grads.share(0, 1).start()
    reduce.total(total)

    inputs = hidden_out[...]
    inv_scale = rms_scale(inputs)
    unit_rows = inputs * inv_scale
    grad_unit = total[...] * gain[...]
    mean = jnp.mean(grad_unit * unit_rows, axis=-1, keepdims=True)
    grad_rows = cot[...].astype(jnp.float32) + inv_scale * (grad_unit - unit_rows * mean)
    grad_hidden[...] = grad_rows
    branch[...] = grad_rows.astype(jnp.bfloat16)
    back.start()
    gain_term[...] = jnp.sum(total[...] * unit_rows, axis=0, keepdims=True)
    grads.relay(0)
    back.relay_b()
    for cut in range(2):
        weight_grad(1, cut * 4, cut * 4 + 4)
        grads.share(1, cut).start()
    for elem in order:
        back.relay(0, elem)
    grads.relay(1)
    contribute(0)
    contribute(1)
    for elem in order:
        back.relay(1, elem)
    contribute(2)
    contribute(3)
    grads.finish(0)
    for elem in order:
        back.relay(2, elem)
    grads.finish(1)
    back.finish()
    reduce.finish()
    stage_store(3).wait()
    for line in range(LINE):
        for elem in (0, 1):
            gather.across(line, elem).wait_send()
    gather.finish_sends()


def core(attended, out_w, gate, up, wd, tokens, gain, cot, cot_all):
    eight, depth, part = gate.shape
    rows, width = tokens.shape
    hidden = 2 * part

    def room(*dims, dtype=jnp.bfloat16):
        return pltpu.VMEM(dims, dtype)

    def shape(*dims, dtype=jnp.bfloat16):
        return jax.ShapeDtypeStruct(dims, dtype)

    f32 = jnp.float32
    return pl.pallas_call(
        core_kernel,
        out_shape=(
            shape(rows, width, dtype=f32),
            shape(8, rows, hidden),
            shape(8, rows, width),
            shape(8, rows, width),
            shape(rows, width, dtype=f32),
            shape(1, width, dtype=f32),
            shape(8, depth, part),
            shape(8, depth, part),
        ),
        in_specs=[INSIDE, INSIDE, ANY, ANY, ANY, INSIDE, INSIDE, INSIDE, ANY],
        out_specs=(INSIDE, INSIDE, ANY, ANY, INSIDE, INSIDE, INSIDE, INSIDE),
        scratch_shapes=[
            room(8, rows, width), room(rows, width), room(rows, width, dtype=f32),
            room(eight, 2, depth, hidden), room(eight, 2, depth, hidden), room(2, 2, *wd.shape),
            room(8, rows, hidden), room(8, rows, hidden),
            room(2, 2, rows, width), room(8, rows, width), room(2, rows, width),
            room(8, rows, hidden), room(8, rows, hidden), room(rows, width),
            dma(2), dma(),
        ]
        + Gather.scratch()
        + Gather.scratch()
        + MlpShare.scratch()
        + DownSpread.scratch()
        + Reduce.scratch(width)
        + QuarterReduce.scratch(depth, hidden),
        compiler_params=kernel_params(8),
        name="core",
    )(attended, out_w, gate, up, wd, tokens, gain, cot, cot_all)


def column_of(row):
    size = row.shape[1]
    same = lax.broadcasted_iota(jnp.int32, (size, size), 0) == lax.broadcasted_iota(jnp.int32, (size, size), 1)
    return jnp.sum(jnp.where(same, row, 0.0), axis=1, keepdims=True)


def row_of(column):
    size = column.shape[0]
    same = lax.broadcasted_iota(jnp.int32, (size, size), 0) == lax.broadcasted_iota(jnp.int32, (size, size), 1)
    return jnp.sum(jnp.where(same, column, 0.0), axis=0, keepdims=True)


def front_kernel(
    tokens, cot, note, inv_freqs, wq, wk, wv, wo, wg, wu,
    kv_out, normed_out, qkv_out, out_w, notes, gain, mlp_gain, cos_table, sine_table, query, attended_out, attended_low_out,
    log_out, cot_out, gate, up,
    gathered, normed, qkv_w, query_ids, key_ids, kv, keys, scores, total,
    own, x_s, x_r, c_s, c_r, store_s, *sems,
):
    z, y, c, h = place()
    tok_sems, note_sems, attn_sems, cot_sems, mlp_sems = split_refs(sems, (8, 3, AttnSpread.COUNT, 8, 3))
    greet_all(16, 2)
    rows, width = tokens.shape[0], HD
    pair = 2 * rows
    tok = Gather(tokens, gathered, tok_sems)
    notices = NoteSpread(note, notes, note_sems)
    attn = AttnSpread((wq, wk, wv, wo), (qkv_w, out_w), attn_sems)
    cots = Gather(cot, cot_out, cot_sems)
    mlp = MlpSpread((wg, wu), (gate, up), mlp_sems)

    def keep(cut):
        part = pl.ds(cut * 2, 2)
        return local(kv.at[part], keys.at[part, c, h], own.at[cut])

    def over(cut, half):
        part = pl.ds(cut * 2, 2)
        return remote(kv.at[part], keys.at[part, c, half], x_s.at[cut], x_r.at[cut], device(z, y, c, 1 - h))

    def share(cut, core):
        ref = keys.at[pl.ds(cut * 2, 2), core]
        return remote(ref, ref, c_s.at[cut], c_r.at[cut], device(z, y, 1 - c, h))

    def tables():
        for blk in range(16):
            gain[:, pl.ds(blk * rows, rows)] = notes[blk, 4:5, :]
            mlp_gain[:, pl.ds(blk * rows, rows)] = notes[blk, 5:6, :]
        for chip in range(8):
            part = pl.ds(chip * rows, rows)
            mine = notes[2 * chip + c]
            angles = column_of(jnp.where(h == 0, mine[0:1], mine[1:2])) * inv_freqs[...]
            cos_table[part] = jnp.cos(angles)
            sine_table[part] = jnp.sin(angles)
            query_ids[part] = column_of(jnp.where(h == 0, mine[2:3], mine[3:4]))
            for piece in range(4):
                key_ids[chip, :, pl.ds(piece * rows, rows)] = notes[2 * chip + piece // 2, 2 + piece % 2 : 3 + piece % 2, :]

    def project(cut):
        part = pl.ds(cut * pair, pair)
        inputs = gathered[pl.ds(cut * 2, 2)].reshape(pair, tokens.shape[1]).astype(jnp.float32)
        rows_normed = (inputs * rms_scale(inputs) * gain[...]).astype(jnp.bfloat16)
        normed[part] = rows_normed
        cos_rows, sine_rows = cos_table[part], sine_table[part]

        def turn(lower, upper):
            return (
                (lower * cos_rows - upper * sine_rows).astype(jnp.bfloat16),
                (upper * cos_rows + lower * sine_rows).astype(jnp.bfloat16),
            )

        def weight(columns):
            return qkv_w[:, :, :, columns].reshape(tokens.shape[1], columns.size)

        half = width // 2
        projected = product(rows_normed, weight(pl.ds(0, width)))
        lower, upper = turn(projected[:, :half], projected[:, half:])
        query[part, :half] = (lower.astype(jnp.float32) * HD**-0.5).astype(jnp.bfloat16)
        query[part, half:] = (upper.astype(jnp.float32) * HD**-0.5).astype(jnp.bfloat16)
        projected = product(rows_normed, weight(pl.ds(width, 2 * width)))
        lower, upper = turn(projected[:, :half], projected[:, half:width])
        both = pl.ds(cut * 2, 2)
        kv[both, :, :half] = lower.reshape(2, rows, half)
        kv[both, :, half:width] = upper.reshape(2, rows, half)
        kv[both, :, width:] = projected[:, width:].astype(jnp.bfloat16).reshape(2, rows, width)
        over(cut, h).start()
        keep(cut).start()

    def pass_on(cut):
        keep(cut).wait()
        over(cut, 1 - h).wait_recv()
        share(cut, c).start()

    def attend(place_at):
        part = pl.ds(place_at * pair, pair)
        count = min(2 * place_at + 3, 8)
        ids = query_ids[part]

        def maxima(block, best):
            key = keys[block, :, :, :, :width].reshape(4 * rows, width)
            part_scores = times_transposed(query[part], key)
            part_scores = jnp.where(key_ids[block] <= ids, part_scores, -1e30)
            scores[block] = part_scores
            for lane in range(4 * rows // 128):
                best = jnp.maximum(best, part_scores[:, lane * 128 : lane * 128 + 128])
            return best

        best = lax.fori_loop(0, count, maxima, jnp.full((pair, 128), -1e30, jnp.float32))
        row_max = jnp.max(best, axis=1, keepdims=True)
        total[...] = jnp.zeros_like(total)

        def mix(block, sums):
            weights = jnp.exp(scores[block] - row_max)
            value = keys[block, :, :, :, width:].reshape(4 * rows, width)
            total[...] += product(weights.astype(jnp.bfloat16), value)
            for lane in range(4 * rows // 128):
                sums = sums + weights[:, lane * 128 : lane * 128 + 128]
            return sums

        sums = lax.fori_loop(0, count, mix, jnp.zeros((pair, 128), jnp.float32))
        row_sum = jnp.sum(sums, axis=1, keepdims=True)
        mixed = total[...] / row_sum
        attended_out[part] = mixed
        attended_low_out[part] = mixed.astype(jnp.bfloat16)
        log_out[place_at] = row_of(row_max + jnp.log(row_sum))

    order = (2, 0, 1, 3)
    attn.start()
    tok.start()
    notices.start()
    tok.relay_b()
    attn.relay(0)
    for elem in order:
        tok.relay(0, elem)
    attn.relay(1)
    attn.relay(2)
    for elem in order:
        tok.relay(1, elem)
    attn.relay(3)
    attn.relay_out()
    notices.finish()
    tables()
    for elem in order:
        tok.relay(2, elem)
    cots.start()
    mlp.start()
    for step in range(LINE):
        attn.relay_share(step)
    attn.relay_out_share()
    tok.finish()
    attn.finish()
    store_qkv = local(qkv_w, qkv_out, store_s.at[0])
    store_qkv.start()
    for cut in range(LINE):
        project(cut)
    store_normed = local(normed, normed_out, store_s.at[1])
    store_normed.start()
    cots.relay_b()
    for elem in order:
        cots.relay(0, elem)
    pass_on(0)
    pass_on(1)
    share(0, 1 - c).wait_recv()
    share(1, 1 - c).wait_recv()
    attend(0)
    for elem in order:
        cots.relay(1, elem)
    pass_on(2)
    share(2, 1 - c).wait_recv()
    attend(1)
    pass_on(3)
    share(3, 1 - c).wait_recv()
    store = local(keys, kv_out, store_s.at[2])
    store.start()
    attend(2)
    for elem in order:
        cots.relay(2, elem)
    attend(3)
    cots.finish()
    mlp.finish()
    for cut in range(LINE):
        share(cut, c).wait_send()
        over(cut, h).wait_send()
    store.wait()
    store_normed.wait()
    store_qkv.wait()


def front(tokens, cot, note, inv_freqs, wq, wk, wv, wo, wg, wu):
    rows, width = tokens.shape
    depth, part = wg.shape[0], wg.shape[1] // 8
    token_rows = 8 * rows

    def room(*dims, dtype=jnp.bfloat16):
        return pltpu.VMEM(dims, dtype)

    def shape(*dims, dtype=jnp.bfloat16):
        return jax.ShapeDtypeStruct(dims, dtype)

    f32 = jnp.float32
    return pl.pallas_call(
        front_kernel,
        out_shape=(
            shape(8, 2, 2, rows, 2 * HD),
            shape(token_rows, width),
            shape(8, 2, depth, 3 * HD),
            shape(2, 2, wo.shape[0], width),
            shape(16, *note.shape, dtype=f32),
            shape(1, width, dtype=f32),
            shape(1, width, dtype=f32),
            shape(token_rows, HD // 2, dtype=f32),
            shape(token_rows, HD // 2, dtype=f32),
            shape(token_rows, HD),
            shape(token_rows, HD, dtype=f32),
            shape(token_rows, HD),
            shape(LINE, 1, token_rows // LINE, dtype=f32),
            shape(8, *cot.shape),
            shape(8, depth, part),
            shape(8, depth, part),
        ),
        in_specs=[INSIDE] * 10,
        out_specs=(ANY, ANY, ANY, ANY) + (INSIDE,) * 9 + (ANY, ANY, ANY),
        scratch_shapes=[
            room(8, rows, width),
            room(token_rows, width),
            room(8, 2, depth, 3 * HD),
            room(token_rows, 1, dtype=f32),
            room(8, 1, 4 * rows, dtype=f32),
            room(8, rows, 2 * HD),
            room(8, 2, 2, rows, 2 * HD),
            room(8, token_rows // LINE, 4 * rows, dtype=f32),
            room(token_rows // LINE, HD, dtype=f32),
        ]
        + [dma(4)] * 5
        + [dma(3)]
        + Gather.scratch()
        + NoteSpread.scratch()
        + AttnSpread.scratch(depth)
        + Gather.scratch()
        + MlpSpread.scratch(),
        compiler_params=kernel_params(3),
        name="front",
    )(tokens, cot, note, inv_freqs, wq, wk, wv, wo, wg, wu)


class QuarterReduce:
    @staticmethod
    def scratch(depth, wide):
        sib = pltpu.VMEM((8, depth, wide), jnp.bfloat16)
        over = pltpu.VMEM((8, depth, wide // 2), jnp.bfloat16)
        return [sib, sib, over, over] + [dma(2, 2)] * 4

    def __init__(self, store, outs, refs):
        self.store, self.outs = store, outs
        self.sib, self.box = refs[0:2], refs[2:4]
        self.c_s, self.c_r, self.x_s, self.x_r = refs[4:]
        self.z, self.y, self.c, self.h = place()
        self.part = self.box[0].shape[2]

    def columns(self, half):
        return pl.ds(pl.multiple_of(half * self.part, self.part), self.part)

    def share(self, kind, cut):
        chips = pl.ds(cut * 4, 4)
        return remote(
            self.store[kind].at[chips, 1 - self.c], self.sib[kind].at[chips], self.c_s.at[kind, cut],
            self.c_r.at[kind, cut], device(self.z, self.y, 1 - self.c, self.h),
        )

    def over(self, kind, cut):
        chips = pl.ds(cut * 4, 4)
        return remote(
            self.store[kind].at[chips, self.c, :, self.columns(1 - self.h)], self.box[kind].at[chips],
            self.x_s.at[kind, cut], self.x_r.at[kind, cut], device(self.z, self.y, self.c, 1 - self.h),
        )

    def relay(self, kind):
        columns = self.columns(1 - self.h)
        for cut in range(2):
            self.share(kind, cut).wait_recv()

            @pl.loop(cut * 4, cut * 4 + 4)
            def _(chip):
                add_into(self.store[kind].at[chip, self.c, :, columns], self.sib[kind].at[chip, :, columns])

            self.over(kind, cut).start()

    def finish(self, kind):
        columns = self.columns(self.h)
        for cut in range(2):
            self.over(kind, cut).wait_recv()

            @pl.loop(cut * 4, cut * 4 + 4)
            def _(chip):
                total = self.store[kind][chip, self.c, :, columns].astype(jnp.float32)
                total += self.sib[kind][chip, :, columns].astype(jnp.float32)
                total += self.box[kind][chip].astype(jnp.float32)
                self.outs[kind][chip] = total.astype(jnp.bfloat16)

        for cut in range(2):
            self.share(kind, cut).wait_send()
            self.over(kind, cut).wait_send()


class QuarterScatter:
    @staticmethod
    def scratch():
        return [dma(2, 8), dma(2, 8), dma(2)]

    def __init__(self, quarters, outs, sems):
        self.quarters, self.outs = quarters, outs
        self.s, self.r, self.own = sems
        self.z, self.y, self.c, self.h = place()
        self.chip = self.z * 2 + self.y
        self.part = quarters[0].shape[2]

    def columns(self, chip):
        return pl.ds(pl.multiple_of(chip * self.part, self.part), self.part)

    def push(self, kind, step):
        target = (self.chip + step) % 8
        return remote(
            self.quarters[kind].at[target], self.outs[kind].at[:, self.columns(self.chip)], self.s.at[kind, step],
            self.r.at[kind, step], device(target // 2, target % 2, self.c, self.h),
        )

    def pull(self, kind, step):
        ref = self.outs[kind].at[:, self.columns((self.chip + 8 - step) % 8)]
        return remote(ref, ref, self.s.at[kind, step], self.r.at[kind, step], device(self.z, self.y, self.c, self.h))

    def keep(self, kind):
        return local(self.quarters[kind].at[self.chip], self.outs[kind].at[:, self.columns(self.chip)], self.own.at[kind])

    def start(self):
        for kind in range(2):
            self.keep(kind).start()
            for step in range(1, 8):
                self.push(kind, step).start()

    def finish(self):
        for kind in range(2):
            self.keep(kind).wait()
            for step in range(1, 8):
                self.pull(kind, step).wait_recv()
                self.push(kind, step).wait_send()


class DownReduce:
    @staticmethod
    def scratch(rows, width):
        return [
            pltpu.VMEM((2, 2, rows, width), jnp.bfloat16),
            pltpu.VMEM((2, rows, width), jnp.bfloat16),
            pltpu.VMEM((rows, width), jnp.bfloat16),
            dma(2), dma(2),
        ]

    def __init__(self, out, refs):
        self.out = out
        self.store, self.sib, self.box, self.c_sr, self.x_sr = refs
        self.z, self.y, self.c, self.h = place()

    def share(self):
        return remote(
            self.store.at[:, 1 - self.c], self.sib, self.c_sr.at[0], self.c_sr.at[1],
            device(self.z, self.y, 1 - self.c, self.h),
        )

    def over(self):
        return remote(
            self.store.at[1 - self.h, self.c], self.box, self.x_sr.at[0], self.x_sr.at[1],
            device(self.z, self.y, self.c, 1 - self.h),
        )

    def relay(self):
        self.share().wait_recv()
        add_into(self.store.at[1 - self.h, self.c], self.sib.at[1 - self.h])
        self.over().start()

    def finish(self):
        self.over().wait_recv()
        total = self.store[self.h, self.c].astype(jnp.float32) + self.sib[self.h].astype(jnp.float32)
        self.out[...] = total + self.box[...].astype(jnp.float32)
        self.share().wait_send()
        self.over().wait_send()


class OutGrad:
    @staticmethod
    def scratch(rows, width):
        def room(*dims):
            return pltpu.VMEM(dims, jnp.bfloat16)

        return [room(2, 2, rows, width), room(2, rows, width), room(2, rows, width), dma(2), dma(2), dma(2), dma(1)]

    def __init__(self, out, refs):
        self.out = out
        self.store, self.sib, self.box, self.c_sr, self.x_sr, self.y_sr, self.own = refs
        self.z, self.y, self.c, self.h = place()
        self.me = device(self.z, self.y, self.c, self.h)
        self.owner = self.h == self.y

    def share(self):
        return remote(
            self.store.at[:, 1 - self.c], self.sib, self.c_sr.at[0], self.c_sr.at[1],
            device(self.z, self.y, 1 - self.c, self.h),
        )

    def over(self):
        return remote(
            self.store.at[:, self.c], self.box, self.x_sr.at[0], self.x_sr.at[1],
            device(self.z, self.y, self.c, 1 - self.h),
        )

    def move(self):
        return remote(
            self.store.at[1 - self.y, self.c], self.out, self.y_sr.at[0], self.y_sr.at[1],
            device(self.z, 1 - self.y, self.c, self.h),
        )

    def keep(self):
        return local(self.store.at[self.y, self.c], self.out, self.own.at[0])

    def relay(self):
        self.share().wait_recv()
        for pair in range(2):
            add_into(self.store.at[pair, self.c], self.sib.at[pair])

        @pl.when(jnp.logical_not(self.owner))
        def _():
            self.over().start()

    def send(self):
        @pl.when(self.owner)
        def _():
            self.over().wait_recv()
            for pair in range(2):
                add_into(self.store.at[pair, self.c], self.box.at[pair])
            self.move().start()
            self.keep().start()

    def finish(self):
        self.share().wait_send()

        @pl.when(jnp.logical_not(self.owner))
        def _():
            remote(self.out, self.out, self.y_sr.at[0], self.y_sr.at[1], self.me).wait_recv()
            self.over().wait_send()

        @pl.when(self.owner)
        def _():
            self.keep().wait()
            self.move().wait_send()


def attend_back_kernel(
    query, keys_in, branch_in, mlp_part, hidden, out_w, attended, attended_low, log_row, notes, cos_table, sine_table,
    gate_in, up_in,
    side_out, grad_query, output, gate, up, out_grad,
    mlp_parts, mlp_total, keys, branch, grad_out, delta_row, query_row, key_column, grad_rot, parts, grad_key, grad_value, sib_in, x_in, z_in,
    load_s, c_s, c_r, x_s, x_r, z_s, z_r, *sems,
):
    z, y, c, h = place()
    mate = z + 1 - 2 * (z % 2)
    loads = [local(keys_in, keys, load_s.at[0]), local(branch_in, branch, load_s.at[1])]
    load_mlp = local(mlp_part, mlp_parts, load_s.at[2])
    load_mlp.start()
    for load in loads:
        load.start()
    greet_all(16, 2)
    scatter_sems, out_refs, reduce_refs = split_refs(sems, (3, 7, Reduce.COUNT))
    reduce = Reduce(mlp_parts, reduce_refs)
    load_mlp.wait()
    for place_at in range(4):
        reduce.start(place_at)
    scatter = QuarterScatter((gate_in, up_in), (gate, up), scatter_sems)
    outs = OutGrad(out_grad, out_refs)
    scatter.start()
    width = query.shape[1]
    rows = branch.shape[1]
    pair = 2 * rows
    block_rows = 4 * rows

    def share(block):
        return remote(
            parts.at[block, 1 - c], sib_in.at[block], c_s.at[block], c_r.at[block], device(z, y, 1 - c, h)
        )

    def over(block):
        return remote(
            parts.at[block, c, 1 - h], x_in.at[block], x_s.at[block], x_r.at[block], device(z, y, c, 1 - h)
        )

    def columns(kind):
        return pl.ds(pl.multiple_of(kind * width, width), width)

    def across(block):
        return remote(
            parts.at[block, c, h, :, columns(1 - z % 2)], z_in.at[block], z_s.at[block], z_r.at[block],
            device(mate, y, c, h),
        )

    def stage_two(block):
        share(block).wait_recv()
        add_into(parts.at[block, c, 1 - h], sib_in.at[block, 1 - h])
        over(block).start()

    def stage_three(block):
        over(block).wait_recv()
        add_into(parts.at[block, c, h], sib_in.at[block, h], x_in.at[block])
        across(block).start()

    def turn_back(values, part):
        half = width // 2
        lower, upper = values[:, :half], values[:, half:]
        cos_rows, sine_rows = cos_table[part], sine_table[part]
        return (
            (lower * cos_rows + upper * sine_rows).astype(jnp.bfloat16),
            (upper * cos_rows - lower * sine_rows).astype(jnp.bfloat16),
        )

    def stage_four(block):
        across(block).wait_recv()
        total = parts[block, c, h, :, columns(z % 2)].astype(jnp.float32) + z_in[block].astype(jnp.float32)
        part = pl.ds(block * rows, rows)

        @pl.when(z % 2 == 0)
        def _():
            lower, upper = turn_back(total, part)
            side_out[part, : width // 2] = lower
            side_out[part, width // 2 :] = upper

        @pl.when(z % 2 == 1)
        def _():
            side_out[part] = total.astype(jnp.bfloat16)

    for chip in range(8):
        mine = notes[2 * chip + c]
        query_row[chip // 2, :, pl.ds((chip % 2) * rows, rows)] = jnp.where(h == 0, mine[2:3], mine[3:4])
        for piece in range(4):
            row = notes[2 * chip + piece // 2, 2 + piece % 2 : 3 + piece % 2, :]
            key_column[chip, pl.ds(piece * rows, rows)] = column_of(row)
    for load in loads:
        load.wait()
    grad_rot[...] = jnp.zeros_like(grad_rot)
    for place_at in range(LINE):
        part = pl.ds(place_at * pair, pair)
        grad_rows = times_transposed(branch[pl.ds(place_at * 2, 2)].reshape(pair, branch.shape[2]), out_w[...])
        grad_rows = grad_rows.astype(jnp.bfloat16)
        grad_out[part] = grad_rows
        delta = jnp.sum(grad_rows.astype(jnp.float32) * attended[part], axis=1, keepdims=True)
        delta_row[place_at] = row_of(delta)
    out_store = out_refs[0]

    @pl.loop(0, 4)
    def _(tile):
        tile_columns = pl.ds(pl.multiple_of(tile * 512, 512), 512)
        part = transposed_times(attended_low[...], branch[:, :, tile_columns].reshape(8 * rows, 512))
        out_store[:, :, :, tile_columns] = part.astype(jnp.bfloat16).reshape(2, 2, out_store.shape[2], 512)

    outs.share().start()
    for block in range(8):
        key = keys[block, :, :, :, :width].reshape(block_rows, width)
        value = keys[block, :, :, :, width:].reshape(block_rows, width)
        grad_key[...] = jnp.zeros_like(grad_key)
        grad_value[...] = jnp.zeros_like(grad_value)

        @pl.loop(max(0, (block - 1) // 2), LINE)
        def _(place_at):
            part = pl.ds(pl.multiple_of(place_at * pair, pair), pair)
            part_scores = times_transposed(key, query[part])
            visible = key_column[block] <= query_row[place_at]
            weights = jnp.where(visible, jnp.exp(part_scores - log_row[place_at]), 0.0)
            grad_weights = times_transposed(value, grad_out[part])
            grad_scores = (weights * (grad_weights - delta_row[place_at])).astype(jnp.bfloat16)
            grad_key[...] += product(grad_scores, query[part])
            grad_value[...] += product(weights.astype(jnp.bfloat16), grad_out[part])
            grad_rot[part] += transposed_times(grad_scores, key)

        parts[block, :, :, :, :width] = grad_key[...].astype(jnp.bfloat16).reshape(2, 2, rows, width)
        parts[block, :, :, :, width:] = grad_value[...].astype(jnp.bfloat16).reshape(2, 2, rows, width)
        share(block).start()
        if block == 0:
            outs.relay()
        if block >= 1:
            stage_two(block - 1)
        if block >= 4:
            stage_three(block - 4)
    stage_two(7)
    outs.send()

    @pl.when(jnp.logical_or(z == 0, z == LINE - 1))
    def _():
        reduce.relay(0)

    for place_at in range(LINE):
        part = pl.ds(place_at * pair, pair)
        lower, upper = turn_back(grad_rot[part] * HD**-0.5, part)
        grad_query[part, : width // 2] = lower
        grad_query[part, width // 2 :] = upper
    for block in range(4, 8):
        stage_three(block)
        stage_four(block - 4)

    @pl.when(jnp.logical_and(z > 0, z < LINE - 1))
    def _():
        reduce.relay(0)

    for block in range(4, 8):
        stage_four(block)
    reduce.relay(1)
    reduce.relay(2)
    for block in range(8):
        share(block).wait_send()
        over(block).wait_send()
        across(block).wait_send()
    outs.finish()
    reduce.total(mlp_total)
    output[...] = (hidden[...] + mlp_total[...]).astype(jnp.bfloat16)
    scatter.finish()
    reduce.finish()


def attend_back(
    query, keys, branch, mlp_part, hidden, out_w, attended, attended_low, log_row, notes, cos_table, sine_table, gate, up,
    out_rows,
):
    eight, _, _, rows, width = keys.shape
    tokens = query.shape[0]
    depth, part = gate.shape[1:]

    def room(*dims, dtype=jnp.bfloat16):
        return pltpu.VMEM(dims, dtype)

    def shape(*dims, dtype=jnp.bfloat16):
        return jax.ShapeDtypeStruct(dims, dtype)

    f32 = jnp.float32
    return pl.pallas_call(
        attend_back_kernel,
        out_shape=(
            shape(tokens, HD),
            shape(tokens, HD),
            shape(*hidden.shape),
            shape(depth, 8 * part),
            shape(depth, 8 * part),
            shape(out_rows, out_w.shape[1]),
        ),
        in_specs=[INSIDE, ANY, ANY, ANY] + [INSIDE] * 10,
        out_specs=(INSIDE, INSIDE, INSIDE, ANY, ANY, ANY),
        scratch_shapes=[
            room(*mlp_part.shape), room(*hidden.shape, dtype=f32), room(*keys.shape), room(*branch.shape), room(tokens, HD),
            room(LINE, 1, tokens // LINE, dtype=f32), room(LINE, 1, tokens // LINE, dtype=f32),
            room(8, 4 * rows, 1, dtype=f32), room(tokens, HD, dtype=f32), room(*keys.shape),
            room(4 * rows, HD, dtype=f32), room(4 * rows, HD, dtype=f32),
            room(eight, 2, rows, width), room(eight, rows, width), room(eight, rows, HD),
            dma(3),
        ]
        + [dma(8)] * 6
        + QuarterScatter.scratch()
        + OutGrad.scratch(out_rows, out_w.shape[1])
        + Reduce.scratch(hidden.shape[1]),
        compiler_params=kernel_params(11),
        name="attend_back",
    )(
        query, keys, branch, mlp_part, hidden, out_w, attended, attended_low, log_row, notes, cos_table, sine_table, gate, up
    )


class HeadGrads:
    @staticmethod
    def scratch(depth):
        def room(*dims):
            return pltpu.VMEM(dims, jnp.bfloat16)

        return [
            room(LINE, 2, 2, depth, HD), room(LINE, 2, 2, depth, HD),
            room(LINE, 2, depth, HD), room(LINE, 2, depth, HD),
            room(LINE, depth, HD), room(LINE, depth, HD),
            dma(2), dma(2), dma(2), dma(2), dma(3, 4), dma(3, 4), dma(3),
        ]

    def __init__(self, outs, refs):
        self.outs = outs
        self.store, self.sib, self.box = refs[0:2], refs[2:4], refs[4:6]
        (self.c_s, self.c_r, self.x_s, self.x_r, self.s, self.r, self.own) = refs[6:]
        self.z, self.y, self.c, self.h = place()
        self.me = device(self.z, self.y, self.c, self.h)

    def share(self, i):
        return remote(
            self.store[i].at[:, :, 1 - self.c], self.sib[i], self.c_s.at[i], self.c_r.at[i],
            device(self.z, self.y, 1 - self.c, self.h),
        )

    def over(self, i):
        return remote(
            self.store[i].at[:, 1 - self.h, self.c], self.box[i], self.x_s.at[i], self.x_r.at[i],
            device(self.z, self.y, self.c, 1 - self.h),
        )

    def target(self, kind, line):
        start = line * HD if kind == 0 else (line // 2) * HD
        return self.outs[kind].at[:, pl.ds(pl.multiple_of(start, HD), HD)]

    def push(self, kind, step):
        line = (self.z + step) % LINE
        return remote(
            self.store[min(kind, 1)].at[line, self.h, self.c], self.target(kind, self.z), self.s.at[kind, step],
            self.r.at[kind, self.z], device(line, self.h, self.c, self.y),
        )

    def keep(self, kind):
        return local(self.store[min(kind, 1)].at[self.z, self.h, self.c], self.target(kind, self.z), self.own.at[kind])

    def stays(self, step):
        return self.h == self.y if step == 0 else self.h < 0

    def pull(self, kind, line):
        ref = self.target(kind, line)
        return remote(ref, ref, self.s.at[kind, 0], self.r.at[kind, line], self.me)

    def relay(self, i):
        self.share(i).wait_recv()

        @pl.loop(0, LINE)
        def _(line):
            for pair in range(2):
                add_into(self.store[i].at[line, pair, self.c], self.sib[i].at[line, pair])

        self.over(i).start()

    def each_kind(self, i, act):
        if i == 0:
            act(0)
        else:
            for kind in (1, 2):

                @pl.when(self.z % 2 == kind - 1)
                def _():
                    act(kind)

    def scatter(self, i):
        self.over(i).wait_recv()

        @pl.loop(0, LINE)
        def _(line):
            add_into(self.store[i].at[line, self.h, self.c], self.box[i].at[line])

        def act(kind):
            for step in range(4):

                @pl.when(self.stays(step))
                def _():
                    self.keep(kind).start()

                @pl.when(jnp.logical_not(self.stays(step)))
                def _():
                    self.push(kind, step).start()

        self.each_kind(i, act)

    def finish(self):
        for kind in range(3):
            for line in range(LINE):
                if kind and line % 2 != kind - 1:
                    continue
                from_self = (self.z == line) & (self.y == self.h)

                @pl.when(from_self)
                def _():
                    self.keep(kind).wait()

                @pl.when(jnp.logical_not(from_self))
                def _():
                    self.pull(kind, line).wait_recv()

        def act(kind):
            for step in range(4):

                @pl.when(jnp.logical_not(self.stays(step)))
                def _():
                    self.push(kind, step).wait_send()

        for i in range(2):
            self.each_kind(i, act)
            self.over(i).wait_send()
            self.share(i).wait_send()


class GainSum:
    @staticmethod
    def scratch(rows):
        return [
            pltpu.VMEM((16, 8, rows), jnp.float32), pltpu.VMEM((32, 8, rows), jnp.float32), dma(32), dma(32),
        ]

    def __init__(self, out, refs):
        self.out = out
        self.terms, self.box, self.s, self.r = refs
        self.blk, self.h = lax.axis_index("blk"), lax.axis_index("head")

    def push(self, step):
        other = (self.blk + step // 2) % 16
        return remote(
            self.terms.at[other], self.box.at[step], self.s.at[step], self.r.at[step], (other, (self.h + step % 2) % 2)
        )

    def start(self, attn_term, mlp_term):
        rows = self.terms.shape[2]
        self.terms[...] = jnp.zeros_like(self.terms)
        for blk in range(16):
            part = pl.ds(blk * rows, rows)
            self.terms[blk, 0:1] = attn_term[:, part]
            self.terms[blk, 1:2] = mlp_term[:, part]
        for step in range(1, 32):
            self.push(step).start()

    def finish(self):
        total = self.terms[self.blk]
        for step in range(1, 32):
            self.push(step).wait_recv()
            total += self.box[step]
        self.out[...] = total
        for step in range(1, 32):
            self.push(step).wait_send()


def close_kernel(
    normed_in, qkv_w, active_in, cot_in, grad_query, grad_side, grad_hidden, tokens, gain, mlp_term,
    tokens_grad, gains, down, query, key, value,
    normed, weight, parts, active, cot, total, attn_term, load_s, *refs,
):
    reduce_refs, head_refs, gain_refs, down_refs = split_refs(refs, (Reduce.COUNT, 13, 4, 5))
    z, y, c, h = place()
    loads = [
        local(active_in, active, load_s.at[3]),
        local(cot_in, cot, load_s.at[4]),
    ]
    load = local(normed_in, normed, load_s.at[0])
    load_q = local(qkv_w.at[:, :, :, pl.ds(0, HD)], weight.at[0], load_s.at[1])
    side_columns = pl.ds(pl.multiple_of((1 + z % 2) * HD, HD), HD)
    load_side = local(qkv_w.at[:, :, :, side_columns], weight.at[1], load_s.at[2])
    load_q.start()
    load_side.start()
    load.start()
    for later in loads:
        later.start()
    greet_all(16, 2)
    reduce = Reduce(parts, reduce_refs)
    downs = DownReduce(down, down_refs)
    heads = HeadGrads((query, key, value), head_refs)
    gain_sum = GainSum(gains, gain_refs)
    rows, width = parts.shape[1:]
    pair = 2 * rows
    depth = head_refs[0].shape[3]
    load_q.wait()
    load_side.wait()
    load.wait()
    attn_term[...] = jnp.zeros_like(attn_term)
    for place_at in range(4):
        line = reduce.order[place_at]
        both = pl.ds(pl.multiple_of(line * pair, pair), pair)

        @pl.loop(0, 4)
        def _(tile):
            columns = pl.ds(pl.multiple_of(tile * (width // 4), width // 4), width // 4)
            part = times_transposed(grad_query[both], weight[0, pl.ds(tile * 2, 2)].reshape(width // 4, HD))
            part += times_transposed(grad_side[both], weight[1, pl.ds(tile * 2, 2)].reshape(width // 4, HD))
            parts[pl.ds(line * 2, 2), :, columns] = part.astype(jnp.bfloat16).reshape(2, rows, width // 4)
            scaled = part * normed[both, columns].astype(jnp.float32)
            attn_term[:, columns] += jnp.sum(scaled, axis=0, keepdims=True)

        reduce.start(place_at)
    attn_term[...] = attn_term[...] / gain[...]
    gain_sum.start(attn_term, mlp_term)
    for i, source in enumerate((grad_query, grad_side)):

        @pl.loop(0, 4)
        def _(tile):
            columns = pl.ds(pl.multiple_of(tile * 4 * depth, 4 * depth), 4 * depth)
            part = transposed_times(normed[:, columns], source[...])
            head_refs[i][tile] = part.astype(jnp.bfloat16).reshape(2, 2, depth, HD)

        heads.share(i).start()
    heads.relay(0)
    heads.relay(1)
    reduce.relay(0)
    for later in loads:
        later.wait()
    down_rows = down.shape[0]

    def down_grad(tile):
        columns = pl.ds(tile * down_rows, down_rows)

        @pl.loop(0, 4)
        def _(piece):
            wide = pl.ds(pl.multiple_of(piece * (width // 4), width // 4), width // 4)
            part = transposed_times(
                active[:, :, columns].reshape(8 * rows, down_rows), cot[:, :, wide].reshape(8 * rows, width // 4)
            )
            down_refs[0][tile // 2, tile % 2, :, wide] = part.astype(jnp.bfloat16)

    for tile in range(4):
        down_grad(tile)
    downs.share().start()
    heads.scatter(0)
    reduce.relay(1)
    heads.scatter(1)
    downs.relay()
    reduce.relay(2)
    reduce.total(total)
    inputs = tokens[...].astype(jnp.float32)
    inv_scale = rms_scale(inputs)
    unit_rows = inputs * inv_scale
    grad_unit = total[...] * gain[...]
    mean = jnp.mean(grad_unit * unit_rows, axis=-1, keepdims=True)
    tokens_grad[...] = (grad_hidden[...] + inv_scale * (grad_unit - unit_rows * mean)).astype(jnp.bfloat16)
    gain_sum.finish()
    downs.finish()
    heads.finish()
    reduce.finish()


def close(normed, qkv_w, active, cot, grad_query, grad_side, grad_hidden, tokens, gain, mlp_term):
    rows, width = tokens.shape
    down_rows = active.shape[2] // 4
    depth = qkv_w.shape[2]

    def room(*dims, dtype=jnp.bfloat16):
        return pltpu.VMEM(dims, dtype)

    def shape(*dims, dtype=jnp.bfloat16):
        return jax.ShapeDtypeStruct(dims, dtype)

    f32 = jnp.float32
    return pl.pallas_call(
        close_kernel,
        out_shape=(
            shape(rows, width),
            shape(8, rows, dtype=f32),
            shape(down_rows, width, dtype=f32),
            shape(depth, 4 * HD), shape(depth, 2 * HD), shape(depth, 2 * HD),
        ),
        in_specs=[ANY] * 4 + [INSIDE] * 6,
        out_specs=(INSIDE, INSIDE, INSIDE, ANY, ANY, ANY),
        scratch_shapes=[
            room(*normed.shape), room(2, 8, 2, depth, HD), room(8, rows, width),
            room(*active.shape), room(*cot.shape),
            room(rows, width, dtype=f32), room(1, width, dtype=f32), dma(5),
        ]
        + Reduce.scratch(width)
        + HeadGrads.scratch(depth)
        + GainSum.scratch(rows)
        + DownReduce.scratch(down_rows, width),
        compiler_params=kernel_params(6),
        name="close",
    )(normed, qkv_w, active, cot, grad_query, grad_side, grad_hidden, tokens, gain, mlp_term)


def widen_kernel(*refs):
    half = len(refs) // 2
    for source, target in zip(refs[:half], refs[half:]):
        target[...] = source[...].astype(target.dtype)


def widen(arrays, dtypes):
    return pl.pallas_call(
        widen_kernel,
        out_shape=tuple(jax.ShapeDtypeStruct(array.shape, dtype) for array, dtype in zip(arrays, dtypes)),
        in_specs=[INSIDE] * len(arrays),
        out_specs=(INSIDE,) * len(arrays),
        compiler_params=pltpu.CompilerParams(vmem_limit_bytes=VMEM_BYTES),
        name="widen",
    )(*arrays)


def fast_body(
    tokens,
    attn_gain,
    w_query,
    w_key,
    w_value,
    w_out,
    mlp_gain,
    w_gate,
    w_up,
    w_down,
    block_ids,
    positions,
    cotangent,
):
    rows, width = tokens.shape
    token_rows = 8 * rows
    f32, bf16 = jnp.float32, jnp.bfloat16

    note = jnp.concatenate(
        [
            positions.astype(f32).reshape(2, rows),
            block_ids.astype(f32).reshape(2, rows),
            attn_gain.astype(f32)[None],
            mlp_gain.astype(f32)[None],
            jnp.zeros((2, rows), f32),
        ]
    )
    inv_freqs = jnp.asarray((rope_base ** (-2.0 * np.arange(HD // 2) / HD)).astype(np.float32))
    (
        keys_values, normed, qkv_w, out_w, notes, gain_attn, gain_mlp, cos_table, sine_table, scaled_query, attended, attended_low,
        log_total, cot_all, gate_w, up_w,
    ) = front(tokens, cotangent, note, inv_freqs[None], w_query, w_key, w_value, w_out, w_gate, w_up)
    out_w = out_w.reshape(HD, width)
    hidden, active, mlp_part, grad_branch, grad_hidden, mlp_term, gate_quarter, up_quarter = core(
        attended_low, out_w, gate_w, up_w, w_down, tokens, gain_mlp, cotangent, cot_all
    )

    side_grad, grad_query, output, gate_grad, up_grad, out_grad = attend_back(
        scaled_query,
        keys_values,
        grad_branch,
        mlp_part,
        hidden,
        out_w,
        attended,
        attended_low,
        log_total,
        notes,
        cos_table,
        sine_table,
        gate_quarter,
        up_quarter,
        w_out.shape[0],
    )
    tokens_grad, gain_grads, down_grad, query_grad, key_grad, value_grad = close(
        normed,
        qkv_w,
        active,
        cot_all,
        grad_query,
        side_grad,
        grad_hidden,
        tokens,
        gain_attn,
        mlp_term,
    )
    arrays = (output, tokens_grad, query_grad, key_grad, value_grad, out_grad, gate_grad, up_grad, down_grad)
    output, tokens_grad, query_grad, key_grad, value_grad, out_grad, gate_grad, up_grad, down_grad = widen(
        arrays, (bf16, bf16) + (f32,) * 7
    )
    return (
        output,
        tokens_grad,
        gain_grads[0],
        query_grad,
        key_grad,
        value_grad,
        out_grad,
        gain_grads[1],
        gate_grad,
        up_grad,
        down_grad,
    )


def solution(mesh):
    placed = (
        P(("blk", "head"), None),
        P("blk"),
        P("blk", "head"),
        P("blk", "head"),
        P("blk", "head"),
        P(("head", "blk"), None),
        P("blk"),
        P("blk", "head"),
        P("blk", "head"),
        P(("head", "blk"), None),
        P("blk"),
        P("blk"),
        P(("blk", "head"), None),
    )
    fits = mesh.shape["blk"] == 16 and mesh.shape["head"] == 2
    return jax.shard_map(
        fast_body if fits else body,
        mesh=mesh,
        in_specs=placed,
        out_specs=(
            P(("blk", "head"), None),
            P(("blk", "head"), None),
            P("blk"),
            P("blk", "head"),
            P("blk", "head"),
            P("blk", "head"),
            P(("head", "blk"), None),
            P("blk"),
            P("blk", "head"),
            P("blk", "head"),
            P(("head", "blk"), None),
        ),
        check_vma=False,
    )
```

```python
import jax
import jax.numpy as jnp
from jax import lax
import numpy as np
from jax.experimental import pallas as pl
from jax.experimental.pallas import tpu as pltpu
from jax.sharding import PartitionSpec as P

HD = 256


eps_norm = 1e-06
rope_base = 1000042.0


def rms_scale(rows):
    return lax.rsqrt(jnp.mean(rows * rows, axis=-1, keepdims=True) + eps_norm)


def rope_tables(positions):
    inv_freqs = rope_base ** (-2.0 * jnp.arange(HD // 2, dtype=jnp.float32) / HD)
    angles = positions.astype(jnp.float32)[:, None] * inv_freqs[None, :]
    return (jnp.cos(angles)[:, None, :], jnp.sin(angles)[:, None, :])


def rotate(heads, cos_table, sine_table):
    half_size = heads.shape[-1] // 2
    lower_half = heads[..., :half_size]
    upper_half = heads[..., half_size:]
    return jnp.concatenate(
        [
            lower_half * cos_table - upper_half * sine_table,
            upper_half * cos_table + lower_half * sine_table,
        ],
        axis=-1,
    )


def product(left, right):
    return jnp.dot(left, right, preferred_element_type=jnp.float32)


def times_transposed(left, right):
    return lax.dot_general(
        left, right, (((1,), (1,)), ((), ())), preferred_element_type=jnp.float32
    )


def transposed_times(left, right):
    return lax.dot_general(
        left, right, (((0,), (0,)), ((), ())), preferred_element_type=jnp.float32
    )


def norm_backward(grad_normed, inputs, inv_scale, gain_rows):
    unit_rows = inputs * inv_scale
    grad_unit = grad_normed * gain_rows
    gain_term = jnp.sum(grad_normed * unit_rows, axis=0)
    grad_inputs = inv_scale * (
        grad_unit - unit_rows * jnp.mean(grad_unit * unit_rows, axis=-1, keepdims=True)
    )
    return (grad_inputs, gain_term)


def body(
    tokens,
    attn_gain,
    w_query,
    w_key,
    w_value,
    w_out,
    mlp_gain,
    w_gate,
    w_up,
    w_down,
    block_ids,
    positions,
    cotangent,
):
    rows_own = tokens.shape[0]
    head_rank = lax.axis_index("head")
    tokens_all, cot_all = (
        lax.all_gather(tokens, "head", axis=0, tiled=True),
        lax.all_gather(cotangent, "head", axis=0, tiled=True),
    )
    rows_all = tokens_all.shape[0]
    gain_attn, query_w, key_w, value_w, out_w = (
        lax.all_gather(attn_gain, "blk", axis=0, tiled=True),
        lax.all_gather(w_query, "blk", axis=0, tiled=True),
        lax.all_gather(w_key, "blk", axis=0, tiled=True),
        lax.all_gather(w_value, "blk", axis=0, tiled=True),
        lax.all_gather(w_out, "blk", axis=0, tiled=True),
    )
    gain_mlp, gate_w, up_w, down_w = (
        lax.all_gather(mlp_gain, "blk", axis=0, tiled=True),
        lax.all_gather(w_gate, "blk", axis=0, tiled=True),
        lax.all_gather(w_up, "blk", axis=0, tiled=True),
        lax.all_gather(w_down, "blk", axis=0, tiled=True),
    )
    key_ids = lax.all_gather(block_ids, "blk", axis=0, tiled=True)
    heads_local = query_w.shape[1] // HD
    kv_local = key_w.shape[1] // HD
    kv_width = kv_local * HD
    group_size = heads_local // kv_local
    cos_table, sine_table = rope_tables(positions)
    score_scale = HD ** (-0.5)
    seq_len = key_ids.shape[0]
    key_block = min(2048, seq_len)
    block_total = seq_len // key_block
    block_steps = jnp.arange(block_total)
    top_query = jnp.max(block_ids)
    inputs = tokens_all.astype(jnp.float32)
    inv_attn = rms_scale(inputs)
    normed = (inputs * inv_attn * gain_attn.astype(jnp.float32)).astype(jnp.bfloat16)
    queries = rotate(
        product(normed, query_w).reshape(rows_all, heads_local, HD), cos_table, sine_table
    ).astype(jnp.bfloat16)
    keys_own = rotate(product(normed, key_w).reshape(rows_all, kv_local, HD), cos_table, sine_table)
    keys_own = keys_own.astype(jnp.bfloat16).reshape(rows_all, kv_width)
    values_own = product(normed, value_w).astype(jnp.bfloat16)
    keys_all, values_all = (
        lax.all_gather(keys_own, "blk", axis=0, tiled=True),
        lax.all_gather(values_own, "blk", axis=0, tiled=True),
    )
    grouped = queries.reshape(rows_all, kv_local, group_size, HD)

    def slice_keys(key_start, count):
        key_rows = lax.dynamic_slice_in_dim(keys_all, key_start, count, 0).reshape(
            count, kv_local, HD
        )
        value_rows = lax.dynamic_slice_in_dim(values_all, key_start, count, 0).reshape(
            count, kv_local, HD
        )
        block_keys = lax.dynamic_slice_in_dim(key_ids, key_start, count, 0)
        return (key_rows, value_rows, block_keys)

    def scores_for(key_rows, block_keys):
        scores = (
            jnp.einsum("qkgd,ckd->kgqc", grouped, key_rows, preferred_element_type=jnp.float32)
            * score_scale
        )
        visible = (block_keys[None, :] <= block_ids[:, None])[None, None]
        return (scores, visible)

    def max_sum(state_pair, step_index):
        key_start = step_index * key_block

        def max_live(pair):
            run_max, run_sum = pair
            key_rows, value_rows, block_keys = slice_keys(key_start, key_block)
            scores, visible = scores_for(key_rows, block_keys)
            scores = jnp.where(visible, scores, -1e30)
            new_max = jnp.maximum(run_max, jnp.max(scores, axis=-1))
            kept_terms = jnp.where(visible, jnp.exp(scores - new_max[..., None]), 0.0)
            return (new_max, run_sum * jnp.exp(run_max - new_max) + jnp.sum(kept_terms, axis=-1))

        def max_skipped(pair):
            return pair

        return (lax.cond(key_ids[key_start] <= top_query, max_live, max_skipped, state_pair), None)

    start_max = jnp.full((kv_local, group_size, rows_all), -1e30, jnp.float32)
    start_sum = jnp.zeros((kv_local, group_size, rows_all), jnp.float32)
    (run_max, run_sum), unused_max = lax.scan(max_sum, (start_max, start_sum), block_steps)
    log_total = run_max + jnp.log(run_sum)

    def weighted(accum_rows, step_index):
        key_start = step_index * key_block

        def weighted_live(accum):
            key_rows, value_rows, block_keys = slice_keys(key_start, key_block)
            scores, visible = scores_for(key_rows, block_keys)
            probabilities = jnp.where(visible, jnp.exp(scores - log_total[..., None]), 0.0).astype(
                jnp.bfloat16
            )
            return accum + jnp.einsum(
                "kgqc,ckd->qkgd", probabilities, value_rows, preferred_element_type=jnp.float32
            )

        def weighted_skipped(accum):
            return accum

        return (
            lax.cond(key_ids[key_start] <= top_query, weighted_live, weighted_skipped, accum_rows),
            None,
        )

    attended, unused_rows = lax.scan(
        weighted, jnp.zeros((rows_all, kv_local, group_size, HD), jnp.float32), block_steps
    )
    attended_low = attended.reshape(rows_all, heads_local * HD).astype(jnp.bfloat16)
    branch_sum = lax.psum(product(attended_low, out_w).astype(jnp.bfloat16), "head").astype(
        jnp.float32
    )
    hidden = inputs + branch_sum
    inv_mlp = rms_scale(hidden)
    normed_mlp = (hidden * inv_mlp * gain_mlp.astype(jnp.float32)).astype(jnp.bfloat16)
    gate_pre = product(normed_mlp, gate_w)
    up_pre = product(normed_mlp, up_w)
    sigmoid_gate = jax.nn.sigmoid(gate_pre)
    active = (gate_pre * sigmoid_gate * up_pre).astype(jnp.bfloat16)
    mlp_own = lax.psum_scatter(
        product(active, down_w).astype(jnp.bfloat16), "head", scatter_dimension=0, tiled=True
    ).astype(jnp.float32)
    hidden_own = lax.dynamic_slice_in_dim(hidden, head_rank * rows_own, rows_own, 0)
    output = (hidden_own + mlp_own).astype(jnp.bfloat16)
    gain_attn, query_w, key_w, value_w, out_w = (
        lax.all_gather(attn_gain, "blk", axis=0, tiled=True),
        lax.all_gather(w_query, "blk", axis=0, tiled=True),
        lax.all_gather(w_key, "blk", axis=0, tiled=True),
        lax.all_gather(w_value, "blk", axis=0, tiled=True),
        lax.all_gather(w_out, "blk", axis=0, tiled=True),
    )
    gain_mlp, gate_w, up_w, down_w = (
        lax.all_gather(mlp_gain, "blk", axis=0, tiled=True),
        lax.all_gather(w_gate, "blk", axis=0, tiled=True),
        lax.all_gather(w_up, "blk", axis=0, tiled=True),
        lax.all_gather(w_down, "blk", axis=0, tiled=True),
    )
    grad_active = times_transposed(cot_all, down_w)
    grad_gate = (
        grad_active * up_pre * sigmoid_gate * (1.0 + gate_pre * (1.0 - sigmoid_gate))
    ).astype(jnp.bfloat16)
    grad_up = (grad_active * gate_pre * sigmoid_gate).astype(jnp.bfloat16)
    grad_gate_w = transposed_times(normed_mlp, grad_gate)
    grad_up_w = transposed_times(normed_mlp, grad_up)
    grad_down_w = transposed_times(active, cot_all)
    grad_normed_part = times_transposed(grad_gate, gate_w) + times_transposed(grad_up, up_w)
    grad_normed_mlp = lax.psum(grad_normed_part.astype(jnp.bfloat16), "head").astype(jnp.float32)
    grad_hidden_norm, gain_mlp_term = norm_backward(
        grad_normed_mlp, hidden, inv_mlp, gain_mlp.astype(jnp.float32)
    )
    grad_hidden = cot_all.astype(jnp.float32) + grad_hidden_norm
    mlp_results = (
        lax.psum_scatter(gain_mlp_term, "blk", scatter_dimension=0, tiled=True),
        lax.psum_scatter(grad_gate_w, "blk", scatter_dimension=0, tiled=True),
        lax.psum_scatter(grad_up_w, "blk", scatter_dimension=0, tiled=True),
        lax.psum_scatter(grad_down_w, "blk", scatter_dimension=0, tiled=True),
    )
    grad_branch = grad_hidden.astype(jnp.bfloat16)
    grad_out_w = transposed_times(attended_low, grad_branch)
    grad_attended = times_transposed(grad_branch, out_w).astype(jnp.bfloat16)
    grad_grouped = grad_attended.reshape(rows_all, kv_local, group_size, HD)
    delta_rows = jnp.transpose(
        jnp.sum(grad_grouped.astype(jnp.float32) * attended, axis=-1), (1, 2, 0)
    )

    def pair_backward(key_rows, value_rows, block_keys):
        count = key_rows.shape[0]
        scores, visible = scores_for(key_rows, block_keys)
        probabilities = jnp.where(visible, jnp.exp(scores - log_total[..., None]), 0.0)
        grad_probs = jnp.einsum(
            "qkgd,ckd->kgqc", grad_grouped, value_rows, preferred_element_type=jnp.float32
        )
        grad_scores = (probabilities * (grad_probs - delta_rows[..., None])).astype(jnp.bfloat16)
        query_terms = jnp.einsum(
            "kgqc,ckd->qkgd", grad_scores, key_rows, preferred_element_type=jnp.float32
        )
        key_terms = (
            jnp.einsum("kgqc,qkgd->ckd", grad_scores, grouped, preferred_element_type=jnp.float32)
            * score_scale
        )
        value_terms = jnp.einsum(
            "kgqc,qkgd->ckd",
            probabilities.astype(jnp.bfloat16),
            grad_grouped,
            preferred_element_type=jnp.float32,
        )
        return (
            query_terms,
            key_terms.reshape(count, kv_width),
            value_terms.reshape(count, kv_width),
        )

    query_zeros = jnp.zeros((rows_all, kv_local, group_size, HD), jnp.float32)

    def backward_block(accum_rows, step_index):
        key_start = step_index * key_block

        def backward_live(unused_arg):
            key_rows, value_rows, block_keys = slice_keys(key_start, key_block)
            return pair_backward(key_rows, value_rows, block_keys)

        def backward_skipped(unused_arg):
            empty_terms = jnp.zeros((key_block, kv_width), jnp.float32)
            return (query_zeros, empty_terms, empty_terms)

        query_terms, key_terms, value_terms = lax.cond(
            key_ids[key_start] <= top_query, backward_live, backward_skipped, 0
        )
        return (accum_rows + query_terms, (key_terms, value_terms))

    grad_query_rot, (key_terms, value_terms) = lax.scan(backward_block, query_zeros, block_steps)
    key_terms = key_terms.reshape(seq_len, kv_width)
    value_terms = value_terms.reshape(seq_len, kv_width)
    key_grad_own, value_grad_own = (
        lax.psum_scatter(key_terms, "blk", scatter_dimension=0, tiled=True),
        lax.psum_scatter(value_terms, "blk", scatter_dimension=0, tiled=True),
    )
    grad_query_rot = grad_query_rot * score_scale
    grad_key = rotate(key_grad_own.reshape(rows_all, kv_local, HD), cos_table, -sine_table)
    grad_key = grad_key.reshape(rows_all, kv_width).astype(jnp.bfloat16)
    grad_value = value_grad_own.astype(jnp.bfloat16)
    grad_query = rotate(grad_query_rot.reshape(rows_all, heads_local, HD), cos_table, -sine_table)
    grad_query = grad_query.reshape(rows_all, heads_local * HD).astype(jnp.bfloat16)
    grad_query_w = transposed_times(normed, grad_query)
    grad_key_w = transposed_times(normed, grad_key)
    grad_value_w = transposed_times(normed, grad_value)
    grad_normed_part = (
        times_transposed(grad_query, query_w)
        + times_transposed(grad_key, key_w)
        + times_transposed(grad_value, value_w)
    )
    grad_normed = lax.psum(grad_normed_part.astype(jnp.bfloat16), "head").astype(jnp.float32)
    grad_inputs_norm, gain_attn_term = norm_backward(
        grad_normed, inputs, inv_attn, gain_attn.astype(jnp.float32)
    )
    grad_inputs = grad_hidden + grad_inputs_norm
    grad_own = lax.dynamic_slice_in_dim(grad_inputs, head_rank * rows_own, rows_own, 0).astype(
        jnp.bfloat16
    )
    attn_results = (
        lax.psum_scatter(gain_attn_term, "blk", scatter_dimension=0, tiled=True),
        lax.psum_scatter(grad_query_w, "blk", scatter_dimension=0, tiled=True),
        lax.psum_scatter(grad_key_w, "blk", scatter_dimension=0, tiled=True),
        lax.psum_scatter(grad_value_w, "blk", scatter_dimension=0, tiled=True),
        lax.psum_scatter(grad_out_w, "blk", scatter_dimension=0, tiled=True),
    )
    return (
        output,
        grad_own,
        attn_results[0],
        attn_results[1],
        attn_results[2],
        attn_results[3],
        attn_results[4],
        mlp_results[0],
        mlp_results[1],
        mlp_results[2],
        mlp_results[3],
    )


MESH = pl.DeviceIdType.MESH
LINE = 4
VMEM_BYTES = 60 * 2**20


def place():
    blk, head = lax.axis_index("blk"), lax.axis_index("head")
    return blk // 4, (blk // 2) % 2, blk % 2, head


def device(z, y, c, h):
    return (z * 4 + y * 2 + c, h)


def remote(src, dst, send_sem, recv_sem, target):
    return pltpu.make_async_remote_copy(
        src_ref=src,
        dst_ref=dst,
        send_sem=send_sem,
        recv_sem=recv_sem,
        device_id=target,
        device_id_type=MESH,
    )


def greet(target):
    pl.semaphore_signal(
        pltpu.get_barrier_semaphore(), inc=1, device_id=target, device_id_type=MESH
    )


def greet_all(blk_total, head_total):
    blk, head = lax.axis_index("blk"), lax.axis_index("head")
    for other in range(blk_total):
        for half in range(head_total):

            @pl.when(jnp.logical_or(blk != other, head != half))
            def _():
                greet((jnp.int32(other), jnp.int32(half)))

    pl.semaphore_wait(pltpu.get_barrier_semaphore(), blk_total * head_total - 1)


def greet_plane(more=0):
    z, y, c, h = place()

    @pl.when(z > 0)
    def _():
        greet(device(z - 1, y, c, h))

    @pl.when(z < LINE - 1)
    def _():
        greet(device(z + 1, y, c, h))

    greet(device(z, 1 - y, c, h))
    pl.semaphore_wait(
        pltpu.get_barrier_semaphore(),
        1 + more + (z + LINE - 1) // LINE + (LINE - 1 - z + LINE - 1) // LINE,
    )


class Gather:
    CUTS = ((0, 64), (64, 48), (112, 16), (112, 16))
    SEMS = [(3, 4)] * 4 + [(4, 2)] * 2 + [(2,)]

    @staticmethod
    def scratch():
        return [pltpu.SemaphoreType.DMA(shape) for shape in Gather.SEMS] + [
            pltpu.SemaphoreType.DMA
        ]

    def __init__(self, src, out, sems):
        self.src, self.out = src, out
        (self.up_s, self.up_r, self.dn_s, self.dn_r, self.y_s, self.y_r, self.b_sr, self.own_sem) = sems
        self.z, self.y, self.c, self.h = place()

    def piece(self, line, elem):
        y = 1 - self.y if elem == 3 else self.y
        start, size = self.CUTS[elem]
        return self.out.at[line * 2 + y, pl.ds(start, size)]

    def first(self, elem):
        if elem == 3:
            return self.piece(self.z, 3)
        start, size = self.CUTS[elem]
        return self.src.at[pl.ds(start, size)]

    def up(self, step, elem):
        src = self.first(elem) if step == 0 else self.piece(self.z - step, elem)
        return remote(
            src, self.piece(self.z - step, elem), self.up_s.at[step, elem], self.up_r.at[step, elem],
            device(self.z + 1, self.y, self.c, self.h),
        )

    def down(self, step, elem):
        src = self.first(elem) if step == 0 else self.piece(self.z + step, elem)
        return remote(
            src, self.piece(self.z + step, elem), self.dn_s.at[step, elem], self.dn_r.at[step, elem],
            device(self.z - 1, self.y, self.c, self.h),
        )

    def up_in(self, step, elem):
        ref = self.piece(self.z - 1 - step, elem)
        return remote(ref, ref, self.up_s.at[step, elem], self.up_r.at[step, elem], device(self.z, self.y, self.c, self.h))

    def down_in(self, step, elem):
        ref = self.piece(self.z + 1 + step, elem)
        return remote(ref, ref, self.dn_s.at[step, elem], self.dn_r.at[step, elem], device(self.z, self.y, self.c, self.h))

    def across(self, line, elem, own=False):
        src = self.first(elem) if own else self.piece(line, elem)
        return remote(
            src, self.piece(line, elem), self.y_s.at[line, elem], self.y_r.at[line, elem],
            device(self.z, 1 - self.y, self.c, self.h),
        )

    def across_in(self, line, elem):
        start, size = self.CUTS[elem]
        ref = self.out.at[line * 2 + 1 - self.y, pl.ds(start, size)]
        return remote(ref, ref, self.y_s.at[line, elem], self.y_r.at[line, elem], device(self.z, self.y, self.c, self.h))

    def across_b(self):
        return remote(
            self.first(2), self.piece(self.z, 2), self.b_sr.at[0], self.b_sr.at[1],
            device(self.z, 1 - self.y, self.c, self.h),
        )

    def across_b_in(self):
        ref = self.piece(self.z, 3)
        return remote(ref, ref, self.b_sr.at[0], self.b_sr.at[1], device(self.z, self.y, self.c, self.h))

    def own_copy(self):
        return pltpu.make_async_copy(self.src, self.out.at[self.z * 2 + self.y], self.own_sem)

    def start(self):
        self.own_copy().start()
        self.across_b().start()
        for elem in (0, 1, 2):

            @pl.when(self.z < LINE - 1)
            def _():
                self.up(0, elem).start()

            @pl.when(self.z > 0)
            def _():
                self.down(0, elem).start()

            if elem < 2:
                self.across(self.z, elem, own=True).start()

    def relay_b(self):
        self.across_b_in().wait_recv()

        @pl.when(self.z < LINE - 1)
        def _():
            self.up(0, 3).start()

        @pl.when(self.z > 0)
        def _():
            self.down(0, 3).start()

    def relay(self, step, elem):
        @pl.when(self.z - 1 - step >= 0)
        def _():
            self.up_in(step, elem).wait_recv()
            if step < LINE - 2:

                @pl.when(self.z < LINE - 1)
                def _():
                    self.up(step + 1, elem).start()

            if elem < 2:
                self.across(self.z - 1 - step, elem).start()

        @pl.when(self.z + 1 + step <= LINE - 1)
        def _():
            self.down_in(step, elem).wait_recv()
            if step < LINE - 2:

                @pl.when(self.z > 0)
                def _():
                    self.down(step + 1, elem).start()

            if elem < 2:
                self.across(self.z + 1 + step, elem).start()

    def relays(self):
        self.relay_b()
        for step in range(LINE - 1):
            for elem in (0, 1, 2, 3):
                self.relay(step, elem)

    def finish(self):
        for line in range(LINE):
            for elem in (0, 1):
                self.across_in(line, elem).wait_recv()
        for line in range(LINE):
            for elem in (0, 1):
                self.across(line, elem).wait_send()
        self.finish_sends()
        self.own_copy().wait()

    def finish_sends(self):
        self.across_b().wait_send()
        for step in range(LINE - 1):
            for elem in range(4):

                @pl.when(jnp.logical_and(self.z < LINE - 1, self.z - step >= 0))
                def _():
                    self.up(step, elem).wait_send()

                @pl.when(jnp.logical_and(self.z > 0, self.z + step <= LINE - 1))
                def _():
                    self.down(step, elem).wait_send()


ANY = pl.BlockSpec(memory_space=pl.ANY)
INSIDE = pl.BlockSpec(memory_space=pltpu.VMEM)


def kernel_params(collective_id):
    return pltpu.CompilerParams(
        collective_id=collective_id, has_side_effects=True, vmem_limit_bytes=VMEM_BYTES
    )


def add_into(target, *others):
    total = target[...].astype(jnp.float32)
    for other in others:
        total += other[...].astype(jnp.float32)
    target[...] = total.astype(target.dtype)


class Reduce:
    CUTS = ((0, 64), (64, 48))
    LAST = (112, 16)

    @staticmethod
    def scratch(width):
        inbox = pltpu.VMEM((LINE, 112, width), jnp.bfloat16)
        last = pltpu.VMEM((LINE, 2, 16, width), jnp.bfloat16)
        sems = [pltpu.SemaphoreType.DMA((LINE, 2))] * 10 + [pltpu.SemaphoreType.DMA((2,))]
        return [inbox] * 3 + [last] * 2 + [pltpu.VMEM((16, width), jnp.bfloat16)] + sems

    COUNT = 17

    def __init__(self, parts, refs):
        self.parts = parts
        self.y_in, self.up_in, self.dn_in, self.up_last, self.dn_last, self.y_last = refs[:6]
        (
            self.y_s, self.y_r, self.up_s, self.up_r, self.dn_s, self.dn_r,
            self.ul_s, self.ul_r, self.dl_s, self.dl_r, self.yl_sr,
        ) = refs[6:]
        self.z, self.y, self.c, self.h = place()
        z = self.z
        self.order = (3 - 3 * (z // 2), (2 + 3 * z) % 5, 1 + z % 2, z)

    def rows(self, cut):
        return pl.ds(*self.CUTS[cut])

    def across(self, line, cut):
        return remote(
            self.parts.at[line * 2 + 1 - self.y, self.rows(cut)], self.y_in.at[line, self.rows(cut)],
            self.y_s.at[line, cut], self.y_r.at[line, cut], device(self.z, 1 - self.y, self.c, self.h),
        )

    def up(self, line, cut):
        return remote(
            self.parts.at[line * 2 + self.y, self.rows(cut)], self.up_in.at[line, self.rows(cut)],
            self.up_s.at[line, cut], self.up_r.at[line, cut], device(self.z + 1, self.y, self.c, self.h),
        )

    def down(self, line, cut):
        return remote(
            self.parts.at[line * 2 + self.y, self.rows(cut)], self.dn_in.at[line, self.rows(cut)],
            self.dn_s.at[line, cut], self.dn_r.at[line, cut], device(self.z - 1, self.y, self.c, self.h),
        )

    def last(self, line, column):
        return self.parts.at[line * 2 + column, pl.ds(*self.LAST)]

    def last_up(self, line, column):
        return remote(
            self.last(line, column), self.up_last.at[line, column], self.ul_s.at[line, column],
            self.ul_r.at[line, column], device(self.z + 1, self.y, self.c, self.h),
        )

    def last_down(self, line, column):
        return remote(
            self.last(line, column), self.dn_last.at[line, column], self.dl_s.at[line, column],
            self.dl_r.at[line, column], device(self.z - 1, self.y, self.c, self.h),
        )

    def last_across(self):
        return remote(
            self.last(self.z, 1 - self.y), self.y_last, self.yl_sr.at[0], self.yl_sr.at[1],
            device(self.z, 1 - self.y, self.c, self.h),
        )

    def start(self, place_at):
        line = self.order[place_at]
        for cut in range(2):
            self.across(line, cut).start()

        @pl.when(jnp.logical_and(line > self.z, self.z == 0))
        def _():
            for column in range(2):
                self.last_up(line, column).start()

        @pl.when(jnp.logical_and(line < self.z, self.z == LINE - 1))
        def _():
            for column in range(2):
                self.last_down(line, column).start()

    def relay_last(self, line):
        @pl.when(jnp.logical_and(line > self.z, self.z > 0))
        def _():
            for column in range(2):
                self.last_up(line, column).wait_recv()
                add_into(self.last(line, column), self.up_last.at[line, column])
                self.last_up(line, column).start()

        @pl.when(jnp.logical_and(line < self.z, self.z < LINE - 1))
        def _():
            for column in range(2):
                self.last_down(line, column).wait_recv()
                add_into(self.last(line, column), self.dn_last.at[line, column])
                self.last_down(line, column).start()

    def relay(self, place_at):
        line = self.order[place_at]
        for cut in range(2):
            rows = self.rows(cut)
            self.across(line, cut).wait_recv()
            target = self.parts.at[line * 2 + self.y, rows]

            @pl.when(line > self.z)
            def _():
                @pl.when(self.z > 0)
                def _():
                    self.up(line, cut).wait_recv()
                    add_into(target, self.y_in.at[line, rows], self.up_in.at[line, rows])

                @pl.when(self.z == 0)
                def _():
                    add_into(target, self.y_in.at[line, rows])

                self.up(line, cut).start()

            @pl.when(line < self.z)
            def _():
                @pl.when(self.z < LINE - 1)
                def _():
                    self.down(line, cut).wait_recv()
                    add_into(target, self.y_in.at[line, rows], self.dn_in.at[line, rows])

                @pl.when(self.z == LINE - 1)
                def _():
                    add_into(target, self.y_in.at[line, rows])

                self.down(line, cut).start()

            if cut == 0:
                self.relay_last(line)

    def total(self, out):
        line = self.z
        last = pl.ds(*self.LAST)
        own, other = line * 2 + self.y, line * 2 + 1 - self.y

        @pl.when(self.z > 0)
        def _():
            for column in range(2):
                self.last_up(line, column).wait_recv()
                add_into(self.last(line, column), self.up_last.at[line, column])

        @pl.when(self.z < LINE - 1)
        def _():
            for column in range(2):
                self.last_down(line, column).wait_recv()
                add_into(self.last(line, column), self.dn_last.at[line, column])

        self.last_across().start()
        for cut in range(2):
            rows = self.rows(cut)
            self.across(line, cut).wait_recv()
            out[rows] = self.parts[own, rows].astype(jnp.float32) + self.y_in[line, rows].astype(jnp.float32)
        for cut in range(2):
            rows = self.rows(cut)

            @pl.when(self.z > 0)
            def _():
                self.up(line, cut).wait_recv()
                out[rows] += self.up_in[line, rows].astype(jnp.float32)

            @pl.when(self.z < LINE - 1)
            def _():
                self.down(line, cut).wait_recv()
                out[rows] += self.dn_in[line, rows].astype(jnp.float32)

        self.last_across().wait_recv()
        out[last] = self.parts[own, last].astype(jnp.float32) + self.y_last[...].astype(jnp.float32)

    def finish(self):
        for line in range(LINE):
            for cut in range(2):
                self.across(line, cut).wait_send()

                @pl.when(self.z < line)
                def _():
                    self.up(line, cut).wait_send()
                    self.last_up(line, cut).wait_send()

                @pl.when(self.z > line)
                def _():
                    self.down(line, cut).wait_send()
                    self.last_down(line, cut).wait_send()

        self.last_across().wait_send()


def dma(*shape):
    return pltpu.SemaphoreType.DMA(shape) if shape else pltpu.SemaphoreType.DMA


def local(src, dst, sem):
    return pltpu.make_async_copy(src, dst, sem)


class AttnSpread:
    @staticmethod
    def scratch(depth):
        return [pltpu.VMEM((LINE, depth, 3 * HD), jnp.bfloat16)] + [
            dma(3, 4), dma(3, 4), dma(3), dma(4), dma(4), dma(4), dma(4), dma(4), dma(4), dma(4), dma(4), dma(4), dma(4),
        ]

    COUNT = 14

    def __init__(self, weights, outs, refs):
        self.weights, (self.qkv, self.out_w) = weights, outs
        (
            self.stage, self.s, self.r, self.own, self.x_s, self.x_r, self.a_s, self.a_r, self.b_s, self.b_r,
            self.c_s, self.c_r, self.o_s, self.o_r,
        ) = refs
        self.z, self.y, self.c, self.h = place()
        self.me = device(self.z, self.y, self.c, self.h)
        self.owner = self.h == self.y

    def source(self, kind, line):
        start = line * HD if kind == 0 else (line // 2) * HD
        return self.weights[kind].at[:, pl.ds(pl.multiple_of(start, HD), HD)]

    def slot(self, kind, line, owner):
        columns = pl.ds(kind * HD, HD)
        if owner:
            return self.qkv.at[line * 2 + self.y, self.c, :, columns]
        return self.stage.at[line, :, columns]

    def push(self, kind, step, owner):
        line = (self.z + step) % LINE
        return remote(
            self.source(kind, line), self.slot(kind, self.z, owner), self.s.at[kind, step], self.r.at[kind, self.z],
            device(line, self.y, self.c, self.h),
        )

    def pull(self, kind, line, owner):
        ref = self.slot(kind, line, owner)
        return remote(ref, ref, self.s.at[kind, 0], self.r.at[kind, line], self.me)

    def keep(self, kind, owner):
        return local(self.source(kind, self.z), self.slot(kind, self.z, owner), self.own.at[kind])

    def over(self, line):
        ref = self.qkv.at[line * 2 + self.y, self.c]
        return remote(ref, ref, self.x_s.at[line], self.x_r.at[line], device(self.z, self.y, self.c, 1 - self.h))

    def over_in(self, line):
        ref = self.qkv.at[line * 2 + self.y, self.c]
        return remote(ref, ref, self.x_s.at[line], self.x_r.at[line], self.me)

    def across(self, line):
        return remote(
            self.stage.at[line], self.qkv.at[line * 2 + self.y, self.c], self.a_s.at[line], self.a_r.at[line],
            device(self.z, 1 - self.y, self.c, self.h),
        )

    def across_far(self, line):
        return remote(
            self.stage.at[line], self.qkv.at[line * 2 + self.y, self.c], self.b_s.at[line], self.b_r.at[line],
            device(self.z, 1 - self.y, self.c, 1 - self.h),
        )

    def far_in(self, line, owner):
        ref = self.qkv.at[line * 2 + 1 - self.y, self.c]
        s, r = (self.a_s, self.a_r) if owner else (self.b_s, self.b_r)
        return remote(ref, ref, s.at[line], r.at[line], self.me)

    def share(self, line, core):
        ref = self.qkv.at[pl.ds(line * 2, 2), core]
        return remote(ref, ref, self.c_s.at[line], self.c_r.at[line], device(self.z, self.y, 1 - self.c, self.h))

    def out_push(self):
        return remote(
            self.weights[3], self.out_w.at[self.y, self.c], self.o_s.at[0], self.o_r.at[0],
            device(self.z, 1 - self.y, self.c, self.h),
        )

    def out_keep(self):
        return local(self.weights[3], self.out_w.at[self.y, self.c], self.o_s.at[1])

    def out_pull(self):
        ref = self.out_w.at[1 - self.y, self.c]
        return remote(ref, ref, self.o_s.at[0], self.o_r.at[0], self.me)

    def out_over(self):
        ref = self.out_w.at[:, self.c]
        return remote(ref, ref, self.o_s.at[2], self.o_r.at[2], device(self.z, self.y, self.c, 1 - self.h))

    def out_share(self, core):
        ref = self.out_w.at[:, core]
        return remote(ref, ref, self.o_s.at[3], self.o_r.at[3], device(self.z, self.y, 1 - self.c, self.h))

    def each(self, act):
        @pl.when(self.owner)
        def _():
            act(True)

        @pl.when(jnp.logical_not(self.owner))
        def _():
            act(False)

    def start(self):
        def act(owner):
            for kind in range(3):
                self.keep(kind, owner).start()
            for step in range(1, LINE):
                for kind in range(3):
                    self.push(kind, step, owner).start()
            if owner:
                self.out_keep().start()
            else:
                self.out_push().start()

        self.each(act)

    def relay(self, step):
        line = (self.z + LINE - step) % LINE

        def act(owner):
            for kind in range(3):
                if step:
                    self.pull(kind, line, owner).wait_recv()
                else:
                    self.keep(kind, owner).wait()
            if owner:
                self.over(line).start()
            else:
                self.across(line).start()
                self.across_far(line).start()

        self.each(act)

    def relay_out(self):
        @pl.when(self.owner)
        def _():
            self.out_keep().wait()
            self.out_pull().wait_recv()
            self.out_over().start()

    def relay_share(self, step):
        line = (self.z + LINE - step) % LINE

        def act(owner):
            if not owner:
                self.over_in(line).wait_recv()
            self.far_in(line, owner).wait_recv()

        self.each(act)
        self.share(line, self.c).start()

    def relay_out_share(self):
        @pl.when(jnp.logical_not(self.owner))
        def _():
            self.out_over().wait_recv()

        self.out_share(self.c).start()

    def finish(self):
        for line in range(LINE):
            self.share(line, 1 - self.c).wait_recv()
            self.share(line, self.c).wait_send()
        self.out_share(1 - self.c).wait_recv()
        self.out_share(self.c).wait_send()

        def act(owner):
            for kind in range(3):
                for step in range(1, LINE):
                    self.push(kind, step, owner).wait_send()
            for line in range(LINE):
                if owner:
                    self.over(line).wait_send()
                else:
                    self.across(line).wait_send()
                    self.across_far(line).wait_send()
            if owner:
                self.out_over().wait_send()
            else:
                self.out_push().wait_send()

        self.each(act)


class MlpSpread:
    @staticmethod
    def scratch():
        return [dma(2, 8), dma(2, 8), dma(2)]

    def __init__(self, weights, outs, sems):
        self.weights, self.outs = weights, outs
        self.s, self.r, self.own = sems
        self.z, self.y, self.c, self.h = place()
        self.chip = self.z * 2 + self.y
        self.part = weights[0].shape[1] // 8

    def columns(self, index):
        return pl.ds(pl.multiple_of(index * self.part, self.part), self.part)

    def push(self, kind, step):
        chip = (self.chip + step) % 8
        return remote(
            self.weights[kind].at[:, self.columns(chip)], self.outs[kind].at[self.chip], self.s.at[kind, step],
            self.r.at[kind, step], device(chip // 2, chip % 2, self.c, self.h),
        )

    def pull(self, kind, step):
        ref = self.outs[kind].at[(self.chip + 8 - step) % 8]
        return remote(ref, ref, self.s.at[kind, step], self.r.at[kind, step], device(self.z, self.y, self.c, self.h))

    def keep(self, kind):
        return local(self.weights[kind].at[:, self.columns(self.chip)], self.outs[kind].at[self.chip], self.own.at[kind])

    def start(self):
        for kind in range(2):
            self.keep(kind).start()
            for step in range(1, 8):
                self.push(kind, step).start()

    def finish(self):
        for kind in range(2):
            self.keep(kind).wait()
            for step in range(1, 8):
                self.pull(kind, step).wait_recv()
                self.push(kind, step).wait_send()


class MlpShare:
    @staticmethod
    def scratch():
        return [dma(2), dma(2, 2), dma(2, 2), dma(2, 2), dma(2, 2)]

    def __init__(self, quarters, outs, sems):
        self.quarters, self.outs = quarters, outs
        self.own, self.x_s, self.x_r, self.c_s, self.c_r = sems
        self.z, self.y, self.c, self.h = place()
        self.part = quarters[0].shape[2]

    def slot(self, kind, cut, half):
        columns = pl.ds(pl.multiple_of(half * self.part, self.part), self.part)
        return self.outs[kind].at[pl.ds(cut * 4, 4), self.c, :, columns]

    def keep(self, kind):
        columns = pl.ds(pl.multiple_of(self.h * self.part, self.part), self.part)
        return local(self.quarters[kind], self.outs[kind].at[:, self.c, :, columns], self.own.at[kind])

    def over(self, kind, cut, half):
        return remote(
            self.quarters[kind].at[pl.ds(cut * 4, 4)], self.slot(kind, cut, half), self.x_s.at[kind, cut],
            self.x_r.at[kind, cut], device(self.z, self.y, self.c, 1 - self.h),
        )

    def share(self, kind, cut, core):
        ref = self.outs[kind].at[pl.ds(cut * 4, 4), core]
        return remote(
            ref, ref, self.c_s.at[kind, cut], self.c_r.at[kind, cut], device(self.z, self.y, 1 - self.c, self.h)
        )

    def start(self):
        for kind in range(2):
            for cut in range(2):
                self.over(kind, cut, self.h).start()
            self.keep(kind).start()

    def relay(self):
        for kind in range(2):
            self.keep(kind).wait()
            for cut in range(2):
                self.over(kind, cut, 1 - self.h).wait_recv()
                self.share(kind, cut, self.c).start()

    def finish(self):
        for kind in range(2):
            for cut in range(2):
                self.share(kind, cut, 1 - self.c).wait_recv()
                self.share(kind, cut, self.c).wait_send()
                self.over(kind, cut, self.h).wait_send()


class DownSpread:
    @staticmethod
    def scratch():
        return [dma(1), dma(2), dma(2)]

    def __init__(self, weight, out, sems):
        self.weight, self.out = weight, out
        self.d_own, self.d_x, self.d_sib = sems
        self.z, self.y, self.c, self.h = place()

    def keep(self):
        return local(self.weight, self.out.at[self.h, self.c], self.d_own.at[0])

    def over(self):
        return remote(
            self.weight, self.out.at[self.h, self.c], self.d_x.at[0], self.d_x.at[1],
            device(self.z, self.y, self.c, 1 - self.h),
        )

    def over_in(self):
        ref = self.out.at[1 - self.h, self.c]
        return remote(ref, ref, self.d_x.at[0], self.d_x.at[1], device(self.z, self.y, self.c, self.h))

    def share(self):
        ref = self.out.at[:, self.c]
        return remote(ref, ref, self.d_sib.at[0], self.d_sib.at[1], device(self.z, self.y, 1 - self.c, self.h))

    def share_in(self):
        ref = self.out.at[:, 1 - self.c]
        return remote(ref, ref, self.d_sib.at[0], self.d_sib.at[1], device(self.z, self.y, self.c, self.h))

    def start(self):
        self.keep().start()
        self.over().start()

    def relay(self):
        self.keep().wait()
        self.over_in().wait_recv()
        self.share().start()

    def finish(self):
        self.share_in().wait_recv()
        self.share().wait_send()
        self.over().wait_send()


class NoteSpread:
    @staticmethod
    def scratch():
        return [dma(16), dma(16), dma(1)]

    def __init__(self, note, out, sems):
        self.note, self.out = note, out
        self.s, self.r, self.own = sems
        self.blk, self.h = lax.axis_index("blk"), lax.axis_index("head")

    def push(self, step):
        other = (self.blk + step) % 16
        return remote(self.note, self.out.at[self.blk], self.s.at[step], self.r.at[step], (other, self.h))

    def pull(self, step):
        ref = self.out.at[(self.blk + 16 - step) % 16]
        return remote(ref, ref, self.s.at[step], self.r.at[step], (self.blk, self.h))

    def keep(self):
        return local(self.note, self.out.at[self.blk], self.own.at[0])

    def start(self):
        self.keep().start()
        for step in range(1, 16):
            self.push(step).start()

    def finish(self):
        self.keep().wait()
        for step in range(1, 16):
            self.pull(step).wait_recv()
            self.push(step).wait_send()


def split_refs(refs, counts):
    groups, at = [], 0
    for count in counts:
        groups.append(refs[at : at + count])
        at += count
    return groups


def core_kernel(
    attended, out_w, gate_in, up_in, wd, tokens, gain, cot, cot_in,
    hidden_out, active, mlp_part, gathered, grad_hidden, gain_term, gate, up,
    normed, src, total, gate_w, up_w, down_w, gate_factor, up_factor, cot_pairs, parts, stage, gate_grad, up_grad, branch,
    cot_s, stage_s, *refs,
):
    gather_sems, back_sems, share_sems, down_sems, reduce_refs, quarter_refs = split_refs(
        refs, (8, 8, 5, 3, Reduce.COUNT, 8)
    )
    z, y, c, h = place()
    greet(device(z, y, 1 - c, h))
    greet(device(z, y, c, 1 - h))
    greet_plane(2)
    gather = Gather(src, normed, gather_sems)
    back = Gather(branch, gathered, back_sems)
    share = MlpShare((gate_in, up_in), (gate_w, up_w), share_sems)
    downs = DownSpread(wd, down_w, down_sems)
    reduce = Reduce(parts, reduce_refs)
    grads = QuarterReduce((gate_w, up_w), (gate, up), quarter_refs)
    rows, width = normed.shape[1:]
    hidden = gate_w.shape[3]
    step = hidden // 2
    pair = 2 * rows
    order = (2, 0, 1, 3)

    def cot_load(place_at):
        return local(cot_in.at[pl.ds(reduce.order[place_at] * 2, 2)], cot_pairs.at[place_at % 2], cot_s.at[place_at % 2])

    cot_load(0).start()
    cot_load(1).start()

    share.start()
    for place_at in range(4):
        line = reduce.order[place_at]
        both = attended[pl.ds(pl.multiple_of(line * pair, pair), pair)]
        parts[pl.ds(line * 2, 2)] = product(both, out_w[...]).astype(jnp.bfloat16).reshape(2, rows, width)
        reduce.start(place_at)
    for place_at in range(3):
        reduce.relay(place_at)
    reduce.total(total)
    hidden_rows = tokens[...].astype(jnp.float32) + total[...]
    hidden_out[...] = hidden_rows
    src[...] = (hidden_rows * rms_scale(hidden_rows) * gain[...]).astype(jnp.bfloat16)
    gather.start()
    share.relay()
    downs.start()
    reduce.finish()

    def forward(chip, own=False):
        shard = src if own else normed.at[chip]

        @pl.loop(0, 2)
        def _(tile):
            columns = pl.ds(pl.multiple_of(tile * step, step), step)
            gate_part = product(shard[...], gate_w[:, :, :, columns].reshape(width, step))
            up_part = product(shard[...], up_w[:, :, :, columns].reshape(width, step))
            sigmoid = jax.nn.sigmoid(gate_part)
            silu = gate_part * sigmoid
            slope = sigmoid * (1.0 + gate_part * (1.0 - sigmoid))
            gate_factor[chip, :, columns] = (up_part * slope).astype(jnp.bfloat16)
            up_factor[chip, :, columns] = silu.astype(jnp.bfloat16)
            active[chip, :, columns] = (silu * up_part).astype(jnp.bfloat16)

    def forward_own(distance):
        @pl.when(z - distance >= 0)
        def _():
            forward((z - distance) * 2 + y)

        @pl.when(z + distance <= LINE - 1)
        def _():
            forward((z + distance) * 2 + y)

    def forward_other(distance):
        def one(line):
            for elem in (0, 1):
                gather.across_in(line, elem).wait_recv()
            forward(line * 2 + 1 - y)

        if distance == 0:
            one(z)
        else:

            @pl.when(z - distance >= 0)
            def _():
                one(z - distance)

            @pl.when(z + distance <= LINE - 1)
            def _():
                one(z + distance)

    def relay(distance):
        for elem in order:
            gather.relay(distance - 1, elem)

    gather.relay_b()
    share.finish()
    forward(z * 2 + y, own=True)
    relay(1)
    forward_other(0)
    forward_own(1)
    relay(2)
    forward_other(1)
    forward_own(2)
    relay(3)
    downs.relay()
    forward_other(2)
    forward_own(3)
    forward_other(3)
    gather.own_copy().wait()
    downs.finish()

    def backward(place_at):
        line = reduce.order[place_at]
        both = pl.ds(line * 2, 2)
        cot_load(place_at).wait()

        @pl.loop(0, 2)
        def _(tile):
            columns = pl.ds(pl.multiple_of(tile * step, step), step)
            grad_active = times_transposed(
                cot_pairs[place_at % 2].reshape(pair, width), down_w[tile].reshape(step, width)
            ).reshape(2, rows, step)
            gate_grad[both, :, columns] = (grad_active * gate_factor[both, :, columns].astype(jnp.float32)).astype(jnp.bfloat16)
            up_grad[both, :, columns] = (grad_active * up_factor[both, :, columns].astype(jnp.float32)).astype(jnp.bfloat16)

        if place_at < 2:
            cot_load(place_at + 2).start()

        @pl.loop(0, 4)
        def _(tile):
            columns = pl.ds(pl.multiple_of(tile * (width // 4), width // 4), width // 4)
            chips = pl.ds(tile * 2, 2)
            part = times_transposed(gate_grad[both].reshape(pair, hidden), gate_w[chips].reshape(width // 4, hidden))
            part += times_transposed(up_grad[both].reshape(pair, hidden), up_w[chips].reshape(width // 4, hidden))
            parts[both, :, columns] = part.astype(jnp.bfloat16).reshape(2, rows, width // 4)

    def stage_store(line):
        return local(stage, mlp_part.at[pl.ds(line * 2, 2)], stage_s)

    def contribute(line):
        if line:
            stage_store(line - 1).wait()

        @pl.loop(0, 4)
        def _(tile):
            columns = pl.ds(pl.multiple_of(tile * (width // 4), width // 4), width // 4)
            part = product(
                active[pl.ds(line * 2, 2)].reshape(pair, hidden), down_w[:, :, :, columns].reshape(hidden, width // 4)
            )
            stage[:, :, columns] = part.astype(jnp.bfloat16).reshape(2, rows, width // 4)

        stage_store(line).start()

    def weight_grad(kind, first, last):
        source = (gate_grad, up_grad)[kind]
        store = (gate_w, up_w)[kind]

        @pl.loop(first, last)
        def _(tile):
            columns = pl.ds(pl.multiple_of(tile * pair, pair), pair)
            part = transposed_times(
                normed[:, :, columns].reshape(8 * rows, pair), source[...].reshape(8 * rows, hidden)
            )
            store[tile] = part.astype(jnp.bfloat16).reshape(2, rows, hidden)

    at_end = jnp.logical_or(z == 0, z == LINE - 1)
    inside = jnp.logical_not(at_end)
    for place_at in range(3):
        backward(place_at)
        reduce.start(place_at)

    @pl.when(at_end)
    def _():
        reduce.relay(0)

    backward(3)
    reduce.start(3)

    @pl.when(at_end)
    def _():
        reduce.relay(1)

    @pl.when(inside)
    def _():
        reduce.relay(0)

    weight_grad(0, 0, 4)
    grads.share(0, 0).start()

    @pl.when(inside)
    def _():
        reduce.relay(1)

    reduce.relay(2)
    weight_grad(0, 4, 8)
    grads.share(0, 1).start()
    reduce.total(total)

    inputs = hidden_out[...]
    inv_scale = rms_scale(inputs)
    unit_rows = inputs * inv_scale
    grad_unit = total[...] * gain[...]
    mean = jnp.mean(grad_unit * unit_rows, axis=-1, keepdims=True)
    grad_rows = cot[...].astype(jnp.float32) + inv_scale * (grad_unit - unit_rows * mean)
    grad_hidden[...] = grad_rows
    branch[...] = grad_rows.astype(jnp.bfloat16)
    back.start()
    gain_term[...] = jnp.sum(total[...] * unit_rows, axis=0, keepdims=True)
    grads.relay(0)
    back.relay_b()
    for cut in range(2):
        weight_grad(1, cut * 4, cut * 4 + 4)
        grads.share(1, cut).start()
    for elem in order:
        back.relay(0, elem)
    grads.relay(1)
    contribute(0)
    contribute(1)
    for elem in order:
        back.relay(1, elem)
    contribute(2)
    contribute(3)
    grads.finish(0)
    for elem in order:
        back.relay(2, elem)
    grads.finish(1)
    back.finish()
    reduce.finish()
    stage_store(3).wait()
    for line in range(LINE):
        for elem in (0, 1):
            gather.across(line, elem).wait_send()
    gather.finish_sends()


def core(attended, out_w, gate, up, wd, tokens, gain, cot, cot_all):
    eight, depth, part = gate.shape
    rows, width = tokens.shape
    hidden = 2 * part

    def room(*dims, dtype=jnp.bfloat16):
        return pltpu.VMEM(dims, dtype)

    def shape(*dims, dtype=jnp.bfloat16):
        return jax.ShapeDtypeStruct(dims, dtype)

    f32 = jnp.float32
    return pl.pallas_call(
        core_kernel,
        out_shape=(
            shape(rows, width, dtype=f32),
            shape(8, rows, hidden),
            shape(8, rows, width),
            shape(8, rows, width),
            shape(rows, width, dtype=f32),
            shape(1, width, dtype=f32),
            shape(8, depth, part),
            shape(8, depth, part),
        ),
        in_specs=[INSIDE, INSIDE, ANY, ANY, ANY, INSIDE, INSIDE, INSIDE, ANY],
        out_specs=(INSIDE, INSIDE, ANY, ANY, INSIDE, INSIDE, INSIDE, INSIDE),
        scratch_shapes=[
            room(8, rows, width), room(rows, width), room(rows, width, dtype=f32),
            room(eight, 2, depth, hidden), room(eight, 2, depth, hidden), room(2, 2, *wd.shape),
            room(8, rows, hidden), room(8, rows, hidden),
            room(2, 2, rows, width), room(8, rows, width), room(2, rows, width),
            room(8, rows, hidden), room(8, rows, hidden), room(rows, width),
            dma(2), dma(),
        ]
        + Gather.scratch()
        + Gather.scratch()
        + MlpShare.scratch()
        + DownSpread.scratch()
        + Reduce.scratch(width)
        + QuarterReduce.scratch(depth, hidden),
        compiler_params=kernel_params(8),
        name="core",
    )(attended, out_w, gate, up, wd, tokens, gain, cot, cot_all)


def column_of(row):
    size = row.shape[1]
    same = lax.broadcasted_iota(jnp.int32, (size, size), 0) == lax.broadcasted_iota(jnp.int32, (size, size), 1)
    return jnp.sum(jnp.where(same, row, 0.0), axis=1, keepdims=True)


def row_of(column):
    size = column.shape[0]
    same = lax.broadcasted_iota(jnp.int32, (size, size), 0) == lax.broadcasted_iota(jnp.int32, (size, size), 1)
    return jnp.sum(jnp.where(same, column, 0.0), axis=0, keepdims=True)


def front_kernel(
    tokens, cot, note, inv_freqs, wq, wk, wv, wo, wg, wu,
    kv_out, normed_out, qkv_out, out_w, notes, gain, mlp_gain, cos_table, sine_table, query, attended_out, attended_low_out,
    log_out, cot_out, gate, up,
    gathered, normed, qkv_w, query_ids, key_ids, kv, keys, scores, total,
    own, x_s, x_r, c_s, c_r, store_s, *sems,
):
    z, y, c, h = place()
    tok_sems, note_sems, attn_sems, cot_sems, mlp_sems = split_refs(sems, (8, 3, AttnSpread.COUNT, 8, 3))
    greet_all(16, 2)
    rows, width = tokens.shape[0], HD
    pair = 2 * rows
    tok = Gather(tokens, gathered, tok_sems)
    notices = NoteSpread(note, notes, note_sems)
    attn = AttnSpread((wq, wk, wv, wo), (qkv_w, out_w), attn_sems)
    cots = Gather(cot, cot_out, cot_sems)
    mlp = MlpSpread((wg, wu), (gate, up), mlp_sems)

    def keep(cut):
        part = pl.ds(cut * 2, 2)
        return local(kv.at[part], keys.at[part, c, h], own.at[cut])

    def over(cut, half):
        part = pl.ds(cut * 2, 2)
        return remote(kv.at[part], keys.at[part, c, half], x_s.at[cut], x_r.at[cut], device(z, y, c, 1 - h))

    def share(cut, core):
        ref = keys.at[pl.ds(cut * 2, 2), core]
        return remote(ref, ref, c_s.at[cut], c_r.at[cut], device(z, y, 1 - c, h))

    def tables():
        for blk in range(16):
            gain[:, pl.ds(blk * rows, rows)] = notes[blk, 4:5, :]
            mlp_gain[:, pl.ds(blk * rows, rows)] = notes[blk, 5:6, :]
        for chip in range(8):
            part = pl.ds(chip * rows, rows)
            mine = notes[2 * chip + c]
            angles = column_of(jnp.where(h == 0, mine[0:1], mine[1:2])) * inv_freqs[...]
            cos_table[part] = jnp.cos(angles)
            sine_table[part] = jnp.sin(angles)
            query_ids[part] = column_of(jnp.where(h == 0, mine[2:3], mine[3:4]))
            for piece in range(4):
                key_ids[chip, :, pl.ds(piece * rows, rows)] = notes[2 * chip + piece // 2, 2 + piece % 2 : 3 + piece % 2, :]

    def project(cut):
        part = pl.ds(cut * pair, pair)
        inputs = gathered[pl.ds(cut * 2, 2)].reshape(pair, tokens.shape[1]).astype(jnp.float32)
        rows_normed = (inputs * rms_scale(inputs) * gain[...]).astype(jnp.bfloat16)
        normed[part] = rows_normed
        cos_rows, sine_rows = cos_table[part], sine_table[part]

        def turn(lower, upper):
            return (
                (lower * cos_rows - upper * sine_rows).astype(jnp.bfloat16),
                (upper * cos_rows + lower * sine_rows).astype(jnp.bfloat16),
            )

        def weight(columns):
            return qkv_w[:, :, :, columns].reshape(tokens.shape[1], columns.size)

        half = width // 2
        projected = product(rows_normed, weight(pl.ds(0, width)))
        lower, upper = turn(projected[:, :half], projected[:, half:])
        query[part, :half] = (lower.astype(jnp.float32) * HD**-0.5).astype(jnp.bfloat16)
        query[part, half:] = (upper.astype(jnp.float32) * HD**-0.5).astype(jnp.bfloat16)
        projected = product(rows_normed, weight(pl.ds(width, 2 * width)))
        lower, upper = turn(projected[:, :half], projected[:, half:width])
        both = pl.ds(cut * 2, 2)
        kv[both, :, :half] = lower.reshape(2, rows, half)
        kv[both, :, half:width] = upper.reshape(2, rows, half)
        kv[both, :, width:] = projected[:, width:].astype(jnp.bfloat16).reshape(2, rows, width)
        over(cut, h).start()
        keep(cut).start()

    def pass_on(cut):
        keep(cut).wait()
        over(cut, 1 - h).wait_recv()
        share(cut, c).start()

    def attend(place_at):
        part = pl.ds(place_at * pair, pair)
        count = min(2 * place_at + 3, 8)
        ids = query_ids[part]

        def maxima(block, best):
            key = keys[block, :, :, :, :width].reshape(4 * rows, width)
            part_scores = times_transposed(query[part], key)
            part_scores = jnp.where(key_ids[block] <= ids, part_scores, -1e30)
            scores[block] = part_scores
            for lane in range(4 * rows // 128):
                best = jnp.maximum(best, part_scores[:, lane * 128 : lane * 128 + 128])
            return best

        best = lax.fori_loop(0, count, maxima, jnp.full((pair, 128), -1e30, jnp.float32))
        row_max = jnp.max(best, axis=1, keepdims=True)
        total[...] = jnp.zeros_like(total)

        def mix(block, sums):
            weights = jnp.exp(scores[block] - row_max)
            value = keys[block, :, :, :, width:].reshape(4 * rows, width)
            total[...] += product(weights.astype(jnp.bfloat16), value)
            for lane in range(4 * rows // 128):
                sums = sums + weights[:, lane * 128 : lane * 128 + 128]
            return sums

        sums = lax.fori_loop(0, count, mix, jnp.zeros((pair, 128), jnp.float32))
        row_sum = jnp.sum(sums, axis=1, keepdims=True)
        mixed = total[...] / row_sum
        attended_out[part] = mixed
        attended_low_out[part] = mixed.astype(jnp.bfloat16)
        log_out[place_at] = row_of(row_max + jnp.log(row_sum))

    order = (2, 0, 1, 3)
    attn.start()
    tok.start()
    notices.start()
    tok.relay_b()
    attn.relay(0)
    for elem in order:
        tok.relay(0, elem)
    attn.relay(1)
    attn.relay(2)
    for elem in order:
        tok.relay(1, elem)
    attn.relay(3)
    attn.relay_out()
    notices.finish()
    tables()
    for elem in order:
        tok.relay(2, elem)
    cots.start()
    mlp.start()
    for step in range(LINE):
        attn.relay_share(step)
    attn.relay_out_share()
    tok.finish()
    attn.finish()
    store_qkv = local(qkv_w, qkv_out, store_s.at[0])
    store_qkv.start()
    for cut in range(LINE):
        project(cut)
    store_normed = local(normed, normed_out, store_s.at[1])
    store_normed.start()
    cots.relay_b()
    for elem in order:
        cots.relay(0, elem)
    pass_on(0)
    pass_on(1)
    share(0, 1 - c).wait_recv()
    share(1, 1 - c).wait_recv()
    attend(0)
    for elem in order:
        cots.relay(1, elem)
    pass_on(2)
    share(2, 1 - c).wait_recv()
    attend(1)
    pass_on(3)
    share(3, 1 - c).wait_recv()
    store = local(keys, kv_out, store_s.at[2])
    store.start()
    attend(2)
    for elem in order:
        cots.relay(2, elem)
    attend(3)
    cots.finish()
    mlp.finish()
    for cut in range(LINE):
        share(cut, c).wait_send()
        over(cut, h).wait_send()
    store.wait()
    store_normed.wait()
    store_qkv.wait()


def front(tokens, cot, note, inv_freqs, wq, wk, wv, wo, wg, wu):
    rows, width = tokens.shape
    depth, part = wg.shape[0], wg.shape[1] // 8
    token_rows = 8 * rows

    def room(*dims, dtype=jnp.bfloat16):
        return pltpu.VMEM(dims, dtype)

    def shape(*dims, dtype=jnp.bfloat16):
        return jax.ShapeDtypeStruct(dims, dtype)

    f32 = jnp.float32
    return pl.pallas_call(
        front_kernel,
        out_shape=(
            shape(8, 2, 2, rows, 2 * HD),
            shape(token_rows, width),
            shape(8, 2, depth, 3 * HD),
            shape(2, 2, wo.shape[0], width),
            shape(16, *note.shape, dtype=f32),
            shape(1, width, dtype=f32),
            shape(1, width, dtype=f32),
            shape(token_rows, HD // 2, dtype=f32),
            shape(token_rows, HD // 2, dtype=f32),
            shape(token_rows, HD),
            shape(token_rows, HD, dtype=f32),
            shape(token_rows, HD),
            shape(LINE, 1, token_rows // LINE, dtype=f32),
            shape(8, *cot.shape),
            shape(8, depth, part),
            shape(8, depth, part),
        ),
        in_specs=[INSIDE] * 10,
        out_specs=(ANY, ANY, ANY, ANY) + (INSIDE,) * 9 + (ANY, ANY, ANY),
        scratch_shapes=[
            room(8, rows, width),
            room(token_rows, width),
            room(8, 2, depth, 3 * HD),
            room(token_rows, 1, dtype=f32),
            room(8, 1, 4 * rows, dtype=f32),
            room(8, rows, 2 * HD),
            room(8, 2, 2, rows, 2 * HD),
            room(8, token_rows // LINE, 4 * rows, dtype=f32),
            room(token_rows // LINE, HD, dtype=f32),
        ]
        + [dma(4)] * 5
        + [dma(3)]
        + Gather.scratch()
        + NoteSpread.scratch()
        + AttnSpread.scratch(depth)
        + Gather.scratch()
        + MlpSpread.scratch(),
        compiler_params=kernel_params(3),
        name="front",
    )(tokens, cot, note, inv_freqs, wq, wk, wv, wo, wg, wu)


class QuarterReduce:
    @staticmethod
    def scratch(depth, wide):
        sib = pltpu.VMEM((8, depth, wide), jnp.bfloat16)
        over = pltpu.VMEM((8, depth, wide // 2), jnp.bfloat16)
        return [sib, sib, over, over] + [dma(2, 2)] * 4

    def __init__(self, store, outs, refs):
        self.store, self.outs = store, outs
        self.sib, self.box = refs[0:2], refs[2:4]
        self.c_s, self.c_r, self.x_s, self.x_r = refs[4:]
        self.z, self.y, self.c, self.h = place()
        self.part = self.box[0].shape[2]

    def columns(self, half):
        return pl.ds(pl.multiple_of(half * self.part, self.part), self.part)

    def share(self, kind, cut):
        chips = pl.ds(cut * 4, 4)
        return remote(
            self.store[kind].at[chips, 1 - self.c], self.sib[kind].at[chips], self.c_s.at[kind, cut],
            self.c_r.at[kind, cut], device(self.z, self.y, 1 - self.c, self.h),
        )

    def over(self, kind, cut):
        chips = pl.ds(cut * 4, 4)
        return remote(
            self.store[kind].at[chips, self.c, :, self.columns(1 - self.h)], self.box[kind].at[chips],
            self.x_s.at[kind, cut], self.x_r.at[kind, cut], device(self.z, self.y, self.c, 1 - self.h),
        )

    def relay(self, kind):
        columns = self.columns(1 - self.h)
        for cut in range(2):
            self.share(kind, cut).wait_recv()

            @pl.loop(cut * 4, cut * 4 + 4)
            def _(chip):
                add_into(self.store[kind].at[chip, self.c, :, columns], self.sib[kind].at[chip, :, columns])

            self.over(kind, cut).start()

    def finish(self, kind):
        columns = self.columns(self.h)
        for cut in range(2):
            self.over(kind, cut).wait_recv()

            @pl.loop(cut * 4, cut * 4 + 4)
            def _(chip):
                total = self.store[kind][chip, self.c, :, columns].astype(jnp.float32)
                total += self.sib[kind][chip, :, columns].astype(jnp.float32)
                total += self.box[kind][chip].astype(jnp.float32)
                self.outs[kind][chip] = total.astype(jnp.bfloat16)

        for cut in range(2):
            self.share(kind, cut).wait_send()
            self.over(kind, cut).wait_send()


class QuarterScatter:
    @staticmethod
    def scratch():
        return [dma(2, 8), dma(2, 8), dma(2)]

    def __init__(self, quarters, outs, sems):
        self.quarters, self.outs = quarters, outs
        self.s, self.r, self.own = sems
        self.z, self.y, self.c, self.h = place()
        self.chip = self.z * 2 + self.y
        self.part = quarters[0].shape[2]

    def columns(self, chip):
        return pl.ds(pl.multiple_of(chip * self.part, self.part), self.part)

    def push(self, kind, step):
        target = (self.chip + step) % 8
        return remote(
            self.quarters[kind].at[target], self.outs[kind].at[:, self.columns(self.chip)], self.s.at[kind, step],
            self.r.at[kind, step], device(target // 2, target % 2, self.c, self.h),
        )

    def pull(self, kind, step):
        ref = self.outs[kind].at[:, self.columns((self.chip + 8 - step) % 8)]
        return remote(ref, ref, self.s.at[kind, step], self.r.at[kind, step], device(self.z, self.y, self.c, self.h))

    def keep(self, kind):
        return local(self.quarters[kind].at[self.chip], self.outs[kind].at[:, self.columns(self.chip)], self.own.at[kind])

    def start(self):
        for kind in range(2):
            self.keep(kind).start()
            for step in range(1, 8):
                self.push(kind, step).start()

    def finish(self):
        for kind in range(2):
            self.keep(kind).wait()
            for step in range(1, 8):
                self.pull(kind, step).wait_recv()
                self.push(kind, step).wait_send()


class DownReduce:
    @staticmethod
    def scratch(rows, width):
        return [
            pltpu.VMEM((2, 2, rows, width), jnp.bfloat16),
            pltpu.VMEM((2, rows, width), jnp.bfloat16),
            pltpu.VMEM((rows, width), jnp.bfloat16),
            dma(2), dma(2),
        ]

    def __init__(self, out, refs):
        self.out = out
        self.store, self.sib, self.box, self.c_sr, self.x_sr = refs
        self.z, self.y, self.c, self.h = place()

    def share(self):
        return remote(
            self.store.at[:, 1 - self.c], self.sib, self.c_sr.at[0], self.c_sr.at[1],
            device(self.z, self.y, 1 - self.c, self.h),
        )

    def over(self):
        return remote(
            self.store.at[1 - self.h, self.c], self.box, self.x_sr.at[0], self.x_sr.at[1],
            device(self.z, self.y, self.c, 1 - self.h),
        )

    def relay(self):
        self.share().wait_recv()
        add_into(self.store.at[1 - self.h, self.c], self.sib.at[1 - self.h])
        self.over().start()

    def finish(self):
        self.over().wait_recv()
        total = self.store[self.h, self.c].astype(jnp.float32) + self.sib[self.h].astype(jnp.float32)
        self.out[...] = total + self.box[...].astype(jnp.float32)
        self.share().wait_send()
        self.over().wait_send()


class OutGrad:
    @staticmethod
    def scratch(rows, width):
        def room(*dims):
            return pltpu.VMEM(dims, jnp.bfloat16)

        return [room(2, 2, rows, width), room(2, rows, width), room(2, rows, width), dma(2), dma(2), dma(2), dma(1)]

    def __init__(self, out, refs):
        self.out = out
        self.store, self.sib, self.box, self.c_sr, self.x_sr, self.y_sr, self.own = refs
        self.z, self.y, self.c, self.h = place()
        self.me = device(self.z, self.y, self.c, self.h)
        self.owner = self.h == self.y

    def share(self):
        return remote(
            self.store.at[:, 1 - self.c], self.sib, self.c_sr.at[0], self.c_sr.at[1],
            device(self.z, self.y, 1 - self.c, self.h),
        )

    def over(self):
        return remote(
            self.store.at[:, self.c], self.box, self.x_sr.at[0], self.x_sr.at[1],
            device(self.z, self.y, self.c, 1 - self.h),
        )

    def move(self):
        return remote(
            self.store.at[1 - self.y, self.c], self.out, self.y_sr.at[0], self.y_sr.at[1],
            device(self.z, 1 - self.y, self.c, self.h),
        )

    def keep(self):
        return local(self.store.at[self.y, self.c], self.out, self.own.at[0])

    def relay(self):
        self.share().wait_recv()
        for pair in range(2):
            add_into(self.store.at[pair, self.c], self.sib.at[pair])

        @pl.when(jnp.logical_not(self.owner))
        def _():
            self.over().start()

    def send(self):
        @pl.when(self.owner)
        def _():
            self.over().wait_recv()
            for pair in range(2):
                add_into(self.store.at[pair, self.c], self.box.at[pair])
            self.move().start()
            self.keep().start()

    def finish(self):
        self.share().wait_send()

        @pl.when(jnp.logical_not(self.owner))
        def _():
            remote(self.out, self.out, self.y_sr.at[0], self.y_sr.at[1], self.me).wait_recv()
            self.over().wait_send()

        @pl.when(self.owner)
        def _():
            self.keep().wait()
            self.move().wait_send()


def attend_back_kernel(
    query, keys_in, branch_in, mlp_part, hidden, out_w, attended, attended_low, log_row, notes, cos_table, sine_table,
    gate_in, up_in,
    side_out, grad_query, output, gate, up, out_grad,
    mlp_parts, mlp_total, keys, branch, grad_out, delta_row, query_row, key_column, grad_rot, parts, grad_key, grad_value, sib_in, x_in, z_in,
    load_s, c_s, c_r, x_s, x_r, z_s, z_r, *sems,
):
    z, y, c, h = place()
    mate = z + 1 - 2 * (z % 2)
    loads = [local(keys_in, keys, load_s.at[0]), local(branch_in, branch, load_s.at[1])]
    load_mlp = local(mlp_part, mlp_parts, load_s.at[2])
    load_mlp.start()
    for load in loads:
        load.start()
    greet_all(16, 2)
    scatter_sems, out_refs, reduce_refs = split_refs(sems, (3, 7, Reduce.COUNT))
    reduce = Reduce(mlp_parts, reduce_refs)
    load_mlp.wait()
    for place_at in range(4):
        reduce.start(place_at)
    scatter = QuarterScatter((gate_in, up_in), (gate, up), scatter_sems)
    outs = OutGrad(out_grad, out_refs)
    scatter.start()
    width = query.shape[1]
    rows = branch.shape[1]
    pair = 2 * rows
    block_rows = 4 * rows

    def share(block):
        return remote(
            parts.at[block, 1 - c], sib_in.at[block], c_s.at[block], c_r.at[block], device(z, y, 1 - c, h)
        )

    def over(block):
        return remote(
            parts.at[block, c, 1 - h], x_in.at[block], x_s.at[block], x_r.at[block], device(z, y, c, 1 - h)
        )

    def columns(kind):
        return pl.ds(pl.multiple_of(kind * width, width), width)

    def across(block):
        return remote(
            parts.at[block, c, h, :, columns(1 - z % 2)], z_in.at[block], z_s.at[block], z_r.at[block],
            device(mate, y, c, h),
        )

    def stage_two(block):
        share(block).wait_recv()
        add_into(parts.at[block, c, 1 - h], sib_in.at[block, 1 - h])
        over(block).start()

    def stage_three(block):
        over(block).wait_recv()
        add_into(parts.at[block, c, h], sib_in.at[block, h], x_in.at[block])
        across(block).start()

    def turn_back(values, part):
        half = width // 2
        lower, upper = values[:, :half], values[:, half:]
        cos_rows, sine_rows = cos_table[part], sine_table[part]
        return (
            (lower * cos_rows + upper * sine_rows).astype(jnp.bfloat16),
            (upper * cos_rows - lower * sine_rows).astype(jnp.bfloat16),
        )

    def stage_four(block):
        across(block).wait_recv()
        total = parts[block, c, h, :, columns(z % 2)].astype(jnp.float32) + z_in[block].astype(jnp.float32)
        part = pl.ds(block * rows, rows)

        @pl.when(z % 2 == 0)
        def _():
            lower, upper = turn_back(total, part)
            side_out[part, : width // 2] = lower
            side_out[part, width // 2 :] = upper

        @pl.when(z % 2 == 1)
        def _():
            side_out[part] = total.astype(jnp.bfloat16)

    for chip in range(8):
        mine = notes[2 * chip + c]
        query_row[chip // 2, :, pl.ds((chip % 2) * rows, rows)] = jnp.where(h == 0, mine[2:3], mine[3:4])
        for piece in range(4):
            row = notes[2 * chip + piece // 2, 2 + piece % 2 : 3 + piece % 2, :]
            key_column[chip, pl.ds(piece * rows, rows)] = column_of(row)
    for load in loads:
        load.wait()
    grad_rot[...] = jnp.zeros_like(grad_rot)
    for place_at in range(LINE):
        part = pl.ds(place_at * pair, pair)
        grad_rows = times_transposed(branch[pl.ds(place_at * 2, 2)].reshape(pair, branch.shape[2]), out_w[...])
        grad_rows = grad_rows.astype(jnp.bfloat16)
        grad_out[part] = grad_rows
        delta = jnp.sum(grad_rows.astype(jnp.float32) * attended[part], axis=1, keepdims=True)
        delta_row[place_at] = row_of(delta)
    out_store = out_refs[0]

    @pl.loop(0, 4)
    def _(tile):
        tile_columns = pl.ds(pl.multiple_of(tile * 512, 512), 512)
        part = transposed_times(attended_low[...], branch[:, :, tile_columns].reshape(8 * rows, 512))
        out_store[:, :, :, tile_columns] = part.astype(jnp.bfloat16).reshape(2, 2, out_store.shape[2], 512)

    outs.share().start()
    for block in range(8):
        key = keys[block, :, :, :, :width].reshape(block_rows, width)
        value = keys[block, :, :, :, width:].reshape(block_rows, width)
        grad_key[...] = jnp.zeros_like(grad_key)
        grad_value[...] = jnp.zeros_like(grad_value)

        @pl.loop(max(0, (block - 1) // 2), LINE)
        def _(place_at):
            part = pl.ds(pl.multiple_of(place_at * pair, pair), pair)
            part_scores = times_transposed(key, query[part])
            visible = key_column[block] <= query_row[place_at]
            weights = jnp.where(visible, jnp.exp(part_scores - log_row[place_at]), 0.0)
            grad_weights = times_transposed(value, grad_out[part])
            grad_scores = (weights * (grad_weights - delta_row[place_at])).astype(jnp.bfloat16)
            grad_key[...] += product(grad_scores, query[part])
            grad_value[...] += product(weights.astype(jnp.bfloat16), grad_out[part])
            grad_rot[part] += transposed_times(grad_scores, key)

        parts[block, :, :, :, :width] = grad_key[...].astype(jnp.bfloat16).reshape(2, 2, rows, width)
        parts[block, :, :, :, width:] = grad_value[...].astype(jnp.bfloat16).reshape(2, 2, rows, width)
        share(block).start()
        if block == 0:
            outs.relay()
        if block >= 1:
            stage_two(block - 1)
        if block >= 4:
            stage_three(block - 4)
    stage_two(7)
    outs.send()

    @pl.when(jnp.logical_or(z == 0, z == LINE - 1))
    def _():
        reduce.relay(0)

    for place_at in range(LINE):
        part = pl.ds(place_at * pair, pair)
        lower, upper = turn_back(grad_rot[part] * HD**-0.5, part)
        grad_query[part, : width // 2] = lower
        grad_query[part, width // 2 :] = upper
    for block in range(4, 8):
        stage_three(block)
        stage_four(block - 4)

    @pl.when(jnp.logical_and(z > 0, z < LINE - 1))
    def _():
        reduce.relay(0)

    for block in range(4, 8):
        stage_four(block)
    reduce.relay(1)
    reduce.relay(2)
    for block in range(8):
        share(block).wait_send()
        over(block).wait_send()
        across(block).wait_send()
    outs.finish()
    reduce.total(mlp_total)
    output[...] = (hidden[...] + mlp_total[...]).astype(jnp.bfloat16)
    scatter.finish()
    reduce.finish()


def attend_back(
    query, keys, branch, mlp_part, hidden, out_w, attended, attended_low, log_row, notes, cos_table, sine_table, gate, up,
    out_rows,
):
    eight, _, _, rows, width = keys.shape
    tokens = query.shape[0]
    depth, part = gate.shape[1:]

    def room(*dims, dtype=jnp.bfloat16):
        return pltpu.VMEM(dims, dtype)

    def shape(*dims, dtype=jnp.bfloat16):
        return jax.ShapeDtypeStruct(dims, dtype)

    f32 = jnp.float32
    return pl.pallas_call(
        attend_back_kernel,
        out_shape=(
            shape(tokens, HD),
            shape(tokens, HD),
            shape(*hidden.shape),
            shape(depth, 8 * part),
            shape(depth, 8 * part),
            shape(out_rows, out_w.shape[1]),
        ),
        in_specs=[INSIDE, ANY, ANY, ANY] + [INSIDE] * 10,
        out_specs=(INSIDE, INSIDE, INSIDE, ANY, ANY, ANY),
        scratch_shapes=[
            room(*mlp_part.shape), room(*hidden.shape, dtype=f32), room(*keys.shape), room(*branch.shape), room(tokens, HD),
            room(LINE, 1, tokens // LINE, dtype=f32), room(LINE, 1, tokens // LINE, dtype=f32),
            room(8, 4 * rows, 1, dtype=f32), room(tokens, HD, dtype=f32), room(*keys.shape),
            room(4 * rows, HD, dtype=f32), room(4 * rows, HD, dtype=f32),
            room(eight, 2, rows, width), room(eight, rows, width), room(eight, rows, HD),
            dma(3),
        ]
        + [dma(8)] * 6
        + QuarterScatter.scratch()
        + OutGrad.scratch(out_rows, out_w.shape[1])
        + Reduce.scratch(hidden.shape[1]),
        compiler_params=kernel_params(11),
        name="attend_back",
    )(
        query, keys, branch, mlp_part, hidden, out_w, attended, attended_low, log_row, notes, cos_table, sine_table, gate, up
    )


class HeadGrads:
    @staticmethod
    def scratch(depth):
        def room(*dims):
            return pltpu.VMEM(dims, jnp.bfloat16)

        return [
            room(LINE, 2, 2, depth, HD), room(LINE, 2, 2, depth, HD),
            room(LINE, 2, depth, HD), room(LINE, 2, depth, HD),
            room(LINE, depth, HD), room(LINE, depth, HD),
            dma(2), dma(2), dma(2), dma(2), dma(3, 4), dma(3, 4), dma(3),
        ]

    def __init__(self, outs, refs):
        self.outs = outs
        self.store, self.sib, self.box = refs[0:2], refs[2:4], refs[4:6]
        (self.c_s, self.c_r, self.x_s, self.x_r, self.s, self.r, self.own) = refs[6:]
        self.z, self.y, self.c, self.h = place()
        self.me = device(self.z, self.y, self.c, self.h)

    def share(self, i):
        return remote(
            self.store[i].at[:, :, 1 - self.c], self.sib[i], self.c_s.at[i], self.c_r.at[i],
            device(self.z, self.y, 1 - self.c, self.h),
        )

    def over(self, i):
        return remote(
            self.store[i].at[:, 1 - self.h, self.c], self.box[i], self.x_s.at[i], self.x_r.at[i],
            device(self.z, self.y, self.c, 1 - self.h),
        )

    def target(self, kind, line):
        start = line * HD if kind == 0 else (line // 2) * HD
        return self.outs[kind].at[:, pl.ds(pl.multiple_of(start, HD), HD)]

    def push(self, kind, step):
        line = (self.z + step) % LINE
        return remote(
            self.store[min(kind, 1)].at[line, self.h, self.c], self.target(kind, self.z), self.s.at[kind, step],
            self.r.at[kind, self.z], device(line, self.h, self.c, self.y),
        )

    def keep(self, kind):
        return local(self.store[min(kind, 1)].at[self.z, self.h, self.c], self.target(kind, self.z), self.own.at[kind])

    def stays(self, step):
        return self.h == self.y if step == 0 else self.h < 0

    def pull(self, kind, line):
        ref = self.target(kind, line)
        return remote(ref, ref, self.s.at[kind, 0], self.r.at[kind, line], self.me)

    def relay(self, i):
        self.share(i).wait_recv()

        @pl.loop(0, LINE)
        def _(line):
            for pair in range(2):
                add_into(self.store[i].at[line, pair, self.c], self.sib[i].at[line, pair])

        self.over(i).start()

    def each_kind(self, i, act):
        if i == 0:
            act(0)
        else:
            for kind in (1, 2):

                @pl.when(self.z % 2 == kind - 1)
                def _():
                    act(kind)

    def scatter(self, i):
        self.over(i).wait_recv()

        @pl.loop(0, LINE)
        def _(line):
            add_into(self.store[i].at[line, self.h, self.c], self.box[i].at[line])

        def act(kind):
            for step in range(4):

                @pl.when(self.stays(step))
                def _():
                    self.keep(kind).start()

                @pl.when(jnp.logical_not(self.stays(step)))
                def _():
                    self.push(kind, step).start()

        self.each_kind(i, act)

    def finish(self):
        for kind in range(3):
            for line in range(LINE):
                if kind and line % 2 != kind - 1:
                    continue
                from_self = (self.z == line) & (self.y == self.h)

                @pl.when(from_self)
                def _():
                    self.keep(kind).wait()

                @pl.when(jnp.logical_not(from_self))
                def _():
                    self.pull(kind, line).wait_recv()

        def act(kind):
            for step in range(4):

                @pl.when(jnp.logical_not(self.stays(step)))
                def _():
                    self.push(kind, step).wait_send()

        for i in range(2):
            self.each_kind(i, act)
            self.over(i).wait_send()
            self.share(i).wait_send()


class GainSum:
    @staticmethod
    def scratch(rows):
        return [
            pltpu.VMEM((16, 8, rows), jnp.float32), pltpu.VMEM((32, 8, rows), jnp.float32), dma(32), dma(32),
        ]

    def __init__(self, out, refs):
        self.out = out
        self.terms, self.box, self.s, self.r = refs
        self.blk, self.h = lax.axis_index("blk"), lax.axis_index("head")

    def push(self, step):
        other = (self.blk + step // 2) % 16
        return remote(
            self.terms.at[other], self.box.at[step], self.s.at[step], self.r.at[step], (other, (self.h + step % 2) % 2)
        )

    def start(self, attn_term, mlp_term):
        rows = self.terms.shape[2]
        self.terms[...] = jnp.zeros_like(self.terms)
        for blk in range(16):
            part = pl.ds(blk * rows, rows)
            self.terms[blk, 0:1] = attn_term[:, part]
            self.terms[blk, 1:2] = mlp_term[:, part]
        for step in range(1, 32):
            self.push(step).start()

    def finish(self):
        total = self.terms[self.blk]
        for step in range(1, 32):
            self.push(step).wait_recv()
            total += self.box[step]
        self.out[...] = total
        for step in range(1, 32):
            self.push(step).wait_send()


def close_kernel(
    normed_in, qkv_w, active_in, cot_in, grad_query, grad_side, grad_hidden, tokens, gain, mlp_term,
    tokens_grad, gains, down, query, key, value,
    normed, weight, parts, active, cot, total, attn_term, load_s, *refs,
):
    reduce_refs, head_refs, gain_refs, down_refs = split_refs(refs, (Reduce.COUNT, 13, 4, 5))
    z, y, c, h = place()
    loads = [
        local(active_in, active, load_s.at[3]),
        local(cot_in, cot, load_s.at[4]),
    ]
    load = local(normed_in, normed, load_s.at[0])
    load_q = local(qkv_w.at[:, :, :, pl.ds(0, HD)], weight.at[0], load_s.at[1])
    side_columns = pl.ds(pl.multiple_of((1 + z % 2) * HD, HD), HD)
    load_side = local(qkv_w.at[:, :, :, side_columns], weight.at[1], load_s.at[2])
    load_q.start()
    load_side.start()
    load.start()
    for later in loads:
        later.start()
    greet_all(16, 2)
    reduce = Reduce(parts, reduce_refs)
    downs = DownReduce(down, down_refs)
    heads = HeadGrads((query, key, value), head_refs)
    gain_sum = GainSum(gains, gain_refs)
    rows, width = parts.shape[1:]
    pair = 2 * rows
    depth = head_refs[0].shape[3]
    load_q.wait()
    load_side.wait()
    load.wait()
    attn_term[...] = jnp.zeros_like(attn_term)
    for place_at in range(4):
        line = reduce.order[place_at]
        both = pl.ds(pl.multiple_of(line * pair, pair), pair)

        @pl.loop(0, 4)
        def _(tile):
            columns = pl.ds(pl.multiple_of(tile * (width // 4), width // 4), width // 4)
            part = times_transposed(grad_query[both], weight[0, pl.ds(tile * 2, 2)].reshape(width // 4, HD))
            part += times_transposed(grad_side[both], weight[1, pl.ds(tile * 2, 2)].reshape(width // 4, HD))
            parts[pl.ds(line * 2, 2), :, columns] = part.astype(jnp.bfloat16).reshape(2, rows, width // 4)
            scaled = part * normed[both, columns].astype(jnp.float32)
            attn_term[:, columns] += jnp.sum(scaled, axis=0, keepdims=True)

        reduce.start(place_at)
    attn_term[...] = attn_term[...] / gain[...]
    gain_sum.start(attn_term, mlp_term)
    for i, source in enumerate((grad_query, grad_side)):

        @pl.loop(0, 4)
        def _(tile):
            columns = pl.ds(pl.multiple_of(tile * 4 * depth, 4 * depth), 4 * depth)
            part = transposed_times(normed[:, columns], source[...])
            head_refs[i][tile] = part.astype(jnp.bfloat16).reshape(2, 2, depth, HD)

        heads.share(i).start()
    heads.relay(0)
    heads.relay(1)
    reduce.relay(0)
    for later in loads:
        later.wait()
    down_rows = down.shape[0]

    def down_grad(tile):
        columns = pl.ds(tile * down_rows, down_rows)

        @pl.loop(0, 4)
        def _(piece):
            wide = pl.ds(pl.multiple_of(piece * (width // 4), width // 4), width // 4)
            part = transposed_times(
                active[:, :, columns].reshape(8 * rows, down_rows), cot[:, :, wide].reshape(8 * rows, width // 4)
            )
            down_refs[0][tile // 2, tile % 2, :, wide] = part.astype(jnp.bfloat16)

    for tile in range(4):
        down_grad(tile)
    downs.share().start()
    heads.scatter(0)
    reduce.relay(1)
    heads.scatter(1)
    downs.relay()
    reduce.relay(2)
    reduce.total(total)
    inputs = tokens[...].astype(jnp.float32)
    inv_scale = rms_scale(inputs)
    unit_rows = inputs * inv_scale
    grad_unit = total[...] * gain[...]
    mean = jnp.mean(grad_unit * unit_rows, axis=-1, keepdims=True)
    tokens_grad[...] = (grad_hidden[...] + inv_scale * (grad_unit - unit_rows * mean)).astype(jnp.bfloat16)
    gain_sum.finish()
    downs.finish()
    heads.finish()
    reduce.finish()


def close(normed, qkv_w, active, cot, grad_query, grad_side, grad_hidden, tokens, gain, mlp_term):
    rows, width = tokens.shape
    down_rows = active.shape[2] // 4
    depth = qkv_w.shape[2]

    def room(*dims, dtype=jnp.bfloat16):
        return pltpu.VMEM(dims, dtype)

    def shape(*dims, dtype=jnp.bfloat16):
        return jax.ShapeDtypeStruct(dims, dtype)

    f32 = jnp.float32
    return pl.pallas_call(
        close_kernel,
        out_shape=(
            shape(rows, width),
            shape(8, rows, dtype=f32),
            shape(down_rows, width, dtype=f32),
            shape(depth, 4 * HD), shape(depth, 2 * HD), shape(depth, 2 * HD),
        ),
        in_specs=[ANY] * 4 + [INSIDE] * 6,
        out_specs=(INSIDE, INSIDE, INSIDE, ANY, ANY, ANY),
        scratch_shapes=[
            room(*normed.shape), room(2, 8, 2, depth, HD), room(8, rows, width),
            room(*active.shape), room(*cot.shape),
            room(rows, width, dtype=f32), room(1, width, dtype=f32), dma(5),
        ]
        + Reduce.scratch(width)
        + HeadGrads.scratch(depth)
        + GainSum.scratch(rows)
        + DownReduce.scratch(down_rows, width),
        compiler_params=kernel_params(6),
        name="close",
    )(normed, qkv_w, active, cot, grad_query, grad_side, grad_hidden, tokens, gain, mlp_term)


def widen_kernel(*refs):
    half = len(refs) // 2
    for source, target in zip(refs[:half], refs[half:]):
        target[...] = source[...].astype(target.dtype)


def widen(arrays, dtypes):
    return pl.pallas_call(
        widen_kernel,
        out_shape=tuple(jax.ShapeDtypeStruct(array.shape, dtype) for array, dtype in zip(arrays, dtypes)),
        in_specs=[INSIDE] * len(arrays),
        out_specs=(INSIDE,) * len(arrays),
        compiler_params=pltpu.CompilerParams(vmem_limit_bytes=VMEM_BYTES),
        name="widen",
    )(*arrays)


def fast_body(
    tokens,
    attn_gain,
    w_query,
    w_key,
    w_value,
    w_out,
    mlp_gain,
    w_gate,
    w_up,
    w_down,
    block_ids,
    positions,
    cotangent,
):
    rows, width = tokens.shape
    token_rows = 8 * rows
    f32, bf16 = jnp.float32, jnp.bfloat16

    note = jnp.concatenate(
        [
            positions.astype(f32).reshape(2, rows),
            block_ids.astype(f32).reshape(2, rows),
            attn_gain.astype(f32)[None],
            mlp_gain.astype(f32)[None],
            jnp.zeros((2, rows), f32),
        ]
    )
    inv_freqs = jnp.asarray((rope_base ** (-2.0 * np.arange(HD // 2) / HD)).astype(np.float32))
    (
        keys_values, normed, qkv_w, out_w, notes, gain_attn, gain_mlp, cos_table, sine_table, scaled_query, attended, attended_low,
        log_total, cot_all, gate_w, up_w,
    ) = front(tokens, cotangent, note, inv_freqs[None], w_query, w_key, w_value, w_out, w_gate, w_up)
    out_w = out_w.reshape(HD, width)
    hidden, active, mlp_part, grad_branch, grad_hidden, mlp_term, gate_quarter, up_quarter = core(
        attended_low, out_w, gate_w, up_w, w_down, tokens, gain_mlp, cotangent, cot_all
    )

    side_grad, grad_query, output, gate_grad, up_grad, out_grad = attend_back(
        scaled_query,
        keys_values,
        grad_branch,
        mlp_part,
        hidden,
        out_w,
        attended,
        attended_low,
        log_total,
        notes,
        cos_table,
        sine_table,
        gate_quarter,
        up_quarter,
        w_out.shape[0],
    )
    tokens_grad, gain_grads, down_grad, query_grad, key_grad, value_grad = close(
        normed,
        qkv_w,
        active,
        cot_all,
        grad_query,
        side_grad,
        grad_hidden,
        tokens,
        gain_attn,
        mlp_term,
    )
    arrays = (output, tokens_grad, query_grad, key_grad, value_grad, out_grad, gate_grad, up_grad, down_grad)
    output, tokens_grad, query_grad, key_grad, value_grad, out_grad, gate_grad, up_grad, down_grad = widen(
        arrays, (bf16, bf16) + (f32,) * 7
    )
    return (
        output,
        tokens_grad,
        gain_grads[0],
        query_grad,
        key_grad,
        value_grad,
        out_grad,
        gain_grads[1],
        gate_grad,
        up_grad,
        down_grad,
    )


def solution(mesh):
    placed = (
        P(("blk", "head"), None),
        P("blk"),
        P("blk", "head"),
        P("blk", "head"),
        P("blk", "head"),
        P(("head", "blk"), None),
        P("blk"),
        P("blk", "head"),
        P("blk", "head"),
        P(("head", "blk"), None),
        P("blk"),
        P("blk"),
        P(("blk", "head"), None),
    )
    fits = mesh.shape["blk"] == 16 and mesh.shape["head"] == 2
    return jax.shard_map(
        fast_body if fits else body,
        mesh=mesh,
        in_specs=placed,
        out_specs=(
            P(("blk", "head"), None),
            P(("blk", "head"), None),
            P("blk"),
            P("blk", "head"),
            P("blk", "head"),
            P("blk", "head"),
            P(("head", "blk"), None),
            P("blk"),
            P("blk", "head"),
            P("blk", "head"),
            P(("head", "blk"), None),
        ),
        check_vma=False,
    )
```
